32 devices in a mesh: groups: 2 (over y), fsdp: 4 (over z), tp: 2 (over x), rep: 2 (over core).
Axes of the slice: x: 2, y: 2, z: 4, core: 2. Of those that a mesh axis runs over, the one named last changes fastest.
Arguments:
- hidden: bfloat16 [1280, 16384], P(('groups', 'tp'), ('fsdp', 'rep')), parts along dimension 0, may hold values from -6 to 6
- w_query: bfloat16 [16384, 16384], P(('fsdp', 'rep'), 'tp'), may hold values from -0.046875 to 0.046875
- w_key: bfloat16 [16384, 1024], P(('fsdp', 'rep'), 'tp'), may hold values from -0.046875 to 0.046875
- w_value: bfloat16 [16384, 1024], P(('fsdp', 'rep'), 'tp'), may hold values from -0.046875 to 0.046875
- canary_rows: int32 [1280], P('groups'), parts along dimension 0, may hold values from 0 to 639, each once
- positions: int32 [1280], P('groups'), parts along dimension 0, may hold values from 0 to 4095
Outputs:
- scores: bfloat16 [2, 64, 1280, 640], P('tp', 'fsdp', 'groups'), parts along dimension 2
- values: bfloat16 [1280, 1024], P('groups', 'tp'), parts along dimension 0
The draws below stay inside these ranges and needn't reach their ends.
There are 2 independent parts, one for each index of `groups`. The reference program is written for one: setup_inputs(seed, part) draws one part's arguments, and reference() takes and returns one part's arrays. A program takes and returns all parts, laid end to end along the dimension named above; an argument that names none is the same for every part. Nothing has to cross between parts.
All inputs are finite; a program needn't handle non-finite values.
Results may differ from the reference program's by a relative error of at most 0.0058.
Values may be sent and summed in bfloat16 or wider, within the bound.
No kernel may reach another device: no remote copies, remote signals or barrier semaphores. Data moves between devices by JAX's collectives and lax.ppermute only.
A program may use at most 256 MiB of HBM per device.

```python
import math
import jax
import jax.numpy as jnp

D = 16384
HQ = 128
KV = 8
DH = 128
R = 640
N_TP = 2


def place_ends(entries, key, smallest, high):
    longest = entries.shape.index(max(entries.shape))
    spots = []
    for shift in (0, 1):
        where = [jax.random.randint(jax.random.fold_in(key, axis), (), 0, length) for axis, length in enumerate(entries.shape)]
        where[longest] = (where[longest] + shift) % entries.shape[longest]
        spots.append(tuple(where))
    return entries.at[spots[0]].set(smallest).at[spots[1]].set(high)


def steps_of(own_key, extent, split, smallest, high):
    def one(position, blocks):
        heights = jax.random.uniform(jax.random.fold_in(jax.random.fold_in(own_key, 6), position), (blocks,), jnp.float32, smallest / len(split), high / len(split))
        return jnp.repeat(jnp.exp(heights), extent[position] // blocks).reshape((-1,) + (1,) * (len(extent) - position - 1))

    gain = one(*split[0])
    for cut in split[1:]:
        gain = gain * one(*cut)
    return gain


def scatter_about(own_key, shape, deviation, bound, split=(), kind=jnp.bfloat16):
    gain = steps_of(own_key, shape, split, -0.22, 0.18) if split else 1.0
    drawn = jax.random.normal(own_key, shape, jnp.float32) * deviation * gain
    return jnp.minimum(jnp.maximum(drawn, -bound), bound).astype(kind)


def setup_inputs(seed: int = 0, part: int = 0) -> dict:
    key_of = jax.random.split(jax.random.key(seed), 7)
    part_keys = jax.random.split(jax.random.fold_in(key_of[6], part), 7)
    return {
        "hidden": scatter_about(part_keys[0], (R, D), 1.0, 6.0, ((0, 2), (1, 8))),
        "w_query": scatter_about(key_of[1], (D, HQ * DH), D ** -0.5, 0.046875, ((0, 8), (1, 2))),
        "w_key": scatter_about(key_of[2], (D, KV * DH), D ** -0.5, 0.046875, ((0, 8), (1, 2))),
        "w_value": scatter_about(key_of[3], (D, KV * DH), D ** -0.5, 0.046875, ((0, 8), (1, 2))),
        "canary_rows": jax.random.permutation(part_keys[4], R).astype(jnp.int32),
        "positions": place_ends(jax.random.randint(part_keys[5], (R,), 0, 4096), jax.random.fold_in(part_keys[5], 1), 0, 4095).astype(jnp.int32),
    }


def rope_tables(positions, width):
    half = width // 2
    expo = jnp.arange(half, dtype=jnp.float32) * (2.0 / width)
    freq = jnp.power(jnp.float32(500000.0), -expo)
    wavelen = 2.0 * math.pi / freq
    smooth = (8192.0 / wavelen - 1.0) / 3.0
    mixed = (1.0 - smooth) * freq / 8.0 + smooth * freq
    freq = jnp.where(wavelen > 8192.0, freq / 8.0, jnp.where(wavelen < 2048.0, freq, mixed))
    angle = positions.astype(jnp.float32)[:, None] * freq[None, :]
    return jnp.cos(angle)[:, None, :], jnp.sin(angle)[:, None, :]


def rotate(heads, cosine, sine):
    half = heads.shape[-1] // 2
    first = heads[..., :half]
    second = heads[..., half:]
    return jnp.concatenate([first * cosine - second * sine, second * cosine + first * sine], axis=-1)


def reference(hidden, w_query, w_key, w_value, canary_rows, positions):
    chosen = jnp.take(hidden, canary_rows.astype(jnp.int32), axis=0)
    query = jnp.dot(chosen, w_query, preferred_element_type=jnp.float32).reshape(R, HQ, DH)
    key = jnp.dot(chosen, w_key, preferred_element_type=jnp.float32).reshape(R, KV, DH)
    values = jnp.dot(chosen, w_value, preferred_element_type=jnp.float32).astype(jnp.bfloat16)
    cosine, sine = rope_tables(positions, DH)
    query_rot = rotate(query, cosine, sine).astype(jnp.bfloat16)
    key_rot = rotate(key, cosine, sine).astype(jnp.bfloat16)
    key_wide = jnp.repeat(key_rot, HQ // KV, axis=1)
    scale = DH ** -0.5
    products = jnp.einsum("ihd,jhd->hij", query_rot.astype(jnp.float32), key_wide.astype(jnp.float32))
    scores = (products * scale).astype(jnp.bfloat16).reshape(N_TP, HQ // N_TP, R, R)
    return scores, values
```

```python
import math

import jax
import jax.numpy as jnp
from jax import lax
from jax.sharding import PartitionSpec as P

HQ = 128
KV = 8
DH = 128


def rope_tables(positions, width):
    half = width // 2
    expo = jnp.arange(half, dtype=jnp.float32) * (2.0 / width)
    freq = jnp.power(jnp.float32(500000.0), -expo)
    wavelen = 2.0 * math.pi / freq
    smooth = (8192.0 / wavelen - 1.0) / 3.0
    mixed = (1.0 - smooth) * freq / 8.0 + smooth * freq
    freq = jnp.where(wavelen > 8192.0, freq / 8.0, jnp.where(wavelen < 2048.0, freq, mixed))
    angle = positions.astype(jnp.float32)[:, None] * freq[None, :]
    return (jnp.cos(angle)[:, None, :], jnp.sin(angle)[:, None, :])


def rotate(heads, cosine, sine):
    half = heads.shape[-1] // 2
    first = heads[..., :half]
    second = heads[..., half:]
    return jnp.concatenate(
        [first * cosine - second * sine, second * cosine + first * sine], axis=-1
    )


def body(hidden, w_query, w_key, w_value, canary_rows, positions):
    shards = lax.axis_size("fsdp")
    findex = lax.axis_index("fsdp")
    cols = w_query.shape[1]
    head_cols = cols // shards
    kv_cols = w_key.shape[1]
    rows_all = lax.all_gather(hidden, "tp", axis=0, tiled=True)
    rows = rows_all.shape[0]
    key_part = jnp.dot(rows_all, w_key, preferred_element_type=jnp.float32)
    value_part = jnp.dot(rows_all, w_value, preferred_element_type=jnp.float32)
    query_part = jnp.dot(rows_all, w_query, preferred_element_type=jnp.float32)
    rep = lax.axis_size("rep")
    rindex = lax.axis_index("rep")
    own = rows // rep
    query_bf = query_part.astype(jnp.bfloat16).reshape(rep, own, cols)
    mine = lax.dynamic_index_in_dim(query_bf, rindex, 0, keepdims=False).astype(jnp.float32)
    for step in range(1, rep):
        give = lax.dynamic_index_in_dim(query_bf, (rindex + step) % rep, 0, keepdims=False)
        got = lax.ppermute(give, "rep", [(i, (i + step) % rep) for i in range(rep)])
        mine = mine + got.astype(jnp.float32)
    pieces = mine.astype(jnp.bfloat16).reshape(own, shards, head_cols)
    pieces = pieces.transpose(1, 0, 2)
    landed = lax.all_to_all(pieces, "fsdp", split_axis=0, concat_axis=0, tiled=True)
    query_own = jnp.sum(landed.astype(jnp.float32), axis=0).astype(jnp.bfloat16)
    query_sum = lax.all_gather(query_own, "rep", axis=0, tiled=True).astype(jnp.float32)
    heads_here = head_cols // DH
    cosine, sine = rope_tables(positions, DH)
    key_sum, value_sum = lax.psum((key_part, value_part), ("fsdp", "rep"))
    key_sel = jnp.take(key_sum, canary_rows, axis=0).reshape(rows, kv_cols // DH, DH)
    values = jnp.take(value_sum, canary_rows, axis=0).astype(jnp.bfloat16)
    key_rot = rotate(key_sel, cosine, sine).astype(jnp.bfloat16)
    query_sel = jnp.take(query_sum, canary_rows, axis=0).reshape(rows, heads_here, DH)
    query_rot = rotate(query_sel, cosine, sine).astype(jnp.bfloat16)
    kv_local = (findex * heads_here + jnp.arange(heads_here, dtype=jnp.int32)) // (HQ // KV)
    key_heads = jnp.take(key_rot, kv_local, axis=1)
    products = jnp.einsum("ihd,jhd->hij", query_rot, key_heads, preferred_element_type=jnp.float32)
    scores = (products * DH ** (-0.5)).astype(jnp.bfloat16).reshape(1, heads_here, rows, rows)
    return (scores, values)


def solution(mesh):
    in_specs = (
        P(("groups", "tp"), ("fsdp", "rep")),
        P(("fsdp", "rep"), "tp"),
        P(("fsdp", "rep"), "tp"),
        P(("fsdp", "rep"), "tp"),
        P("groups"),
        P("groups"),
    )
    out_specs = (P("tp", "fsdp", "groups", None), P("groups", "tp"))
    return jax.shard_map(body, mesh=mesh, in_specs=in_specs, out_specs=out_specs, check_vma=False)
```

```python
import functools
import math

import jax
import jax.numpy as jnp
from jax import lax
from jax.experimental import pallas as pl
from jax.experimental.pallas import tpu as pltpu
from jax.sharding import PartitionSpec as P

HQ = 128
KV = 8
DH = 128
VMEM_BYTES = 40 * 1024 * 1024


def rope_tables(positions):
    half = DH // 2
    expo = jnp.arange(half, dtype=jnp.float32) * (2.0 / DH)
    freq = jnp.power(jnp.float32(500000.0), -expo)
    wavelen = 2.0 * math.pi / freq
    smooth = (8192.0 / wavelen - 1.0) / 3.0
    mixed = (1.0 - smooth) * freq / 8.0 + smooth * freq
    freq = jnp.where(wavelen > 8192.0, freq / 8.0, jnp.where(wavelen < 2048.0, freq, mixed))
    angle = positions.astype(jnp.float32)[:, None] * freq[None, :]
    cosine, sine = jnp.cos(angle), jnp.sin(angle)
    return jnp.concatenate([cosine, cosine], axis=1), jnp.concatenate([-sine, sine], axis=1)


def split_rows(place_ref, result, keep_ref, give_ref):
    half = result.shape[0] // 2
    first = place_ref[0] == 0
    top, low = result[:half], result[half:]
    keep_ref[0] = jnp.where(first, top, low).astype(keep_ref.dtype)
    give_ref[0] = jnp.where(first, low, top).astype(give_ref.dtype)


def query_kernel(place_ref, x_ref, w_ref, keep_ref, give_ref):
    result = jnp.dot(x_ref[...], w_ref[...], preferred_element_type=jnp.float32)
    split_rows(place_ref, result, keep_ref, give_ref)


def project_query(rindex, findex, slots, x, w, cols):
    rows, depth = x.shape
    tile = min(512, cols)
    tiles = cols // tile
    place = jnp.stack([rindex] + [findex ^ slot for slot in slots]).astype(jnp.int32)
    out = pl.BlockSpec((1, rows // 2, tile), lambda s, j, place: (s, 0, j))
    shape = (len(slots), rows // 2, cols)
    return pl.pallas_call(
        query_kernel,
        grid_spec=pltpu.PrefetchScalarGridSpec(
            num_scalar_prefetch=1,
            grid=(len(slots), tiles),
            in_specs=[
                pl.BlockSpec((rows, depth), lambda s, j, place: (0, 0)),
                pl.BlockSpec((depth, tile), lambda s, j, place: (0, place[1 + s] * tiles + j)),
            ],
            out_specs=[out, out],
        ),
        out_shape=[
            jax.ShapeDtypeStruct(shape, jnp.float32),
            jax.ShapeDtypeStruct(shape, jnp.bfloat16),
        ],
        compiler_params=pltpu.CompilerParams(vmem_limit_bytes=VMEM_BYTES),
        cost_estimate=pl.CostEstimate(
            flops=2 * rows * depth * cols * len(slots),
            bytes_accessed=2 * depth * cols * len(slots),
            transcendentals=0,
        ),
        name="query_products",
    )(place, x, w)


def pair_kernel(place_ref, x_ref, wk_ref, wv_ref, keep_ref, give_ref):
    weights = jnp.concatenate([wk_ref[...], wv_ref[...]], axis=1)
    result = jnp.dot(x_ref[...], weights, preferred_element_type=jnp.float32)
    split_rows(place_ref, result, keep_ref, give_ref)


def project_pair(rindex, findex, slots, x, w_key, w_value):
    rows, depth = x.shape
    place = jnp.stack([rindex] + [findex ^ slot for slot in slots]).astype(jnp.int32)
    weight = pl.BlockSpec((depth, DH), lambda s, place: (0, place[1 + s]))
    out = pl.BlockSpec((1, rows // 2, 2 * DH), lambda s, place: (s, 0, 0))
    shape = jax.ShapeDtypeStruct((len(slots), rows // 2, 2 * DH), jnp.float32)
    return pl.pallas_call(
        pair_kernel,
        grid_spec=pltpu.PrefetchScalarGridSpec(
            num_scalar_prefetch=1,
            grid=(len(slots),),
            in_specs=[pl.BlockSpec((rows, depth), lambda s, place: (0, 0)), weight, weight],
            out_specs=[out, out],
        ),
        out_shape=[shape, shape],
        compiler_params=pltpu.CompilerParams(vmem_limit_bytes=VMEM_BYTES),
        cost_estimate=pl.CostEstimate(
            flops=4 * rows * depth * DH * len(slots),
            bytes_accessed=4 * depth * DH * len(slots),
            transcendentals=0,
        ),
        name="key_value_products",
    )(place, x, w_key, w_value)


def rotate_kernel(cos_ref, sin_ref, *refs):
    *terms, out_ref = refs
    total = terms[0][...].astype(jnp.float32)
    for term in terms[1:]:
        total = total + term[...].astype(jnp.float32)
    cosine, sine = cos_ref[...], sin_ref[...]
    for head in range(total.shape[1] // DH):
        part = total[:, head * DH : (head + 1) * DH]
        turned = pltpu.roll(part, DH // 2, axis=1)
        out_ref[:, head * DH : (head + 1) * DH] = (part * cosine + turned * sine).astype(out_ref.dtype)


def sum_and_rotate(cosine, sine, terms):
    rows, cols = terms[0].shape
    tile = min(512, cols)
    table = pl.BlockSpec((rows, DH), lambda j: (0, 0))
    block = pl.BlockSpec((rows, tile), lambda j: (0, j))
    return pl.pallas_call(
        rotate_kernel,
        grid=(cols // tile,),
        in_specs=[table, table] + [block] * len(terms),
        out_specs=block,
        out_shape=jax.ShapeDtypeStruct((rows, cols), jnp.bfloat16),
        compiler_params=pltpu.CompilerParams(vmem_limit_bytes=VMEM_BYTES),
        cost_estimate=pl.CostEstimate(
            flops=8 * rows * cols, bytes_accessed=12 * rows * cols, transcendentals=0
        ),
        name="sum_and_rotate",
    )(cosine, sine, *terms)


def score_kernel(canary_ref, ids_ref, key_ref, *refs):
    *queries, out_ref, order_ref, key_t_ref = refs

    @pl.when(pl.program_id(0) == 0)
    def _():
        order = jnp.where(canary_ref[...] == ids_ref[...], 1.0, 0.0).astype(jnp.bfloat16)
        order_ref[...] = order
        keys = jnp.dot(order, key_ref[...], preferred_element_type=jnp.float32)
        key_t_ref[...] = keys.T.astype(jnp.bfloat16)

    stacked = jnp.concatenate([query[...] for query in queries], axis=0)
    chosen = jnp.dot(order_ref[...], stacked, preferred_element_type=jnp.float32).astype(jnp.bfloat16)
    for head in range(stacked.shape[1] // DH):
        products = jnp.dot(
            chosen[:, head * DH : (head + 1) * DH], key_t_ref[...], preferred_element_type=jnp.float32
        )
        out_ref[0, head] = (products * DH ** (-0.5)).astype(out_ref.dtype)


def score_heads(canary_rows, ids, key, queries):
    rows = key.shape[0]
    part, cols = queries[0].shape
    heads = cols // DH
    step = 2 if heads % 2 == 0 else 1
    return pl.pallas_call(
        score_kernel,
        grid=(heads // step,),
        in_specs=[
            pl.BlockSpec((rows, 1), lambda j: (0, 0)),
            pl.BlockSpec((1, rows), lambda j: (0, 0)),
            pl.BlockSpec((rows, DH), lambda j: (0, 0)),
        ]
        + [pl.BlockSpec((part, step * DH), lambda j: (0, j))] * len(queries),
        out_specs=pl.BlockSpec((1, step, rows, rows), lambda j: (0, j, 0, 0)),
        out_shape=jax.ShapeDtypeStruct((1, heads, rows, rows), jnp.bfloat16),
        scratch_shapes=[pltpu.VMEM((rows, rows), jnp.bfloat16), pltpu.VMEM((DH, rows), jnp.bfloat16)],
        compiler_params=pltpu.CompilerParams(vmem_limit_bytes=VMEM_BYTES),
        cost_estimate=pl.CostEstimate(
            flops=4 * rows * rows * cols, bytes_accessed=2 * rows * rows * heads, transcendentals=0
        ),
        name="score_heads",
    )(canary_rows.reshape(rows, 1), ids.reshape(1, rows), key, *queries)


def body(hidden, w_query, w_key, w_value, canary_rows, positions):
    shards = lax.axis_size("fsdp")
    findex = lax.axis_index("fsdp")
    tps = lax.axis_size("tp")
    tindex = lax.axis_index("tp")
    rindex = lax.axis_index("rep")
    local, depth = hidden.shape
    half = local // 2
    rows = local * tps
    head_cols = w_query.shape[1] // shards
    heads_here = head_cols // DH
    group = HQ // KV
    assert shards & (shards - 1) == 0 and lax.axis_size("rep") == 2

    def swap(x, bit):
        return lax.ppermute(x, "fsdp", [(i, i ^ bit) for i in range(shards)])

    def other_core(x):
        return lax.ppermute(x, "rep", [(0, 1), (1, 0)])

    def low(x):
        return x.astype(jnp.bfloat16)

    far = [x for x in range(3, shards, 2)]
    even = [x for x in range(0, shards, 2)]

    def finish(own_terms, live):
        terms = list(own_terms)
        bit = 2
        while bit < shards:
            sent = [x for x in sorted(live) if x & bit]
            landed = swap(jnp.stack([low(live[x]) for x in sent]), bit)
            for k, x in enumerate(sent):
                if x == bit:
                    terms.append(landed[k])
                else:
                    live[x ^ bit] = live[x ^ bit] + landed[k].astype(jnp.float32)
                del live[x]
            bit *= 2
        return terms

    blocks = [hidden] + [
        lax.ppermute(hidden, "tp", [(i, (i - b) % tps) for i in range(tps)]) for b in range(1, tps)
    ]

    block_ids = ((tindex + jnp.arange(tps, dtype=jnp.int32)) % tps * local)[:, None]
    own_ids = (block_ids + rindex * half + jnp.arange(half, dtype=jnp.int32)[None]).reshape(-1)
    other_ids = (block_ids + (1 - rindex) * half + jnp.arange(half, dtype=jnp.int32)[None]).reshape(-1)
    ids = jnp.concatenate([own_ids, other_ids])
    own_positions = jnp.sum(
        jnp.where(own_ids[:, None] == canary_rows[None, :], positions[None, :], 0), axis=1
    )
    cosine, sine = rope_tables(own_positions)

    queries = []
    for b, block in enumerate(blocks):
        far_keep, far_give = project_query(rindex, findex, far, block, w_query, head_cols)
        far_got = other_core(far_give)
        near_keep, near_give = project_query(rindex, findex, [1], block, w_query, head_cols)
        far_landed = swap(low(far_keep + far_got.astype(jnp.float32)), 1)
        near_got = other_core(near_give)
        even_keep, even_give = project_query(rindex, findex, even[1:] + [0], block, w_query, head_cols)
        near_landed = swap(low(near_keep + near_got.astype(jnp.float32)), 1)
        even_got = other_core(even_give)
        live = {
            x: even_keep[k] + even_got[k].astype(jnp.float32) + far_landed[k].astype(jnp.float32)
            for k, x in enumerate(even[1:])
        }
        terms = finish([even_keep[-1], even_got[-1], near_landed[0]], live)
        table = slice(b * half, (b + 1) * half)
        queries.append(sum_and_rotate(cosine[table], sine[table], terms))

    if heads_here == group:
        kept, got = [], []
        for block in blocks:
            keep, give = project_pair(rindex, findex, list(range(shards)), block, w_key, w_value)
            kept.append(keep)
            got.append(other_core(give))
        pair = jnp.concatenate([k + g for k, g in zip(kept, got)], axis=1)
        odd_landed = swap(low(pair[1::2]), 1).astype(jnp.float32)
        live = {x: pair[x] + odd_landed[x // 2] for x in even}
        own = live.pop(0)
        for term in finish([], live):
            own = own + term.astype(jnp.float32)
        key_own, value_own = own[:, :DH], low(own[:, DH:])
        value_both = jnp.concatenate([value_own, other_core(value_own)], axis=0)
        value_rows = lax.all_gather(value_both, "fsdp", axis=1, tiled=True)
    else:
        x = jnp.concatenate(blocks, axis=0)
        key_sum, value_sum = lax.psum(
            (
                jnp.dot(x, w_key, preferred_element_type=jnp.float32),
                jnp.dot(x, w_value, preferred_element_type=jnp.float32),
            ),
            ("fsdp", "rep"),
        )

        def of_core(y, core):
            parts = y.reshape(tps, 2, half, -1)
            return lax.dynamic_index_in_dim(parts, core, 1, keepdims=False).reshape(tps * half, -1)

        mine = lax.dynamic_slice_in_dim(key_sum, findex * heads_here // group * DH, DH, 1)
        key_own = of_core(mine, rindex)
        value_rows = low(jnp.concatenate([of_core(value_sum, rindex), of_core(value_sum, 1 - rindex)]))

    key_rot = sum_and_rotate(cosine, sine, [key_own])
    key_both = jnp.concatenate([key_rot, other_core(key_rot)], axis=0)
    order = (canary_rows[:, None] == ids[None, :]).astype(jnp.bfloat16)
    values = low(jnp.dot(order, value_rows, preferred_element_type=jnp.float32))
    scores = score_heads(canary_rows, ids, key_both, queries + [other_core(q) for q in queries])
    return (scores, values)


def solution(mesh):
    in_specs = (
        P(("groups", "tp"), ("fsdp", "rep")),
        P(("fsdp", "rep"), "tp"),
        P(("fsdp", "rep"), "tp"),
        P(("fsdp", "rep"), "tp"),
        P("groups"),
        P("groups"),
    )
    out_specs = (P("tp", "fsdp", "groups", None), P("groups", "tp"))
    return jax.shard_map(body, mesh=mesh, in_specs=in_specs, out_specs=out_specs, check_vma=False)
```

```python
import functools
import math

import jax
import jax.numpy as jnp
from jax import lax
from jax.experimental import pallas as pl
from jax.experimental.pallas import tpu as pltpu
from jax.sharding import PartitionSpec as P

HQ = 128
KV = 8
DH = 128
VMEM_BYTES = 26 * 1024 * 1024
LIGHT = pl.CostEstimate(flops=1000, bytes_accessed=1000, transcendentals=0)


def rope_tables(positions):
    half = DH // 2
    expo = jnp.arange(half, dtype=jnp.float32) * (2.0 / DH)
    freq = jnp.power(jnp.float32(500000.0), -expo)
    wavelen = 2.0 * math.pi / freq
    smooth = (8192.0 / wavelen - 1.0) / 3.0
    mixed = (1.0 - smooth) * freq / 8.0 + smooth * freq
    freq = jnp.where(wavelen > 8192.0, freq / 8.0, jnp.where(wavelen < 2048.0, freq, mixed))
    angle = positions.astype(jnp.float32)[:, None] * freq[None, :]
    cosine, sine = jnp.cos(angle), jnp.sin(angle)
    return jnp.concatenate([cosine, cosine], axis=1), jnp.concatenate([-sine, sine], axis=1)


def ordered_rows(place_ref, x_ref, rows_ref):
    half = x_ref.shape[0] // 2
    core = place_ref[0]
    rows_ref[:half] = x_ref[pl.ds(pl.multiple_of(core * half, 16), half)]
    rows_ref[half:] = x_ref[pl.ds(pl.multiple_of((1 - core) * half, 16), half)]


def query_kernel(pieces, width, place_ref, x_ref, w_ref, *refs):
    keep_ref, *give_refs, rows_ref = refs[-2 - pieces :]
    tile = pl.program_id(1)
    each = keep_ref.shape[2] // width

    @pl.when((pl.program_id(0) == 0) & (tile == 0))
    def _():
        ordered_rows(place_ref, x_ref, rows_ref)

    result = jnp.dot(rows_ref[...], w_ref[...], preferred_element_type=jnp.float32)
    half = result.shape[0] // 2
    keep_ref[0] = result[:half]
    for j, give_ref in enumerate(give_refs):

        @pl.when(tile == j // each)
        def _():
            start = j % each * width
            give_ref[0] = result[half:, start : start + width].astype(give_ref.dtype)


def project_query(rindex, findex, slots, x, w, cols, tile, width, after=()):
    rows, depth = x.shape
    tiles = cols // tile
    place = jnp.stack([rindex] + [findex ^ slot for slot in slots]).astype(jnp.int32)
    pieces = cols // width
    outs = pl.pallas_call(
        functools.partial(query_kernel, pieces, width),
        grid_spec=pltpu.PrefetchScalarGridSpec(
            num_scalar_prefetch=1,
            grid=(len(slots), tiles),
            in_specs=[
                pl.BlockSpec((rows, depth), lambda s, j, place: (0, 0)),
                pl.BlockSpec((depth, tile), lambda s, j, place: (0, place[1 + s] * tiles + j)),
            ]
            + [pl.BlockSpec(memory_space=pl.ANY)] * len(after),
            out_specs=[pl.BlockSpec((1, rows // 2, tile), lambda s, j, place: (s, 0, j))]
            + [pl.BlockSpec((1, rows // 2, width), lambda s, j, place: (s, 0, 0))] * pieces,
            scratch_shapes=[pltpu.VMEM((rows, depth), x.dtype)],
        ),
        out_shape=[jax.ShapeDtypeStruct((len(slots), rows // 2, cols), jnp.float32)]
        + [jax.ShapeDtypeStruct((len(slots), rows // 2, width), jnp.bfloat16)] * pieces,
        compiler_params=pltpu.CompilerParams(vmem_limit_bytes=VMEM_BYTES),
        cost_estimate=LIGHT,
        name="query_products",
    )(place, x, w, *after)
    return outs[0], outs[1:]


def pair_kernel(place_ref, x_ref, wk_ref, wv_ref, *refs):
    keep_ref, give_ref, rows_ref = refs[-3:]

    @pl.when(pl.program_id(0) == 0)
    def _():
        ordered_rows(place_ref, x_ref, rows_ref)

    weights = jnp.concatenate([wk_ref[...], wv_ref[...]], axis=1)
    result = jnp.dot(rows_ref[...], weights, preferred_element_type=jnp.float32)
    half = result.shape[0] // 2
    keep_ref[0] = result[:half]
    give_ref[0] = result[half:].astype(give_ref.dtype)


def project_pair(rindex, findex, slots, x, w_key, w_value, after=()):
    rows, depth = x.shape
    place = jnp.stack([rindex] + [findex ^ slot for slot in slots]).astype(jnp.int32)
    weight = pl.BlockSpec((depth, DH), lambda s, place: (0, place[1 + s]))
    out = pl.BlockSpec((1, rows // 2, 2 * DH), lambda s, place: (s, 0, 0))
    shape = jax.ShapeDtypeStruct((len(slots), rows // 2, 2 * DH), jnp.float32)
    return pl.pallas_call(
        pair_kernel,
        grid_spec=pltpu.PrefetchScalarGridSpec(
            num_scalar_prefetch=1,
            grid=(len(slots),),
            in_specs=[pl.BlockSpec((rows, depth), lambda s, place: (0, 0)), weight, weight]
            + [pl.BlockSpec(memory_space=pl.ANY)] * len(after),
            out_specs=[out, out],
            scratch_shapes=[pltpu.VMEM((rows, depth), x.dtype)],
        ),
        out_shape=[shape, jax.ShapeDtypeStruct(shape.shape, jnp.bfloat16)],
        compiler_params=pltpu.CompilerParams(vmem_limit_bytes=VMEM_BYTES),
        cost_estimate=LIGHT,
        name="key_value_products",
    )(place, x, w_key, w_value, *after)


def add_kernel(tiles, extra, *refs):
    keep_ref, give_refs, out_ref = refs[0], refs[1 : 1 + tiles], refs[-1]
    for j, give_ref in enumerate(give_refs):

        @pl.when(pl.program_id(1) == j)
        def _():
            total = keep_ref[0] + give_ref[0].astype(jnp.float32)
            if extra:
                total = total + refs[1 + tiles][0].astype(jnp.float32)
            out_ref[0] = total.astype(out_ref.dtype)


def add_rows(keep, gots, count, landed=(), after=()):
    _, rows, cols = keep.shape
    tiles = len(gots)
    tile = cols // tiles
    full = pl.BlockSpec((1, rows, tile), lambda s, j: (s, 0, j))
    return pl.pallas_call(
        functools.partial(add_kernel, tiles, len(landed)),
        grid=(count, tiles),
        in_specs=[full]
        + [pl.BlockSpec((1, rows, tile), lambda s, j: (s, 0, 0))] * tiles
        + [full] * len(landed)
        + [pl.BlockSpec(memory_space=pl.ANY)] * len(after),
        out_specs=full,
        out_shape=jax.ShapeDtypeStruct((count, rows, cols), jnp.bfloat16),
        compiler_params=pltpu.CompilerParams(vmem_limit_bytes=VMEM_BYTES),
        cost_estimate=LIGHT,
        name="add_rows",
    )(keep, *gots, *landed, *after)


def rotate_kernel(count, pieces, cos_ref, sin_ref, *refs):
    terms, gots, out_ref = refs[:count], refs[count : count + pieces], refs[-1]
    total = terms[0][0].astype(jnp.float32)
    for term in terms[1:]:
        total = total + term[0].astype(jnp.float32)
    cosine, sine = cos_ref[...], sin_ref[...]

    def write(total):
        for head in range(total.shape[1] // DH):
            part = total[:, head * DH : (head + 1) * DH]
            turned = pltpu.roll(part, DH // 2, axis=1)
            value = part * cosine + turned * sine
            out_ref[:, head * DH : (head + 1) * DH] = value.astype(out_ref.dtype)

    if not gots:
        write(total)
    for j, got in enumerate(gots):

        @pl.when(pl.program_id(0) == j)
        def _():
            write(total + got[0].astype(jnp.float32))


def sum_and_rotate(cosine, sine, terms, gots, cols, after=()):
    rows = cosine.shape[0]
    slot_of_gots, gots = gots
    tile = cols // max(1, len(gots))
    table = pl.BlockSpec((rows, DH), lambda j: (0, 0))

    def block(slot, start):
        return pl.BlockSpec((1, rows, tile), lambda j: (slot, 0, start // tile + j))

    return pl.pallas_call(
        functools.partial(rotate_kernel, len(terms), len(gots)),
        grid=(cols // tile,),
        in_specs=[table, table]
        + [block(slot, start) for _, slot, start in terms]
        + [pl.BlockSpec((1, rows, tile), lambda j: (slot_of_gots, 0, 0))] * len(gots)
        + [pl.BlockSpec(memory_space=pl.ANY)] * len(after),
        out_specs=pl.BlockSpec((rows, tile), lambda j: (0, j)),
        out_shape=jax.ShapeDtypeStruct((rows, cols), jnp.bfloat16),
        compiler_params=pltpu.CompilerParams(vmem_limit_bytes=VMEM_BYTES),
        cost_estimate=LIGHT,
        name="sum_and_rotate",
    )(cosine, sine, *[term for term, _, _ in terms], *gots, *after)


def split_kernel(count, cos_ref, sin_ref, *refs):
    terms, (key_ref, value_ref) = refs[:count], refs[-2:]
    total = terms[0][0].astype(jnp.float32)
    for term in terms[1:]:
        total = total + term[0].astype(jnp.float32)
    key, value = total[:, :DH], total[:, DH:]
    turned = pltpu.roll(key, DH // 2, axis=1)
    key_ref[...] = (key * cos_ref[...] + turned * sin_ref[...]).astype(key_ref.dtype)
    value_ref[0] = value.astype(value_ref.dtype)


def split_and_rotate(cosine, sine, terms, after):
    rows = cosine.shape[0]
    table = pl.BlockSpec((rows, DH), lambda j: (0, 0))
    return pl.pallas_call(
        functools.partial(split_kernel, len(terms)),
        grid=(1,),
        in_specs=[table, table]
        + [pl.BlockSpec((1, rows, 2 * DH), lambda j: (0, 0, 0))] * len(terms)
        + [pl.BlockSpec(memory_space=pl.ANY)] * len(after),
        out_specs=[table, pl.BlockSpec((1, rows, DH), lambda j: (0, 0, 0))],
        out_shape=[
            jax.ShapeDtypeStruct((rows, DH), jnp.bfloat16),
            jax.ShapeDtypeStruct((1, rows, DH), jnp.bfloat16),
        ],
        compiler_params=pltpu.CompilerParams(vmem_limit_bytes=VMEM_BYTES),
        cost_estimate=LIGHT,
        name="split_and_rotate",
    )(cosine, sine, *terms, *after)


def prepare_kernel(canary_ref, ids_ref, own_ref, other_ref, order_ref, key_t_ref):
    order = jnp.where(canary_ref[...] == ids_ref[...], 1.0, 0.0).astype(jnp.bfloat16)
    order_ref[...] = order
    key = jnp.concatenate([own_ref[...], other_ref[...]], axis=0)
    key_t_ref[...] = jnp.dot(order, key, preferred_element_type=jnp.float32).T.astype(jnp.bfloat16)


def prepare(canary_rows, ids, own, other):
    rows = ids.shape[0]
    return pl.pallas_call(
        prepare_kernel,
        out_shape=[
            jax.ShapeDtypeStruct((rows, rows), jnp.bfloat16),
            jax.ShapeDtypeStruct((DH, rows), jnp.bfloat16),
        ],
        compiler_params=pltpu.CompilerParams(vmem_limit_bytes=VMEM_BYTES),
        name="order_and_keys",
    )(canary_rows.reshape(rows, 1), ids.reshape(1, rows), own, other)


def value_kernel(place_ref, order_ref, own_ref, other_ref, out_ref, mark_ref):
    mark_ref[...] = jnp.zeros_like(mark_ref)
    rows = jnp.concatenate([own_ref[0], other_ref[0]], axis=0)
    out_ref[...] = jnp.dot(order_ref[...], rows, preferred_element_type=jnp.float32).astype(out_ref.dtype)


def order_values(findex, order, own, other):
    rows = order.shape[0]
    slots, part, width = own.shape
    place = jnp.stack([findex ^ s for s in range(slots)]).astype(jnp.int32)
    block = pl.BlockSpec((1, part, width), lambda s, place: (place[s], 0, 0))
    return pl.pallas_call(
        value_kernel,
        grid_spec=pltpu.PrefetchScalarGridSpec(
            num_scalar_prefetch=1,
            grid=(slots,),
            in_specs=[pl.BlockSpec((rows, rows), lambda s, place: (0, 0)), block, block],
            out_specs=[
                pl.BlockSpec((rows, width), lambda s, place: (0, s)),
                pl.BlockSpec((8, DH), lambda s, place: (0, 0)),
            ],
        ),
        out_shape=[
            jax.ShapeDtypeStruct((rows, slots * width), jnp.bfloat16),
            jax.ShapeDtypeStruct((8, DH), jnp.float32),
        ],
        compiler_params=pltpu.CompilerParams(vmem_limit_bytes=VMEM_BYTES),
        name="order_values",
    )(place, order, own, other)


def score_kernel(count, order_ref, key_t_ref, *refs):
    queries, (out_ref, mark_ref) = refs[:count], refs[-2:]
    mark_ref[...] = jnp.zeros_like(mark_ref)
    stacked = jnp.concatenate([query[...] for query in queries], axis=0)
    chosen = jnp.dot(order_ref[...], stacked, preferred_element_type=jnp.float32).astype(jnp.bfloat16)
    for head in range(stacked.shape[1] // DH):
        products = jnp.dot(
            chosen[:, head * DH : (head + 1) * DH], key_t_ref[...], preferred_element_type=jnp.float32
        )
        out_ref[0, head] = (products * DH ** (-0.5)).astype(out_ref.dtype)


def score_heads(order, key_t, heads, start, count, queries, earlier, after=()):
    rows = order.shape[0]
    step = 2 if count % 2 == 0 else 1

    def block(query, first):
        return pl.BlockSpec((query.shape[0], step * DH), lambda j: (0, first // step + j))

    return pl.pallas_call(
        functools.partial(score_kernel, len(queries)),
        grid=(count // step,),
        in_specs=[
            pl.BlockSpec((rows, rows), lambda j: (0, 0)),
            pl.BlockSpec((DH, rows), lambda j: (0, 0)),
        ]
        + [block(query, first) for query, first in queries]
        + [pl.BlockSpec(memory_space=pl.ANY)] * (len(earlier) + len(after)),
        out_specs=[
            pl.BlockSpec((1, step, rows, rows), lambda j: (0, start // step + j, 0, 0)),
            pl.BlockSpec((8, DH), lambda j: (0, 0)),
        ],
        out_shape=[
            jax.ShapeDtypeStruct((1, heads, rows, rows), jnp.bfloat16),
            jax.ShapeDtypeStruct((8, DH), jnp.float32),
        ],
        input_output_aliases={2 + len(queries): 0} if earlier else {},
        compiler_params=pltpu.CompilerParams(vmem_limit_bytes=VMEM_BYTES),
        cost_estimate=LIGHT,
        name="score_heads",
    )(order, key_t, *[query for query, _ in queries], *earlier, *after)


def body(hidden, w_query, w_key, w_value, canary_rows, positions):
    shards = lax.axis_size("fsdp")
    findex = lax.axis_index("fsdp")
    tps = lax.axis_size("tp")
    tindex = lax.axis_index("tp")
    rindex = lax.axis_index("rep")
    local, depth = hidden.shape
    half = local // 2
    rows = local * tps
    head_cols = w_query.shape[1] // shards
    heads_here = head_cols // DH
    group = HQ // KV
    assert shards & (shards - 1) == 0 and lax.axis_size("rep") == 2

    def swap(x, bit):
        return lax.ppermute(x, "fsdp", [(i, i ^ bit) for i in range(shards)])

    def other_core(x):
        return lax.ppermute(x, "rep", [(0, 1), (1, 0)])

    def low(x):
        return x.astype(jnp.bfloat16)

    odd = list(range(3, shards, 2)) + [1]
    even = list(range(2, shards, 2)) + [0]
    fast_pair = heads_here == group

    def spread(live):
        terms, first = [], None
        bit = 2
        while bit < shards:
            sent = [x for x in sorted(live) if x & bit]
            pack = jnp.stack([low(live[x]) for x in sent])
            first = pack if first is None else first
            landed = swap(pack, bit)
            for k, x in enumerate(sent):
                if x == bit:
                    terms.append(landed)
                else:
                    live[x ^ bit] = live[x ^ bit] + landed[k].astype(jnp.float32)
                del live[x]
            bit *= 2
        return terms, first

    blocks = [hidden] + [
        lax.ppermute(hidden, "tp", [(i, (i - b) % tps) for i in range(tps)]) for b in range(1, tps)
    ]

    block_ids = ((tindex + jnp.arange(tps, dtype=jnp.int32)) % tps * local)[:, None]
    own_ids = (block_ids + rindex * half + jnp.arange(half, dtype=jnp.int32)[None]).reshape(-1)
    other_ids = (block_ids + (1 - rindex) * half + jnp.arange(half, dtype=jnp.int32)[None]).reshape(-1)
    ids = jnp.concatenate([own_ids, other_ids])
    own_positions = jnp.sum(
        jnp.where(own_ids[:, None] == canary_rows[None, :], positions[None, :], 0), axis=1
    )
    cosine, sine = rope_tables(own_positions)

    tile = min(1024, head_cols)

    def project(slots, block, width, after=()):
        keep, gives = project_query(
            rindex, findex, slots, block, w_query, head_cols, tile, width, after
        )
        return keep, [other_core(give) for give in gives], gives[0]

    def project_heads(block, after):
        keep, give = project_pair(
            rindex, findex, list(range(shards)), block, w_key, w_value, (after,)
        )
        return keep + other_core(give).astype(jnp.float32), give

    def rotate(b, p, split, terms, behind):
        keep, got = evens[b]
        cols, each = head_cols // split, len(got) // split
        table = slice(b * half, (b + 1) * half)
        added = [(keep, len(even) - 1, p * cols), (fars[b], len(odd) - 1, p * cols)]
        added += [(term, 0, 0) for term in terms]
        gots = (len(even) - 1, got[p * each : (p + 1) * each])
        turned = sum_and_rotate(cosine[table], sine[table], added, gots, cols, behind)
        return turned, other_core(turned)

    def add_even(b, parts, behind):
        keep, got = evens[b]
        landed = (fars[b],) if shards > 2 else ()
        summed = add_rows(keep, got, len(even) - 1, landed, behind)
        cols = head_cols // parts
        spreads = []
        for p in range(parts):
            live = {x: summed[k][:, p * cols : (p + 1) * cols] for k, x in enumerate(even[:-1])}
            spreads.append(spread(live))
        return [terms for terms, _ in spreads], spreads[-1][1]

    last, split = tps - 1, head_cols // tile
    evens, fars, pairs, terms, after, behind = [], [], [], [], (), ()
    for b, block in enumerate(blocks):
        odd_keep, odd_got, _ = project(odd, block, tile, after)
        odd_sent = add_rows(odd_keep, odd_got, len(odd))
        fars.append(swap(odd_sent, 1))
        if b > 0:
            parts, first = add_even(b - 1, 1, (odd_sent,))
            terms.append(parts)
            behind = (first,)
        even_keep, even_got, given = project(even, block, tile, (odd_sent,) + behind)
        evens.append((even_keep, even_got))
        if fast_pair:
            pair, given = project_heads(block, given)
            pairs.append(pair)
        after = (given,)
    if fast_pair:
        pair = jnp.concatenate(pairs, axis=1)
        pair_landed = swap(low(pair[1::2]), 1)
        live = {x: pair[x] + pair_landed[x // 2].astype(jnp.float32) for x in even[:-1]}
        pair_terms, first = spread(live)
        after = (first,)
    parts, first = add_even(last, split, after)
    terms.append(parts)
    after = (first,)

    if fast_pair:
        key_rot, held = split_and_rotate(cosine, sine, [pair, pair_landed] + pair_terms, after)
        bit = 1
        while bit < shards:
            held = jnp.concatenate([held, swap(held, bit)])
            bit *= 2
        held_other = other_core(held)
    else:
        x = jnp.concatenate(blocks, axis=0)
        key_sum, value_sum = lax.psum(
            (
                jnp.dot(x, w_key, preferred_element_type=jnp.float32),
                jnp.dot(x, w_value, preferred_element_type=jnp.float32),
            ),
            ("fsdp", "rep"),
        )

        def of_core(y, core):
            parts = y.reshape(tps, 2, half, -1)
            return lax.dynamic_index_in_dim(parts, core, 1, keepdims=False).reshape(tps * half, -1)

        mine = lax.dynamic_slice_in_dim(key_sum, findex * heads_here // group * DH, DH, 1)
        key_own = of_core(mine, rindex)
        key_rot = sum_and_rotate(cosine, sine, [(key_own[None], 0, 0)], (0, []), DH, after)
        value_rows = low(jnp.concatenate([of_core(value_sum, rindex), of_core(value_sum, 1 - rindex)]))

    order, key_t = prepare(canary_rows, ids, key_rot, other_core(key_rot))
    if fast_pair:
        values, values_mark = order_values(findex, order, held, held_other)
    else:
        values_mark = key_t
        values = low(jnp.dot(order, value_rows, preferred_element_type=jnp.float32))

    rotated = [rotate(b, 0, 1, terms[b][0], after) for b in range(last)]
    count = heads_here // split
    scores, mark = (), ()
    for p in range(split):
        turned = rotate(last, p, split, terms[last][p], (key_t,) + mark)
        queries = [(row[0], p * count) for row in rotated] + [(turned[0], 0)]
        queries += [(row[1], p * count) for row in rotated] + [(turned[1], 0)]
        behind = (values_mark,) if p == split - 1 else ()
        *scores, mark = score_heads(
            order, key_t, heads_here, p * count, count, queries, scores, behind
        )
        mark = (mark,)
    return (scores[0], values)


def solution(mesh):
    in_specs = (
        P(("groups", "tp"), ("fsdp", "rep")),
        P(("fsdp", "rep"), "tp"),
        P(("fsdp", "rep"), "tp"),
        P(("fsdp", "rep"), "tp"),
        P("groups"),
        P("groups"),
    )
    out_specs = (P("tp", "fsdp", "groups", None), P("groups", "tp"))
    return jax.shard_map(body, mesh=mesh, in_specs=in_specs, out_specs=out_specs, check_vma=False)
```

```python
import functools
import math

import jax
import jax.numpy as jnp
from jax import lax
from jax.experimental import pallas as pl
from jax.experimental.pallas import tpu as pltpu
from jax.sharding import PartitionSpec as P

HQ = 128
KV = 8
DH = 128
VMEM_BYTES = 28 * 1024 * 1024
LIGHT = pl.CostEstimate(flops=1000, bytes_accessed=1000, transcendentals=0)
HEAVY = pl.CostEstimate(flops=10**11, bytes_accessed=10**8, transcendentals=0)


def in_hbm(arrays):
    return [pltpu.with_memory_space_constraint(x, pltpu.HBM) for x in arrays]


def rope_tables(positions):
    half = DH // 2
    expo = jnp.arange(half, dtype=jnp.float32) * (2.0 / DH)
    freq = jnp.power(jnp.float32(500000.0), -expo)
    wavelen = 2.0 * math.pi / freq
    smooth = (8192.0 / wavelen - 1.0) / 3.0
    mixed = (1.0 - smooth) * freq / 8.0 + smooth * freq
    freq = jnp.where(wavelen > 8192.0, freq / 8.0, jnp.where(wavelen < 2048.0, freq, mixed))
    angle = positions.astype(jnp.float32)[:, None] * freq[None, :]
    cosine, sine = jnp.cos(angle), jnp.sin(angle)
    return jnp.concatenate([cosine, cosine], axis=1), jnp.concatenate([-sine, sine], axis=1)


def ordered_rows(place_ref, x_refs, rows_ref):
    core = place_ref[0]
    half = x_refs[0].shape[0] // 2
    for b, x_ref in enumerate(x_refs):
        kept, given = b * half, (len(x_refs) + b) * half
        rows_ref[kept : kept + half] = x_ref[pl.ds(pl.multiple_of(core * half, 16), half)]
        rows_ref[given : given + half] = x_ref[pl.ds(pl.multiple_of((1 - core) * half, 16), half)]


def query_kernel(count, pieces, width, place_ref, *refs):
    x_refs, w_ref = refs[:count], refs[count]
    keep_ref, *give_refs, rows_ref = refs[-2 - pieces :]
    tile = pl.program_id(1)
    each = keep_ref.shape[2] // width

    @pl.when((pl.program_id(0) == 0) & (tile == 0))
    def _():
        ordered_rows(place_ref, x_refs, rows_ref)

    result = jnp.dot(rows_ref[...], w_ref[...], preferred_element_type=jnp.float32)
    half = result.shape[0] // 2
    keep_ref[0] = result[:half]
    for j, give_ref in enumerate(give_refs):

        @pl.when(tile == j // each)
        def _():
            start = j % each * width
            give_ref[0] = result[half:, start : start + width].astype(give_ref.dtype)


def project_query(rindex, findex, slots, blocks, w, cols, tile, width, after, cost):
    rows, depth = blocks[0].shape
    count = len(blocks)
    half = rows // 2 * count
    tiles, pieces = cols // tile, cols // width
    place = jnp.stack([rindex] + [findex ^ slot for slot in slots]).astype(jnp.int32)
    x_spec = pl.BlockSpec((rows, depth), lambda s, j, place: (0, 0), pipeline_mode=pl.Buffered(1))
    outs = pl.pallas_call(
        functools.partial(query_kernel, count, pieces, width),
        grid_spec=pltpu.PrefetchScalarGridSpec(
            num_scalar_prefetch=1,
            grid=(len(slots), tiles),
            in_specs=[x_spec] * count
            + [pl.BlockSpec((depth, tile), lambda s, j, place: (0, place[1 + s] * tiles + j))]
            + [pl.BlockSpec(memory_space=pl.ANY)] * len(after),
            out_specs=[pl.BlockSpec((1, half, tile), lambda s, j, place: (s, 0, j))]
            + [pl.BlockSpec((1, half, width), lambda s, j, place: (s, 0, 0))] * pieces,
            scratch_shapes=[pltpu.VMEM((2 * half, depth), w.dtype)],
        ),
        out_shape=[pltpu.HBM((len(slots), half, cols), jnp.float32)]
        + [pltpu.HBM((len(slots), half, width), jnp.bfloat16)] * pieces,
        compiler_params=pltpu.CompilerParams(vmem_limit_bytes=VMEM_BYTES),
        cost_estimate=cost,
        name="query_products",
    )(place, *blocks, *in_hbm([w]), *in_hbm(after[:1]), *after[1:])
    return outs[0], outs[1:]


def pair_kernel(count, place_ref, *refs):
    x_refs, (wk_ref, wv_ref) = refs[:count], refs[count : count + 2]
    keep_ref, give_ref, rows_ref = refs[-3:]

    @pl.when(pl.program_id(0) == 0)
    def _():
        ordered_rows(place_ref, x_refs, rows_ref)

    weights = jnp.concatenate([wk_ref[...], wv_ref[...]], axis=1)
    result = jnp.dot(rows_ref[...], weights, preferred_element_type=jnp.float32)
    half, width = x_refs[0].shape[0] // 2, weights.shape[1]
    for b in range(count):
        kept, given = b * half, (count + b) * half
        cols = slice(b * width, (b + 1) * width)
        keep_ref[0, :, cols] = result[kept : kept + half]
        give_ref[0, :, cols] = result[given : given + half].astype(give_ref.dtype)


def project_pair(rindex, findex, slots, blocks, w_key, w_value, after=()):
    rows, depth = blocks[0].shape
    count = len(blocks)
    place = jnp.stack([rindex] + [findex ^ slot for slot in slots]).astype(jnp.int32)
    weight = pl.BlockSpec((depth, DH), lambda s, place: (0, place[1 + s]))
    shape = (len(slots), rows // 2, 2 * DH * count)
    out = pl.BlockSpec((1,) + shape[1:], lambda s, place: (s, 0, 0))
    return pl.pallas_call(
        functools.partial(pair_kernel, count),
        grid_spec=pltpu.PrefetchScalarGridSpec(
            num_scalar_prefetch=1,
            grid=(len(slots),),
            in_specs=[pl.BlockSpec((rows, depth), lambda s, place: (0, 0))] * count
            + [weight, weight]
            + [pl.BlockSpec(memory_space=pl.ANY)] * len(after),
            out_specs=[out, out],
            scratch_shapes=[pltpu.VMEM((count * rows, depth), blocks[0].dtype)],
        ),
        out_shape=[
            pltpu.HBM(shape, jnp.float32),
            pltpu.HBM(shape, jnp.bfloat16),
        ],
        compiler_params=pltpu.CompilerParams(vmem_limit_bytes=VMEM_BYTES),
        cost_estimate=LIGHT,
        name="key_value_products",
    )(place, *blocks, *in_hbm([w_key, w_value, *after]))


def add_kernel(tiles, per, paired, extra, *refs):
    keep_ref, give_refs, out_ref = refs[0], refs[1 : 1 + tiles], refs[-1]
    pair_refs = refs[1 + tiles : 1 + tiles + 2 * paired]
    landed_refs = refs[1 + tiles + 2 * paired :][:extra]
    j = pl.program_id(1)

    def write(first_ref, second_ref):
        total = first_ref[0] + second_ref[0].astype(jnp.float32)
        for landed_ref in landed_refs:
            total = total + landed_ref[0].astype(jnp.float32)
        out_ref[0] = total.astype(out_ref.dtype)

    for t, give_ref in enumerate(give_refs):

        @pl.when(j // per == t)
        def _():
            write(keep_ref, give_ref)

    if paired:

        @pl.when(j >= tiles * per)
        def _():
            write(*pair_refs)


def add_rows(count, rows, b, keep, gots, start, pair=(), slot=0, landed=(), after=()):
    whole = keep.shape[2]
    width = gots[0].shape[2]
    step = math.gcd(width, pair[0].shape[2]) if pair else width
    per, query = width // step, len(gots) * width // step
    total = query + (pair[0].shape[2] // step if pair else 0)
    first = start // step

    def got(t):
        return pl.BlockSpec((1, rows, step), lambda s, j: (s, b, jnp.clip(j - t * per, 0, per - 1)))

    def columns(s, j):
        return (s, 0, jnp.where(j < query, first + j, whole // step + j - query))

    paired = pl.BlockSpec((1, rows, step), lambda s, j: (slot + s, 0, jnp.maximum(j - query, 0)))
    return pl.pallas_call(
        functools.partial(add_kernel, len(gots), per, len(pair) // 2, len(landed)),
        grid=(count, total),
        in_specs=[
            pl.BlockSpec((1, rows, step), lambda s, j: (s, b, first + jnp.minimum(j, query - 1)))
        ]
        + [got(t) for t in range(len(gots))]
        + [paired] * len(pair)
        + [pl.BlockSpec((1, rows, step), columns)] * len(landed)
        + [pl.BlockSpec(memory_space=pl.ANY)] * len(after),
        out_specs=pl.BlockSpec((1, rows, step), lambda s, j: (s, 0, j)),
        out_shape=pltpu.HBM((count, rows, total * step), jnp.bfloat16),
        compiler_params=pltpu.CompilerParams(vmem_limit_bytes=VMEM_BYTES),
        cost_estimate=LIGHT,
        name="add_rows",
    )(*in_hbm([keep]), *gots, *in_hbm(pair[:1]), *pair[1:], *landed, *in_hbm(after))


def rotate_kernel(count, pieces, cos_ref, sin_ref, *refs):
    terms, gots, out_ref = refs[:count], refs[count : count + pieces], refs[-1]
    total = terms[0][0].astype(jnp.float32)
    for term in terms[1:]:
        total = total + term[0].astype(jnp.float32)
    cosine, sine = cos_ref[...], sin_ref[...]

    def write(total):
        for head in range(total.shape[1] // DH):
            part = total[:, head * DH : (head + 1) * DH]
            turned = pltpu.roll(part, DH // 2, axis=1)
            value = part * cosine + turned * sine
            out_ref[:, head * DH : (head + 1) * DH] = value.astype(out_ref.dtype)

    if not gots:
        write(total)
    for j, got in enumerate(gots):

        @pl.when(pl.program_id(0) == j)
        def _():
            write(total + got[0].astype(jnp.float32))


def sum_and_rotate(cosine, sine, terms, gots, cols, after=()):
    rows = cosine.shape[0]
    slot_of_gots, block_of_gots, gots = gots
    tile = cols // max(1, len(gots))
    table = pl.BlockSpec((rows, DH), lambda j: (0, 0))

    def block(slot, b, start):
        return pl.BlockSpec((1, rows, tile), lambda j: (slot, b, start // tile + j))

    return pl.pallas_call(
        functools.partial(rotate_kernel, len(terms), len(gots)),
        grid=(cols // tile,),
        in_specs=[table, table]
        + [block(slot, b, start) for _, slot, b, start in terms]
        + [pl.BlockSpec((1, rows, tile), lambda j: (slot_of_gots, block_of_gots, 0))] * len(gots)
        + [pl.BlockSpec(memory_space=pl.ANY)] * len(after),
        out_specs=pl.BlockSpec((rows, tile), lambda j: (0, j)),
        out_shape=jax.ShapeDtypeStruct((rows, cols), jnp.bfloat16),
        compiler_params=pltpu.CompilerParams(vmem_limit_bytes=VMEM_BYTES),
        cost_estimate=LIGHT,
        name="sum_and_rotate",
    )(cosine, sine, *in_hbm([terms[0][0]]), *[term[0] for term in terms[1:]], *gots, *after)


def split_kernel(count, cos_ref, sin_ref, *refs):
    terms, (key_ref, value_ref) = refs[:count], refs[-2:]
    total = terms[0][0].astype(jnp.float32)
    for term in terms[1:]:
        total = total + term[0].astype(jnp.float32)
    half = total.shape[0]
    for b in range(total.shape[1] // (2 * DH)):
        rows = slice(b * half, (b + 1) * half)
        key = total[:, 2 * b * DH : (2 * b + 1) * DH]
        turned = pltpu.roll(key, DH // 2, axis=1)
        key_ref[rows] = (key * cos_ref[rows] + turned * sin_ref[rows]).astype(key_ref.dtype)
        value_ref[0, rows] = total[:, (2 * b + 1) * DH : (2 * b + 2) * DH].astype(value_ref.dtype)


def split_and_rotate(cosine, sine, terms, width):
    rows = cosine.shape[0]
    half = terms[0][0].shape[1]
    table = pl.BlockSpec((rows, DH), lambda j: (0, 0))

    def block(slot, start):
        return pl.BlockSpec((1, half, width), lambda j: (slot, 0, start // width))

    return pl.pallas_call(
        functools.partial(split_kernel, len(terms)),
        grid=(1,),
        in_specs=[table, table] + [block(slot, start) for _, slot, start in terms],
        out_specs=[table, pl.BlockSpec((1, rows, DH), lambda j: (0, 0, 0))],
        out_shape=[
            jax.ShapeDtypeStruct((rows, DH), jnp.bfloat16),
            jax.ShapeDtypeStruct((1, rows, DH), jnp.bfloat16),
        ],
        compiler_params=pltpu.CompilerParams(vmem_limit_bytes=VMEM_BYTES),
        cost_estimate=LIGHT,
        name="split_and_rotate",
    )(cosine, sine, *in_hbm([terms[0][0]]), *[term for term, _, _ in terms[1:]])


def prepare_kernel(canary_ref, ids_ref, own_ref, other_ref, order_ref, key_t_ref):
    order = jnp.where(canary_ref[...] == ids_ref[...], 1.0, 0.0).astype(jnp.bfloat16)
    order_ref[...] = order
    key = jnp.concatenate([own_ref[...], other_ref[...]], axis=0)
    key_t_ref[...] = jnp.dot(order, key, preferred_element_type=jnp.float32).T.astype(jnp.bfloat16)


def prepare(canary_rows, ids, own, other):
    rows = ids.shape[0]
    return pl.pallas_call(
        prepare_kernel,
        out_shape=[
            jax.ShapeDtypeStruct((rows, rows), jnp.bfloat16),
            jax.ShapeDtypeStruct((DH, rows), jnp.bfloat16),
        ],
        compiler_params=pltpu.CompilerParams(vmem_limit_bytes=VMEM_BYTES),
        name="order_and_keys",
    )(canary_rows.reshape(rows, 1), ids.reshape(1, rows), own, other)


def value_kernel(place_ref, order_ref, own_ref, other_ref, out_ref, mark_ref):
    mark_ref[...] = jnp.zeros_like(mark_ref)
    rows = jnp.concatenate([own_ref[0], other_ref[0]], axis=0)
    out_ref[...] = jnp.dot(order_ref[...], rows, preferred_element_type=jnp.float32).astype(out_ref.dtype)


def order_values(findex, order, own, other):
    rows = order.shape[0]
    slots, part, width = own.shape
    place = jnp.stack([findex ^ s for s in range(slots)]).astype(jnp.int32)
    block = pl.BlockSpec((1, part, width), lambda s, place: (place[s], 0, 0))
    return pl.pallas_call(
        value_kernel,
        grid_spec=pltpu.PrefetchScalarGridSpec(
            num_scalar_prefetch=1,
            grid=(slots,),
            in_specs=[pl.BlockSpec((rows, rows), lambda s, place: (0, 0)), block, block],
            out_specs=[
                pl.BlockSpec((rows, width), lambda s, place: (0, s)),
                pl.BlockSpec((8, DH), lambda s, place: (0, 0)),
            ],
        ),
        out_shape=[
            jax.ShapeDtypeStruct((rows, slots * width), jnp.bfloat16),
            jax.ShapeDtypeStruct((8, DH), jnp.float32),
        ],
        compiler_params=pltpu.CompilerParams(vmem_limit_bytes=VMEM_BYTES),
        name="order_values",
    )(place, order, own, other)


def score_kernel(count, order_ref, key_t_ref, *refs):
    queries, (out_ref, mark_ref) = refs[:count], refs[-2:]
    mark_ref[...] = jnp.zeros_like(mark_ref)
    stacked = jnp.concatenate([query[...] for query in queries], axis=0)
    chosen = jnp.dot(order_ref[...], stacked, preferred_element_type=jnp.float32).astype(jnp.bfloat16)
    for head in range(stacked.shape[1] // DH):
        products = jnp.dot(
            chosen[:, head * DH : (head + 1) * DH], key_t_ref[...], preferred_element_type=jnp.float32
        )
        out_ref[0, head] = (products * DH ** (-0.5)).astype(out_ref.dtype)


def score_heads(order, key_t, heads, start, count, queries, earlier, after=()):
    rows = order.shape[0]
    step = 2 if count % 2 == 0 else 1

    def block(query, first):
        return pl.BlockSpec((query.shape[0], step * DH), lambda j: (0, first // step + j))

    return pl.pallas_call(
        functools.partial(score_kernel, len(queries)),
        grid=(count // step,),
        in_specs=[
            pl.BlockSpec((rows, rows), lambda j: (0, 0)),
            pl.BlockSpec((DH, rows), lambda j: (0, 0)),
        ]
        + [block(query, first) for query, first in queries]
        + [pl.BlockSpec(memory_space=pl.ANY)] * (len(earlier) + len(after)),
        out_specs=[
            pl.BlockSpec((1, step, rows, rows), lambda j: (0, start // step + j, 0, 0)),
            pl.BlockSpec((8, DH), lambda j: (0, 0)),
        ],
        out_shape=[
            jax.ShapeDtypeStruct((1, heads, rows, rows), jnp.bfloat16),
            jax.ShapeDtypeStruct((8, DH), jnp.float32),
        ],
        input_output_aliases={2 + len(queries): 0} if earlier else {},
        compiler_params=pltpu.CompilerParams(vmem_limit_bytes=VMEM_BYTES),
        cost_estimate=LIGHT,
        name="score_heads",
    )(order, key_t, *[query for query, _ in queries], *earlier, *after)


def body(hidden, w_query, w_key, w_value, canary_rows, positions):
    shards = lax.axis_size("fsdp")
    findex = lax.axis_index("fsdp")
    tps = lax.axis_size("tp")
    tindex = lax.axis_index("tp")
    rindex = lax.axis_index("rep")
    local, depth = hidden.shape
    half = local // 2
    rows = local * tps
    head_cols = w_query.shape[1] // shards
    heads_here = head_cols // DH
    group = HQ // KV
    assert shards & (shards - 1) == 0 and lax.axis_size("rep") == 2

    def swap(x, bit):
        return lax.ppermute(x, "fsdp", [(i, i ^ bit) for i in range(shards)])

    def other_core(x):
        return lax.ppermute(x, "rep", [(0, 1), (1, 0)])

    def low(x):
        return x.astype(jnp.bfloat16)

    odd = list(range(3, shards, 2)) + [1]
    even = list(range(2, shards, 2)) + [0]
    fast_pair = heads_here == group

    def spread(live):
        terms, first = [], None
        bit = 2
        while bit < shards:
            sent = [x for x in sorted(live) if x & bit]
            pack = jnp.stack([low(live[x]) for x in sent])
            first = pack if first is None else first
            landed = swap(pack, bit)
            for k, x in enumerate(sent):
                if x == bit:
                    terms.append(landed)
                else:
                    live[x ^ bit] = live[x ^ bit] + landed[k].astype(jnp.float32)
                del live[x]
            bit *= 2
        return terms, first

    blocks = [hidden] + [
        lax.ppermute(hidden, "tp", [(i, (i - b) % tps) for i in range(tps)]) for b in range(1, tps)
    ]

    block_ids = ((tindex + jnp.arange(tps, dtype=jnp.int32)) % tps * local)[:, None]
    own_ids = (block_ids + rindex * half + jnp.arange(half, dtype=jnp.int32)[None]).reshape(-1)
    other_ids = (block_ids + (1 - rindex) * half + jnp.arange(half, dtype=jnp.int32)[None]).reshape(-1)
    ids = jnp.concatenate([own_ids, other_ids])
    own_positions = jnp.sum(
        jnp.where(own_ids[:, None] == canary_rows[None, :], positions[None, :], 0), axis=1
    )
    cosine, sine = rope_tables(own_positions)

    tile = min(1024, head_cols)

    def project(slots, blocks, width, after=(), cost=LIGHT):
        keep, gives = project_query(
            rindex, findex, slots, blocks, w_query, head_cols, tile, width, after, cost
        )
        return keep, [other_core(give) for give in gives], gives[0]

    def rotate(b, p, split, terms, behind):
        cols, each = head_cols // split, len(even_got) // split
        table = slice(b * half, (b + 1) * half)
        added = [(even_keep, len(even) - 1, b, p * cols), (fars[b], len(odd) - 1, 0, p * cols)]
        added += [(term, 0, 0, 0) for term in terms]
        gots = (len(even) - 1, b, even_got[p * each : (p + 1) * each])
        turned = sum_and_rotate(cosine[table], sine[table], added, gots, cols, behind)
        return turned, other_core(turned)

    last, split = tps - 1, head_cols // tile
    fars, pair, after = [], (), ()
    placed = in_hbm(blocks[:1]) + blocks[1:]
    for b, block in enumerate(placed):
        if fast_pair and b == last:
            pair_keep, give = project_pair(rindex, findex, odd + even, placed, w_key, w_value, after)
            pair = (pair_keep, other_core(give))
            after = (give,)
        odd_keep, odd_got, _ = project(odd, [block], tile, after)
        odd_sent = add_rows(len(odd), half, 0, odd_keep, odd_got, 0, pair)
        fars.append(swap(odd_sent, 1))
        after = (odd_sent,)

    even_keep, even_got, given = project(even, placed, min(512, tile), after + tuple(fars[:last]), HEAVY)
    after = (given,)

    def add_even(b, start, gots, pair, behind):
        landed = (fars[b],) if shards > 2 else ()
        summed = add_rows(
            len(even) - 1, half, b, even_keep, gots, start, pair, len(odd), landed, behind
        )
        return spread({x: summed[k] for k, x in enumerate(even[:-1])})

    terms = []
    for b in range(tps):
        parts = split if b == last else 1
        each = len(even_got) // parts
        row = []
        for p in range(parts):
            gots = even_got[p * each : (p + 1) * each]
            cols = p * head_cols // parts
            paired = pair if b == last and p == 0 else ()
            added, first = add_even(b, cols, gots, paired, after)
            row.append(added)
            after = (first,)
        terms.append(row)
    parts = terms[last]

    if fast_pair:
        width = 2 * DH * tps
        pieces = [(array, shards - 1, 0) for array in pair]
        pieces += [(fars[last], len(odd) - 1, head_cols)] + [(term, 0, tile) for term in parts[0]]
        key_rot, held = split_and_rotate(cosine, sine, pieces, width)
        bit = 1
        while bit < shards:
            held = jnp.concatenate([held, swap(held, bit)])
            bit *= 2
        held_other = other_core(held)
    else:
        x = jnp.concatenate(blocks, axis=0)
        key_sum, value_sum = lax.psum(
            (
                jnp.dot(x, w_key, preferred_element_type=jnp.float32),
                jnp.dot(x, w_value, preferred_element_type=jnp.float32),
            ),
            ("fsdp", "rep"),
        )

        def of_core(y, core):
            parts = y.reshape(tps, 2, half, -1)
            return lax.dynamic_index_in_dim(parts, core, 1, keepdims=False).reshape(tps * half, -1)

        mine = lax.dynamic_slice_in_dim(key_sum, findex * heads_here // group * DH, DH, 1)
        key_own = of_core(mine, rindex)
        key_rot = sum_and_rotate(cosine, sine, [(key_own[None], 0, 0, 0)], (0, 0, []), DH, after)
        value_rows = low(jnp.concatenate([of_core(value_sum, rindex), of_core(value_sum, 1 - rindex)]))

    order, key_t = prepare(canary_rows, ids, key_rot, other_core(key_rot))
    if fast_pair:
        values, values_mark = order_values(findex, order, held, held_other)
    else:
        values_mark = key_t
        values = low(jnp.dot(order, value_rows, preferred_element_type=jnp.float32))

    rotated = [rotate(b, 0, 1, terms[b][0], after) for b in range(last)]
    count = heads_here // split
    scores, mark = (), ()
    for p in range(split):
        turned = rotate(last, p, split, terms[last][p], (key_t,) + mark)
        queries = [(row[0], p * count) for row in rotated] + [(turned[0], 0)]
        queries += [(row[1], p * count) for row in rotated] + [(turned[1], 0)]
        behind = (values_mark,) if p == split - 1 else ()
        *scores, mark = score_heads(
            order, key_t, heads_here, p * count, count, queries, scores, behind
        )
        mark = (mark,)
    return (scores[0], values)


def solution(mesh):
    in_specs = (
        P(("groups", "tp"), ("fsdp", "rep")),
        P(("fsdp", "rep"), "tp"),
        P(("fsdp", "rep"), "tp"),
        P(("fsdp", "rep"), "tp"),
        P("groups"),
        P("groups"),
    )
    out_specs = (P("tp", "fsdp", "groups", None), P("groups", "tp"))
    return jax.shard_map(body, mesh=mesh, in_specs=in_specs, out_specs=out_specs, check_vma=False)
```

```python
import functools
import math

import jax
import jax.numpy as jnp
from jax import lax
from jax.experimental import pallas as pl
from jax.experimental.pallas import tpu as pltpu
from jax.sharding import PartitionSpec as P

HQ = 128
KV = 8
DH = 128
VMEM_BYTES = 28 * 1024 * 1024
LIGHT = pl.CostEstimate(flops=1000, bytes_accessed=1000, transcendentals=0)
HEAVY = pl.CostEstimate(flops=10**11, bytes_accessed=10**8, transcendentals=0)


def in_hbm(arrays):
    return [pltpu.with_memory_space_constraint(x, pltpu.HBM) for x in arrays]


def rope_tables(positions):
    half = DH // 2
    expo = jnp.arange(half, dtype=jnp.float32) * (2.0 / DH)
    freq = jnp.power(jnp.float32(500000.0), -expo)
    wavelen = 2.0 * math.pi / freq
    smooth = (8192.0 / wavelen - 1.0) / 3.0
    mixed = (1.0 - smooth) * freq / 8.0 + smooth * freq
    freq = jnp.where(wavelen > 8192.0, freq / 8.0, jnp.where(wavelen < 2048.0, freq, mixed))
    angle = positions.astype(jnp.float32)[:, None] * freq[None, :]
    cosine, sine = jnp.cos(angle), jnp.sin(angle)
    return jnp.concatenate([cosine, cosine], axis=1), jnp.concatenate([-sine, sine], axis=1)


def ordered_rows(place_ref, x_refs, rows_ref):
    core = place_ref[0]
    half = x_refs[0].shape[0] // 2
    for b, x_ref in enumerate(x_refs):
        kept, given = b * half, (len(x_refs) + b) * half
        rows_ref[kept : kept + half] = x_ref[pl.ds(pl.multiple_of(core * half, 16), half)]
        rows_ref[given : given + half] = x_ref[pl.ds(pl.multiple_of((1 - core) * half, 16), half)]


def query_kernel(count, pieces, place_ref, *refs):
    x_refs, w_ref = refs[:count], refs[count]
    keep_ref, *give_refs, rows_ref = refs[-2 - pieces :]
    tile = pl.program_id(1)
    size = give_refs[0].shape[2]
    each = keep_ref.shape[2] // size

    @pl.when((pl.program_id(0) == 0) & (tile == 0))
    def _():
        ordered_rows(place_ref, x_refs, rows_ref)

    result = jnp.dot(rows_ref[...], w_ref[...], preferred_element_type=jnp.float32)
    half = result.shape[0] // 2
    keep_ref[0] = result[:half]
    for j, give_ref in enumerate(give_refs):

        @pl.when((tile == j // each) | (pieces == 1))
        def _():
            start = j % each * size
            give_ref[0] = result[half:, start : start + size].astype(give_ref.dtype)


def project_query(rindex, findex, slots, blocks, w, cols, tile, width, after, cost):
    rows, depth = blocks[0].shape
    count = len(blocks)
    half = rows // 2 * count
    tiles, pieces = cols // tile, cols // width
    place = jnp.stack([rindex] + [findex ^ slot for slot in slots]).astype(jnp.int32)
    keep_spec = pl.BlockSpec((1, half, tile), lambda s, j, place: (s, 0, j))
    give_spec = pl.BlockSpec((1, half, width), lambda s, j, place: (s, 0, 0))
    x_spec = pl.BlockSpec((rows, depth), lambda s, j, place: (0, 0), pipeline_mode=pl.Buffered(1))
    outs = pl.pallas_call(
        functools.partial(query_kernel, count, pieces),
        grid_spec=pltpu.PrefetchScalarGridSpec(
            num_scalar_prefetch=1,
            grid=(len(slots), tiles),
            in_specs=[x_spec] * count
            + [pl.BlockSpec((depth, tile), lambda s, j, place: (0, place[1 + s] * tiles + j))]
            + [pl.BlockSpec(memory_space=pl.ANY)] * len(after),
            out_specs=[keep_spec] + ([keep_spec] if pieces == 1 else [give_spec] * pieces),
            scratch_shapes=[pltpu.VMEM((2 * half, depth), w.dtype)],
        ),
        out_shape=[pltpu.HBM((len(slots), half, cols), jnp.float32)]
        + [pltpu.HBM((len(slots), half, width), jnp.bfloat16)] * pieces,
        compiler_params=pltpu.CompilerParams(vmem_limit_bytes=VMEM_BYTES),
        cost_estimate=cost,
        name="query_products",
    )(place, *blocks, *in_hbm([w]), *in_hbm(after[:1]), *after[1:])
    return outs[0], outs[1:]


def pair_kernel(count, place_ref, *refs):
    x_refs, (wk_ref, wv_ref) = refs[:count], refs[count : count + 2]
    keep_ref, give_ref, rows_ref = refs[-3:]

    @pl.when(pl.program_id(0) == 0)
    def _():
        ordered_rows(place_ref, x_refs, rows_ref)

    weights = jnp.concatenate([wk_ref[...], wv_ref[...]], axis=1)
    result = jnp.dot(rows_ref[...], weights, preferred_element_type=jnp.float32)
    half, width = x_refs[0].shape[0] // 2, weights.shape[1]
    for b in range(count):
        kept, given = b * half, (count + b) * half
        cols = slice(b * width, (b + 1) * width)
        keep_ref[0, :, cols] = result[kept : kept + half]
        give_ref[0, :, cols] = result[given : given + half].astype(give_ref.dtype)


def project_pair(rindex, findex, slots, blocks, w_key, w_value, after=()):
    rows, depth = blocks[0].shape
    count = len(blocks)
    place = jnp.stack([rindex] + [findex ^ slot for slot in slots]).astype(jnp.int32)
    weight = pl.BlockSpec((depth, DH), lambda s, place: (0, place[1 + s]))
    shape = (len(slots), rows // 2, 2 * DH * count)
    out = pl.BlockSpec((1,) + shape[1:], lambda s, place: (s, 0, 0))
    return pl.pallas_call(
        functools.partial(pair_kernel, count),
        grid_spec=pltpu.PrefetchScalarGridSpec(
            num_scalar_prefetch=1,
            grid=(len(slots),),
            in_specs=[pl.BlockSpec((rows, depth), lambda s, place: (0, 0))] * count
            + [weight, weight]
            + [pl.BlockSpec(memory_space=pl.ANY)] * len(after),
            out_specs=[out, out],
            scratch_shapes=[pltpu.VMEM((count * rows, depth), blocks[0].dtype)],
        ),
        out_shape=[
            pltpu.HBM(shape, jnp.float32),
            pltpu.HBM(shape, jnp.bfloat16),
        ],
        compiler_params=pltpu.CompilerParams(vmem_limit_bytes=VMEM_BYTES),
        cost_estimate=LIGHT,
        name="key_value_products",
    )(place, *blocks, *in_hbm([w_key, w_value, *after]))


def add_kernel(gots, paired, extra, *refs):
    keep_ref, got_refs, out_ref = refs[0], refs[1 : 1 + gots], refs[-1]
    pair_refs = refs[1 + gots : 1 + gots + 2 * paired]
    landed_refs = refs[1 + gots + 2 * paired :][: extra * (1 + paired)]
    width = got_refs[0].shape[2]
    cols = gots * width

    def total(first, second, landed):
        value = first + second.astype(jnp.float32)
        for term in landed:
            value = value + term.astype(jnp.float32)
        return value.astype(out_ref.dtype)

    for t, got_ref in enumerate(got_refs):
        part = slice(t * width, (t + 1) * width)
        landed = [landed_refs[0][0, :, part]] if extra else []
        out_ref[0, :, part] = total(keep_ref[0, :, part], got_ref[0], landed)
    if paired:
        landed = [landed_refs[1][0]] if extra else []
        out_ref[0, :, cols:] = total(pair_refs[0][0], pair_refs[1][0], landed)


def add_rows(first, count, rows, b, keep, gots, start, cols, pair=(), slot=0, landed=(), after=()):
    whole = keep.shape[2]
    width = cols // len(gots)
    shift = start // cols if gots[0].shape[2] == whole else 0
    more = pair[0].shape[2] if pair else 0
    keep_spec = pl.BlockSpec((1, rows, cols), lambda s: (first + s, b, start // cols))
    got_spec = pl.BlockSpec((1, rows, width), lambda s: (first + s, b, shift))
    pair_spec = pl.BlockSpec((1, rows, more), lambda s: (slot + s, 0, 0))
    landed_specs = [pl.BlockSpec((1, rows, cols), lambda s: (s, 0, start // cols))]
    if pair:
        landed_specs.append(pl.BlockSpec((1, rows, more), lambda s: (s, 0, whole // more)))
    landed_specs = landed_specs * len(landed)
    return pl.pallas_call(
        functools.partial(add_kernel, len(gots), len(pair) // 2, len(landed)),
        grid=(count,),
        in_specs=[keep_spec]
        + [got_spec] * len(gots)
        + [pair_spec] * len(pair)
        + landed_specs
        + [pl.BlockSpec(memory_space=pl.ANY)] * len(after),
        out_specs=pl.BlockSpec((1, rows, cols + more), lambda s: (s, 0, 0)),
        out_shape=pltpu.HBM((count, rows, cols + more), jnp.bfloat16),
        compiler_params=pltpu.CompilerParams(vmem_limit_bytes=VMEM_BYTES),
        cost_estimate=LIGHT,
        name="add_rows",
    )(
        *in_hbm([keep]),
        *gots,
        *in_hbm(pair[:1]),
        *pair[1:],
        *(list(landed) * (2 if pair else 1)),
        *in_hbm(after[:1]),
        *after[1:],
    )


def rotate_kernel(count, pieces, cos_ref, sin_ref, *refs):
    terms, gots, out_ref = refs[:count], refs[count : count + pieces], refs[-1]
    total = terms[0][0].astype(jnp.float32)
    for term in terms[1:]:
        total = total + term[0].astype(jnp.float32)
    cosine, sine = cos_ref[...], sin_ref[...]

    def write(total):
        for head in range(total.shape[1] // DH):
            part = total[:, head * DH : (head + 1) * DH]
            turned = pltpu.roll(part, DH // 2, axis=1)
            value = part * cosine + turned * sine
            out_ref[:, head * DH : (head + 1) * DH] = value.astype(out_ref.dtype)

    if not gots:
        write(total)
    for j, got in enumerate(gots):

        @pl.when(pl.program_id(0) == j)
        def _():
            write(total + got[0].astype(jnp.float32))


def sum_and_rotate(cosine, sine, terms, gots, cols, after=()):
    rows = cosine.shape[0]
    slot_of_gots, block_of_gots, shift, gots = gots
    tile = cols // max(1, len(gots))
    table = pl.BlockSpec((rows, DH), lambda j: (0, 0))

    def block(slot, b, start):
        return pl.BlockSpec((1, rows, tile), lambda j: (slot, b, start // tile + j))

    return pl.pallas_call(
        functools.partial(rotate_kernel, len(terms), len(gots)),
        grid=(cols // tile,),
        in_specs=[table, table]
        + [block(slot, b, start) for _, slot, b, start in terms]
        + [pl.BlockSpec((1, rows, tile), lambda j: (slot_of_gots, block_of_gots, shift))] * len(gots)
        + [pl.BlockSpec(memory_space=pl.ANY)] * len(after),
        out_specs=pl.BlockSpec((rows, tile), lambda j: (0, j)),
        out_shape=jax.ShapeDtypeStruct((rows, cols), jnp.bfloat16),
        compiler_params=pltpu.CompilerParams(vmem_limit_bytes=VMEM_BYTES),
        cost_estimate=LIGHT,
        name="sum_and_rotate",
    )(cosine, sine, *in_hbm([terms[0][0]]), *[term[0] for term in terms[1:]], *gots, *after)


def split_kernel(count, cos_ref, sin_ref, *refs):
    terms, (key_ref, value_ref) = refs[:count], refs[-2:]
    total = terms[0][0].astype(jnp.float32)
    for term in terms[1:]:
        total = total + term[0].astype(jnp.float32)
    half = total.shape[0]
    for b in range(total.shape[1] // (2 * DH)):
        rows = slice(b * half, (b + 1) * half)
        key = total[:, 2 * b * DH : (2 * b + 1) * DH]
        turned = pltpu.roll(key, DH // 2, axis=1)
        key_ref[rows] = (key * cos_ref[rows] + turned * sin_ref[rows]).astype(key_ref.dtype)
        value_ref[0, rows] = total[:, (2 * b + 1) * DH : (2 * b + 2) * DH].astype(value_ref.dtype)


def split_and_rotate(cosine, sine, terms, width):
    rows = cosine.shape[0]
    half = terms[0][0].shape[1]
    table = pl.BlockSpec((rows, DH), lambda j: (0, 0))

    def block(slot, start):
        return pl.BlockSpec((1, half, width), lambda j: (slot, 0, start // width))

    return pl.pallas_call(
        functools.partial(split_kernel, len(terms)),
        grid=(1,),
        in_specs=[table, table] + [block(slot, start) for _, slot, start in terms],
        out_specs=[table, pl.BlockSpec((1, rows, DH), lambda j: (0, 0, 0))],
        out_shape=[
            jax.ShapeDtypeStruct((rows, DH), jnp.bfloat16),
            jax.ShapeDtypeStruct((1, rows, DH), jnp.bfloat16),
        ],
        compiler_params=pltpu.CompilerParams(vmem_limit_bytes=VMEM_BYTES),
        cost_estimate=LIGHT,
        name="split_and_rotate",
    )(cosine, sine, *in_hbm([terms[0][0]]), *[term for term, _, _ in terms[1:]])


def prepare_kernel(canary_ref, ids_ref, own_ref, other_ref, order_ref, key_t_ref):
    order = jnp.where(canary_ref[...] == ids_ref[...], 1.0, 0.0).astype(jnp.bfloat16)
    order_ref[...] = order
    key = jnp.concatenate([own_ref[...], other_ref[...]], axis=0)
    key_t_ref[...] = jnp.dot(order, key, preferred_element_type=jnp.float32).T.astype(jnp.bfloat16)


def prepare(canary_rows, ids, own, other):
    rows = ids.shape[0]
    return pl.pallas_call(
        prepare_kernel,
        out_shape=[
            jax.ShapeDtypeStruct((rows, rows), jnp.bfloat16),
            jax.ShapeDtypeStruct((DH, rows), jnp.bfloat16),
        ],
        compiler_params=pltpu.CompilerParams(vmem_limit_bytes=VMEM_BYTES),
        name="order_and_keys",
    )(canary_rows.reshape(rows, 1), ids.reshape(1, rows), own, other)


def value_kernel(place_ref, order_ref, own_ref, other_ref, out_ref, mark_ref):
    mark_ref[...] = jnp.zeros_like(mark_ref)
    rows = jnp.concatenate([own_ref[0], other_ref[0]], axis=0)
    out_ref[...] = jnp.dot(order_ref[...], rows, preferred_element_type=jnp.float32).astype(out_ref.dtype)


def order_values(findex, order, own, other):
    rows = order.shape[0]
    slots, part, width = own.shape
    place = jnp.stack([findex ^ s for s in range(slots)]).astype(jnp.int32)
    block = pl.BlockSpec((1, part, width), lambda s, place: (place[s], 0, 0))
    return pl.pallas_call(
        value_kernel,
        grid_spec=pltpu.PrefetchScalarGridSpec(
            num_scalar_prefetch=1,
            grid=(slots,),
            in_specs=[pl.BlockSpec((rows, rows), lambda s, place: (0, 0)), block, block],
            out_specs=[
                pl.BlockSpec((rows, width), lambda s, place: (0, s)),
                pl.BlockSpec((8, DH), lambda s, place: (0, 0)),
            ],
        ),
        out_shape=[
            jax.ShapeDtypeStruct((rows, slots * width), jnp.bfloat16),
            jax.ShapeDtypeStruct((8, DH), jnp.float32),
        ],
        compiler_params=pltpu.CompilerParams(vmem_limit_bytes=VMEM_BYTES),
        name="order_values",
    )(place, order, own, other)


def score_kernel(count, order_ref, key_t_ref, *refs):
    queries, (out_ref, mark_ref) = refs[:count], refs[-2:]
    mark_ref[...] = jnp.zeros_like(mark_ref)
    stacked = jnp.concatenate([query[...] for query in queries], axis=0)
    chosen = jnp.dot(order_ref[...], stacked, preferred_element_type=jnp.float32).astype(jnp.bfloat16)
    for head in range(stacked.shape[1] // DH):
        products = jnp.dot(
            chosen[:, head * DH : (head + 1) * DH], key_t_ref[...], preferred_element_type=jnp.float32
        )
        out_ref[0, head] = (products * DH ** (-0.5)).astype(out_ref.dtype)


def score_heads(order, key_t, heads, start, count, queries, earlier, after=()):
    rows = order.shape[0]
    step = 2 if count % 2 == 0 else 1

    def block(query, first):
        return pl.BlockSpec((query.shape[0], step * DH), lambda j: (0, first // step + j))

    return pl.pallas_call(
        functools.partial(score_kernel, len(queries)),
        grid=(count // step,),
        in_specs=[
            pl.BlockSpec((rows, rows), lambda j: (0, 0)),
            pl.BlockSpec((DH, rows), lambda j: (0, 0)),
        ]
        + [block(query, first) for query, first in queries]
        + [pl.BlockSpec(memory_space=pl.ANY)] * (len(earlier) + len(after)),
        out_specs=[
            pl.BlockSpec((1, step, rows, rows), lambda j: (0, start // step + j, 0, 0)),
            pl.BlockSpec((8, DH), lambda j: (0, 0)),
        ],
        out_shape=[
            jax.ShapeDtypeStruct((1, heads, rows, rows), jnp.bfloat16),
            jax.ShapeDtypeStruct((8, DH), jnp.float32),
        ],
        input_output_aliases={2 + len(queries): 0} if earlier else {},
        compiler_params=pltpu.CompilerParams(vmem_limit_bytes=VMEM_BYTES),
        cost_estimate=LIGHT,
        name="score_heads",
    )(order, key_t, *[query for query, _ in queries], *earlier, *after)


def body(hidden, w_query, w_key, w_value, canary_rows, positions):
    shards = lax.axis_size("fsdp")
    findex = lax.axis_index("fsdp")
    tps = lax.axis_size("tp")
    tindex = lax.axis_index("tp")
    rindex = lax.axis_index("rep")
    local, depth = hidden.shape
    half = local // 2
    rows = local * tps
    head_cols = w_query.shape[1] // shards
    heads_here = head_cols // DH
    group = HQ // KV
    assert shards & (shards - 1) == 0 and lax.axis_size("rep") == 2

    def swap(x, bit):
        return lax.ppermute(x, "fsdp", [(i, i ^ bit) for i in range(shards)])

    def other_core(x):
        return lax.ppermute(x, "rep", [(0, 1), (1, 0)])

    def low(x):
        return x.astype(jnp.bfloat16)

    odd = list(range(3, shards, 2)) + [1]
    even = list(range(2, shards, 2))
    fast_pair = heads_here == group

    def spread(live):
        terms, first = [], None
        bit = 2
        while bit < shards:
            sent = [x for x in sorted(live) if x & bit]
            pack = jnp.stack([low(live[x]) for x in sent])
            first = pack if first is None else first
            landed = swap(pack, bit)
            for k, x in enumerate(sent):
                if x == bit:
                    terms.append(landed)
                else:
                    live[x ^ bit] = live[x ^ bit] + landed[k].astype(jnp.float32)
                del live[x]
            bit *= 2
        return terms, first

    blocks = [hidden] + [
        lax.ppermute(hidden, "tp", [(i, (i - b) % tps) for i in range(tps)]) for b in range(1, tps)
    ]

    block_ids = ((tindex + jnp.arange(tps, dtype=jnp.int32)) % tps * local)[:, None]
    own_ids = (block_ids + rindex * half + jnp.arange(half, dtype=jnp.int32)[None]).reshape(-1)
    other_ids = (block_ids + (1 - rindex) * half + jnp.arange(half, dtype=jnp.int32)[None]).reshape(-1)
    ids = jnp.concatenate([own_ids, other_ids])
    own_positions = jnp.sum(
        jnp.where(own_ids[:, None] == canary_rows[None, :], positions[None, :], 0), axis=1
    )
    cosine, sine = rope_tables(own_positions)

    tile = min(1024, head_cols)

    def project(slots, blocks, width, after=(), cost=LIGHT):
        keep, gives = project_query(
            rindex, findex, slots, blocks, w_query, head_cols, tile, width, after, cost
        )
        return keep, [other_core(give) for give in gives], gives[0]

    def rotate(b, p, split, terms, behind):
        cols = head_cols // split
        table = slice(b * half, (b + 1) * half)
        added = [(own_keep, 0, b, p * cols)] + terms
        turned = sum_and_rotate(cosine[table], sine[table], added, (0, b, p, own_got), cols, behind)
        return turned, other_core(turned)

    def add_even(b, start, cols, pair, behind):
        if shards == 2:
            return [], behind
        keep, got = evens[b]
        each = len(got) * cols // head_cols
        got = got[start // cols * each :][:each]
        summed = add_rows(
            0, len(even), half, 0, keep, got, start, cols, pair, len(odd), (fars[b],), behind
        )
        terms, first = spread({x: summed[k] for k, x in enumerate(even)})
        return [(term, 0, 0, 0) for term in terms], (first,)

    last, split = tps - 1, head_cols // tile
    placed = in_hbm(blocks[:1]) + blocks[1:]
    evens, fars, terms, pair, after = [], [], [], (), ()
    for b, block in enumerate(placed):
        if fast_pair and b == last:
            slots = odd + even + [0]
            pair_keep, give = project_pair(rindex, findex, slots, placed, w_key, w_value, after)
            pair = (pair_keep, other_core(give))
            after = (give,)
        odd_keep, odd_got, given = project(odd, [block], tile, after)
        count = len(odd) - 1 if b == last else len(odd)
        odd_sent = add_rows(0, count, half, 0, odd_keep, odd_got, 0, head_cols, pair)
        fars.append(swap(odd_sent, 1))
        after = (odd_sent,)
        if b > 0:
            added, after = add_even(b - 1, 0, head_cols, (), after)
            terms.append([(fars[b - 1], len(odd) - 1, 0, 0)] + added)
            after = (odd_sent,) + after
        if b == last:
            own_keep, own_got, given = project([0], placed, head_cols, after, HEAVY)
            after = (given,)
        even_keep, even_got, given = project(even, [block], tile, after)
        evens.append((even_keep, even_got))
        after = (given,)
    parts, behind = [], tuple(term[0] for row in terms for term in row[1:])
    for p in range(split):
        near_sent = add_rows(
            len(odd) - 1, 1, half, 0, odd_keep, odd_got[p : p + 1], p * tile, tile,
            pair if p == 0 else (), len(odd) - 1, (), after,
        )
        parts.append([(swap(near_sent, 1), 0, 0, 0)])
        after = (near_sent,)
    after = after + behind
    for p in range(split):
        added, after = add_even(last, p * tile, tile, pair if p == 0 else (), after)
        parts[p] += added

    if fast_pair:
        width = 2 * DH * tps
        pieces = [(array, shards - 1, 0) for array in pair]
        pieces += [(term, 0, tile) for term, _, _, _ in parts[0]]
        key_rot, held = split_and_rotate(cosine, sine, pieces, width)
        bit = 1
        while bit < shards:
            held = jnp.concatenate([held, swap(held, bit)])
            bit *= 2
        held_other = other_core(held)
    else:
        x = jnp.concatenate(blocks, axis=0)
        key_sum, value_sum = lax.psum(
            (
                jnp.dot(x, w_key, preferred_element_type=jnp.float32),
                jnp.dot(x, w_value, preferred_element_type=jnp.float32),
            ),
            ("fsdp", "rep"),
        )

        def of_core(y, core):
            parts = y.reshape(tps, 2, half, -1)
            return lax.dynamic_index_in_dim(parts, core, 1, keepdims=False).reshape(tps * half, -1)

        mine = lax.dynamic_slice_in_dim(key_sum, findex * heads_here // group * DH, DH, 1)
        key_own = of_core(mine, rindex)
        key_rot = sum_and_rotate(cosine, sine, [(key_own[None], 0, 0, 0)], (0, 0, 0, []), DH, after)
        value_rows = low(jnp.concatenate([of_core(value_sum, rindex), of_core(value_sum, 1 - rindex)]))

    order, key_t = prepare(canary_rows, ids, key_rot, other_core(key_rot))
    if fast_pair:
        values, values_mark = order_values(findex, order, held, held_other)
    else:
        values_mark = key_t
        values = low(jnp.dot(order, value_rows, preferred_element_type=jnp.float32))

    rotated = [rotate(b, 0, 1, terms[b], (key_rot,)) for b in range(last)]
    count = heads_here // split
    scores, mark = (), ()
    for p in range(split):
        turned = rotate(last, p, split, parts[p], (key_t,) + mark)
        queries = [(row[0], p * count) for row in rotated] + [(turned[0], 0)]
        queries += [(row[1], p * count) for row in rotated] + [(turned[1], 0)]
        *scores, mark = score_heads(
            order, key_t, heads_here, p * count, count, queries, scores
        )
        mark = (mark,)
    return (scores[0], values)


def solution(mesh):
    in_specs = (
        P(("groups", "tp"), ("fsdp", "rep")),
        P(("fsdp", "rep"), "tp"),
        P(("fsdp", "rep"), "tp"),
        P(("fsdp", "rep"), "tp"),
        P("groups"),
        P("groups"),
    )
    out_specs = (P("tp", "fsdp", "groups", None), P("groups", "tp"))
    return jax.shard_map(body, mesh=mesh, in_specs=in_specs, out_specs=out_specs, check_vma=False)
```

```python
import functools
import math

import jax
import jax.numpy as jnp
from jax import lax
from jax.experimental import pallas as pl
from jax.experimental.pallas import tpu as pltpu
from jax.sharding import PartitionSpec as P

HQ = 128
KV = 8
DH = 128
VMEM_BYTES = 28 * 1024 * 1024
LIGHT = pl.CostEstimate(flops=1000, bytes_accessed=1000, transcendentals=0)
HEAVY = pl.CostEstimate(flops=10**11, bytes_accessed=10**8, transcendentals=0)


def in_hbm(arrays):
    return [pltpu.with_memory_space_constraint(x, pltpu.HBM) for x in arrays]


def rope_tables(positions):
    half = DH // 2
    expo = jnp.arange(half, dtype=jnp.float32) * (2.0 / DH)
    freq = jnp.power(jnp.float32(500000.0), -expo)
    wavelen = 2.0 * math.pi / freq
    smooth = (8192.0 / wavelen - 1.0) / 3.0
    mixed = (1.0 - smooth) * freq / 8.0 + smooth * freq
    freq = jnp.where(wavelen > 8192.0, freq / 8.0, jnp.where(wavelen < 2048.0, freq, mixed))
    angle = positions.astype(jnp.float32)[:, None] * freq[None, :]
    cosine, sine = jnp.cos(angle), jnp.sin(angle)
    return jnp.concatenate([cosine, cosine], axis=1), jnp.concatenate([-sine, sine], axis=1)


def ordered_rows(place_ref, x_refs, rows_ref):
    core = place_ref[0]
    half = x_refs[0].shape[0] // 2
    for b, x_ref in enumerate(x_refs):
        kept, given = b * half, (len(x_refs) + b) * half
        rows_ref[kept : kept + half] = x_ref[pl.ds(pl.multiple_of(core * half, 16), half)]
        rows_ref[given : given + half] = x_ref[pl.ds(pl.multiple_of((1 - core) * half, 16), half)]


def query_kernel(count, pieces, place_ref, *refs):
    x_refs, w_ref = refs[:count], refs[count]
    keep_ref, *give_refs, rows_ref = refs[-2 - pieces :]
    tile = pl.program_id(1)
    size = give_refs[0].shape[2]
    each = keep_ref.shape[2] // size

    @pl.when((pl.program_id(0) == 0) & (tile == 0))
    def _():
        ordered_rows(place_ref, x_refs, rows_ref)

    result = jnp.dot(rows_ref[...], w_ref[...], preferred_element_type=jnp.float32)
    half = result.shape[0] // 2
    keep_ref[0] = result[:half]
    for j, give_ref in enumerate(give_refs):

        @pl.when((tile == j // each) | (pieces == 1))
        def _():
            start = j % each * size
            give_ref[0] = result[half:, start : start + size].astype(give_ref.dtype)


def project_query(rindex, findex, slots, blocks, w, cols, tile, width, after, cost):
    rows, depth = blocks[0].shape
    count = len(blocks)
    half = rows // 2 * count
    tiles, pieces = cols // tile, cols // width
    place = jnp.stack([rindex] + [findex ^ slot for slot in slots]).astype(jnp.int32)
    keep_spec = pl.BlockSpec((1, half, tile), lambda s, j, place: (s, 0, j))
    give_spec = pl.BlockSpec((1, half, width), lambda s, j, place: (s, 0, 0))
    x_spec = pl.BlockSpec((rows, depth), lambda s, j, place: (0, 0), pipeline_mode=pl.Buffered(1))
    outs = pl.pallas_call(
        functools.partial(query_kernel, count, pieces),
        grid_spec=pltpu.PrefetchScalarGridSpec(
            num_scalar_prefetch=1,
            grid=(len(slots), tiles),
            in_specs=[x_spec] * count
            + [pl.BlockSpec((depth, tile), lambda s, j, place: (0, place[1 + s] * tiles + j))]
            + [pl.BlockSpec(memory_space=pl.ANY)] * len(after),
            out_specs=[keep_spec] + ([keep_spec] if pieces == 1 else [give_spec] * pieces),
            scratch_shapes=[pltpu.VMEM((2 * half, depth), w.dtype)],
        ),
        out_shape=[pltpu.HBM((len(slots), half, cols), jnp.float32)]
        + [pltpu.HBM((len(slots), half, width), jnp.bfloat16)] * pieces,
        compiler_params=pltpu.CompilerParams(vmem_limit_bytes=VMEM_BYTES),
        cost_estimate=cost,
        name="query_products",
    )(place, *blocks, *in_hbm([w]), *in_hbm(after[:1]), *after[1:])
    return outs[0], outs[1:]


def pair_kernel(count, place_ref, *refs):
    x_refs, (wk_ref, wv_ref) = refs[:count], refs[count : count + 2]
    keep_ref, give_ref, rows_ref = refs[-3:]

    @pl.when(pl.program_id(0) == 0)
    def _():
        ordered_rows(place_ref, x_refs, rows_ref)

    weights = jnp.concatenate([wk_ref[...], wv_ref[...]], axis=1)
    result = jnp.dot(rows_ref[...], weights, preferred_element_type=jnp.float32)
    half, width = x_refs[0].shape[0] // 2, weights.shape[1]
    for b in range(count):
        kept, given = b * half, (count + b) * half
        cols = slice(b * width, (b + 1) * width)
        keep_ref[0, :, cols] = result[kept : kept + half]
        give_ref[0, :, cols] = result[given : given + half].astype(give_ref.dtype)


def project_pair(rindex, findex, slots, blocks, w_key, w_value, after=()):
    rows, depth = blocks[0].shape
    count = len(blocks)
    place = jnp.stack([rindex] + [findex ^ slot for slot in slots]).astype(jnp.int32)
    weight = pl.BlockSpec((depth, DH), lambda s, place: (0, place[1 + s]))
    shape = (len(slots), rows // 2, 2 * DH * count)
    out = pl.BlockSpec((1,) + shape[1:], lambda s, place: (s, 0, 0))
    return pl.pallas_call(
        functools.partial(pair_kernel, count),
        grid_spec=pltpu.PrefetchScalarGridSpec(
            num_scalar_prefetch=1,
            grid=(len(slots),),
            in_specs=[pl.BlockSpec((rows, depth), lambda s, place: (0, 0))] * count
            + [weight, weight]
            + [pl.BlockSpec(memory_space=pl.ANY)] * len(after),
            out_specs=[out, out],
            scratch_shapes=[pltpu.VMEM((count * rows, depth), blocks[0].dtype)],
        ),
        out_shape=[
            pltpu.HBM(shape, jnp.float32),
            pltpu.HBM(shape, jnp.bfloat16),
        ],
        compiler_params=pltpu.CompilerParams(vmem_limit_bytes=VMEM_BYTES),
        cost_estimate=LIGHT,
        name="key_value_products",
    )(place, *blocks, *in_hbm([w_key, w_value, *after]))


def add_kernel(gots, paired, extra, *refs):
    keep_ref, got_refs, out_ref = refs[0], refs[1 : 1 + gots], refs[-1]
    pair_refs = refs[1 + gots : 1 + gots + 2 * paired]
    landed_refs = refs[1 + gots + 2 * paired :][: extra * (1 + paired)]
    width = got_refs[0].shape[2]
    cols = gots * width

    def total(first, second, landed):
        value = first + second.astype(jnp.float32)
        for term in landed:
            value = value + term.astype(jnp.float32)
        return value.astype(out_ref.dtype)

    for t, got_ref in enumerate(got_refs):
        part = slice(t * width, (t + 1) * width)
        landed = [landed_refs[0][0, :, part]] if extra else []
        out_ref[0, :, part] = total(keep_ref[0, :, part], got_ref[0], landed)
    if paired:
        landed = [landed_refs[1][0]] if extra else []
        out_ref[0, :, cols:] = total(pair_refs[0][0], pair_refs[1][0], landed)


def add_rows(first, count, rows, b, keep, gots, start, cols, pair=(), slot=0, landed=(), after=()):
    whole = keep.shape[2]
    width = cols // len(gots)
    shift = start // cols if gots[0].shape[2] == whole else 0
    more = pair[0].shape[2] if pair else 0
    keep_spec = pl.BlockSpec((1, rows, cols), lambda s: (first + s, b, start // cols))
    got_spec = pl.BlockSpec((1, rows, width), lambda s: (first + s, b, shift))
    pair_spec = pl.BlockSpec((1, rows, more), lambda s: (slot + s, 0, 0))
    landed_specs = [pl.BlockSpec((1, rows, cols), lambda s: (s, 0, start // cols))]
    if pair:
        landed_specs.append(pl.BlockSpec((1, rows, more), lambda s: (s, 0, whole // more)))
    landed_specs = landed_specs * len(landed)
    return pl.pallas_call(
        functools.partial(add_kernel, len(gots), len(pair) // 2, len(landed)),
        grid=(count,),
        in_specs=[keep_spec]
        + [got_spec] * len(gots)
        + [pair_spec] * len(pair)
        + landed_specs
        + [pl.BlockSpec(memory_space=pl.ANY)] * len(after),
        out_specs=pl.BlockSpec((1, rows, cols + more), lambda s: (s, 0, 0)),
        out_shape=pltpu.HBM((count, rows, cols + more), jnp.bfloat16),
        compiler_params=pltpu.CompilerParams(vmem_limit_bytes=VMEM_BYTES),
        cost_estimate=LIGHT,
        name="add_rows",
    )(
        *in_hbm([keep]),
        *gots,
        *in_hbm(pair[:1]),
        *pair[1:],
        *(list(landed) * (2 if pair else 1)),
        *in_hbm(after[:1]),
        *after[1:],
    )


def rotate_kernel(count, pieces, cos_ref, sin_ref, *refs):
    terms, gots, out_ref = refs[:count], refs[count : count + pieces], refs[-1]
    total = terms[0][0].astype(jnp.float32)
    for term in terms[1:]:
        total = total + term[0].astype(jnp.float32)
    cosine, sine = cos_ref[...], sin_ref[...]

    def write(total):
        for head in range(total.shape[1] // DH):
            part = total[:, head * DH : (head + 1) * DH]
            turned = pltpu.roll(part, DH // 2, axis=1)
            value = part * cosine + turned * sine
            out_ref[:, head * DH : (head + 1) * DH] = value.astype(out_ref.dtype)

    if not gots:
        write(total)
    for j, got in enumerate(gots):

        @pl.when(pl.program_id(0) == j)
        def _():
            write(total + got[0].astype(jnp.float32))


def sum_and_rotate(cosine, sine, terms, gots, cols, after=()):
    rows = cosine.shape[0]
    slot_of_gots, block_of_gots, shift, gots = gots
    tile = cols // max(1, len(gots))
    table = pl.BlockSpec((rows, DH), lambda j: (0, 0))

    def block(slot, b, start):
        return pl.BlockSpec((1, rows, tile), lambda j: (slot, b, start // tile + j))

    return pl.pallas_call(
        functools.partial(rotate_kernel, len(terms), len(gots)),
        grid=(cols // tile,),
        in_specs=[table, table]
        + [block(slot, b, start) for _, slot, b, start in terms]
        + [pl.BlockSpec((1, rows, tile), lambda j: (slot_of_gots, block_of_gots, shift))] * len(gots)
        + [pl.BlockSpec(memory_space=pl.ANY)] * len(after),
        out_specs=pl.BlockSpec((rows, tile), lambda j: (0, j)),
        out_shape=jax.ShapeDtypeStruct((rows, cols), jnp.bfloat16),
        compiler_params=pltpu.CompilerParams(vmem_limit_bytes=VMEM_BYTES),
        cost_estimate=LIGHT,
        name="sum_and_rotate",
    )(cosine, sine, *in_hbm([terms[0][0]]), *[term[0] for term in terms[1:]], *gots, *after)


def split_kernel(count, cos_ref, sin_ref, *refs):
    terms, (key_ref, value_ref) = refs[:count], refs[-2:]
    total = terms[0][0].astype(jnp.float32)
    for term in terms[1:]:
        total = total + term[0].astype(jnp.float32)
    half = total.shape[0]
    for b in range(total.shape[1] // (2 * DH)):
        rows = slice(b * half, (b + 1) * half)
        key = total[:, 2 * b * DH : (2 * b + 1) * DH]
        turned = pltpu.roll(key, DH // 2, axis=1)
        key_ref[rows] = (key * cos_ref[rows] + turned * sin_ref[rows]).astype(key_ref.dtype)
        value_ref[0, rows] = total[:, (2 * b + 1) * DH : (2 * b + 2) * DH].astype(value_ref.dtype)


def split_and_rotate(cosine, sine, terms, width, after):
    rows = cosine.shape[0]
    half = terms[0][0].shape[1]
    table = pl.BlockSpec((rows, DH), lambda j: (0, 0))

    def block(slot, start):
        return pl.BlockSpec((1, half, width), lambda j: (slot, 0, start // width))

    return pl.pallas_call(
        functools.partial(split_kernel, len(terms)),
        grid=(1,),
        in_specs=[table, table]
        + [block(slot, start) for _, slot, start in terms]
        + [pl.BlockSpec(memory_space=pl.ANY)] * len(after),
        out_specs=[table, pl.BlockSpec((1, rows, DH), lambda j: (0, 0, 0))],
        out_shape=[
            jax.ShapeDtypeStruct((rows, DH), jnp.bfloat16),
            jax.ShapeDtypeStruct((1, rows, DH), jnp.bfloat16),
        ],
        compiler_params=pltpu.CompilerParams(vmem_limit_bytes=VMEM_BYTES),
        cost_estimate=LIGHT,
        name="split_and_rotate",
    )(cosine, sine, *in_hbm([terms[0][0]]), *[term for term, _, _ in terms[1:]], *after)


def prepare_kernel(canary_ref, ids_ref, own_ref, other_ref, order_ref, key_t_ref):
    order = jnp.where(canary_ref[...] == ids_ref[...], 1.0, 0.0).astype(jnp.bfloat16)
    order_ref[...] = order
    key = jnp.concatenate([own_ref[...], other_ref[...]], axis=0)
    key_t_ref[...] = jnp.dot(order, key, preferred_element_type=jnp.float32).T.astype(jnp.bfloat16)


def prepare(canary_rows, ids, own, other):
    rows = ids.shape[0]
    return pl.pallas_call(
        prepare_kernel,
        out_shape=[
            jax.ShapeDtypeStruct((rows, rows), jnp.bfloat16),
            jax.ShapeDtypeStruct((DH, rows), jnp.bfloat16),
        ],
        compiler_params=pltpu.CompilerParams(vmem_limit_bytes=VMEM_BYTES),
        name="order_and_keys",
    )(canary_rows.reshape(rows, 1), ids.reshape(1, rows), own, other)


def stack_kernel(count, *refs):
    out_ref, start = refs[-1], 0
    for ref in refs[:count]:
        out_ref[start : start + ref.shape[0]] = ref[...]
        start += ref.shape[0]


def stack_slots(arrays, after):
    slots = sum(x.shape[0] for x in arrays)
    shape = (slots,) + arrays[0].shape[1:]
    return pl.pallas_call(
        functools.partial(stack_kernel, len(arrays)),
        grid=(1,),
        in_specs=[pl.BlockSpec(x.shape, lambda j: (0, 0, 0)) for x in arrays]
        + [pl.BlockSpec(memory_space=pl.ANY)] * len(after),
        out_specs=pl.BlockSpec(shape, lambda j: (0, 0, 0)),
        out_shape=jax.ShapeDtypeStruct(shape, arrays[0].dtype),
        compiler_params=pltpu.CompilerParams(vmem_limit_bytes=VMEM_BYTES),
        cost_estimate=LIGHT,
        name="stack_slots",
    )(*arrays, *after)


def value_kernel(place_ref, order_ref, own_ref, other_ref, out_ref):
    rows = jnp.concatenate([own_ref[0], other_ref[0]], axis=0)
    out_ref[...] = jnp.dot(order_ref[...], rows, preferred_element_type=jnp.float32).astype(out_ref.dtype)


def order_values(findex, order, own, other):
    rows = order.shape[0]
    slots, part, width = own.shape
    place = jnp.stack([findex ^ s for s in range(slots)]).astype(jnp.int32)
    block = pl.BlockSpec((1, part, width), lambda s, place: (place[s], 0, 0))
    return pl.pallas_call(
        value_kernel,
        grid_spec=pltpu.PrefetchScalarGridSpec(
            num_scalar_prefetch=1,
            grid=(slots,),
            in_specs=[pl.BlockSpec((rows, rows), lambda s, place: (0, 0)), block, block],
            out_specs=pl.BlockSpec((rows, width), lambda s, place: (0, s)),
        ),
        out_shape=jax.ShapeDtypeStruct((rows, slots * width), jnp.bfloat16),
        compiler_params=pltpu.CompilerParams(vmem_limit_bytes=VMEM_BYTES),
        name="order_values",
    )(place, order, own, other)


def score_kernel(count, order_ref, key_t_ref, *refs):
    queries, (out_ref, mark_ref) = refs[:count], refs[-2:]
    mark_ref[...] = jnp.zeros_like(mark_ref)
    stacked = jnp.concatenate([query[...] for query in queries], axis=0)
    chosen = jnp.dot(order_ref[...], stacked, preferred_element_type=jnp.float32).astype(jnp.bfloat16)
    for head in range(stacked.shape[1] // DH):
        products = jnp.dot(
            chosen[:, head * DH : (head + 1) * DH], key_t_ref[...], preferred_element_type=jnp.float32
        )
        out_ref[0, head] = (products * DH ** (-0.5)).astype(out_ref.dtype)


def score_heads(order, key_t, heads, start, count, queries, earlier, after=()):
    rows = order.shape[0]
    step = 2 if count % 2 == 0 else 1

    def block(query, first):
        return pl.BlockSpec((query.shape[0], step * DH), lambda j: (0, first // step + j))

    return pl.pallas_call(
        functools.partial(score_kernel, len(queries)),
        grid=(count // step,),
        in_specs=[
            pl.BlockSpec((rows, rows), lambda j: (0, 0)),
            pl.BlockSpec((DH, rows), lambda j: (0, 0)),
        ]
        + [block(query, first) for query, first in queries]
        + [pl.BlockSpec(memory_space=pl.ANY)] * (len(earlier) + len(after)),
        out_specs=[
            pl.BlockSpec((1, step, rows, rows), lambda j: (0, start // step + j, 0, 0)),
            pl.BlockSpec((8, DH), lambda j: (0, 0)),
        ],
        out_shape=[
            jax.ShapeDtypeStruct((1, heads, rows, rows), jnp.bfloat16),
            jax.ShapeDtypeStruct((8, DH), jnp.float32),
        ],
        input_output_aliases={2 + len(queries): 0} if earlier else {},
        compiler_params=pltpu.CompilerParams(vmem_limit_bytes=VMEM_BYTES),
        cost_estimate=LIGHT,
        name="score_heads",
    )(order, key_t, *[query for query, _ in queries], *earlier, *after)


def body(hidden, w_query, w_key, w_value, canary_rows, positions):
    shards = lax.axis_size("fsdp")
    findex = lax.axis_index("fsdp")
    tps = lax.axis_size("tp")
    tindex = lax.axis_index("tp")
    rindex = lax.axis_index("rep")
    local, depth = hidden.shape
    half = local // 2
    rows = local * tps
    head_cols = w_query.shape[1] // shards
    heads_here = head_cols // DH
    group = HQ // KV
    assert shards & (shards - 1) == 0 and lax.axis_size("rep") == 2

    def swap(x, bit):
        return lax.ppermute(x, "fsdp", [(i, i ^ bit) for i in range(shards)])

    def other_core(x):
        return lax.ppermute(x, "rep", [(0, 1), (1, 0)])

    def low(x):
        return x.astype(jnp.bfloat16)

    odd = list(range(3, shards, 2)) + [1]
    even = list(range(2, shards, 2))
    fast_pair = heads_here == group

    def spread(live):
        terms, first = [], None
        bit = 2
        while bit < shards:
            sent = [x for x in sorted(live) if x & bit]
            pack = jnp.stack([low(live[x]) for x in sent])
            first = pack if first is None else first
            landed = swap(pack, bit)
            for k, x in enumerate(sent):
                if x == bit:
                    terms.append(landed)
                else:
                    live[x ^ bit] = live[x ^ bit] + landed[k].astype(jnp.float32)
                del live[x]
            bit *= 2
        return terms, first

    blocks = [hidden] + [
        lax.ppermute(hidden, "tp", [(i, (i - b) % tps) for i in range(tps)]) for b in range(1, tps)
    ]

    block_ids = ((tindex + jnp.arange(tps, dtype=jnp.int32)) % tps * local)[:, None]
    own_ids = (block_ids + rindex * half + jnp.arange(half, dtype=jnp.int32)[None]).reshape(-1)
    other_ids = (block_ids + (1 - rindex) * half + jnp.arange(half, dtype=jnp.int32)[None]).reshape(-1)
    ids = jnp.concatenate([own_ids, other_ids])
    own_positions = jnp.sum(
        jnp.where(own_ids[:, None] == canary_rows[None, :], positions[None, :], 0), axis=1
    )
    cosine, sine = rope_tables(own_positions)

    tile = min(1024, head_cols)

    def project(slots, blocks, width, after=(), cost=LIGHT):
        keep, gives = project_query(
            rindex, findex, slots, blocks, w_query, head_cols, tile, width, after, cost
        )
        return keep, [other_core(give) for give in gives], gives[0]

    def rotate(b, p, split, terms, behind):
        cols = head_cols // split
        table = slice(b * half, (b + 1) * half)
        keep, got = owns[b]
        added = [(keep, 0, 0, p * cols)] + terms
        turned = sum_and_rotate(cosine[table], sine[table], added, (0, 0, p, got), cols, behind)
        return turned, other_core(turned)

    def add_even(b, start, cols, pair, behind):
        if shards == 2:
            return [], behind
        keep, got = evens[b]
        each = len(got) * cols // head_cols
        got = got[start // cols * each :][:each]
        summed = add_rows(
            0, len(even), half, 0, keep, got, start, cols, pair, len(odd), (fars[b],), behind
        )
        terms, first = spread({x: summed[k] for k, x in enumerate(even)})
        return [(term, 0, 0, 0) for term in terms], (first,)

    last, split = tps - 1, head_cols // tile
    placed = in_hbm(blocks[:1]) + blocks[1:]
    evens, owns, fars, terms, pair, after = [], [], [], [], (), ()
    for b, block in enumerate(placed):
        if fast_pair and b == last:
            slots = odd + even + [0]
            pair_keep, give = project_pair(rindex, findex, slots, placed, w_key, w_value, after)
            pair = (pair_keep, other_core(give))
            after = (give,)
        odd_keep, odd_got, given = project(odd, [block], tile, after)
        count = len(odd) - 1 if b == last else len(odd)
        odd_sent = add_rows(0, count, half, 0, odd_keep, odd_got, 0, head_cols, pair)
        fars.append(swap(odd_sent, 1))
        after = (odd_sent,)
        if b > 0:
            added, after = add_even(b - 1, 0, head_cols, (), after)
            terms.append([(fars[b - 1], len(odd) - 1, 0, 0)] + added)
            after = (odd_sent,) + after
        if b == last:
            for c, near in enumerate(placed):
                cost = LIGHT if c else HEAVY
                own_keep, own_got, given = project([0], [near], head_cols, after, cost)
                owns.append((own_keep, own_got))
                after = (given,)
        even_keep, even_got, given = project(even, [block], tile, after)
        evens.append((even_keep, even_got))
        after = (given,)
    parts, behind = [], tuple(term[0] for row in terms for term in row[1:])
    for p in range(split):
        near_sent = add_rows(
            len(odd) - 1, 1, half, 0, odd_keep, odd_got[p : p + 1], p * tile, tile,
            pair if p == 0 else (), len(odd) - 1, (), after,
        )
        parts.append([(swap(near_sent, 1), 0, 0, 0)])
        after = (near_sent,)
    after = after + behind
    for p in range(split):
        added, after = add_even(last, p * tile, tile, pair if p == 0 else (), after)
        parts[p] += added

    if fast_pair:
        width = 2 * DH * tps
        pieces = [(array, shards - 1, 0) for array in pair]
        pieces += [(term, 0, tile) for term, _, _, _ in parts[0]]
        key_rot, held = split_and_rotate(cosine, sine, pieces, width, after)
        held = [held]
        while 2 ** len(held) <= shards:
            known = held[0] if len(held) == 1 else jnp.concatenate(held)
            held.append(swap(known, 2 ** (len(held) - 1)))
    else:
        x = jnp.concatenate(blocks, axis=0)
        key_sum, value_sum = lax.psum(
            (
                jnp.dot(x, w_key, preferred_element_type=jnp.float32),
                jnp.dot(x, w_value, preferred_element_type=jnp.float32),
            ),
            ("fsdp", "rep"),
        )

        def of_core(y, core):
            parts = y.reshape(tps, 2, half, -1)
            return lax.dynamic_index_in_dim(parts, core, 1, keepdims=False).reshape(tps * half, -1)

        mine = lax.dynamic_slice_in_dim(key_sum, findex * heads_here // group * DH, DH, 1)
        key_own = of_core(mine, rindex)
        key_rot = sum_and_rotate(cosine, sine, [(key_own[None], 0, 0, 0)], (0, 0, 0, []), DH, after)
        value_rows = low(jnp.concatenate([of_core(value_sum, rindex), of_core(value_sum, 1 - rindex)]))

    order, key_t = prepare(canary_rows, ids, key_rot, other_core(key_rot))
    if not fast_pair:
        values = low(jnp.dot(order, value_rows, preferred_element_type=jnp.float32))

    rotated = [rotate(b, 0, 1, terms[b], after) for b in range(last)]
    count = heads_here // split
    scores, mark = (), ()
    for p in range(split):
        turned = rotate(last, p, split, parts[p], mark)
        queries = [(row[0], p * count) for row in rotated] + [(turned[0], 0)]
        queries += [(row[1], p * count) for row in rotated] + [(turned[1], 0)]
        *scores, mark = score_heads(
            order, key_t, heads_here, p * count, count, queries, scores
        )
        mark = (mark,)
        if fast_pair and p == 0:
            held = stack_slots(held, mark)
            values = order_values(findex, order, held, other_core(held))
    return (scores[0], values)


def solution(mesh):
    in_specs = (
        P(("groups", "tp"), ("fsdp", "rep")),
        P(("fsdp", "rep"), "tp"),
        P(("fsdp", "rep"), "tp"),
        P(("fsdp", "rep"), "tp"),
        P("groups"),
        P("groups"),
    )
    out_specs = (P("tp", "fsdp", "groups", None), P("groups", "tp"))
    return jax.shard_map(body, mesh=mesh, in_specs=in_specs, out_specs=out_specs, check_vma=False)
```

```python
import functools
import math

import jax
import jax.numpy as jnp
from jax import lax
from jax.experimental import pallas as pl
from jax.experimental.pallas import tpu as pltpu
from jax.sharding import PartitionSpec as P

HQ = 128
KV = 8
DH = 128
VMEM_BYTES = 28 * 1024 * 1024
LIGHT = pl.CostEstimate(flops=1000, bytes_accessed=1000, transcendentals=0)
HEAVY = pl.CostEstimate(flops=10**11, bytes_accessed=10**8, transcendentals=0)


def in_hbm(arrays):
    return [pltpu.with_memory_space_constraint(x, pltpu.HBM) for x in arrays]


def rope_tables(positions):
    half = DH // 2
    expo = jnp.arange(half, dtype=jnp.float32) * (2.0 / DH)
    freq = jnp.power(jnp.float32(500000.0), -expo)
    wavelen = 2.0 * math.pi / freq
    smooth = (8192.0 / wavelen - 1.0) / 3.0
    mixed = (1.0 - smooth) * freq / 8.0 + smooth * freq
    freq = jnp.where(wavelen > 8192.0, freq / 8.0, jnp.where(wavelen < 2048.0, freq, mixed))
    angle = positions.astype(jnp.float32)[:, None] * freq[None, :]
    cosine, sine = jnp.cos(angle), jnp.sin(angle)
    return jnp.concatenate([cosine, cosine], axis=1), jnp.concatenate([-sine, sine], axis=1)


def ordered_rows(place_ref, x_refs, rows_ref):
    core = place_ref[0]
    half = x_refs[0].shape[0] // 2
    for b, x_ref in enumerate(x_refs):
        kept, given = b * half, (len(x_refs) + b) * half
        rows_ref[kept : kept + half] = x_ref[pl.ds(pl.multiple_of(core * half, 16), half)]
        rows_ref[given : given + half] = x_ref[pl.ds(pl.multiple_of((1 - core) * half, 16), half)]


def query_kernel(count, pieces, by_slot, place_ref, *refs):
    x_refs, w_ref = refs[:count], refs[count]
    keep_ref, *give_refs, rows_ref = refs[-2 - pieces :]
    tile = pl.program_id(1)
    size = give_refs[0].shape[2]
    each = keep_ref.shape[2] // size

    @pl.when((pl.program_id(0) == 0) & (tile == 0))
    def _():
        ordered_rows(place_ref, x_refs, rows_ref)

    result = jnp.dot(rows_ref[...], w_ref[...], preferred_element_type=jnp.float32)
    half = result.shape[0] // 2
    keep_ref[0] = result[:half]
    for j, give_ref in enumerate(give_refs):

        @pl.when(pl.program_id(0) == j if by_slot else (tile == j // each) | (pieces == 1))
        def _():
            start = j % each * size
            give_ref[0] = result[half:, start : start + size].astype(give_ref.dtype)


def project_query(rindex, findex, slots, blocks, w, cols, tile, width, after, cost, by_slot):
    rows, depth = blocks[0].shape
    count = len(blocks)
    half = rows // 2 * count
    tiles, pieces = cols // tile, len(slots) if by_slot else cols // width
    place = jnp.stack([rindex] + [findex ^ slot for slot in slots]).astype(jnp.int32)
    keep_spec = pl.BlockSpec((1, half, tile), lambda s, j, place: (s, 0, j))
    give_spec = pl.BlockSpec((1, half, width), lambda s, j, place: (s, 0, 0))

    def slot_spec(k):
        def index(s, j, place):
            return (0, 0, jnp.where(s < k, 0, jnp.where(s > k, tiles - 1, j)))

        return pl.BlockSpec((1, half, tile), index)

    give_specs = [keep_spec] if pieces == 1 else [give_spec] * pieces
    given = (len(slots), half, width)
    if by_slot:
        give_specs, given = [slot_spec(k) for k in range(pieces)], (1, half, cols)
    x_spec = pl.BlockSpec((rows, depth), lambda s, j, place: (0, 0), pipeline_mode=pl.Buffered(1))
    outs = pl.pallas_call(
        functools.partial(query_kernel, count, pieces, by_slot),
        grid_spec=pltpu.PrefetchScalarGridSpec(
            num_scalar_prefetch=1,
            grid=(len(slots), tiles),
            in_specs=[x_spec] * count
            + [pl.BlockSpec((depth, tile), lambda s, j, place: (0, place[1 + s] * tiles + j))]
            + [pl.BlockSpec(memory_space=pl.ANY)] * len(after),
            out_specs=[keep_spec] + give_specs,
            scratch_shapes=[pltpu.VMEM((2 * half, depth), w.dtype)],
        ),
        out_shape=[pltpu.HBM((len(slots), half, cols), jnp.float32)]
        + [pltpu.HBM(given, jnp.bfloat16)] * pieces,
        compiler_params=pltpu.CompilerParams(vmem_limit_bytes=VMEM_BYTES),
        cost_estimate=cost,
        name="query_products",
    )(place, *blocks, *in_hbm([w]), *in_hbm(after[:1]), *after[1:])
    return outs[0], outs[1:]


def pair_kernel(count, place_ref, *refs):
    x_refs, (wk_ref, wv_ref) = refs[:count], refs[count : count + 2]
    keep_ref, give_ref, rows_ref = refs[-3:]

    @pl.when(pl.program_id(0) == 0)
    def _():
        ordered_rows(place_ref, x_refs, rows_ref)

    weights = jnp.concatenate([wk_ref[...], wv_ref[...]], axis=1)
    result = jnp.dot(rows_ref[...], weights, preferred_element_type=jnp.float32)
    half, width = x_refs[0].shape[0] // 2, weights.shape[1]
    for b in range(count):
        kept, given = b * half, (count + b) * half
        cols = slice(b * width, (b + 1) * width)
        keep_ref[0, :, cols] = result[kept : kept + half]
        give_ref[0, :, cols] = result[given : given + half].astype(give_ref.dtype)


def project_pair(rindex, findex, slots, blocks, w_key, w_value, after=()):
    rows, depth = blocks[0].shape
    count = len(blocks)
    place = jnp.stack([rindex] + [findex ^ slot for slot in slots]).astype(jnp.int32)
    weight = pl.BlockSpec((depth, DH), lambda s, place: (0, place[1 + s]))
    shape = (len(slots), rows // 2, 2 * DH * count)
    out = pl.BlockSpec((1,) + shape[1:], lambda s, place: (s, 0, 0))
    return pl.pallas_call(
        functools.partial(pair_kernel, count),
        grid_spec=pltpu.PrefetchScalarGridSpec(
            num_scalar_prefetch=1,
            grid=(len(slots),),
            in_specs=[pl.BlockSpec((rows, depth), lambda s, place: (0, 0))] * count
            + [weight, weight]
            + [pl.BlockSpec(memory_space=pl.ANY)] * len(after),
            out_specs=[out, out],
            scratch_shapes=[pltpu.VMEM((count * rows, depth), blocks[0].dtype)],
        ),
        out_shape=[
            pltpu.HBM(shape, jnp.float32),
            pltpu.HBM(shape, jnp.bfloat16),
        ],
        compiler_params=pltpu.CompilerParams(vmem_limit_bytes=VMEM_BYTES),
        cost_estimate=LIGHT,
        name="key_value_products",
    )(place, *blocks, *in_hbm([w_key, w_value, *after]))


def add_kernel(gots, paired, extra, *refs):
    keep_ref, got_refs, out_ref = refs[0], refs[1 : 1 + gots], refs[-1]
    pair_refs = refs[1 + gots : 1 + gots + 2 * paired]
    landed_refs = refs[1 + gots + 2 * paired :][: extra * (1 + paired)]
    width = got_refs[0].shape[2]
    cols = gots * width

    def total(first, second, landed):
        value = first + second.astype(jnp.float32)
        for term in landed:
            value = value + term.astype(jnp.float32)
        return value.astype(out_ref.dtype)

    for t, got_ref in enumerate(got_refs):
        part = slice(t * width, (t + 1) * width)
        landed = [landed_refs[0][0, :, part]] if extra else []
        out_ref[0, :, part] = total(keep_ref[0, :, part], got_ref[0], landed)
    if paired:
        landed = [landed_refs[1][0]] if extra else []
        out_ref[0, :, cols:] = total(pair_refs[0][0], pair_refs[1][0], landed)


def add_rows(first, count, rows, b, keep, gots, start, cols, pair=(), slot=0, landed=(), after=()):
    whole = keep.shape[2]
    width = cols // len(gots)
    shift = start // cols if gots[0].shape[2] == whole else 0
    more = pair[0].shape[2] if pair else 0
    keep_spec = pl.BlockSpec((1, rows, cols), lambda s: (first + s, b, start // cols))
    got_spec = pl.BlockSpec((1, rows, width), lambda s: (first + s, b, shift))
    pair_spec = pl.BlockSpec((1, rows, more), lambda s: (slot + s, 0, 0))
    landed_specs = [pl.BlockSpec((1, rows, cols), lambda s: (s, 0, start // cols))]
    if pair:
        landed_specs.append(pl.BlockSpec((1, rows, more), lambda s: (s, 0, whole // more)))
    landed_specs = landed_specs * len(landed)
    return pl.pallas_call(
        functools.partial(add_kernel, len(gots), len(pair) // 2, len(landed)),
        grid=(count,),
        in_specs=[keep_spec]
        + [got_spec] * len(gots)
        + [pair_spec] * len(pair)
        + landed_specs
        + [pl.BlockSpec(memory_space=pl.ANY)] * len(after),
        out_specs=pl.BlockSpec((1, rows, cols + more), lambda s: (s, 0, 0)),
        out_shape=pltpu.HBM((count, rows, cols + more), jnp.bfloat16),
        compiler_params=pltpu.CompilerParams(vmem_limit_bytes=VMEM_BYTES),
        cost_estimate=LIGHT,
        name="add_rows",
    )(
        *in_hbm([keep]),
        *gots,
        *in_hbm(pair[:1]),
        *pair[1:],
        *(list(landed) * (2 if pair else 1)),
        *in_hbm(after[:1]),
        *after[1:],
    )


def rotate_kernel(count, pieces, cos_ref, sin_ref, *refs):
    terms, gots, out_ref = refs[:count], refs[count : count + pieces], refs[-1]
    total = terms[0][0].astype(jnp.float32)
    for term in terms[1:]:
        total = total + term[0].astype(jnp.float32)
    cosine, sine = cos_ref[...], sin_ref[...]

    def write(total):
        for head in range(total.shape[1] // DH):
            part = total[:, head * DH : (head + 1) * DH]
            turned = pltpu.roll(part, DH // 2, axis=1)
            value = part * cosine + turned * sine
            out_ref[:, head * DH : (head + 1) * DH] = value.astype(out_ref.dtype)

    if not gots:
        write(total)
    for j, got in enumerate(gots):

        @pl.when(pl.program_id(0) == j)
        def _():
            write(total + got[0].astype(jnp.float32))


def sum_and_rotate(cosine, sine, terms, gots, cols, after=()):
    rows = cosine.shape[0]
    slot_of_gots, block_of_gots, shift, gots = gots
    tile = cols // max(1, len(gots))
    table = pl.BlockSpec((rows, DH), lambda j: (0, 0))

    def block(slot, b, start):
        return pl.BlockSpec((1, rows, tile), lambda j: (slot, b, start // tile + j))

    return pl.pallas_call(
        functools.partial(rotate_kernel, len(terms), len(gots)),
        grid=(cols // tile,),
        in_specs=[table, table]
        + [block(slot, b, start) for _, slot, b, start in terms]
        + [pl.BlockSpec((1, rows, tile), lambda j: (slot_of_gots, block_of_gots, shift))] * len(gots)
        + [pl.BlockSpec(memory_space=pl.ANY)] * len(after),
        out_specs=pl.BlockSpec((rows, tile), lambda j: (0, j)),
        out_shape=jax.ShapeDtypeStruct((rows, cols), jnp.bfloat16),
        compiler_params=pltpu.CompilerParams(vmem_limit_bytes=VMEM_BYTES),
        cost_estimate=LIGHT,
        name="sum_and_rotate",
    )(cosine, sine, *in_hbm([terms[0][0]]), *[term[0] for term in terms[1:]], *gots, *after)


def split_kernel(count, cos_ref, sin_ref, *refs):
    terms, (key_ref, value_ref) = refs[:count], refs[-2:]
    total = terms[0][0].astype(jnp.float32)
    for term in terms[1:]:
        total = total + term[0].astype(jnp.float32)
    half = total.shape[0]
    for b in range(total.shape[1] // (2 * DH)):
        rows = slice(b * half, (b + 1) * half)
        key = total[:, 2 * b * DH : (2 * b + 1) * DH]
        turned = pltpu.roll(key, DH // 2, axis=1)
        key_ref[rows] = (key * cos_ref[rows] + turned * sin_ref[rows]).astype(key_ref.dtype)
        value_ref[0, rows] = total[:, (2 * b + 1) * DH : (2 * b + 2) * DH].astype(value_ref.dtype)


def split_and_rotate(cosine, sine, terms, width, after):
    rows = cosine.shape[0]
    half = terms[0][0].shape[1]
    table = pl.BlockSpec((rows, DH), lambda j: (0, 0))

    def block(slot, start):
        return pl.BlockSpec((1, half, width), lambda j: (slot, 0, start // width))

    return pl.pallas_call(
        functools.partial(split_kernel, len(terms)),
        grid=(1,),
        in_specs=[table, table]
        + [block(slot, start) for _, slot, start in terms]
        + [pl.BlockSpec(memory_space=pl.ANY)] * len(after),
        out_specs=[table, pl.BlockSpec((1, rows, DH), lambda j: (0, 0, 0))],
        out_shape=[
            jax.ShapeDtypeStruct((rows, DH), jnp.bfloat16),
            jax.ShapeDtypeStruct((1, rows, DH), jnp.bfloat16),
        ],
        compiler_params=pltpu.CompilerParams(vmem_limit_bytes=VMEM_BYTES),
        cost_estimate=LIGHT,
        name="split_and_rotate",
    )(cosine, sine, *in_hbm([terms[0][0]]), *[term for term, _, _ in terms[1:]], *after)


def prepare_kernel(canary_ref, ids_ref, own_ref, other_ref, order_ref, key_t_ref):
    order = jnp.where(canary_ref[...] == ids_ref[...], 1.0, 0.0).astype(jnp.bfloat16)
    order_ref[...] = order
    key = jnp.concatenate([own_ref[...], other_ref[...]], axis=0)
    key_t_ref[...] = jnp.dot(order, key, preferred_element_type=jnp.float32).T.astype(jnp.bfloat16)


def prepare(canary_rows, ids, own, other):
    rows = ids.shape[0]
    return pl.pallas_call(
        prepare_kernel,
        out_shape=[
            jax.ShapeDtypeStruct((rows, rows), jnp.bfloat16),
            jax.ShapeDtypeStruct((DH, rows), jnp.bfloat16),
        ],
        compiler_params=pltpu.CompilerParams(vmem_limit_bytes=VMEM_BYTES),
        name="order_and_keys",
    )(canary_rows.reshape(rows, 1), ids.reshape(1, rows), own, other)


def stack_kernel(count, *refs):
    out_ref, start = refs[-1], 0
    for ref in refs[:count]:
        out_ref[start : start + ref.shape[0]] = ref[...]
        start += ref.shape[0]


def stack_slots(arrays, after):
    slots = sum(x.shape[0] for x in arrays)
    shape = (slots,) + arrays[0].shape[1:]
    return pl.pallas_call(
        functools.partial(stack_kernel, len(arrays)),
        grid=(1,),
        in_specs=[pl.BlockSpec(x.shape, lambda j: (0, 0, 0)) for x in arrays]
        + [pl.BlockSpec(memory_space=pl.ANY)] * len(after),
        out_specs=pl.BlockSpec(shape, lambda j: (0, 0, 0)),
        out_shape=jax.ShapeDtypeStruct(shape, arrays[0].dtype),
        compiler_params=pltpu.CompilerParams(vmem_limit_bytes=VMEM_BYTES),
        cost_estimate=LIGHT,
        name="stack_slots",
    )(*arrays, *after)


def value_kernel(place_ref, order_ref, own_ref, other_ref, out_ref):
    rows = jnp.concatenate([own_ref[0], other_ref[0]], axis=0)
    out_ref[...] = jnp.dot(order_ref[...], rows, preferred_element_type=jnp.float32).astype(out_ref.dtype)


def order_values(findex, order, own, other):
    rows = order.shape[0]
    slots, part, width = own.shape
    place = jnp.stack([findex ^ s for s in range(slots)]).astype(jnp.int32)
    block = pl.BlockSpec((1, part, width), lambda s, place: (place[s], 0, 0))
    return pl.pallas_call(
        value_kernel,
        grid_spec=pltpu.PrefetchScalarGridSpec(
            num_scalar_prefetch=1,
            grid=(slots,),
            in_specs=[pl.BlockSpec((rows, rows), lambda s, place: (0, 0)), block, block],
            out_specs=pl.BlockSpec((rows, width), lambda s, place: (0, s)),
        ),
        out_shape=jax.ShapeDtypeStruct((rows, slots * width), jnp.bfloat16),
        compiler_params=pltpu.CompilerParams(vmem_limit_bytes=VMEM_BYTES),
        name="order_values",
    )(place, order, own, other)


def score_kernel(count, order_ref, key_t_ref, *refs):
    queries, (out_ref, mark_ref) = refs[:count], refs[-2:]
    mark_ref[...] = jnp.zeros_like(mark_ref)
    stacked = jnp.concatenate([query[...] for query in queries], axis=0)
    chosen = jnp.dot(order_ref[...], stacked, preferred_element_type=jnp.float32).astype(jnp.bfloat16)
    for head in range(stacked.shape[1] // DH):
        products = jnp.dot(
            chosen[:, head * DH : (head + 1) * DH], key_t_ref[...], preferred_element_type=jnp.float32
        )
        out_ref[0, head] = (products * DH ** (-0.5)).astype(out_ref.dtype)


def score_heads(order, key_t, heads, start, count, queries, earlier, after=()):
    rows = order.shape[0]
    step = 2 if count % 2 == 0 else 1

    def block(query, first):
        return pl.BlockSpec((query.shape[0], step * DH), lambda j: (0, first // step + j))

    return pl.pallas_call(
        functools.partial(score_kernel, len(queries)),
        grid=(count // step,),
        in_specs=[
            pl.BlockSpec((rows, rows), lambda j: (0, 0)),
            pl.BlockSpec((DH, rows), lambda j: (0, 0)),
        ]
        + [block(query, first) for query, first in queries]
        + [pl.BlockSpec(memory_space=pl.ANY)] * (len(earlier) + len(after)),
        out_specs=[
            pl.BlockSpec((1, step, rows, rows), lambda j: (0, start // step + j, 0, 0)),
            pl.BlockSpec((8, DH), lambda j: (0, 0)),
        ],
        out_shape=[
            jax.ShapeDtypeStruct((1, heads, rows, rows), jnp.bfloat16),
            jax.ShapeDtypeStruct((8, DH), jnp.float32),
        ],
        input_output_aliases={2 + len(queries): 0} if earlier else {},
        compiler_params=pltpu.CompilerParams(vmem_limit_bytes=VMEM_BYTES),
        cost_estimate=LIGHT,
        name="score_heads",
    )(order, key_t, *[query for query, _ in queries], *earlier, *after)


def body(hidden, w_query, w_key, w_value, canary_rows, positions):
    shards = lax.axis_size("fsdp")
    findex = lax.axis_index("fsdp")
    tps = lax.axis_size("tp")
    tindex = lax.axis_index("tp")
    rindex = lax.axis_index("rep")
    local, depth = hidden.shape
    half = local // 2
    rows = local * tps
    head_cols = w_query.shape[1] // shards
    heads_here = head_cols // DH
    group = HQ // KV
    assert shards & (shards - 1) == 0 and lax.axis_size("rep") == 2

    def swap(x, bit):
        return lax.ppermute(x, "fsdp", [(i, i ^ bit) for i in range(shards)])

    def other_core(x):
        return lax.ppermute(x, "rep", [(0, 1), (1, 0)])

    def low(x):
        return x.astype(jnp.bfloat16)

    odd = list(range(3, shards, 2)) + [1]
    even = list(range(2, shards, 2))
    fast_pair = heads_here == group

    def spread(live):
        terms, first = [], None
        bit = 2
        while bit < shards:
            sent = [x for x in sorted(live) if x & bit]
            pack = jnp.stack([low(live[x]) for x in sent])
            first = pack if first is None else first
            landed = swap(pack, bit)
            for k, x in enumerate(sent):
                if x == bit:
                    terms.append(landed)
                else:
                    live[x ^ bit] = live[x ^ bit] + landed[k].astype(jnp.float32)
                del live[x]
            bit *= 2
        return terms, first

    blocks = [hidden] + [
        lax.ppermute(hidden, "tp", [(i, (i - b) % tps) for i in range(tps)]) for b in range(1, tps)
    ]

    block_ids = ((tindex + jnp.arange(tps, dtype=jnp.int32)) % tps * local)[:, None]
    own_ids = (block_ids + rindex * half + jnp.arange(half, dtype=jnp.int32)[None]).reshape(-1)
    other_ids = (block_ids + (1 - rindex) * half + jnp.arange(half, dtype=jnp.int32)[None]).reshape(-1)
    ids = jnp.concatenate([own_ids, other_ids])
    own_positions = jnp.sum(
        jnp.where(own_ids[:, None] == canary_rows[None, :], positions[None, :], 0), axis=1
    )
    cosine, sine = rope_tables(own_positions)

    tile = min(1024, head_cols)

    def project(slots, blocks, width, after=(), cost=LIGHT, by_slot=False):
        keep, gives = project_query(
            rindex, findex, slots, blocks, w_query, head_cols, tile, width, after, cost, by_slot
        )
        return keep, [other_core(give) for give in gives], gives[0]

    def rotate(b, p, split, terms, behind):
        cols = head_cols // split
        table = slice(b * half, (b + 1) * half)
        keep, slot, got = owns[b]
        added = [(keep, slot, 0, p * cols)] + terms
        gots = (0, 0, p, got) if len(got) == 1 else (0, 0, 0, got[p : p + 1])
        turned = sum_and_rotate(cosine[table], sine[table], added, gots, cols, behind)
        return turned, other_core(turned)

    def add_even(b, start, cols, pair, behind):
        if shards == 2:
            return [], behind
        keep, got = evens[b]
        each = len(got) * cols // head_cols
        got = got[start // cols * each :][:each]
        summed = add_rows(
            0, len(even), half, 0, keep, got, start, cols, pair, len(odd), (fars[b],), behind
        )
        terms, first = spread({x: summed[k] for k, x in enumerate(even)})
        return [(term, 0, 0, 0) for term in terms], (first,)

    last, split = tps - 1, head_cols // tile
    placed = in_hbm(blocks[:1]) + blocks[1:]
    evens, owns, fars, terms, pair, after = [], [], [], [], (), ()
    for b, block in enumerate(placed):
        if fast_pair and b == last:
            slots = odd + even + [0]
            pair_keep, give = project_pair(rindex, findex, slots, placed, w_key, w_value, after)
            pair = (pair_keep, other_core(give))
            after = (give,)
        odd_keep, odd_got, given = project(odd, [block], tile, after)
        count = len(odd) - 1 if b == last else len(odd)
        odd_sent = add_rows(0, count, half, 0, odd_keep, odd_got, 0, head_cols, pair)
        fars.append(swap(odd_sent, 1))
        after = (odd_sent,)
        if b > 0:
            added, after = add_even(b - 1, 0, head_cols, (), after)
            terms.append([(fars[b - 1], len(odd) - 1, 0, 0)] + added)
            after = (odd_sent,) + after
        if b < last:
            keep, got, given = project(even + [0], [block], head_cols, after, LIGHT, True)
            evens.append((keep, got[:1] if len(even) == 1 else [jnp.concatenate(got[:-1])]))
            owns.append((keep, len(even), got[-1:]))
        else:
            keep, got, given = project(even, [block], tile, after, HEAVY)
            evens.append((keep, got))
        after = (given,)
    parts, behind = [], tuple(term[0] for row in terms for term in row[1:])
    for p in range(split):
        near_sent = add_rows(
            len(odd) - 1, 1, half, 0, odd_keep, odd_got[p : p + 1], p * tile, tile,
            pair if p == 0 else (), len(odd) - 1, (), after,
        )
        parts.append([(swap(near_sent, 1), 0, 0, 0)])
        after = (near_sent,)
    after = after + behind
    for p in range(split):
        added, after = add_even(last, p * tile, tile, pair if p == 0 else (), after)
        parts[p] += added
    keep, got, _ = project([0], placed[last:], tile, after, HEAVY)
    owns.append((keep, 0, got))

    if fast_pair:
        width = 2 * DH * tps
        pieces = [(array, shards - 1, 0) for array in pair]
        pieces += [(term, 0, tile) for term, _, _, _ in parts[0]]
        key_rot, held = split_and_rotate(cosine, sine, pieces, width, after)
    else:
        x = jnp.concatenate(blocks, axis=0)
        key_sum, value_sum = lax.psum(
            (
                jnp.dot(x, w_key, preferred_element_type=jnp.float32),
                jnp.dot(x, w_value, preferred_element_type=jnp.float32),
            ),
            ("fsdp", "rep"),
        )

        def of_core(y, core):
            parts = y.reshape(tps, 2, half, -1)
            return lax.dynamic_index_in_dim(parts, core, 1, keepdims=False).reshape(tps * half, -1)

        mine = lax.dynamic_slice_in_dim(key_sum, findex * heads_here // group * DH, DH, 1)
        key_own = of_core(mine, rindex)
        key_rot = sum_and_rotate(cosine, sine, [(key_own[None], 0, 0, 0)], (0, 0, 0, []), DH, after)
        value_rows = low(jnp.concatenate([of_core(value_sum, rindex), of_core(value_sum, 1 - rindex)]))

    order, key_t = prepare(canary_rows, ids, key_rot, other_core(key_rot))
    if not fast_pair:
        values = low(jnp.dot(order, value_rows, preferred_element_type=jnp.float32))

    rotated = [rotate(b, 0, 1, terms[b], after) for b in range(last)]
    count = heads_here // split
    scores, mark = (), ()
    for p in range(split):
        turned = rotate(last, p, split, parts[p], mark)
        queries = [(row[0], p * count) for row in rotated] + [(turned[0], 0)]
        queries += [(row[1], p * count) for row in rotated] + [(turned[1], 0)]
        *scores, mark = score_heads(
            order, key_t, heads_here, p * count, count, queries, scores
        )
        mark = (mark,)
        if fast_pair and p == 0:
            bit = 1
            while bit < shards:
                held = stack_slots([held, swap(held, bit)], mark)
                bit *= 2
            values = order_values(findex, order, held, other_core(held))
    return (scores[0], values)


def solution(mesh):
    in_specs = (
        P(("groups", "tp"), ("fsdp", "rep")),
        P(("fsdp", "rep"), "tp"),
        P(("fsdp", "rep"), "tp"),
        P(("fsdp", "rep"), "tp"),
        P("groups"),
        P("groups"),
    )
    out_specs = (P("tp", "fsdp", "groups", None), P("groups", "tp"))
    return jax.shard_map(body, mesh=mesh, in_specs=in_specs, out_specs=out_specs, check_vma=False)
```

```python
import functools
import math

import jax
import jax.numpy as jnp
from jax import lax
from jax.experimental import pallas as pl
from jax.experimental.pallas import tpu as pltpu
from jax.sharding import PartitionSpec as P

HQ = 128
KV = 8
DH = 128
VMEM_BYTES = 28 * 1024 * 1024
LIGHT = pl.CostEstimate(flops=1000, bytes_accessed=1000, transcendentals=0)
HEAVY = pl.CostEstimate(flops=10**11, bytes_accessed=10**8, transcendentals=0)


def in_hbm(arrays):
    return [pltpu.with_memory_space_constraint(x, pltpu.HBM) for x in arrays]


def rope_tables(positions):
    half = DH // 2
    expo = jnp.arange(half, dtype=jnp.float32) * (2.0 / DH)
    freq = jnp.power(jnp.float32(500000.0), -expo)
    wavelen = 2.0 * math.pi / freq
    smooth = (8192.0 / wavelen - 1.0) / 3.0
    mixed = (1.0 - smooth) * freq / 8.0 + smooth * freq
    freq = jnp.where(wavelen > 8192.0, freq / 8.0, jnp.where(wavelen < 2048.0, freq, mixed))
    angle = positions.astype(jnp.float32)[:, None] * freq[None, :]
    cosine, sine = jnp.cos(angle), jnp.sin(angle)
    return jnp.concatenate([cosine, cosine], axis=1), jnp.concatenate([-sine, sine], axis=1)


def ordered_rows(place_ref, x_refs, rows_ref):
    core = place_ref[0]
    half = x_refs[0].shape[0] // 2
    for b, x_ref in enumerate(x_refs):
        kept, given = b * half, (len(x_refs) + b) * half
        rows_ref[kept : kept + half] = x_ref[pl.ds(pl.multiple_of(core * half, 16), half)]
        rows_ref[given : given + half] = x_ref[pl.ds(pl.multiple_of((1 - core) * half, 16), half)]


def query_kernel(count, pieces, by_slot, place_ref, *refs):
    x_refs, w_ref = refs[:count], refs[count]
    keep_ref, *give_refs, rows_ref = refs[-2 - pieces :]
    tile = pl.program_id(1)
    size = give_refs[0].shape[2]
    each = keep_ref.shape[2] // size

    @pl.when((pl.program_id(0) == 0) & (tile == 0))
    def _():
        ordered_rows(place_ref, x_refs, rows_ref)

    result = jnp.dot(rows_ref[...], w_ref[...], preferred_element_type=jnp.float32)
    half = result.shape[0] // 2
    keep_ref[0] = result[:half]
    for j, give_ref in enumerate(give_refs):

        @pl.when(pl.program_id(0) == j if by_slot else (tile == j // each) | (pieces == 1))
        def _():
            start = j % each * size
            give_ref[0] = result[half:, start : start + size].astype(give_ref.dtype)


def project_query(rindex, findex, slots, blocks, w, cols, tile, width, after, cost, by_slot):
    rows, depth = blocks[0].shape
    count = len(blocks)
    half = rows // 2 * count
    tiles, pieces = cols // tile, len(slots) if by_slot else cols // width
    place = jnp.stack([rindex] + [findex ^ slot for slot in slots]).astype(jnp.int32)
    keep_spec = pl.BlockSpec((1, half, tile), lambda s, j, place: (s, 0, j))
    give_spec = pl.BlockSpec((1, half, width), lambda s, j, place: (s, 0, 0))

    def slot_spec(k):
        def index(s, j, place):
            return (0, 0, jnp.where(s < k, 0, jnp.where(s > k, tiles - 1, j)))

        return pl.BlockSpec((1, half, tile), index)

    give_specs = [keep_spec] if pieces == 1 else [give_spec] * pieces
    given = (len(slots), half, width)
    if by_slot:
        give_specs, given = [slot_spec(k) for k in range(pieces)], (1, half, cols)
    x_spec = pl.BlockSpec((rows, depth), lambda s, j, place: (0, 0), pipeline_mode=pl.Buffered(1))
    outs = pl.pallas_call(
        functools.partial(query_kernel, count, pieces, by_slot),
        grid_spec=pltpu.PrefetchScalarGridSpec(
            num_scalar_prefetch=1,
            grid=(len(slots), tiles),
            in_specs=[x_spec] * count
            + [pl.BlockSpec((depth, tile), lambda s, j, place: (0, place[1 + s] * tiles + j))]
            + [pl.BlockSpec(memory_space=pl.ANY)] * len(after),
            out_specs=[keep_spec] + give_specs,
            scratch_shapes=[pltpu.VMEM((2 * half, depth), w.dtype)],
        ),
        out_shape=[pltpu.HBM((len(slots), half, cols), jnp.float32)]
        + [pltpu.HBM(given, jnp.bfloat16)] * pieces,
        compiler_params=pltpu.CompilerParams(vmem_limit_bytes=VMEM_BYTES),
        cost_estimate=cost,
        name="query_products",
    )(place, *blocks, *in_hbm([w]), *in_hbm(after[:1]), *after[1:])
    return outs[0], outs[1:]


def pair_kernel(count, place_ref, *refs):
    x_refs, (wk_ref, wv_ref) = refs[:count], refs[count : count + 2]
    keep_ref, give_ref, rows_ref = refs[-3:]

    @pl.when(pl.program_id(0) == 0)
    def _():
        ordered_rows(place_ref, x_refs, rows_ref)

    weights = jnp.concatenate([wk_ref[...], wv_ref[...]], axis=1)
    result = jnp.dot(rows_ref[...], weights, preferred_element_type=jnp.float32)
    half, width = x_refs[0].shape[0] // 2, weights.shape[1]
    for b in range(count):
        kept, given = b * half, (count + b) * half
        cols = slice(b * width, (b + 1) * width)
        keep_ref[0, :, cols] = result[kept : kept + half]
        give_ref[0, :, cols] = result[given : given + half].astype(give_ref.dtype)


def project_pair(rindex, findex, slots, blocks, w_key, w_value, after=()):
    rows, depth = blocks[0].shape
    count = len(blocks)
    place = jnp.stack([rindex] + [findex ^ slot for slot in slots]).astype(jnp.int32)
    weight = pl.BlockSpec((depth, DH), lambda s, place: (0, place[1 + s]))
    shape = (len(slots), rows // 2, 2 * DH * count)
    out = pl.BlockSpec((1,) + shape[1:], lambda s, place: (s, 0, 0))
    return pl.pallas_call(
        functools.partial(pair_kernel, count),
        grid_spec=pltpu.PrefetchScalarGridSpec(
            num_scalar_prefetch=1,
            grid=(len(slots),),
            in_specs=[pl.BlockSpec((rows, depth), lambda s, place: (0, 0))] * count
            + [weight, weight]
            + [pl.BlockSpec(memory_space=pl.ANY)] * len(after),
            out_specs=[out, out],
            scratch_shapes=[pltpu.VMEM((count * rows, depth), blocks[0].dtype)],
        ),
        out_shape=[
            pltpu.HBM(shape, jnp.float32),
            pltpu.HBM(shape, jnp.bfloat16),
        ],
        compiler_params=pltpu.CompilerParams(vmem_limit_bytes=VMEM_BYTES),
        cost_estimate=LIGHT,
        name="key_value_products",
    )(place, *blocks, *in_hbm([w_key, w_value, *after]))


def add_kernel(gots, extra, *refs):
    keep_ref, got_refs, out_ref = refs[0], refs[1 : 1 + gots], refs[-1]
    landed_refs = refs[1 + gots :][:extra]
    width = got_refs[0].shape[2]
    for t, got_ref in enumerate(got_refs):
        part = slice(t * width, (t + 1) * width)
        value = keep_ref[0, :, part] + got_ref[0].astype(jnp.float32)
        for landed_ref in landed_refs:
            value = value + landed_ref[0, :, part].astype(jnp.float32)
        out_ref[0, :, part] = value.astype(out_ref.dtype)


def add_rows(first, count, keep, gots, start, cols, landed=(), after=()):
    rows, width = keep.shape[1], cols // len(gots)
    columns = start // cols
    return pl.pallas_call(
        functools.partial(add_kernel, len(gots), len(landed)),
        grid=(count,),
        in_specs=[pl.BlockSpec((1, rows, cols), lambda s: (first + s, 0, columns))]
        + [pl.BlockSpec((1, rows, width), lambda s: (first + s, 0, 0))] * len(gots)
        + [pl.BlockSpec((1, rows, cols), lambda s: (s, 0, columns))] * len(landed)
        + [pl.BlockSpec(memory_space=pl.ANY)] * len(after),
        out_specs=pl.BlockSpec((1, rows, cols), lambda s: (s, 0, 0)),
        out_shape=pltpu.HBM((count, rows, cols), jnp.bfloat16),
        compiler_params=pltpu.CompilerParams(vmem_limit_bytes=VMEM_BYTES),
        cost_estimate=LIGHT,
        name="add_rows",
    )(*in_hbm([keep]), *gots, *landed, *in_hbm(after[:1]), *after[1:])


def rotate_kernel(count, pieces, cos_ref, sin_ref, *refs):
    terms, gots, out_ref = refs[:count], refs[count : count + pieces], refs[-1]
    total = terms[0][0].astype(jnp.float32)
    for term in terms[1:]:
        total = total + term[0].astype(jnp.float32)
    cosine, sine = cos_ref[...], sin_ref[...]

    def write(total):
        for head in range(total.shape[1] // DH):
            part = total[:, head * DH : (head + 1) * DH]
            turned = pltpu.roll(part, DH // 2, axis=1)
            value = part * cosine + turned * sine
            out_ref[:, head * DH : (head + 1) * DH] = value.astype(out_ref.dtype)

    if not gots:
        write(total)
    for j, got in enumerate(gots):

        @pl.when(pl.program_id(0) == j)
        def _():
            write(total + got[0].astype(jnp.float32))


def sum_and_rotate(cosine, sine, terms, gots, cols, after=()):
    rows = cosine.shape[0]
    slot_of_gots, block_of_gots, shift, gots = gots
    tile = cols // max(1, len(gots))
    table = pl.BlockSpec((rows, DH), lambda j: (0, 0))

    def block(slot, b, start):
        return pl.BlockSpec((1, rows, tile), lambda j: (slot, b, start // tile + j))

    return pl.pallas_call(
        functools.partial(rotate_kernel, len(terms), len(gots)),
        grid=(cols // tile,),
        in_specs=[table, table]
        + [block(slot, b, start) for _, slot, b, start in terms]
        + [pl.BlockSpec((1, rows, tile), lambda j: (slot_of_gots, block_of_gots, shift))] * len(gots)
        + [pl.BlockSpec(memory_space=pl.ANY)] * len(after),
        out_specs=pl.BlockSpec((rows, tile), lambda j: (0, j)),
        out_shape=jax.ShapeDtypeStruct((rows, cols), jnp.bfloat16),
        compiler_params=pltpu.CompilerParams(vmem_limit_bytes=VMEM_BYTES),
        cost_estimate=LIGHT,
        name="sum_and_rotate",
    )(cosine, sine, *in_hbm([terms[0][0]]), *[term[0] for term in terms[1:]], *gots, *after)


def split_kernel(count, cos_ref, sin_ref, *refs):
    terms, (key_ref, value_ref) = refs[:count], refs[-2:]
    total = terms[0][0].astype(jnp.float32)
    for term in terms[1:]:
        total = total + term[0].astype(jnp.float32)
    half = total.shape[0]
    for b in range(total.shape[1] // (2 * DH)):
        rows = slice(b * half, (b + 1) * half)
        key = total[:, 2 * b * DH : (2 * b + 1) * DH]
        turned = pltpu.roll(key, DH // 2, axis=1)
        key_ref[rows] = (key * cos_ref[rows] + turned * sin_ref[rows]).astype(key_ref.dtype)
        value_ref[0, rows] = total[:, (2 * b + 1) * DH : (2 * b + 2) * DH].astype(value_ref.dtype)


def split_and_rotate(cosine, sine, terms, width, after):
    rows = cosine.shape[0]
    half = terms[0][0].shape[1]
    table = pl.BlockSpec((rows, DH), lambda j: (0, 0))

    def block(slot, start):
        return pl.BlockSpec((1, half, width), lambda j: (slot, 0, start // width))

    return pl.pallas_call(
        functools.partial(split_kernel, len(terms)),
        grid=(1,),
        in_specs=[table, table]
        + [block(slot, start) for _, slot, start in terms]
        + [pl.BlockSpec(memory_space=pl.ANY)] * len(after),
        out_specs=[table, pl.BlockSpec((1, rows, DH), lambda j: (0, 0, 0))],
        out_shape=[
            jax.ShapeDtypeStruct((rows, DH), jnp.bfloat16),
            jax.ShapeDtypeStruct((1, rows, DH), jnp.bfloat16),
        ],
        compiler_params=pltpu.CompilerParams(vmem_limit_bytes=VMEM_BYTES),
        cost_estimate=LIGHT,
        name="split_and_rotate",
    )(cosine, sine, *in_hbm([terms[0][0]]), *[term for term, _, _ in terms[1:]], *after)


def prepare_kernel(canary_ref, ids_ref, own_ref, other_ref, order_ref, key_t_ref):
    order = jnp.where(canary_ref[...] == ids_ref[...], 1.0, 0.0).astype(jnp.bfloat16)
    order_ref[...] = order
    key = jnp.concatenate([own_ref[...], other_ref[...]], axis=0)
    key_t_ref[...] = jnp.dot(order, key, preferred_element_type=jnp.float32).T.astype(jnp.bfloat16)


def prepare(canary_rows, ids, own, other):
    rows = ids.shape[0]
    return pl.pallas_call(
        prepare_kernel,
        out_shape=[
            jax.ShapeDtypeStruct((rows, rows), jnp.bfloat16),
            jax.ShapeDtypeStruct((DH, rows), jnp.bfloat16),
        ],
        compiler_params=pltpu.CompilerParams(vmem_limit_bytes=VMEM_BYTES),
        name="order_and_keys",
    )(canary_rows.reshape(rows, 1), ids.reshape(1, rows), own, other)


def stack_kernel(count, *refs):
    out_ref, start = refs[-1], 0
    for ref in refs[:count]:
        out_ref[start : start + ref.shape[0]] = ref[...]
        start += ref.shape[0]


def stack_slots(arrays, after):
    slots = sum(x.shape[0] for x in arrays)
    shape = (slots,) + arrays[0].shape[1:]
    return pl.pallas_call(
        functools.partial(stack_kernel, len(arrays)),
        grid=(1,),
        in_specs=[pl.BlockSpec(x.shape, lambda j: (0, 0, 0)) for x in arrays]
        + [pl.BlockSpec(memory_space=pl.ANY)] * len(after),
        out_specs=pl.BlockSpec(shape, lambda j: (0, 0, 0)),
        out_shape=jax.ShapeDtypeStruct(shape, arrays[0].dtype),
        compiler_params=pltpu.CompilerParams(vmem_limit_bytes=VMEM_BYTES),
        cost_estimate=LIGHT,
        name="stack_slots",
    )(*arrays, *after)


def value_kernel(place_ref, order_ref, own_ref, other_ref, out_ref):
    rows = jnp.concatenate([own_ref[0], other_ref[0]], axis=0)
    out_ref[...] = jnp.dot(order_ref[...], rows, preferred_element_type=jnp.float32).astype(out_ref.dtype)


def order_values(findex, order, own, other):
    rows = order.shape[0]
    slots, part, width = own.shape
    place = jnp.stack([findex ^ s for s in range(slots)]).astype(jnp.int32)
    block = pl.BlockSpec((1, part, width), lambda s, place: (place[s], 0, 0))
    return pl.pallas_call(
        value_kernel,
        grid_spec=pltpu.PrefetchScalarGridSpec(
            num_scalar_prefetch=1,
            grid=(slots,),
            in_specs=[pl.BlockSpec((rows, rows), lambda s, place: (0, 0)), block, block],
            out_specs=pl.BlockSpec((rows, width), lambda s, place: (0, s)),
        ),
        out_shape=jax.ShapeDtypeStruct((rows, slots * width), jnp.bfloat16),
        compiler_params=pltpu.CompilerParams(vmem_limit_bytes=VMEM_BYTES),
        name="order_values",
    )(place, order, own, other)


def score_kernel(count, order_ref, key_t_ref, *refs):
    queries, (out_ref, mark_ref) = refs[:count], refs[-2:]
    mark_ref[...] = jnp.zeros_like(mark_ref)
    stacked = jnp.concatenate([query[...] for query in queries], axis=0)
    chosen = jnp.dot(order_ref[...], stacked, preferred_element_type=jnp.float32).astype(jnp.bfloat16)
    for head in range(stacked.shape[1] // DH):
        products = jnp.dot(
            chosen[:, head * DH : (head + 1) * DH], key_t_ref[...], preferred_element_type=jnp.float32
        )
        out_ref[0, head] = (products * DH ** (-0.5)).astype(out_ref.dtype)


def score_heads(order, key_t, heads, start, count, queries, earlier, after=()):
    rows = order.shape[0]
    step = 2 if count % 2 == 0 else 1

    def block(query, first):
        return pl.BlockSpec((query.shape[0], step * DH), lambda j: (0, first // step + j))

    return pl.pallas_call(
        functools.partial(score_kernel, len(queries)),
        grid=(count // step,),
        in_specs=[
            pl.BlockSpec((rows, rows), lambda j: (0, 0)),
            pl.BlockSpec((DH, rows), lambda j: (0, 0)),
        ]
        + [block(query, first) for query, first in queries]
        + [pl.BlockSpec(memory_space=pl.ANY)] * (len(earlier) + len(after)),
        out_specs=[
            pl.BlockSpec((1, step, rows, rows), lambda j: (0, start // step + j, 0, 0)),
            pl.BlockSpec((8, DH), lambda j: (0, 0)),
        ],
        out_shape=[
            jax.ShapeDtypeStruct((1, heads, rows, rows), jnp.bfloat16),
            jax.ShapeDtypeStruct((8, DH), jnp.float32),
        ],
        input_output_aliases={2 + len(queries): 0} if earlier else {},
        compiler_params=pltpu.CompilerParams(vmem_limit_bytes=VMEM_BYTES),
        cost_estimate=LIGHT,
        name="score_heads",
    )(order, key_t, *[query for query, _ in queries], *earlier, *after)


def body(hidden, w_query, w_key, w_value, canary_rows, positions):
    shards = lax.axis_size("fsdp")
    findex = lax.axis_index("fsdp")
    tps = lax.axis_size("tp")
    tindex = lax.axis_index("tp")
    rindex = lax.axis_index("rep")
    local, depth = hidden.shape
    half = local // 2
    rows = local * tps
    head_cols = w_query.shape[1] // shards
    heads_here = head_cols // DH
    group = HQ // KV
    assert shards & (shards - 1) == 0 and lax.axis_size("rep") == 2

    def swap(x, bit):
        return lax.ppermute(x, "fsdp", [(i, i ^ bit) for i in range(shards)])

    def other_core(x):
        return lax.ppermute(x, "rep", [(0, 1), (1, 0)])

    def low(x):
        return x.astype(jnp.bfloat16)

    odd = list(range(3, shards, 2)) + [1]
    even = list(range(2, shards, 2))
    fast_pair = heads_here == group

    def spread(live):
        terms, first = [], None
        bit = 2
        while bit < shards:
            sent = [x for x in sorted(live) if x & bit]
            pack = jnp.stack([low(live[x]) for x in sent])
            first = pack if first is None else first
            landed = swap(pack, bit)
            for k, x in enumerate(sent):
                if x == bit:
                    terms.append(landed)
                else:
                    live[x ^ bit] = live[x ^ bit] + landed[k].astype(jnp.float32)
                del live[x]
            bit *= 2
        return terms, first

    blocks = [hidden] + [
        lax.ppermute(hidden, "tp", [(i, (i - b) % tps) for i in range(tps)]) for b in range(1, tps)
    ]

    block_ids = ((tindex + jnp.arange(tps, dtype=jnp.int32)) % tps * local)[:, None]
    own_ids = (block_ids + rindex * half + jnp.arange(half, dtype=jnp.int32)[None]).reshape(-1)
    other_ids = (block_ids + (1 - rindex) * half + jnp.arange(half, dtype=jnp.int32)[None]).reshape(-1)
    ids = jnp.concatenate([own_ids, other_ids])
    own_positions = jnp.sum(
        jnp.where(own_ids[:, None] == canary_rows[None, :], positions[None, :], 0), axis=1
    )
    cosine, sine = rope_tables(own_positions)

    tile = min(1024, head_cols)

    def project(slots, blocks, width, after=(), cost=LIGHT, by_slot=False):
        keep, gives = project_query(
            rindex, findex, slots, blocks, w_query, head_cols, tile, width, after, cost, by_slot
        )
        return keep, [other_core(give) for give in gives], gives[0]

    def rotate(b, p, split, terms, behind):
        cols = head_cols // split
        table = slice(b * half, (b + 1) * half)
        keep, slot, got = owns[b]
        added = [(keep, slot, 0, p * cols)] + terms
        gots = (0, 0, p, got) if len(got) == 1 else (0, 0, 0, got[p : p + 1])
        turned = sum_and_rotate(cosine[table], sine[table], added, gots, cols, behind)
        return turned, other_core(turned)

    def add_even(b, start, cols, behind):
        if shards == 2:
            return [], behind
        keep, got = evens[b]
        each = len(got) * cols // head_cols
        got = got[start // cols * each :][:each]
        summed = add_rows(0, len(even), keep, got, start, cols, (fars[b],), behind)
        terms, first = spread({x: summed[k] for k, x in enumerate(even)})
        return [(term, 0, 0, 0) for term in terms], (first,)

    last, split = tps - 1, head_cols // tile
    placed = in_hbm(blocks[:1]) + blocks[1:]
    evens, owns, fars, terms, after = [], [], [], [], ()
    for b, block in enumerate(placed):
        if fast_pair and b == last:
            width = 2 * DH * tps
            slots = odd + even + [0]
            pair, give = project_pair(rindex, findex, slots, placed, w_key, w_value, after)
            pair_got = [other_core(give)]
            after = (give,)
        odd_keep, odd_got, given = project(odd, [block], tile, after)
        after = ()
        if fast_pair and b == last:
            pair_sent = add_rows(0, len(odd), pair, pair_got, 0, width, (), (given,))
            pair_landed = swap(pair_sent, 1)
            after = (pair_sent,)
        count = len(odd) - 1 if b == last else len(odd)
        odd_sent = add_rows(0, count, odd_keep, odd_got, 0, head_cols, (), after)
        fars.append(swap(odd_sent, 1))
        after = (odd_sent,)
        if fast_pair and b == last:
            summed = add_rows(len(odd), len(even), pair, pair_got, 0, width, (pair_landed,), after)
            pair_terms, first = spread({x: summed[k] for k, x in enumerate(even)})
            after = (odd_sent, first)
        if b > 0:
            added, behind = add_even(b - 1, 0, head_cols, after)
            terms.append([(fars[b - 1], len(odd) - 1, 0, 0)] + added)
            after = after + behind
        if b < last:
            keep, got, given = project(even + [0], [block], head_cols, after, LIGHT, True)
            evens.append((keep, got[:1] if len(even) == 1 else [jnp.concatenate(got[:-1])]))
            owns.append((keep, len(even), got[-1:]))
        else:
            keep, got, given = project(even, [block], tile, after, HEAVY)
            evens.append((keep, got))
        after = (given,)
    parts, landed = [], tuple(term[0] for row in terms for term in row[1:])
    for p in range(split):
        near_sent = add_rows(
            len(odd) - 1, 1, odd_keep, odd_got[p : p + 1], p * tile, tile, (), after
        )
        parts.append([(swap(near_sent, 1), 0, 0, 0)])
        after = (near_sent,)
    after = after + landed
    for p in range(split):
        added, after = add_even(last, p * tile, tile, after)
        parts[p] += added
    if fast_pair:
        pieces = [(array, shards - 1, 0) for array in [pair] + pair_got]
        pieces += [(pair_landed, len(odd) - 1, 0)] + [(term, 0, 0) for term in pair_terms]
        key_rot, held = split_and_rotate(cosine, sine, pieces, width, after)
    done = after + ((key_rot,) if fast_pair else ())
    keep, got, _ = project([0], placed[last:], tile, done, HEAVY)
    owns.append((keep, 0, got))

    if fast_pair:
        bit, behind = 1, after
        while bit < shards:
            held = stack_slots([held, swap(held, bit)], behind)
            bit *= 2
    else:
        x = jnp.concatenate(blocks, axis=0)
        key_sum, value_sum = lax.psum(
            (
                jnp.dot(x, w_key, preferred_element_type=jnp.float32),
                jnp.dot(x, w_value, preferred_element_type=jnp.float32),
            ),
            ("fsdp", "rep"),
        )

        def of_core(y, core):
            parts = y.reshape(tps, 2, half, -1)
            return lax.dynamic_index_in_dim(parts, core, 1, keepdims=False).reshape(tps * half, -1)

        mine = lax.dynamic_slice_in_dim(key_sum, findex * heads_here // group * DH, DH, 1)
        key_own = of_core(mine, rindex)
        key_rot = sum_and_rotate(cosine, sine, [(key_own[None], 0, 0, 0)], (0, 0, 0, []), DH, after)
        value_rows = low(jnp.concatenate([of_core(value_sum, rindex), of_core(value_sum, 1 - rindex)]))

    order, key_t = prepare(canary_rows, ids, key_rot, other_core(key_rot))
    if not fast_pair:
        values = low(jnp.dot(order, value_rows, preferred_element_type=jnp.float32))

    rotated = [rotate(b, 0, 1, terms[b], after) for b in range(last)]
    count = heads_here // split
    scores, mark = (), ()
    for p in range(split):
        turned = rotate(last, p, split, parts[p], mark)
        queries = [(row[0], p * count) for row in rotated] + [(turned[0], 0)]
        queries += [(row[1], p * count) for row in rotated] + [(turned[1], 0)]
        *scores, mark = score_heads(
            order, key_t, heads_here, p * count, count, queries, scores
        )
        mark = (mark,)
        if fast_pair and p == 0:
            values = order_values(findex, order, held, other_core(held))
    return (scores[0], values)


def solution(mesh):
    in_specs = (
        P(("groups", "tp"), ("fsdp", "rep")),
        P(("fsdp", "rep"), "tp"),
        P(("fsdp", "rep"), "tp"),
        P(("fsdp", "rep"), "tp"),
        P("groups"),
        P("groups"),
    )
    out_specs = (P("tp", "fsdp", "groups", None), P("groups", "tp"))
    return jax.shard_map(body, mesh=mesh, in_specs=in_specs, out_specs=out_specs, check_vma=False)
```

```python
import functools
import math

import jax
import jax.numpy as jnp
from jax import lax
from jax.experimental import pallas as pl
from jax.experimental.pallas import tpu as pltpu
from jax.sharding import PartitionSpec as P

HQ = 128
KV = 8
DH = 128
VMEM_BYTES = 28 * 1024 * 1024
LIGHT = pl.CostEstimate(flops=1000, bytes_accessed=1000, transcendentals=0)
HEAVY = pl.CostEstimate(flops=10**11, bytes_accessed=10**8, transcendentals=0)


def in_hbm(arrays):
    return [pltpu.with_memory_space_constraint(x, pltpu.HBM) for x in arrays]


def rope_tables(positions):
    half = DH // 2
    expo = jnp.arange(half, dtype=jnp.float32) * (2.0 / DH)
    freq = jnp.power(jnp.float32(500000.0), -expo)
    wavelen = 2.0 * math.pi / freq
    smooth = (8192.0 / wavelen - 1.0) / 3.0
    mixed = (1.0 - smooth) * freq / 8.0 + smooth * freq
    freq = jnp.where(wavelen > 8192.0, freq / 8.0, jnp.where(wavelen < 2048.0, freq, mixed))
    angle = positions.astype(jnp.float32)[:, None] * freq[None, :]
    cosine, sine = jnp.cos(angle), jnp.sin(angle)
    return jnp.concatenate([cosine, cosine], axis=1), jnp.concatenate([-sine, sine], axis=1)


def ordered_rows(place_ref, x_refs, rows_ref):
    core = place_ref[0]
    half = x_refs[0].shape[0] // 2
    for b, x_ref in enumerate(x_refs):
        kept, given = b * half, (len(x_refs) + b) * half
        rows_ref[kept : kept + half] = x_ref[pl.ds(pl.multiple_of(core * half, 16), half)]
        rows_ref[given : given + half] = x_ref[pl.ds(pl.multiple_of((1 - core) * half, 16), half)]


def query_kernel(count, pieces, by_slot, place_ref, *refs):
    x_refs, w_ref = refs[:count], refs[count]
    keep_ref, *give_refs, rows_ref = refs[-2 - pieces :]
    tile = pl.program_id(1)
    size = give_refs[0].shape[2]
    each = keep_ref.shape[2] // size

    @pl.when((pl.program_id(0) == 0) & (tile == 0))
    def _():
        ordered_rows(place_ref, x_refs, rows_ref)

    result = jnp.dot(rows_ref[...], w_ref[...], preferred_element_type=jnp.float32)
    half = result.shape[0] // 2
    keep_ref[0] = result[:half]
    for j, give_ref in enumerate(give_refs):

        @pl.when(pl.program_id(0) == j if by_slot else (tile == j // each) | (pieces == 1))
        def _():
            start = j % each * size
            give_ref[0] = result[half:, start : start + size].astype(give_ref.dtype)


def project_query(rindex, findex, slots, blocks, w, cols, tile, width, after, cost, by_slot):
    rows, depth = blocks[0].shape
    count = len(blocks)
    half = rows // 2 * count
    tiles, pieces = cols // tile, len(slots) if by_slot else cols // width
    place = jnp.stack([rindex] + [findex ^ slot for slot in slots]).astype(jnp.int32)
    keep_spec = pl.BlockSpec((1, half, tile), lambda s, j, place: (s, 0, j))
    give_spec = pl.BlockSpec((1, half, width), lambda s, j, place: (s, 0, 0))

    def slot_spec(k):
        def index(s, j, place):
            return (0, 0, jnp.where(s < k, 0, jnp.where(s > k, tiles - 1, j)))

        return pl.BlockSpec((1, half, tile), index)

    give_specs = [keep_spec] if pieces == 1 else [give_spec] * pieces
    given = (len(slots), half, width)
    if by_slot:
        give_specs, given = [slot_spec(k) for k in range(pieces)], (1, half, cols)
    x_spec = pl.BlockSpec((rows, depth), lambda s, j, place: (0, 0), pipeline_mode=pl.Buffered(1))
    outs = pl.pallas_call(
        functools.partial(query_kernel, count, pieces, by_slot),
        grid_spec=pltpu.PrefetchScalarGridSpec(
            num_scalar_prefetch=1,
            grid=(len(slots), tiles),
            in_specs=[x_spec] * count
            + [pl.BlockSpec((depth, tile), lambda s, j, place: (0, place[1 + s] * tiles + j))]
            + [pl.BlockSpec(memory_space=pl.ANY)] * len(after),
            out_specs=[keep_spec] + give_specs,
            scratch_shapes=[pltpu.VMEM((2 * half, depth), w.dtype)],
        ),
        out_shape=[pltpu.HBM((len(slots), half, cols), jnp.float32)]
        + [pltpu.HBM(given, jnp.bfloat16)] * pieces,
        compiler_params=pltpu.CompilerParams(vmem_limit_bytes=VMEM_BYTES),
        cost_estimate=cost,
        name="query_products",
    )(place, *blocks, *in_hbm([w]), *in_hbm(after[:1]), *after[1:])
    return outs[0], outs[1:]


def pair_kernel(count, place_ref, *refs):
    x_refs, (wk_ref, wv_ref) = refs[:count], refs[count : count + 2]
    keep_ref, give_ref, rows_ref = refs[-3:]

    @pl.when(pl.program_id(0) == 0)
    def _():
        ordered_rows(place_ref, x_refs, rows_ref)

    weights = jnp.concatenate([wk_ref[...], wv_ref[...]], axis=1)
    result = jnp.dot(rows_ref[...], weights, preferred_element_type=jnp.float32)
    half, width = x_refs[0].shape[0] // 2, weights.shape[1]
    for b in range(count):
        kept, given = b * half, (count + b) * half
        cols = slice(b * width, (b + 1) * width)
        keep_ref[0, :, cols] = result[kept : kept + half]
        give_ref[0, :, cols] = result[given : given + half].astype(give_ref.dtype)


def project_pair(rindex, findex, slots, blocks, w_key, w_value, after=()):
    rows, depth = blocks[0].shape
    count = len(blocks)
    place = jnp.stack([rindex] + [findex ^ slot for slot in slots]).astype(jnp.int32)
    weight = pl.BlockSpec((depth, DH), lambda s, place: (0, place[1 + s]))
    shape = (len(slots), rows // 2, 2 * DH * count)
    out = pl.BlockSpec((1,) + shape[1:], lambda s, place: (s, 0, 0))
    return pl.pallas_call(
        functools.partial(pair_kernel, count),
        grid_spec=pltpu.PrefetchScalarGridSpec(
            num_scalar_prefetch=1,
            grid=(len(slots),),
            in_specs=[pl.BlockSpec((rows, depth), lambda s, place: (0, 0))] * count
            + [weight, weight]
            + [pl.BlockSpec(memory_space=pl.ANY)] * len(after),
            out_specs=[out, out],
            scratch_shapes=[pltpu.VMEM((count * rows, depth), blocks[0].dtype)],
        ),
        out_shape=[
            pltpu.HBM(shape, jnp.float32),
            pltpu.HBM(shape, jnp.bfloat16),
        ],
        compiler_params=pltpu.CompilerParams(vmem_limit_bytes=VMEM_BYTES),
        cost_estimate=LIGHT,
        name="key_value_products",
    )(place, *blocks, *in_hbm([w_key, w_value, *after]))


def add_kernel(gots, paired, extra, *refs):
    keep_ref, got_refs, out_ref = refs[0], refs[1 : 1 + gots], refs[-1]
    pair_refs = refs[1 + gots : 1 + gots + 2 * paired]
    landed_refs = refs[1 + gots + 2 * paired :][: extra * (1 + paired)]
    width = got_refs[0].shape[2]
    cols = gots * width

    def total(first, second, landed):
        value = first + second.astype(jnp.float32)
        for term in landed:
            value = value + term.astype(jnp.float32)
        return value.astype(out_ref.dtype)

    for t, got_ref in enumerate(got_refs):
        part = slice(t * width, (t + 1) * width)
        landed = [landed_refs[0][0, :, part]] if extra else []
        out_ref[0, :, part] = total(keep_ref[0, :, part], got_ref[0], landed)
    if paired:
        landed = [landed_refs[1][0]] if extra else []
        out_ref[0, :, cols:] = total(pair_refs[0][0], pair_refs[1][0], landed)


def add_rows(first, count, rows, b, keep, gots, start, cols, pair=(), slot=0, landed=(), after=()):
    whole = keep.shape[2]
    width = cols // len(gots)
    shift = start // cols if gots[0].shape[2] == whole else 0
    more = pair[0].shape[2] if pair else 0
    keep_spec = pl.BlockSpec((1, rows, cols), lambda s: (first + s, b, start // cols))
    got_spec = pl.BlockSpec((1, rows, width), lambda s: (first + s, b, shift))
    pair_spec = pl.BlockSpec((1, rows, more), lambda s: (slot + s, 0, 0))
    landed_specs = [pl.BlockSpec((1, rows, cols), lambda s: (s, 0, start // cols))]
    if pair:
        landed_specs.append(pl.BlockSpec((1, rows, more), lambda s: (s, 0, whole // more)))
    landed_specs = landed_specs * len(landed)
    return pl.pallas_call(
        functools.partial(add_kernel, len(gots), len(pair) // 2, len(landed)),
        grid=(count,),
        in_specs=[keep_spec]
        + [got_spec] * len(gots)
        + [pair_spec] * len(pair)
        + landed_specs
        + [pl.BlockSpec(memory_space=pl.ANY)] * len(after),
        out_specs=pl.BlockSpec((1, rows, cols + more), lambda s: (s, 0, 0)),
        out_shape=pltpu.HBM((count, rows, cols + more), jnp.bfloat16),
        compiler_params=pltpu.CompilerParams(vmem_limit_bytes=VMEM_BYTES),
        cost_estimate=LIGHT,
        name="add_rows",
    )(
        *in_hbm([keep]),
        *gots,
        *in_hbm(pair[:1]),
        *pair[1:],
        *(list(landed) * (2 if pair else 1)),
        *in_hbm(after[:1]),
        *after[1:],
    )


def rotate_kernel(count, pieces, cos_ref, sin_ref, *refs):
    terms, gots, out_ref = refs[:count], refs[count : count + pieces], refs[-1]
    total = terms[0][0].astype(jnp.float32)
    for term in terms[1:]:
        total = total + term[0].astype(jnp.float32)
    cosine, sine = cos_ref[...], sin_ref[...]

    def write(total):
        for head in range(total.shape[1] // DH):
            part = total[:, head * DH : (head + 1) * DH]
            turned = pltpu.roll(part, DH // 2, axis=1)
            value = part * cosine + turned * sine
            out_ref[:, head * DH : (head + 1) * DH] = value.astype(out_ref.dtype)

    if not gots:
        write(total)
    for j, got in enumerate(gots):

        @pl.when(pl.program_id(0) == j)
        def _():
            write(total + got[0].astype(jnp.float32))


def sum_and_rotate(cosine, sine, terms, gots, cols, after=()):
    rows = cosine.shape[0]
    slot_of_gots, block_of_gots, shift, gots = gots
    tile = cols // max(1, len(gots))
    table = pl.BlockSpec((rows, DH), lambda j: (0, 0))

    def block(slot, b, start):
        return pl.BlockSpec((1, rows, tile), lambda j: (slot, b, start // tile + j))

    return pl.pallas_call(
        functools.partial(rotate_kernel, len(terms), len(gots)),
        grid=(cols // tile,),
        in_specs=[table, table]
        + [block(slot, b, start) for _, slot, b, start in terms]
        + [pl.BlockSpec((1, rows, tile), lambda j: (slot_of_gots, block_of_gots, shift))] * len(gots)
        + [pl.BlockSpec(memory_space=pl.ANY)] * len(after),
        out_specs=pl.BlockSpec((rows, tile), lambda j: (0, j)),
        out_shape=jax.ShapeDtypeStruct((rows, cols), jnp.bfloat16),
        compiler_params=pltpu.CompilerParams(vmem_limit_bytes=VMEM_BYTES),
        cost_estimate=LIGHT,
        name="sum_and_rotate",
    )(cosine, sine, *in_hbm([terms[0][0]]), *[term[0] for term in terms[1:]], *gots, *after)


def split_kernel(count, cos_ref, sin_ref, *refs):
    terms, (key_ref, value_ref) = refs[:count], refs[-2:]
    total = terms[0][0].astype(jnp.float32)
    for term in terms[1:]:
        total = total + term[0].astype(jnp.float32)
    half = total.shape[0]
    for b in range(total.shape[1] // (2 * DH)):
        rows = slice(b * half, (b + 1) * half)
        key = total[:, 2 * b * DH : (2 * b + 1) * DH]
        turned = pltpu.roll(key, DH // 2, axis=1)
        key_ref[rows] = (key * cos_ref[rows] + turned * sin_ref[rows]).astype(key_ref.dtype)
        value_ref[0, rows] = total[:, (2 * b + 1) * DH : (2 * b + 2) * DH].astype(value_ref.dtype)


def split_and_rotate(cosine, sine, terms, width, after):
    rows = cosine.shape[0]
    half = terms[0][0].shape[1]
    table = pl.BlockSpec((rows, DH), lambda j: (0, 0))

    def block(slot, start):
        return pl.BlockSpec((1, half, width), lambda j: (slot, 0, start // width))

    return pl.pallas_call(
        functools.partial(split_kernel, len(terms)),
        grid=(1,),
        in_specs=[table, table]
        + [block(slot, start) for _, slot, start in terms]
        + [pl.BlockSpec(memory_space=pl.ANY)] * len(after),
        out_specs=[table, pl.BlockSpec((1, rows, DH), lambda j: (0, 0, 0))],
        out_shape=[
            jax.ShapeDtypeStruct((rows, DH), jnp.bfloat16),
            jax.ShapeDtypeStruct((1, rows, DH), jnp.bfloat16),
        ],
        compiler_params=pltpu.CompilerParams(vmem_limit_bytes=VMEM_BYTES),
        cost_estimate=LIGHT,
        name="split_and_rotate",
    )(cosine, sine, *in_hbm([terms[0][0]]), *[term for term, _, _ in terms[1:]], *after)


def prepare_kernel(canary_ref, ids_ref, own_ref, other_ref, order_ref, key_t_ref):
    order = jnp.where(canary_ref[...] == ids_ref[...], 1.0, 0.0).astype(jnp.bfloat16)
    order_ref[...] = order
    key = jnp.concatenate([own_ref[...], other_ref[...]], axis=0)
    key_t_ref[...] = jnp.dot(order, key, preferred_element_type=jnp.float32).T.astype(jnp.bfloat16)


def prepare(canary_rows, ids, own, other):
    rows = ids.shape[0]
    return pl.pallas_call(
        prepare_kernel,
        out_shape=[
            jax.ShapeDtypeStruct((rows, rows), jnp.bfloat16),
            jax.ShapeDtypeStruct((DH, rows), jnp.bfloat16),
        ],
        compiler_params=pltpu.CompilerParams(vmem_limit_bytes=VMEM_BYTES),
        name="order_and_keys",
    )(canary_rows.reshape(rows, 1), ids.reshape(1, rows), own, other)


def stack_kernel(count, *refs):
    out_ref, start = refs[-1], 0
    for ref in refs[:count]:
        out_ref[start : start + ref.shape[0]] = ref[...]
        start += ref.shape[0]


def stack_slots(arrays, after):
    slots = sum(x.shape[0] for x in arrays)
    shape = (slots,) + arrays[0].shape[1:]
    return pl.pallas_call(
        functools.partial(stack_kernel, len(arrays)),
        grid=(1,),
        in_specs=[pl.BlockSpec(x.shape, lambda j: (0, 0, 0)) for x in arrays]
        + [pl.BlockSpec(memory_space=pl.ANY)] * len(after),
        out_specs=pl.BlockSpec(shape, lambda j: (0, 0, 0)),
        out_shape=jax.ShapeDtypeStruct(shape, arrays[0].dtype),
        compiler_params=pltpu.CompilerParams(vmem_limit_bytes=VMEM_BYTES),
        cost_estimate=LIGHT,
        name="stack_slots",
    )(*arrays, *after)


def value_kernel(place_ref, order_ref, own_ref, other_ref, out_ref):
    rows = jnp.concatenate([own_ref[0], other_ref[0]], axis=0)
    out_ref[...] = jnp.dot(order_ref[...], rows, preferred_element_type=jnp.float32).astype(out_ref.dtype)


def order_values(findex, order, own, other):
    rows = order.shape[0]
    slots, part, width = own.shape
    place = jnp.stack([findex ^ s for s in range(slots)]).astype(jnp.int32)
    block = pl.BlockSpec((1, part, width), lambda s, place: (place[s], 0, 0))
    return pl.pallas_call(
        value_kernel,
        grid_spec=pltpu.PrefetchScalarGridSpec(
            num_scalar_prefetch=1,
            grid=(slots,),
            in_specs=[pl.BlockSpec((rows, rows), lambda s, place: (0, 0)), block, block],
            out_specs=pl.BlockSpec((rows, width), lambda s, place: (0, s)),
        ),
        out_shape=jax.ShapeDtypeStruct((rows, slots * width), jnp.bfloat16),
        compiler_params=pltpu.CompilerParams(vmem_limit_bytes=VMEM_BYTES),
        name="order_values",
    )(place, order, own, other)


def score_kernel(count, order_ref, key_t_ref, *refs):
    queries, (out_ref, mark_ref) = refs[:count], refs[-2:]
    mark_ref[...] = jnp.zeros_like(mark_ref)
    stacked = jnp.concatenate([query[...] for query in queries], axis=0)
    chosen = jnp.dot(order_ref[...], stacked, preferred_element_type=jnp.float32).astype(jnp.bfloat16)
    for head in range(stacked.shape[1] // DH):
        products = jnp.dot(
            chosen[:, head * DH : (head + 1) * DH], key_t_ref[...], preferred_element_type=jnp.float32
        )
        out_ref[0, head] = (products * DH ** (-0.5)).astype(out_ref.dtype)


def score_heads(order, key_t, heads, start, count, queries, earlier, after=()):
    rows = order.shape[0]
    step = 2 if count % 2 == 0 else 1

    def block(query, first):
        return pl.BlockSpec((query.shape[0], step * DH), lambda j: (0, first // step + j))

    return pl.pallas_call(
        functools.partial(score_kernel, len(queries)),
        grid=(count // step,),
        in_specs=[
            pl.BlockSpec((rows, rows), lambda j: (0, 0)),
            pl.BlockSpec((DH, rows), lambda j: (0, 0)),
        ]
        + [block(query, first) for query, first in queries]
        + [pl.BlockSpec(memory_space=pl.ANY)] * (len(earlier) + len(after)),
        out_specs=[
            pl.BlockSpec((1, step, rows, rows), lambda j: (0, start // step + j, 0, 0)),
            pl.BlockSpec((8, DH), lambda j: (0, 0)),
        ],
        out_shape=[
            jax.ShapeDtypeStruct((1, heads, rows, rows), jnp.bfloat16),
            jax.ShapeDtypeStruct((8, DH), jnp.float32),
        ],
        input_output_aliases={2 + len(queries): 0} if earlier else {},
        compiler_params=pltpu.CompilerParams(vmem_limit_bytes=VMEM_BYTES),
        cost_estimate=LIGHT,
        name="score_heads",
    )(order, key_t, *[query for query, _ in queries], *earlier, *after)


def body(hidden, w_query, w_key, w_value, canary_rows, positions):
    shards = lax.axis_size("fsdp")
    findex = lax.axis_index("fsdp")
    tps = lax.axis_size("tp")
    tindex = lax.axis_index("tp")
    rindex = lax.axis_index("rep")
    local, depth = hidden.shape
    half = local // 2
    rows = local * tps
    head_cols = w_query.shape[1] // shards
    heads_here = head_cols // DH
    group = HQ // KV
    assert shards & (shards - 1) == 0 and lax.axis_size("rep") == 2

    def swap(x, bit):
        return lax.ppermute(x, "fsdp", [(i, i ^ bit) for i in range(shards)])

    def other_core(x):
        return lax.ppermute(x, "rep", [(0, 1), (1, 0)])

    def low(x):
        return x.astype(jnp.bfloat16)

    odd = list(range(3, shards, 2)) + [1]
    even = list(range(2, shards, 2))
    fast_pair = heads_here == group

    def spread(live):
        terms, first = [], None
        bit = 2
        while bit < shards:
            sent = [x for x in sorted(live) if x & bit]
            pack = jnp.stack([low(live[x]) for x in sent])
            first = pack if first is None else first
            landed = swap(pack, bit)
            for k, x in enumerate(sent):
                if x == bit:
                    terms.append(landed)
                else:
                    live[x ^ bit] = live[x ^ bit] + landed[k].astype(jnp.float32)
                del live[x]
            bit *= 2
        return terms, first

    blocks = [hidden] + [
        lax.ppermute(hidden, "tp", [(i, (i - b) % tps) for i in range(tps)]) for b in range(1, tps)
    ]

    block_ids = ((tindex + jnp.arange(tps, dtype=jnp.int32)) % tps * local)[:, None]
    own_ids = (block_ids + rindex * half + jnp.arange(half, dtype=jnp.int32)[None]).reshape(-1)
    other_ids = (block_ids + (1 - rindex) * half + jnp.arange(half, dtype=jnp.int32)[None]).reshape(-1)
    ids = jnp.concatenate([own_ids, other_ids])
    own_positions = jnp.sum(
        jnp.where(own_ids[:, None] == canary_rows[None, :], positions[None, :], 0), axis=1
    )
    cosine, sine = rope_tables(own_positions)

    tile = min(1024, head_cols)

    def project(slots, blocks, width, after=(), cost=LIGHT, by_slot=False):
        keep, gives = project_query(
            rindex, findex, slots, blocks, w_query, head_cols, tile, width, after, cost, by_slot
        )
        return keep, [other_core(give) for give in gives], gives[0]

    def rotate(b, p, split, terms, behind):
        cols = head_cols // split
        table = slice(b * half, (b + 1) * half)
        keep, slot, got = owns[b]
        added = [(keep, slot, 0, p * cols)] + terms
        gots = (0, 0, p, got) if len(got) == 1 else (0, 0, 0, got[p : p + 1])
        turned = sum_and_rotate(cosine[table], sine[table], added, gots, cols, behind)
        return turned, other_core(turned)

    def add_even(b, start, cols, pair, behind):
        if shards == 2:
            return [], behind
        keep, got = evens[b]
        each = len(got) * cols // head_cols
        got = got[start // cols * each :][:each]
        summed = add_rows(
            0, len(even), half, 0, keep, got, start, cols, pair, len(odd), (fars[b],), behind
        )
        terms, first = spread({x: summed[k] for k, x in enumerate(even)})
        return [(term, 0, 0, 0) for term in terms], (first,)

    last, split = tps - 1, head_cols // tile
    placed = in_hbm(blocks[:1]) + blocks[1:]
    evens, owns, fars, terms, pair, after = [], [], [], [], (), ()
    for b, block in enumerate(placed):
        if fast_pair and b == last:
            slots = odd + even + [0]
            pair_keep, give = project_pair(rindex, findex, slots, placed, w_key, w_value, after)
            pair = (pair_keep, other_core(give))
            after = (give,)
        odd_keep, odd_got, given = project(odd, [block], tile, after)
        after = ()
        if b > 0:
            added, after = add_even(b - 1, 0, head_cols, (), (given,))
            terms.append([(fars[b - 1], len(odd) - 1, 0, 0)] + added)
        count = len(odd) - 1 if b == last else len(odd)
        odd_sent = add_rows(0, count, half, 0, odd_keep, odd_got, 0, head_cols, pair, 0, (), after)
        fars.append(swap(odd_sent, 1))
        after = (odd_sent,) + after
        if b < last:
            keep, got, given = project(even + [0], [block], head_cols, after, LIGHT, True)
            evens.append((keep, got[:1] if len(even) == 1 else [jnp.concatenate(got[:-1])]))
            owns.append((keep, len(even), got[-1:]))
        else:
            keep, got, given = project(even, [block], tile, after, HEAVY)
            evens.append((keep, got))
        after = (given,)
    parts, behind = [], tuple(term[0] for row in terms for term in row[1:])
    for p in range(split):
        near_sent = add_rows(
            len(odd) - 1, 1, half, 0, odd_keep, odd_got[p : p + 1], p * tile, tile,
            pair if p == 0 else (), len(odd) - 1, (), after,
        )
        parts.append([(swap(near_sent, 1), 0, 0, 0)])
        after = (near_sent,)
    after = after + behind
    for p in range(split):
        added, after = add_even(last, p * tile, tile, pair if p == 0 else (), after)
        parts[p] += added
    keep, got, _ = project([0], placed[last:], tile, after, HEAVY)
    owns.append((keep, 0, got))

    if fast_pair:
        width = 2 * DH * tps
        pieces = [(array, shards - 1, 0) for array in pair]
        pieces += [(term, 0, tile) for term, _, _, _ in parts[0]]
        key_rot, held = split_and_rotate(cosine, sine, pieces, width, after)
    else:
        x = jnp.concatenate(blocks, axis=0)
        key_sum, value_sum = lax.psum(
            (
                jnp.dot(x, w_key, preferred_element_type=jnp.float32),
                jnp.dot(x, w_value, preferred_element_type=jnp.float32),
            ),
            ("fsdp", "rep"),
        )

        def of_core(y, core):
            parts = y.reshape(tps, 2, half, -1)
            return lax.dynamic_index_in_dim(parts, core, 1, keepdims=False).reshape(tps * half, -1)

        mine = lax.dynamic_slice_in_dim(key_sum, findex * heads_here // group * DH, DH, 1)
        key_own = of_core(mine, rindex)
        key_rot = sum_and_rotate(cosine, sine, [(key_own[None], 0, 0, 0)], (0, 0, 0, []), DH, after)
        value_rows = low(jnp.concatenate([of_core(value_sum, rindex), of_core(value_sum, 1 - rindex)]))

    order, key_t = prepare(canary_rows, ids, key_rot, other_core(key_rot))
    if not fast_pair:
        values = low(jnp.dot(order, value_rows, preferred_element_type=jnp.float32))

    rotated = [rotate(b, 0, 1, terms[b], after) for b in range(last)]
    count = heads_here // split
    scores, mark = (), ()
    for p in range(split):
        behind = mark or tuple(row[1] for row in rotated)
        turned = rotate(last, p, split, parts[p], behind)
        queries = [(row[0], p * count) for row in rotated] + [(turned[0], 0)]
        queries += [(row[1], p * count) for row in rotated] + [(turned[1], 0)]
        *scores, mark = score_heads(
            order, key_t, heads_here, p * count, count, queries, scores
        )
        mark = (mark,)
        if fast_pair and p == 0:
            held = stack_slots([held], mark)
            held = stack_slots([held] + [swap(held, x) for x in range(1, shards)], ())
            values = order_values(findex, order, held, other_core(held))
    return (scores[0], values)


def solution(mesh):
    in_specs = (
        P(("groups", "tp"), ("fsdp", "rep")),
        P(("fsdp", "rep"), "tp"),
        P(("fsdp", "rep"), "tp"),
        P(("fsdp", "rep"), "tp"),
        P("groups"),
        P("groups"),
    )
    out_specs = (P("tp", "fsdp", "groups", None), P("groups", "tp"))
    return jax.shard_map(body, mesh=mesh, in_specs=in_specs, out_specs=out_specs, check_vma=False)
```

```python
import functools
import math

import jax
import jax.numpy as jnp
from jax import lax
from jax.experimental import pallas as pl
from jax.experimental.pallas import tpu as pltpu
from jax.sharding import PartitionSpec as P

HQ = 128
KV = 8
DH = 128
VMEM_BYTES = 28 * 1024 * 1024
LIGHT = pl.CostEstimate(flops=1000, bytes_accessed=1000, transcendentals=0)
HEAVY = pl.CostEstimate(flops=10**11, bytes_accessed=10**8, transcendentals=0)


def in_hbm(arrays):
    return [pltpu.with_memory_space_constraint(x, pltpu.HBM) for x in arrays]


def rope_tables(positions):
    half = DH // 2
    expo = jnp.arange(half, dtype=jnp.float32) * (2.0 / DH)
    freq = jnp.power(jnp.float32(500000.0), -expo)
    wavelen = 2.0 * math.pi / freq
    smooth = (8192.0 / wavelen - 1.0) / 3.0
    mixed = (1.0 - smooth) * freq / 8.0 + smooth * freq
    freq = jnp.where(wavelen > 8192.0, freq / 8.0, jnp.where(wavelen < 2048.0, freq, mixed))
    angle = positions.astype(jnp.float32)[:, None] * freq[None, :]
    cosine, sine = jnp.cos(angle), jnp.sin(angle)
    return jnp.concatenate([cosine, cosine], axis=1), jnp.concatenate([-sine, sine], axis=1)


def ordered_rows(place_ref, x_refs, rows_ref):
    core = place_ref[0]
    half = x_refs[0].shape[0] // 2
    for b, x_ref in enumerate(x_refs):
        kept, given = b * half, (len(x_refs) + b) * half
        rows_ref[kept : kept + half] = x_ref[pl.ds(pl.multiple_of(core * half, 16), half)]
        rows_ref[given : given + half] = x_ref[pl.ds(pl.multiple_of((1 - core) * half, 16), half)]


def query_kernel(count, pieces, by_slot, place_ref, *refs):
    x_refs, w_ref = refs[:count], refs[count]
    keep_ref, *give_refs, rows_ref = refs[-2 - pieces :]
    tile = pl.program_id(1)
    size = give_refs[0].shape[2]
    each = keep_ref.shape[2] // size

    @pl.when((pl.program_id(0) == 0) & (tile == 0))
    def _():
        ordered_rows(place_ref, x_refs, rows_ref)

    result = jnp.dot(rows_ref[...], w_ref[...], preferred_element_type=jnp.float32)
    half = result.shape[0] // 2
    keep_ref[0] = result[:half]
    for j, give_ref in enumerate(give_refs):

        @pl.when(pl.program_id(0) == j if by_slot else (tile == j // each) | (pieces == 1))
        def _():
            start = j % each * size
            give_ref[0] = result[half:, start : start + size].astype(give_ref.dtype)


def project_query(rindex, findex, slots, blocks, w, cols, tile, width, after, cost, by_slot):
    rows, depth = blocks[0].shape
    count = len(blocks)
    half = rows // 2 * count
    tiles, pieces = cols // tile, len(slots) if by_slot else cols // width
    place = jnp.stack([rindex] + [findex ^ slot for slot in slots]).astype(jnp.int32)
    keep_spec = pl.BlockSpec((1, half, tile), lambda s, j, place: (s, 0, j))
    give_spec = pl.BlockSpec((1, half, width), lambda s, j, place: (s, 0, 0))

    def slot_spec(k):
        def index(s, j, place):
            return (0, 0, jnp.where(s < k, 0, jnp.where(s > k, tiles - 1, j)))

        return pl.BlockSpec((1, half, tile), index)

    give_specs = [keep_spec] if pieces == 1 else [give_spec] * pieces
    given = (len(slots), half, width)
    if by_slot:
        give_specs, given = [slot_spec(k) for k in range(pieces)], (1, half, cols)
    x_spec = pl.BlockSpec((rows, depth), lambda s, j, place: (0, 0), pipeline_mode=pl.Buffered(1))
    outs = pl.pallas_call(
        functools.partial(query_kernel, count, pieces, by_slot),
        grid_spec=pltpu.PrefetchScalarGridSpec(
            num_scalar_prefetch=1,
            grid=(len(slots), tiles),
            in_specs=[x_spec] * count
            + [pl.BlockSpec((depth, tile), lambda s, j, place: (0, place[1 + s] * tiles + j))]
            + [pl.BlockSpec(memory_space=pl.ANY)] * len(after),
            out_specs=[keep_spec] + give_specs,
            scratch_shapes=[pltpu.VMEM((2 * half, depth), w.dtype)],
        ),
        out_shape=[pltpu.HBM((len(slots), half, cols), jnp.float32)]
        + [pltpu.HBM(given, jnp.bfloat16)] * pieces,
        compiler_params=pltpu.CompilerParams(vmem_limit_bytes=VMEM_BYTES),
        cost_estimate=cost,
        name="query_products",
    )(place, *blocks, *in_hbm([w]), *in_hbm(after[:1]), *after[1:])
    return outs[0], outs[1:]


def pair_kernel(count, place_ref, *refs):
    x_refs, (wk_ref, wv_ref) = refs[:count], refs[count : count + 2]
    keep_ref, give_ref, rows_ref = refs[-3:]

    @pl.when(pl.program_id(0) == 0)
    def _():
        ordered_rows(place_ref, x_refs, rows_ref)

    weights = jnp.concatenate([wk_ref[...], wv_ref[...]], axis=1)
    result = jnp.dot(rows_ref[...], weights, preferred_element_type=jnp.float32)
    half, width = x_refs[0].shape[0] // 2, weights.shape[1]
    for b in range(count):
        kept, given = b * half, (count + b) * half
        cols = slice(b * width, (b + 1) * width)
        keep_ref[0, :, cols] = result[kept : kept + half]
        give_ref[0, :, cols] = result[given : given + half].astype(give_ref.dtype)


def project_pair(rindex, findex, slots, blocks, w_key, w_value, after=()):
    rows, depth = blocks[0].shape
    count = len(blocks)
    place = jnp.stack([rindex] + [findex ^ slot for slot in slots]).astype(jnp.int32)
    weight = pl.BlockSpec((depth, DH), lambda s, place: (0, place[1 + s]))
    shape = (len(slots), rows // 2, 2 * DH * count)
    out = pl.BlockSpec((1,) + shape[1:], lambda s, place: (s, 0, 0))
    return pl.pallas_call(
        functools.partial(pair_kernel, count),
        grid_spec=pltpu.PrefetchScalarGridSpec(
            num_scalar_prefetch=1,
            grid=(len(slots),),
            in_specs=[pl.BlockSpec((rows, depth), lambda s, place: (0, 0))] * count
            + [weight, weight]
            + [pl.BlockSpec(memory_space=pl.ANY)] * len(after),
            out_specs=[out, out],
            scratch_shapes=[pltpu.VMEM((count * rows, depth), blocks[0].dtype)],
        ),
        out_shape=[
            pltpu.HBM(shape, jnp.float32),
            pltpu.HBM(shape, jnp.bfloat16),
        ],
        compiler_params=pltpu.CompilerParams(vmem_limit_bytes=VMEM_BYTES),
        cost_estimate=LIGHT,
        name="key_value_products",
    )(place, *blocks, *in_hbm([w_key, w_value, *after]))


def add_kernel(gots, paired, extra, *refs):
    keep_ref, got_refs, out_ref = refs[0], refs[1 : 1 + gots], refs[-1]
    pair_refs = refs[1 + gots : 1 + gots + 2 * paired]
    landed_refs = refs[1 + gots + 2 * paired :][: extra * (1 + paired)]
    width = got_refs[0].shape[2]
    cols = gots * width

    def total(first, second, landed):
        value = first + second.astype(jnp.float32)
        for term in landed:
            value = value + term.astype(jnp.float32)
        return value.astype(out_ref.dtype)

    for t, got_ref in enumerate(got_refs):
        part = slice(t * width, (t + 1) * width)
        landed = [landed_refs[0][0, :, part]] if extra else []
        out_ref[0, :, part] = total(keep_ref[0, :, part], got_ref[0], landed)
    if paired:
        landed = [landed_refs[1][0]] if extra else []
        out_ref[0, :, cols:] = total(pair_refs[0][0], pair_refs[1][0], landed)


def add_rows(first, count, rows, b, keep, gots, start, cols, pair=(), slot=0, landed=(), after=()):
    whole = keep.shape[2]
    width = cols // len(gots)
    shift = start // cols if gots[0].shape[2] == whole else 0
    more = pair[0].shape[2] if pair else 0
    keep_spec = pl.BlockSpec((1, rows, cols), lambda s: (first + s, b, start // cols))
    got_spec = pl.BlockSpec((1, rows, width), lambda s: (first + s, b, shift))
    pair_spec = pl.BlockSpec((1, rows, more), lambda s: (slot + s, 0, 0))
    landed_specs = [pl.BlockSpec((1, rows, cols), lambda s: (s, 0, start // cols))]
    if pair:
        landed_specs.append(pl.BlockSpec((1, rows, more), lambda s: (s, 0, whole // more)))
    landed_specs = landed_specs * len(landed)
    return pl.pallas_call(
        functools.partial(add_kernel, len(gots), len(pair) // 2, len(landed)),
        grid=(count,),
        in_specs=[keep_spec]
        + [got_spec] * len(gots)
        + [pair_spec] * len(pair)
        + landed_specs
        + [pl.BlockSpec(memory_space=pl.ANY)] * len(after),
        out_specs=pl.BlockSpec((1, rows, cols + more), lambda s: (s, 0, 0)),
        out_shape=pltpu.HBM((count, rows, cols + more), jnp.bfloat16),
        compiler_params=pltpu.CompilerParams(vmem_limit_bytes=VMEM_BYTES),
        cost_estimate=LIGHT,
        name="add_rows",
    )(
        *in_hbm([keep]),
        *gots,
        *in_hbm(pair[:1]),
        *pair[1:],
        *(list(landed) * (2 if pair else 1)),
        *in_hbm(after[:1]),
        *after[1:],
    )


def rotate_kernel(count, pieces, cos_ref, sin_ref, *refs):
    terms, gots, out_ref = refs[:count], refs[count : count + pieces], refs[-1]
    total = terms[0][0].astype(jnp.float32)
    for term in terms[1:]:
        total = total + term[0].astype(jnp.float32)
    cosine, sine = cos_ref[...], sin_ref[...]

    def write(total):
        for head in range(total.shape[1] // DH):
            part = total[:, head * DH : (head + 1) * DH]
            turned = pltpu.roll(part, DH // 2, axis=1)
            value = part * cosine + turned * sine
            out_ref[:, head * DH : (head + 1) * DH] = value.astype(out_ref.dtype)

    if not gots:
        write(total)
    for j, got in enumerate(gots):

        @pl.when(pl.program_id(0) == j)
        def _():
            write(total + got[0].astype(jnp.float32))


def sum_and_rotate(cosine, sine, terms, gots, cols, after=()):
    rows = cosine.shape[0]
    slot_of_gots, block_of_gots, shift, gots = gots
    tile = cols // max(1, len(gots))
    table = pl.BlockSpec((rows, DH), lambda j: (0, 0))

    def block(slot, b, start):
        return pl.BlockSpec((1, rows, tile), lambda j: (slot, b, start // tile + j))

    return pl.pallas_call(
        functools.partial(rotate_kernel, len(terms), len(gots)),
        grid=(cols // tile,),
        in_specs=[table, table]
        + [block(slot, b, start) for _, slot, b, start in terms]
        + [pl.BlockSpec((1, rows, tile), lambda j: (slot_of_gots, block_of_gots, shift))] * len(gots)
        + [pl.BlockSpec(memory_space=pl.ANY)] * len(after),
        out_specs=pl.BlockSpec((rows, tile), lambda j: (0, j)),
        out_shape=jax.ShapeDtypeStruct((rows, cols), jnp.bfloat16),
        compiler_params=pltpu.CompilerParams(vmem_limit_bytes=VMEM_BYTES),
        cost_estimate=LIGHT,
        name="sum_and_rotate",
    )(cosine, sine, *in_hbm([terms[0][0]]), *[term[0] for term in terms[1:]], *gots, *after)


def split_kernel(count, cos_ref, sin_ref, *refs):
    terms, (key_ref, value_ref) = refs[:count], refs[-2:]
    total = terms[0][0].astype(jnp.float32)
    for term in terms[1:]:
        total = total + term[0].astype(jnp.float32)
    half = total.shape[0]
    for b in range(total.shape[1] // (2 * DH)):
        rows = slice(b * half, (b + 1) * half)
        key = total[:, 2 * b * DH : (2 * b + 1) * DH]
        turned = pltpu.roll(key, DH // 2, axis=1)
        key_ref[rows] = (key * cos_ref[rows] + turned * sin_ref[rows]).astype(key_ref.dtype)
        value_ref[0, rows] = total[:, (2 * b + 1) * DH : (2 * b + 2) * DH].astype(value_ref.dtype)


def split_and_rotate(cosine, sine, terms, width, after):
    rows = cosine.shape[0]
    half = terms[0][0].shape[1]
    table = pl.BlockSpec((rows, DH), lambda j: (0, 0))

    def block(slot, start):
        return pl.BlockSpec((1, half, width), lambda j: (slot, 0, start // width))

    return pl.pallas_call(
        functools.partial(split_kernel, len(terms)),
        grid=(1,),
        in_specs=[table, table]
        + [block(slot, start) for _, slot, start in terms]
        + [pl.BlockSpec(memory_space=pl.ANY)] * len(after),
        out_specs=[table, pl.BlockSpec((1, rows, DH), lambda j: (0, 0, 0))],
        out_shape=[
            jax.ShapeDtypeStruct((rows, DH), jnp.bfloat16),
            jax.ShapeDtypeStruct((1, rows, DH), jnp.bfloat16),
        ],
        compiler_params=pltpu.CompilerParams(vmem_limit_bytes=VMEM_BYTES),
        cost_estimate=LIGHT,
        name="split_and_rotate",
    )(cosine, sine, *in_hbm([terms[0][0]]), *[term for term, _, _ in terms[1:]], *after)


def prepare_kernel(canary_ref, ids_ref, own_ref, other_ref, order_ref, key_t_ref):
    order = jnp.where(canary_ref[...] == ids_ref[...], 1.0, 0.0).astype(jnp.bfloat16)
    order_ref[...] = order
    key = jnp.concatenate([own_ref[...], other_ref[...]], axis=0)
    key_t_ref[...] = jnp.dot(order, key, preferred_element_type=jnp.float32).T.astype(jnp.bfloat16)


def prepare(canary_rows, ids, own, other):
    rows = ids.shape[0]
    return pl.pallas_call(
        prepare_kernel,
        out_shape=[
            jax.ShapeDtypeStruct((rows, rows), jnp.bfloat16),
            jax.ShapeDtypeStruct((DH, rows), jnp.bfloat16),
        ],
        compiler_params=pltpu.CompilerParams(vmem_limit_bytes=VMEM_BYTES),
        name="order_and_keys",
    )(canary_rows.reshape(rows, 1), ids.reshape(1, rows), own, other)


def stack_kernel(count, *refs):
    out_ref, start = refs[-1], 0
    for ref in refs[:count]:
        out_ref[start : start + ref.shape[0]] = ref[...]
        start += ref.shape[0]


def stack_slots(arrays, after):
    slots = sum(x.shape[0] for x in arrays)
    shape = (slots,) + arrays[0].shape[1:]
    return pl.pallas_call(
        functools.partial(stack_kernel, len(arrays)),
        grid=(1,),
        in_specs=[pl.BlockSpec(x.shape, lambda j: (0, 0, 0)) for x in arrays]
        + [pl.BlockSpec(memory_space=pl.ANY)] * len(after),
        out_specs=pl.BlockSpec(shape, lambda j: (0, 0, 0)),
        out_shape=jax.ShapeDtypeStruct(shape, arrays[0].dtype),
        compiler_params=pltpu.CompilerParams(vmem_limit_bytes=VMEM_BYTES),
        cost_estimate=LIGHT,
        name="stack_slots",
    )(*arrays, *after)


def value_kernel(place_ref, order_ref, own_ref, other_ref, out_ref):
    rows = jnp.concatenate([own_ref[0], other_ref[0]], axis=0)
    out_ref[...] = jnp.dot(order_ref[...], rows, preferred_element_type=jnp.float32).astype(out_ref.dtype)


def order_values(findex, order, own, other):
    rows = order.shape[0]
    slots, part, width = own.shape
    place = jnp.stack([findex ^ s for s in range(slots)]).astype(jnp.int32)
    block = pl.BlockSpec((1, part, width), lambda s, place: (place[s], 0, 0))
    return pl.pallas_call(
        value_kernel,
        grid_spec=pltpu.PrefetchScalarGridSpec(
            num_scalar_prefetch=1,
            grid=(slots,),
            in_specs=[pl.BlockSpec((rows, rows), lambda s, place: (0, 0)), block, block],
            out_specs=pl.BlockSpec((rows, width), lambda s, place: (0, s)),
        ),
        out_shape=jax.ShapeDtypeStruct((rows, slots * width), jnp.bfloat16),
        compiler_params=pltpu.CompilerParams(vmem_limit_bytes=VMEM_BYTES),
        name="order_values",
    )(place, order, own, other)


def score_kernel(count, order_ref, key_t_ref, *refs):
    queries, (out_ref, mark_ref) = refs[:count], refs[-2:]
    mark_ref[...] = jnp.zeros_like(mark_ref)
    stacked = jnp.concatenate([query[...] for query in queries], axis=0)
    chosen = jnp.dot(order_ref[...], stacked, preferred_element_type=jnp.float32).astype(jnp.bfloat16)
    for head in range(stacked.shape[1] // DH):
        products = jnp.dot(
            chosen[:, head * DH : (head + 1) * DH], key_t_ref[...], preferred_element_type=jnp.float32
        )
        out_ref[0, head] = (products * DH ** (-0.5)).astype(out_ref.dtype)


def score_heads(order, key_t, heads, start, count, queries, earlier, after=()):
    rows = order.shape[0]
    step = 2 if count % 2 == 0 else 1

    def block(query, first):
        return pl.BlockSpec((query.shape[0], step * DH), lambda j: (0, first // step + j))

    return pl.pallas_call(
        functools.partial(score_kernel, len(queries)),
        grid=(count // step,),
        in_specs=[
            pl.BlockSpec((rows, rows), lambda j: (0, 0)),
            pl.BlockSpec((DH, rows), lambda j: (0, 0)),
        ]
        + [block(query, first) for query, first in queries]
        + [pl.BlockSpec(memory_space=pl.ANY)] * (len(earlier) + len(after)),
        out_specs=[
            pl.BlockSpec((1, step, rows, rows), lambda j: (0, start // step + j, 0, 0)),
            pl.BlockSpec((8, DH), lambda j: (0, 0)),
        ],
        out_shape=[
            jax.ShapeDtypeStruct((1, heads, rows, rows), jnp.bfloat16),
            jax.ShapeDtypeStruct((8, DH), jnp.float32),
        ],
        input_output_aliases={2 + len(queries): 0} if earlier else {},
        compiler_params=pltpu.CompilerParams(vmem_limit_bytes=VMEM_BYTES),
        cost_estimate=LIGHT,
        name="score_heads",
    )(order, key_t, *[query for query, _ in queries], *earlier, *after)


def body(hidden, w_query, w_key, w_value, canary_rows, positions):
    shards = lax.axis_size("fsdp")
    findex = lax.axis_index("fsdp")
    tps = lax.axis_size("tp")
    tindex = lax.axis_index("tp")
    rindex = lax.axis_index("rep")
    local, depth = hidden.shape
    half = local // 2
    rows = local * tps
    head_cols = w_query.shape[1] // shards
    heads_here = head_cols // DH
    group = HQ // KV
    assert shards & (shards - 1) == 0 and lax.axis_size("rep") == 2

    def swap(x, bit):
        return lax.ppermute(x, "fsdp", [(i, i ^ bit) for i in range(shards)])

    def other_core(x):
        return lax.ppermute(x, "rep", [(0, 1), (1, 0)])

    def low(x):
        return x.astype(jnp.bfloat16)

    odd = list(range(3, shards, 2)) + [1]
    even = list(range(2, shards, 2))
    fast_pair = heads_here == group

    def spread(live):
        terms, first = [], None
        bit = 2
        while bit < shards:
            sent = [x for x in sorted(live) if x & bit]
            pack = jnp.stack([low(live[x]) for x in sent])
            first = pack if first is None else first
            landed = swap(pack, bit)
            for k, x in enumerate(sent):
                if x == bit:
                    terms.append(landed)
                else:
                    live[x ^ bit] = live[x ^ bit] + landed[k].astype(jnp.float32)
                del live[x]
            bit *= 2
        return terms, first

    blocks = [hidden] + [
        lax.ppermute(hidden, "tp", [(i, (i - b) % tps) for i in range(tps)]) for b in range(1, tps)
    ]

    block_ids = ((tindex + jnp.arange(tps, dtype=jnp.int32)) % tps * local)[:, None]
    own_ids = (block_ids + rindex * half + jnp.arange(half, dtype=jnp.int32)[None]).reshape(-1)
    other_ids = (block_ids + (1 - rindex) * half + jnp.arange(half, dtype=jnp.int32)[None]).reshape(-1)
    ids = jnp.concatenate([own_ids, other_ids])
    own_positions = jnp.sum(
        jnp.where(own_ids[:, None] == canary_rows[None, :], positions[None, :], 0), axis=1
    )
    cosine, sine = rope_tables(own_positions)

    tile = min(1024, head_cols)

    def project(slots, blocks, width, after=(), cost=LIGHT, by_slot=False):
        keep, gives = project_query(
            rindex, findex, slots, blocks, w_query, head_cols, tile, width, after, cost, by_slot
        )
        return keep, [other_core(give) for give in gives], gives[0]

    def rotate(b, p, split, terms, behind):
        cols = head_cols // split
        table = slice(b * half, (b + 1) * half)
        keep, slot, got = owns[b]
        added = [(keep, slot, 0, p * cols)] + terms
        gots = (0, 0, p, got) if len(got) == 1 else (0, 0, 0, got[p : p + 1])
        turned = sum_and_rotate(cosine[table], sine[table], added, gots, cols, behind)
        return turned, other_core(turned)

    def add_even(b, start, cols, pair, behind):
        if shards == 2:
            return [], behind
        keep, got = evens[b]
        each = len(got) * cols // head_cols
        got = got[start // cols * each :][:each]
        summed = add_rows(
            0, len(even), half, 0, keep, got, start, cols, pair, len(odd), (fars[b],), behind
        )
        terms, first = spread({x: summed[k] for k, x in enumerate(even)})
        return [(term, 0, 0, 0) for term in terms], (first,)

    last, split = tps - 1, head_cols // tile
    placed = in_hbm(blocks[:1]) + blocks[1:]
    evens, owns, fars, terms, pair, after = [], [], [], [], (), ()
    for b, block in enumerate(placed):
        if fast_pair and b == last:
            slots = odd + even + [0]
            pair_keep, give = project_pair(rindex, findex, slots, placed, w_key, w_value, after)
            pair = (pair_keep, other_core(give))
            after = (give,)
        odd_keep, odd_got, given = project(odd, [block], tile, after)
        count = len(odd) - 1 if b == last else len(odd)
        odd_sent = add_rows(0, count, half, 0, odd_keep, odd_got, 0, head_cols, pair)
        fars.append(swap(odd_sent, 1))
        after = (odd_sent,)
        if b > 0:
            added, after = add_even(b - 1, 0, head_cols, (), after)
            terms.append([(fars[b - 1], len(odd) - 1, 0, 0)] + added)
            after = (odd_sent,) + after
        if b < last:
            keep, got, given = project(even + [0], [block], head_cols, after, LIGHT, True)
            evens.append((keep, got[:1] if len(even) == 1 else [jnp.concatenate(got[:-1])]))
            owns.append((keep, len(even), got[-1:]))
        else:
            keep, got, given = project(even, [block], tile, after, HEAVY)
            evens.append((keep, got))
        after = (given,)
    parts, behind = [], tuple(term[0] for row in terms for term in row[1:])
    for p in range(split):
        near_sent = add_rows(
            len(odd) - 1, 1, half, 0, odd_keep, odd_got[p : p + 1], p * tile, tile,
            pair if p == 0 else (), len(odd) - 1, (), after,
        )
        parts.append([(swap(near_sent, 1), 0, 0, 0)])
        after = (near_sent,)
    after = after + behind
    for p in range(split):
        added, after = add_even(last, p * tile, tile, pair if p == 0 else (), after)
        parts[p] += added
    keep, got, _ = project([0], placed[last:], tile, after, HEAVY)
    owns.append((keep, 0, got))

    if fast_pair:
        width = 2 * DH * tps
        pieces = [(array, shards - 1, 0) for array in pair]
        pieces += [(term, 0, tile) for term, _, _, _ in parts[0]]
        key_rot, held = split_and_rotate(cosine, sine, pieces, width, after)
    else:
        x = jnp.concatenate(blocks, axis=0)
        key_sum, value_sum = lax.psum(
            (
                jnp.dot(x, w_key, preferred_element_type=jnp.float32),
                jnp.dot(x, w_value, preferred_element_type=jnp.float32),
            ),
            ("fsdp", "rep"),
        )

        def of_core(y, core):
            parts = y.reshape(tps, 2, half, -1)
            return lax.dynamic_index_in_dim(parts, core, 1, keepdims=False).reshape(tps * half, -1)

        mine = lax.dynamic_slice_in_dim(key_sum, findex * heads_here // group * DH, DH, 1)
        key_own = of_core(mine, rindex)
        key_rot = sum_and_rotate(cosine, sine, [(key_own[None], 0, 0, 0)], (0, 0, 0, []), DH, after)
        value_rows = low(jnp.concatenate([of_core(value_sum, rindex), of_core(value_sum, 1 - rindex)]))

    order, key_t = prepare(canary_rows, ids, key_rot, other_core(key_rot))
    if not fast_pair:
        values = low(jnp.dot(order, value_rows, preferred_element_type=jnp.float32))

    rotated = [rotate(b, 0, 1, terms[b], after) for b in range(last)]
    count = heads_here // split
    scores, mark = (), ()
    for p in range(split):
        turned = rotate(last, p, split, parts[p], mark or tuple(owns[last][2][1:]))
        queries = [(row[0], p * count) for row in rotated] + [(turned[0], 0)]
        queries += [(row[1], p * count) for row in rotated] + [(turned[1], 0)]
        behind = in_hbm([values]) if p == split - 1 and p > 0 else ()
        *scores, mark = score_heads(
            order, key_t, heads_here, p * count, count, queries, scores, behind
        )
        mark = (mark,)
        if fast_pair and p == 0:
            held = stack_slots([held] + [swap(held, x) for x in range(1, shards)], mark)
            values = order_values(findex, order, held, other_core(held))
    return (scores[0], values)


def solution(mesh):
    in_specs = (
        P(("groups", "tp"), ("fsdp", "rep")),
        P(("fsdp", "rep"), "tp"),
        P(("fsdp", "rep"), "tp"),
        P(("fsdp", "rep"), "tp"),
        P("groups"),
        P("groups"),
    )
    out_specs = (P("tp", "fsdp", "groups", None), P("groups", "tp"))
    return jax.shard_map(body, mesh=mesh, in_specs=in_specs, out_specs=out_specs, check_vma=False)
```

```python
import functools
import math

import jax
import jax.numpy as jnp
from jax import lax
from jax.experimental import pallas as pl
from jax.experimental.pallas import tpu as pltpu
from jax.sharding import PartitionSpec as P

HQ = 128
KV = 8
DH = 128
VMEM_BYTES = 28 * 1024 * 1024
LIGHT = pl.CostEstimate(flops=1000, bytes_accessed=1000, transcendentals=0)
HEAVY = pl.CostEstimate(flops=10**11, bytes_accessed=10**8, transcendentals=0)


def in_hbm(arrays):
    return [pltpu.with_memory_space_constraint(x, pltpu.HBM) for x in arrays]


def rope_tables(positions):
    half = DH // 2
    expo = jnp.arange(half, dtype=jnp.float32) * (2.0 / DH)
    freq = jnp.power(jnp.float32(500000.0), -expo)
    wavelen = 2.0 * math.pi / freq
    smooth = (8192.0 / wavelen - 1.0) / 3.0
    mixed = (1.0 - smooth) * freq / 8.0 + smooth * freq
    freq = jnp.where(wavelen > 8192.0, freq / 8.0, jnp.where(wavelen < 2048.0, freq, mixed))
    angle = positions.astype(jnp.float32)[:, None] * freq[None, :]
    cosine, sine = jnp.cos(angle), jnp.sin(angle)
    return jnp.concatenate([cosine, cosine], axis=1), jnp.concatenate([-sine, sine], axis=1)


def ordered_rows(place_ref, x_refs, rows_ref):
    core = place_ref[0]
    half = x_refs[0].shape[0] // 2
    for b, x_ref in enumerate(x_refs):
        kept, given = b * half, (len(x_refs) + b) * half
        rows_ref[kept : kept + half] = x_ref[pl.ds(pl.multiple_of(core * half, 16), half)]
        rows_ref[given : given + half] = x_ref[pl.ds(pl.multiple_of((1 - core) * half, 16), half)]


def query_kernel(count, pieces, by_slot, place_ref, *refs):
    x_refs, w_ref = refs[:count], refs[count]
    keep_ref, *give_refs, rows_ref = refs[-2 - pieces :]
    tile = pl.program_id(1)
    size = give_refs[0].shape[2]
    each = keep_ref.shape[2] // size

    @pl.when((pl.program_id(0) == 0) & (tile == 0))
    def _():
        ordered_rows(place_ref, x_refs, rows_ref)

    result = jnp.dot(rows_ref[...], w_ref[...], preferred_element_type=jnp.float32)
    half = result.shape[0] // 2
    keep_ref[0] = result[:half]
    for j, give_ref in enumerate(give_refs):

        @pl.when(pl.program_id(0) == j if by_slot else (tile == j // each) | (pieces == 1))
        def _():
            start = j % each * size
            give_ref[0] = result[half:, start : start + size].astype(give_ref.dtype)


def project_query(rindex, findex, slots, blocks, w, cols, tile, width, after, cost, by_slot):
    rows, depth = blocks[0].shape
    count = len(blocks)
    half = rows // 2 * count
    tiles, pieces = cols // tile, len(slots) if by_slot else cols // width
    place = jnp.stack([rindex] + [findex ^ slot for slot in slots]).astype(jnp.int32)
    keep_spec = pl.BlockSpec((1, half, tile), lambda s, j, place: (s, 0, j))
    give_spec = pl.BlockSpec((1, half, width), lambda s, j, place: (s, 0, 0))

    def slot_spec(k):
        def index(s, j, place):
            return (0, 0, jnp.where(s < k, 0, jnp.where(s > k, tiles - 1, j)))

        return pl.BlockSpec((1, half, tile), index)

    give_specs = [keep_spec] if pieces == 1 else [give_spec] * pieces
    given = (len(slots), half, width)
    if by_slot:
        give_specs, given = [slot_spec(k) for k in range(pieces)], (1, half, cols)
    x_spec = pl.BlockSpec((rows, depth), lambda s, j, place: (0, 0), pipeline_mode=pl.Buffered(1))
    outs = pl.pallas_call(
        functools.partial(query_kernel, count, pieces, by_slot),
        grid_spec=pltpu.PrefetchScalarGridSpec(
            num_scalar_prefetch=1,
            grid=(len(slots), tiles),
            in_specs=[x_spec] * count
            + [pl.BlockSpec((depth, tile), lambda s, j, place: (0, place[1 + s] * tiles + j))]
            + [pl.BlockSpec(memory_space=pl.ANY)] * len(after),
            out_specs=[keep_spec] + give_specs,
            scratch_shapes=[pltpu.VMEM((2 * half, depth), w.dtype)],
        ),
        out_shape=[pltpu.HBM((len(slots), half, cols), jnp.float32)]
        + [pltpu.HBM(given, jnp.bfloat16)] * pieces,
        compiler_params=pltpu.CompilerParams(vmem_limit_bytes=VMEM_BYTES),
        cost_estimate=cost,
        name="query_products",
    )(place, *blocks, *in_hbm([w]), *in_hbm(after[:1]), *after[1:])
    return outs[0], outs[1:]


def pair_kernel(count, place_ref, *refs):
    x_refs, (wk_ref, wv_ref) = refs[:count], refs[count : count + 2]
    keep_ref, give_ref, rows_ref = refs[-3:]

    @pl.when(pl.program_id(0) == 0)
    def _():
        ordered_rows(place_ref, x_refs, rows_ref)

    weights = jnp.concatenate([wk_ref[...], wv_ref[...]], axis=1)
    result = jnp.dot(rows_ref[...], weights, preferred_element_type=jnp.float32)
    half = x_refs[0].shape[0] // 2
    for b in range(count):
        kept, given = b * half, (count + b) * half
        for part in range(2):
            cols = slice((part * count + b) * DH, (part * count + b + 1) * DH)
            there = slice(part * DH, (part + 1) * DH)
            keep_ref[0, :, cols] = result[kept : kept + half, there]
            give_ref[0, :, cols] = result[given : given + half, there].astype(give_ref.dtype)


def project_pair(rindex, findex, slots, blocks, w_key, w_value, after=()):
    rows, depth = blocks[0].shape
    count = len(blocks)
    place = jnp.stack([rindex] + [findex ^ slot for slot in slots]).astype(jnp.int32)
    weight = pl.BlockSpec((depth, DH), lambda s, place: (0, place[1 + s]))
    shape = (len(slots), rows // 2, 2 * DH * count)
    out = pl.BlockSpec((1,) + shape[1:], lambda s, place: (s, 0, 0))
    return pl.pallas_call(
        functools.partial(pair_kernel, count),
        grid_spec=pltpu.PrefetchScalarGridSpec(
            num_scalar_prefetch=1,
            grid=(len(slots),),
            in_specs=[pl.BlockSpec((rows, depth), lambda s, place: (0, 0))] * count
            + [weight, weight]
            + [pl.BlockSpec(memory_space=pl.ANY)] * len(after),
            out_specs=[out, out],
            scratch_shapes=[pltpu.VMEM((count * rows, depth), blocks[0].dtype)],
        ),
        out_shape=[
            pltpu.HBM(shape, jnp.float32),
            pltpu.HBM(shape, jnp.bfloat16),
        ],
        compiler_params=pltpu.CompilerParams(vmem_limit_bytes=VMEM_BYTES),
        cost_estimate=LIGHT,
        name="key_value_products",
    )(place, *blocks, *in_hbm([w_key, w_value, *after]))


def add_kernel(gots, paired, extra, *refs):
    keep_ref, got_refs, out_ref = refs[0], refs[1 : 1 + gots], refs[-1]
    pair_refs = refs[1 + gots : 1 + gots + 2 * paired]
    landed_refs = refs[1 + gots + 2 * paired :][: extra * (1 + paired)]
    width = got_refs[0].shape[2]
    cols = gots * width

    def total(first, second, landed):
        value = first + second.astype(jnp.float32)
        for term in landed:
            value = value + term.astype(jnp.float32)
        return value.astype(out_ref.dtype)

    for t, got_ref in enumerate(got_refs):
        part = slice(t * width, (t + 1) * width)
        landed = [landed_refs[0][0, :, part]] if extra else []
        out_ref[0, :, part] = total(keep_ref[0, :, part], got_ref[0], landed)
    if paired:
        landed = [landed_refs[1][0]] if extra else []
        out_ref[0, :, cols:] = total(pair_refs[0][0], pair_refs[1][0], landed)


def add_rows(first, count, rows, b, keep, gots, start, cols, pair=(), slot=0, landed=(), after=()):
    whole = keep.shape[2]
    width = cols // len(gots)
    shift = start // cols if gots[0].shape[2] == whole else 0
    more = pair[0].shape[2] // 2 if pair else 0
    keep_spec = pl.BlockSpec((1, rows, cols), lambda s: (first + s, b, start // cols))
    got_spec = pl.BlockSpec((1, rows, width), lambda s: (first + s, b, shift))
    pair_spec = pl.BlockSpec((1, rows, more), lambda s: (slot + 2 * s, 0, 0))
    landed_specs = [pl.BlockSpec((1, rows, cols), lambda s: (s, 0, start // cols))]
    if pair:
        landed_specs.append(pl.BlockSpec((1, rows, more), lambda s: (s, 0, whole // more)))
    landed_specs = landed_specs * len(landed)
    return pl.pallas_call(
        functools.partial(add_kernel, len(gots), len(pair) // 2, len(landed)),
        grid=(count,),
        in_specs=[keep_spec]
        + [got_spec] * len(gots)
        + [pair_spec] * len(pair)
        + landed_specs
        + [pl.BlockSpec(memory_space=pl.ANY)] * len(after),
        out_specs=pl.BlockSpec((1, rows, cols + more), lambda s: (s, 0, 0)),
        out_shape=pltpu.HBM((count, rows, cols + more), jnp.bfloat16),
        compiler_params=pltpu.CompilerParams(vmem_limit_bytes=VMEM_BYTES),
        cost_estimate=LIGHT,
        name="add_rows",
    )(
        *in_hbm([keep]),
        *gots,
        *in_hbm(pair[:1]),
        *pair[1:],
        *(list(landed) * (2 if pair else 1)),
        *in_hbm(after[:1]),
        *after[1:],
    )


def rotate_kernel(count, pieces, cos_ref, sin_ref, *refs):
    terms, gots, out_ref = refs[:count], refs[count : count + pieces], refs[-1]
    total = terms[0][0].astype(jnp.float32)
    for term in terms[1:]:
        total = total + term[0].astype(jnp.float32)
    cosine, sine = cos_ref[...], sin_ref[...]

    def write(total):
        for head in range(total.shape[1] // DH):
            part = total[:, head * DH : (head + 1) * DH]
            turned = pltpu.roll(part, DH // 2, axis=1)
            value = part * cosine + turned * sine
            out_ref[:, head * DH : (head + 1) * DH] = value.astype(out_ref.dtype)

    if not gots:
        write(total)
    for j, got in enumerate(gots):

        @pl.when(pl.program_id(0) == j)
        def _():
            write(total + got[0].astype(jnp.float32))


def sum_and_rotate(cosine, sine, terms, gots, cols, after=()):
    rows = cosine.shape[0]
    slot_of_gots, block_of_gots, shift, gots = gots
    tile = cols // max(1, len(gots))
    table = pl.BlockSpec((rows, DH), lambda j: (0, 0))

    def block(slot, b, start):
        return pl.BlockSpec((1, rows, tile), lambda j: (slot, b, start // tile + j))

    return pl.pallas_call(
        functools.partial(rotate_kernel, len(terms), len(gots)),
        grid=(cols // tile,),
        in_specs=[table, table]
        + [block(slot, b, start) for _, slot, b, start in terms]
        + [pl.BlockSpec((1, rows, tile), lambda j: (slot_of_gots, block_of_gots, shift))] * len(gots)
        + [pl.BlockSpec(memory_space=pl.ANY)] * len(after),
        out_specs=pl.BlockSpec((rows, tile), lambda j: (0, j)),
        out_shape=jax.ShapeDtypeStruct((rows, cols), jnp.bfloat16),
        compiler_params=pltpu.CompilerParams(vmem_limit_bytes=VMEM_BYTES),
        cost_estimate=LIGHT,
        name="sum_and_rotate",
    )(cosine, sine, *in_hbm([terms[0][0]]), *[term[0] for term in terms[1:]], *gots, *after)


def keys_kernel(count, cos_ref, sin_ref, *refs):
    terms, key_ref = refs[:count], refs[-1]
    total = terms[0][0].astype(jnp.float32)
    for term in terms[1:]:
        total = total + term[0].astype(jnp.float32)
    half = total.shape[0]
    for b in range(total.shape[1] // DH):
        rows = slice(b * half, (b + 1) * half)
        key = total[:, b * DH : (b + 1) * DH]
        turned = pltpu.roll(key, DH // 2, axis=1)
        key_ref[rows] = (key * cos_ref[rows] + turned * sin_ref[rows]).astype(key_ref.dtype)


def rotate_keys(cosine, sine, terms, width):
    rows = cosine.shape[0]
    half = terms[0][0].shape[1]
    table = pl.BlockSpec((rows, DH), lambda j: (0, 0))

    def block(slot, start):
        return pl.BlockSpec((1, half, width), lambda j: (slot, 0, start // width))

    return pl.pallas_call(
        functools.partial(keys_kernel, len(terms)),
        grid=(1,),
        in_specs=[table, table] + [block(slot, start) for _, slot, start in terms],
        out_specs=table,
        out_shape=jax.ShapeDtypeStruct((rows, DH), jnp.bfloat16),
        compiler_params=pltpu.CompilerParams(vmem_limit_bytes=VMEM_BYTES),
        cost_estimate=LIGHT,
        name="rotate_keys",
    )(cosine, sine, *in_hbm([terms[0][0]]), *[term for term, _, _ in terms[1:]])


def sum_values_kernel(count, blocks, *refs):
    out_ref = refs[-1]
    total = refs[0][0].astype(jnp.float32)
    for ref in refs[1:count]:
        total = total + ref[0].astype(jnp.float32)
    if blocks == 1:
        out_ref[0] = total.astype(out_ref.dtype)
    for b in range(blocks if blocks > 1 else 0):
        half = total.shape[0]
        out_ref[0, b * half : (b + 1) * half] = total[:, b * DH : (b + 1) * DH].astype(out_ref.dtype)


def sum_values(pair, landed, final, after=()):
    slots, half, width = pair[0].shape
    width //= 2
    blocks = width // DH if final else 1
    shape = (slots, half * blocks, width // blocks)

    def block(bit):
        return pl.BlockSpec((1, half, width), lambda s: (s ^ bit, 0, 0))

    return pl.pallas_call(
        functools.partial(sum_values_kernel, 2 + len(landed), blocks),
        grid=(slots,),
        in_specs=[pl.BlockSpec((1, half, width), lambda s: (s, 0, 1))] * 2
        + [block(bit) for _, bit in landed]
        + [pl.BlockSpec(memory_space=pl.ANY)] * len(after),
        out_specs=pl.BlockSpec((1,) + shape[1:], lambda s: (s, 0, 0)),
        out_shape=pltpu.HBM(shape, jnp.bfloat16),
        compiler_params=pltpu.CompilerParams(vmem_limit_bytes=VMEM_BYTES),
        cost_estimate=LIGHT,
        name="sum_values",
    )(*in_hbm(pair[:1]), *pair[1:], *[array for array, _ in landed], *in_hbm(after))


def order_kernel(canary_ref, ids_ref, order_ref):
    order_ref[...] = jnp.where(canary_ref[...] == ids_ref[...], 1.0, 0.0).astype(order_ref.dtype)


def order_matrix(canary_rows, ids):
    rows = ids.shape[0]
    return pl.pallas_call(
        order_kernel,
        out_shape=jax.ShapeDtypeStruct((rows, rows), jnp.bfloat16),
        compiler_params=pltpu.CompilerParams(vmem_limit_bytes=VMEM_BYTES),
        name="order_matrix",
    )(canary_rows.reshape(rows, 1), ids.reshape(1, rows))


def ordered_keys_kernel(order_ref, own_ref, other_ref, key_t_ref):
    key = jnp.concatenate([own_ref[...], other_ref[...]], axis=0)
    keys = jnp.dot(order_ref[...], key, preferred_element_type=jnp.float32)
    key_t_ref[...] = keys.T.astype(key_t_ref.dtype)


def ordered_keys(order, own, other):
    return pl.pallas_call(
        ordered_keys_kernel,
        out_shape=jax.ShapeDtypeStruct((DH, order.shape[0]), jnp.bfloat16),
        compiler_params=pltpu.CompilerParams(vmem_limit_bytes=VMEM_BYTES),
        name="ordered_keys",
    )(order, own, other)


def value_kernel(place_ref, order_ref, own_ref, other_ref, out_ref):
    rows = jnp.concatenate([own_ref[0], other_ref[0]], axis=0)
    out_ref[...] = jnp.dot(order_ref[...], rows, preferred_element_type=jnp.float32).astype(out_ref.dtype)


def order_values(findex, order, own, other):
    rows = order.shape[0]
    slots, part, width = own.shape
    place = jnp.stack([findex ^ s for s in range(slots)]).astype(jnp.int32)
    block = pl.BlockSpec((1, part, width), lambda s, place: (place[s], 0, 0))
    return pl.pallas_call(
        value_kernel,
        grid_spec=pltpu.PrefetchScalarGridSpec(
            num_scalar_prefetch=1,
            grid=(slots,),
            in_specs=[pl.BlockSpec((rows, rows), lambda s, place: (0, 0)), block, block],
            out_specs=pl.BlockSpec((rows, width), lambda s, place: (0, s)),
        ),
        out_shape=jax.ShapeDtypeStruct((rows, slots * width), jnp.bfloat16),
        compiler_params=pltpu.CompilerParams(vmem_limit_bytes=VMEM_BYTES),
        name="order_values",
    )(place, order, own, other)


def score_kernel(count, order_ref, key_t_ref, *refs):
    queries, (out_ref, mark_ref) = refs[:count], refs[-2:]
    mark_ref[...] = jnp.zeros_like(mark_ref)
    stacked = jnp.concatenate([query[...] for query in queries], axis=0)
    chosen = jnp.dot(order_ref[...], stacked, preferred_element_type=jnp.float32).astype(jnp.bfloat16)
    for head in range(stacked.shape[1] // DH):
        products = jnp.dot(
            chosen[:, head * DH : (head + 1) * DH], key_t_ref[...], preferred_element_type=jnp.float32
        )
        out_ref[0, head] = (products * DH ** (-0.5)).astype(out_ref.dtype)


def score_heads(order, key_t, heads, start, count, queries, earlier, after=()):
    rows = order.shape[0]
    step = 2 if count % 2 == 0 else 1

    def block(query, first):
        return pl.BlockSpec((query.shape[0], step * DH), lambda j: (0, first // step + j))

    return pl.pallas_call(
        functools.partial(score_kernel, len(queries)),
        grid=(count // step,),
        in_specs=[
            pl.BlockSpec((rows, rows), lambda j: (0, 0)),
            pl.BlockSpec((DH, rows), lambda j: (0, 0)),
        ]
        + [block(query, first) for query, first in queries]
        + [pl.BlockSpec(memory_space=pl.ANY)] * (len(earlier) + len(after)),
        out_specs=[
            pl.BlockSpec((1, step, rows, rows), lambda j: (0, start // step + j, 0, 0)),
            pl.BlockSpec((8, DH), lambda j: (0, 0)),
        ],
        out_shape=[
            jax.ShapeDtypeStruct((1, heads, rows, rows), jnp.bfloat16),
            jax.ShapeDtypeStruct((8, DH), jnp.float32),
        ],
        input_output_aliases={2 + len(queries): 0} if earlier else {},
        compiler_params=pltpu.CompilerParams(vmem_limit_bytes=VMEM_BYTES),
        cost_estimate=LIGHT,
        name="score_heads",
    )(order, key_t, *[query for query, _ in queries], *earlier, *after)


def body(hidden, w_query, w_key, w_value, canary_rows, positions):
    shards = lax.axis_size("fsdp")
    findex = lax.axis_index("fsdp")
    tps = lax.axis_size("tp")
    tindex = lax.axis_index("tp")
    rindex = lax.axis_index("rep")
    local, depth = hidden.shape
    half = local // 2
    rows = local * tps
    head_cols = w_query.shape[1] // shards
    heads_here = head_cols // DH
    group = HQ // KV
    assert shards & (shards - 1) == 0 and lax.axis_size("rep") == 2

    def swap(x, bit):
        return lax.ppermute(x, "fsdp", [(i, i ^ bit) for i in range(shards)])

    def other_core(x):
        return lax.ppermute(x, "rep", [(0, 1), (1, 0)])

    def low(x):
        return x.astype(jnp.bfloat16)

    odd = list(range(3, shards, 2)) + [1]
    even = list(range(2, shards, 2))
    fast_pair = heads_here == group

    def spread(live):
        terms, first = [], None
        bit = 2
        while bit < shards:
            sent = [x for x in sorted(live) if x & bit]
            pack = jnp.stack([low(live[x]) for x in sent])
            first = pack if first is None else first
            landed = swap(pack, bit)
            for k, x in enumerate(sent):
                if x == bit:
                    terms.append(landed)
                else:
                    live[x ^ bit] = live[x ^ bit] + landed[k].astype(jnp.float32)
                del live[x]
            bit *= 2
        return terms, first

    blocks = [hidden] + [
        lax.ppermute(hidden, "tp", [(i, (i - b) % tps) for i in range(tps)]) for b in range(1, tps)
    ]

    block_ids = ((tindex + jnp.arange(tps, dtype=jnp.int32)) % tps * local)[:, None]
    own_ids = (block_ids + rindex * half + jnp.arange(half, dtype=jnp.int32)[None]).reshape(-1)
    other_ids = (block_ids + (1 - rindex) * half + jnp.arange(half, dtype=jnp.int32)[None]).reshape(-1)
    ids = jnp.concatenate([own_ids, other_ids])
    own_positions = jnp.sum(
        jnp.where(own_ids[:, None] == canary_rows[None, :], positions[None, :], 0), axis=1
    )
    cosine, sine = rope_tables(own_positions)

    tile = min(1024, head_cols)

    def project(slots, blocks, width, after=(), cost=LIGHT, by_slot=False):
        keep, gives = project_query(
            rindex, findex, slots, blocks, w_query, head_cols, tile, width, after, cost, by_slot
        )
        return keep, [other_core(give) for give in gives], gives[0]

    def rotate(b, p, split, terms, behind):
        cols = head_cols // split
        table = slice(b * half, (b + 1) * half)
        keep, slot, got = owns[b]
        added = [(keep, slot, 0, p * cols)] + terms
        gots = (0, 0, p, got) if len(got) == 1 else (0, 0, 0, got[p : p + 1])
        turned = sum_and_rotate(cosine[table], sine[table], added, gots, cols, behind)
        return turned, other_core(turned)

    def add_even(b, start, cols, pair, behind):
        if shards == 2:
            return [], behind
        keep, got = evens[b]
        each = len(got) * cols // head_cols
        got = got[start // cols * each :][:each]
        summed = add_rows(
            0, len(even), half, 0, keep, got, start, cols, pair, 2, (fars[b],), behind
        )
        terms, first = spread({x: summed[k] for k, x in enumerate(even)})
        return [(term, 0, 0, 0) for term in terms], (first,)

    last, split = tps - 1, head_cols // tile
    placed = in_hbm(blocks[:1]) + blocks[1:]
    evens, owns, fars, terms, pair, after = [], [], [], [], (), ()
    for b, block in enumerate(placed):
        if fast_pair and b == last:
            slots = list(range(shards))
            pair_keep, give = project_pair(rindex, findex, slots, placed, w_key, w_value, after)
            pair = (pair_keep, other_core(give))
            after = (give,)
        odd_keep, odd_got, given = project(odd, [block], tile, after)
        count = len(odd) - 1 if b == last else len(odd)
        odd_sent = add_rows(0, count, half, 0, odd_keep, odd_got, 0, head_cols, pair, 3)
        fars.append(swap(odd_sent, 1))
        after = (odd_sent,)
        if fast_pair and b == last:
            value_sums = [(swap(sum_values(pair, [], False, after), 1), 1)]
        if b > 0:
            added, after = add_even(b - 1, 0, head_cols, (), after)
            terms.append([(fars[b - 1], len(odd) - 1, 0, 0)] + added)
            after = (odd_sent,) + after
        if b < last:
            keep, got, given = project(even + [0], [block], head_cols, after, LIGHT, True)
            evens.append((keep, got[:1] if len(even) == 1 else [jnp.concatenate(got[:-1])]))
            owns.append((keep, len(even), got[-1:]))
        else:
            keep, got, given = project(even, [block], tile, after, HEAVY)
            evens.append((keep, got))
        after = (given,)
    if fast_pair:
        bit = 2
        while bit < shards:
            value_sums.append((swap(sum_values(pair, value_sums, False, after), bit), bit))
            bit *= 2
    parts, behind = [], tuple(term[0] for row in terms for term in row[1:])
    for p in range(split):
        near_sent = add_rows(
            len(odd) - 1, 1, half, 0, odd_keep, odd_got[p : p + 1], p * tile, tile,
            pair if p == 0 else (), 1, (), after,
        )
        parts.append([(swap(near_sent, 1), 0, 0, 0)])
        after = (near_sent,)
    after = after + behind
    for p in range(split):
        added, after = add_even(last, p * tile, tile, pair if p == 0 else (), after)
        parts[p] += added
    if fast_pair:
        held = sum_values(pair, value_sums, True, after)
        after = after + (held,)
    keep, got, _ = project([0], placed[last:], tile, after, HEAVY)
    owns.append((keep, 0, got))

    if fast_pair:
        pieces = [(array, 0, 0) for array in pair]
        pieces += [(term, 0, tile) for term, _, _, _ in parts[0]]
        key_rot = rotate_keys(cosine, sine, pieces, DH * tps)
    else:
        x = jnp.concatenate(blocks, axis=0)
        key_sum, value_sum = lax.psum(
            (
                jnp.dot(x, w_key, preferred_element_type=jnp.float32),
                jnp.dot(x, w_value, preferred_element_type=jnp.float32),
            ),
            ("fsdp", "rep"),
        )

        def of_core(y, core):
            parts = y.reshape(tps, 2, half, -1)
            return lax.dynamic_index_in_dim(parts, core, 1, keepdims=False).reshape(tps * half, -1)

        mine = lax.dynamic_slice_in_dim(key_sum, findex * heads_here // group * DH, DH, 1)
        key_own = of_core(mine, rindex)
        key_rot = sum_and_rotate(cosine, sine, [(key_own[None], 0, 0, 0)], (0, 0, 0, []), DH, after)
        value_rows = low(jnp.concatenate([of_core(value_sum, rindex), of_core(value_sum, 1 - rindex)]))

    order = order_matrix(canary_rows, ids)
    key_t = ordered_keys(order, key_rot, other_core(key_rot))
    if fast_pair:
        values = order_values(findex, order, held, other_core(held))
    else:
        values = low(jnp.dot(order, value_rows, preferred_element_type=jnp.float32))

    rotated = [rotate(b, 0, 1, terms[b], after) for b in range(last)]
    count = heads_here // split
    scores, mark = (), ()
    for p in range(split):
        turned = rotate(last, p, split, parts[p], mark or tuple(owns[last][2][1:]) + tuple(in_hbm([values])))
        queries = [(row[0], p * count) for row in rotated] + [(turned[0], 0)]
        queries += [(row[1], p * count) for row in rotated] + [(turned[1], 0)]
        *scores, mark = score_heads(
            order, key_t, heads_here, p * count, count, queries, scores
        )
        mark = (mark,)
    return (scores[0], values)


def solution(mesh):
    in_specs = (
        P(("groups", "tp"), ("fsdp", "rep")),
        P(("fsdp", "rep"), "tp"),
        P(("fsdp", "rep"), "tp"),
        P(("fsdp", "rep"), "tp"),
        P("groups"),
        P("groups"),
    )
    out_specs = (P("tp", "fsdp", "groups", None), P("groups", "tp"))
    return jax.shard_map(body, mesh=mesh, in_specs=in_specs, out_specs=out_specs, check_vma=False)
```

```python
import functools
import math

import jax
import jax.numpy as jnp
from jax import lax
from jax.experimental import pallas as pl
from jax.experimental.pallas import tpu as pltpu
from jax.sharding import PartitionSpec as P

HQ = 128
KV = 8
DH = 128
VMEM_BYTES = 28 * 1024 * 1024
LIGHT = pl.CostEstimate(flops=1000, bytes_accessed=1000, transcendentals=0)
HEAVY = pl.CostEstimate(flops=10**11, bytes_accessed=10**8, transcendentals=0)


def in_hbm(arrays):
    return [pltpu.with_memory_space_constraint(x, pltpu.HBM) for x in arrays]


def rope_tables(positions):
    half = DH // 2
    expo = jnp.arange(half, dtype=jnp.float32) * (2.0 / DH)
    freq = jnp.power(jnp.float32(500000.0), -expo)
    wavelen = 2.0 * math.pi / freq
    smooth = (8192.0 / wavelen - 1.0) / 3.0
    mixed = (1.0 - smooth) * freq / 8.0 + smooth * freq
    freq = jnp.where(wavelen > 8192.0, freq / 8.0, jnp.where(wavelen < 2048.0, freq, mixed))
    angle = positions.astype(jnp.float32)[:, None] * freq[None, :]
    cosine, sine = jnp.cos(angle), jnp.sin(angle)
    return jnp.concatenate([cosine, cosine], axis=1), jnp.concatenate([-sine, sine], axis=1)


def ordered_rows(place_ref, x_refs, rows_ref):
    core = place_ref[0]
    half = x_refs[0].shape[0] // 2
    for b, x_ref in enumerate(x_refs):
        kept, given = b * half, (len(x_refs) + b) * half
        rows_ref[kept : kept + half] = x_ref[pl.ds(pl.multiple_of(core * half, 16), half)]
        rows_ref[given : given + half] = x_ref[pl.ds(pl.multiple_of((1 - core) * half, 16), half)]


def query_kernel(count, pieces, by_slot, place_ref, *refs):
    x_refs, w_ref = refs[:count], refs[count]
    keep_ref, *give_refs, rows_ref = refs[-2 - pieces :]
    tile = pl.program_id(1)
    size = give_refs[0].shape[2]
    each = keep_ref.shape[2] // size

    @pl.when((pl.program_id(0) == 0) & (tile == 0))
    def _():
        ordered_rows(place_ref, x_refs, rows_ref)

    result = jnp.dot(rows_ref[...], w_ref[...], preferred_element_type=jnp.float32)
    half = result.shape[0] // 2
    keep_ref[0] = result[:half]
    for j, give_ref in enumerate(give_refs):

        @pl.when(pl.program_id(0) == j if by_slot else (tile == j // each) | (pieces == 1))
        def _():
            start = j % each * size
            give_ref[0] = result[half:, start : start + size].astype(give_ref.dtype)


def project_query(rindex, findex, slots, blocks, w, cols, tile, width, after, cost, by_slot):
    rows, depth = blocks[0].shape
    count = len(blocks)
    half = rows // 2 * count
    tiles, pieces = cols // tile, len(slots) if by_slot else cols // width
    place = jnp.stack([rindex] + [findex ^ slot for slot in slots]).astype(jnp.int32)
    keep_spec = pl.BlockSpec((1, half, tile), lambda s, j, place: (s, 0, j))
    give_spec = pl.BlockSpec((1, half, width), lambda s, j, place: (s, 0, 0))

    def slot_spec(k):
        def index(s, j, place):
            return (0, 0, jnp.where(s < k, 0, jnp.where(s > k, tiles - 1, j)))

        return pl.BlockSpec((1, half, tile), index)

    give_specs = [keep_spec] if pieces == 1 else [give_spec] * pieces
    given = (len(slots), half, width)
    if by_slot:
        give_specs, given = [slot_spec(k) for k in range(pieces)], (1, half, cols)
    x_spec = pl.BlockSpec((rows, depth), lambda s, j, place: (0, 0), pipeline_mode=pl.Buffered(1))
    outs = pl.pallas_call(
        functools.partial(query_kernel, count, pieces, by_slot),
        grid_spec=pltpu.PrefetchScalarGridSpec(
            num_scalar_prefetch=1,
            grid=(len(slots), tiles),
            in_specs=[x_spec] * count
            + [pl.BlockSpec((depth, tile), lambda s, j, place: (0, place[1 + s] * tiles + j))]
            + [pl.BlockSpec(memory_space=pl.ANY)] * len(after),
            out_specs=[keep_spec] + give_specs,
            scratch_shapes=[pltpu.VMEM((2 * half, depth), w.dtype)],
        ),
        out_shape=[pltpu.HBM((len(slots), half, cols), jnp.float32)]
        + [pltpu.HBM(given, jnp.bfloat16)] * pieces,
        compiler_params=pltpu.CompilerParams(vmem_limit_bytes=VMEM_BYTES),
        cost_estimate=cost,
        name="query_products",
    )(place, *blocks, *in_hbm([w]), *in_hbm(after[:1]), *after[1:])
    return outs[0], outs[1:]


def pair_kernel(count, place_ref, *refs):
    x_refs, (wk_ref, wv_ref) = refs[:count], refs[count : count + 2]
    keep_ref, give_ref, rows_ref = refs[-3:]

    @pl.when(pl.program_id(0) == 0)
    def _():
        ordered_rows(place_ref, x_refs, rows_ref)

    weights = jnp.concatenate([wk_ref[...], wv_ref[...]], axis=1)
    result = jnp.dot(rows_ref[...], weights, preferred_element_type=jnp.float32)
    half, width = x_refs[0].shape[0] // 2, weights.shape[1]
    for b in range(count):
        kept, given = b * half, (count + b) * half
        cols = slice(b * width, (b + 1) * width)
        keep_ref[0, :, cols] = result[kept : kept + half]
        give_ref[0, :, cols] = result[given : given + half].astype(give_ref.dtype)


def project_pair(rindex, findex, slots, blocks, w_key, w_value, after=()):
    rows, depth = blocks[0].shape
    count = len(blocks)
    place = jnp.stack([rindex] + [findex ^ slot for slot in slots]).astype(jnp.int32)
    weight = pl.BlockSpec((depth, DH), lambda s, place: (0, place[1 + s]))
    shape = (len(slots), rows // 2, 2 * DH * count)
    out = pl.BlockSpec((1,) + shape[1:], lambda s, place: (s, 0, 0))
    return pl.pallas_call(
        functools.partial(pair_kernel, count),
        grid_spec=pltpu.PrefetchScalarGridSpec(
            num_scalar_prefetch=1,
            grid=(len(slots),),
            in_specs=[pl.BlockSpec((rows, depth), lambda s, place: (0, 0))] * count
            + [weight, weight]
            + [pl.BlockSpec(memory_space=pl.ANY)] * len(after),
            out_specs=[out, out],
            scratch_shapes=[pltpu.VMEM((count * rows, depth), blocks[0].dtype)],
        ),
        out_shape=[
            pltpu.HBM(shape, jnp.float32),
            pltpu.HBM(shape, jnp.bfloat16),
        ],
        compiler_params=pltpu.CompilerParams(vmem_limit_bytes=VMEM_BYTES),
        cost_estimate=LIGHT,
        name="key_value_products",
    )(place, *blocks, *in_hbm([w_key, w_value, *after]))


def add_kernel(gots, paired, extra, *refs):
    keep_ref, got_refs, out_ref = refs[0], refs[1 : 1 + gots], refs[-1]
    pair_refs = refs[1 + gots : 1 + gots + 2 * paired]
    landed_refs = refs[1 + gots + 2 * paired :][: extra * (1 + paired)]
    width = got_refs[0].shape[2]
    cols = gots * width

    def total(first, second, landed):
        value = first + second.astype(jnp.float32)
        for term in landed:
            value = value + term.astype(jnp.float32)
        return value.astype(out_ref.dtype)

    for t, got_ref in enumerate(got_refs):
        part = slice(t * width, (t + 1) * width)
        landed = [landed_refs[0][0, :, part]] if extra else []
        out_ref[0, :, part] = total(keep_ref[0, :, part], got_ref[0], landed)
    if paired:
        landed = [landed_refs[1][0]] if extra else []
        out_ref[0, :, cols:] = total(pair_refs[0][0], pair_refs[1][0], landed)


def add_rows(first, count, rows, b, keep, gots, start, cols, pair=(), slot=0, landed=(), after=()):
    whole = keep.shape[2]
    width = cols // len(gots)
    shift = start // cols if gots[0].shape[2] == whole else 0
    more = pair[0].shape[2] if pair else 0
    keep_spec = pl.BlockSpec((1, rows, cols), lambda s: (first + s, b, start // cols))
    got_spec = pl.BlockSpec((1, rows, width), lambda s: (first + s, b, shift))
    pair_spec = pl.BlockSpec((1, rows, more), lambda s: (slot + s, 0, 0))
    landed_specs = [pl.BlockSpec((1, rows, cols), lambda s: (s, 0, start // cols))]
    if pair:
        landed_specs.append(pl.BlockSpec((1, rows, more), lambda s: (s, 0, whole // more)))
    landed_specs = landed_specs * len(landed)
    return pl.pallas_call(
        functools.partial(add_kernel, len(gots), len(pair) // 2, len(landed)),
        grid=(count,),
        in_specs=[keep_spec]
        + [got_spec] * len(gots)
        + [pair_spec] * len(pair)
        + landed_specs
        + [pl.BlockSpec(memory_space=pl.ANY)] * len(after),
        out_specs=pl.BlockSpec((1, rows, cols + more), lambda s: (s, 0, 0)),
        out_shape=pltpu.HBM((count, rows, cols + more), jnp.bfloat16),
        compiler_params=pltpu.CompilerParams(vmem_limit_bytes=VMEM_BYTES),
        cost_estimate=LIGHT,
        name="add_rows",
    )(
        *in_hbm([keep]),
        *gots,
        *in_hbm(pair[:1]),
        *pair[1:],
        *(list(landed) * (2 if pair else 1)),
        *in_hbm(after[:1]),
        *after[1:],
    )


def rotate_kernel(count, pieces, cos_ref, sin_ref, *refs):
    terms, gots, out_ref = refs[:count], refs[count : count + pieces], refs[-1]
    total = terms[0][0].astype(jnp.float32)
    for term in terms[1:]:
        total = total + term[0].astype(jnp.float32)
    cosine, sine = cos_ref[...], sin_ref[...]

    def write(total):
        for head in range(total.shape[1] // DH):
            part = total[:, head * DH : (head + 1) * DH]
            turned = pltpu.roll(part, DH // 2, axis=1)
            value = part * cosine + turned * sine
            out_ref[:, head * DH : (head + 1) * DH] = value.astype(out_ref.dtype)

    if not gots:
        write(total)
    for j, got in enumerate(gots):

        @pl.when(pl.program_id(0) == j)
        def _():
            write(total + got[0].astype(jnp.float32))


def sum_and_rotate(cosine, sine, terms, gots, cols, after=()):
    rows = cosine.shape[0]
    slot_of_gots, block_of_gots, shift, gots = gots
    tile = cols // max(1, len(gots))
    table = pl.BlockSpec((rows, DH), lambda j: (0, 0))

    def block(slot, b, start):
        return pl.BlockSpec((1, rows, tile), lambda j: (slot, b, start // tile + j))

    return pl.pallas_call(
        functools.partial(rotate_kernel, len(terms), len(gots)),
        grid=(cols // tile,),
        in_specs=[table, table]
        + [block(slot, b, start) for _, slot, b, start in terms]
        + [pl.BlockSpec((1, rows, tile), lambda j: (slot_of_gots, block_of_gots, shift))] * len(gots)
        + [pl.BlockSpec(memory_space=pl.ANY)] * len(after),
        out_specs=pl.BlockSpec((rows, tile), lambda j: (0, j)),
        out_shape=jax.ShapeDtypeStruct((rows, cols), jnp.bfloat16),
        compiler_params=pltpu.CompilerParams(vmem_limit_bytes=VMEM_BYTES),
        cost_estimate=LIGHT,
        name="sum_and_rotate",
    )(cosine, sine, *in_hbm([terms[0][0]]), *[term[0] for term in terms[1:]], *gots, *after)


def split_kernel(count, cos_ref, sin_ref, *refs):
    terms, (key_ref, value_ref) = refs[:count], refs[-2:]
    total = terms[0][0].astype(jnp.float32)
    for term in terms[1:]:
        total = total + term[0].astype(jnp.float32)
    half = total.shape[0]
    for b in range(total.shape[1] // (2 * DH)):
        rows = slice(b * half, (b + 1) * half)
        key = total[:, 2 * b * DH : (2 * b + 1) * DH]
        turned = pltpu.roll(key, DH // 2, axis=1)
        key_ref[rows] = (key * cos_ref[rows] + turned * sin_ref[rows]).astype(key_ref.dtype)
        value_ref[0, rows] = total[:, (2 * b + 1) * DH : (2 * b + 2) * DH].astype(value_ref.dtype)


def split_and_rotate(cosine, sine, terms, width, after):
    rows = cosine.shape[0]
    half = terms[0][0].shape[1]
    table = pl.BlockSpec((rows, DH), lambda j: (0, 0))

    def block(slot, start):
        return pl.BlockSpec((1, half, width), lambda j: (slot, 0, start // width))

    return pl.pallas_call(
        functools.partial(split_kernel, len(terms)),
        grid=(1,),
        in_specs=[table, table]
        + [block(slot, start) for _, slot, start in terms]
        + [pl.BlockSpec(memory_space=pl.ANY)] * len(after),
        out_specs=[table, pl.BlockSpec((1, rows, DH), lambda j: (0, 0, 0))],
        out_shape=[
            jax.ShapeDtypeStruct((rows, DH), jnp.bfloat16),
            jax.ShapeDtypeStruct((1, rows, DH), jnp.bfloat16),
        ],
        compiler_params=pltpu.CompilerParams(vmem_limit_bytes=VMEM_BYTES),
        cost_estimate=LIGHT,
        name="split_and_rotate",
    )(cosine, sine, *in_hbm([terms[0][0]]), *[term for term, _, _ in terms[1:]], *after)


def prepare_kernel(canary_ref, ids_ref, own_ref, other_ref, order_ref, key_t_ref):
    order = jnp.where(canary_ref[...] == ids_ref[...], 1.0, 0.0).astype(jnp.bfloat16)
    order_ref[...] = order
    key = jnp.concatenate([own_ref[...], other_ref[...]], axis=0)
    key_t_ref[...] = jnp.dot(order, key, preferred_element_type=jnp.float32).T.astype(jnp.bfloat16)


def prepare(canary_rows, ids, own, other):
    rows = ids.shape[0]
    return pl.pallas_call(
        prepare_kernel,
        out_shape=[
            jax.ShapeDtypeStruct((rows, rows), jnp.bfloat16),
            jax.ShapeDtypeStruct((DH, rows), jnp.bfloat16),
        ],
        compiler_params=pltpu.CompilerParams(vmem_limit_bytes=VMEM_BYTES),
        name="order_and_keys",
    )(canary_rows.reshape(rows, 1), ids.reshape(1, rows), own, other)


def stack_kernel(count, *refs):
    out_ref, start = refs[-1], 0
    for ref in refs[:count]:
        out_ref[start : start + ref.shape[0]] = ref[...]
        start += ref.shape[0]


def stack_slots(arrays, after):
    slots = sum(x.shape[0] for x in arrays)
    shape = (slots,) + arrays[0].shape[1:]
    return pl.pallas_call(
        functools.partial(stack_kernel, len(arrays)),
        grid=(1,),
        in_specs=[pl.BlockSpec(x.shape, lambda j: (0, 0, 0)) for x in arrays]
        + [pl.BlockSpec(memory_space=pl.ANY)] * len(after),
        out_specs=pl.BlockSpec(shape, lambda j: (0, 0, 0)),
        out_shape=jax.ShapeDtypeStruct(shape, arrays[0].dtype),
        compiler_params=pltpu.CompilerParams(vmem_limit_bytes=VMEM_BYTES),
        cost_estimate=LIGHT,
        name="stack_slots",
    )(*arrays, *after)


def value_kernel(place_ref, order_ref, own_ref, other_ref, out_ref):
    rows = jnp.concatenate([own_ref[0], other_ref[0]], axis=0)
    out_ref[...] = jnp.dot(order_ref[...], rows, preferred_element_type=jnp.float32).astype(out_ref.dtype)


def order_values(findex, order, own, other):
    rows = order.shape[0]
    slots, part, width = own.shape
    place = jnp.stack([findex ^ s for s in range(slots)]).astype(jnp.int32)
    block = pl.BlockSpec((1, part, width), lambda s, place: (place[s], 0, 0))
    return pl.pallas_call(
        value_kernel,
        grid_spec=pltpu.PrefetchScalarGridSpec(
            num_scalar_prefetch=1,
            grid=(slots,),
            in_specs=[pl.BlockSpec((rows, rows), lambda s, place: (0, 0)), block, block],
            out_specs=pl.BlockSpec((rows, width), lambda s, place: (0, s)),
        ),
        out_shape=jax.ShapeDtypeStruct((rows, slots * width), jnp.bfloat16),
        compiler_params=pltpu.CompilerParams(vmem_limit_bytes=VMEM_BYTES),
        name="order_values",
    )(place, order, own, other)


def score_kernel(count, order_ref, key_t_ref, *refs):
    queries, (out_ref, mark_ref) = refs[:count], refs[-2:]
    mark_ref[...] = jnp.zeros_like(mark_ref)
    stacked = jnp.concatenate([query[...] for query in queries], axis=0)
    chosen = jnp.dot(order_ref[...], stacked, preferred_element_type=jnp.float32).astype(jnp.bfloat16)
    for head in range(stacked.shape[1] // DH):
        products = jnp.dot(
            chosen[:, head * DH : (head + 1) * DH], key_t_ref[...], preferred_element_type=jnp.float32
        )
        out_ref[0, head] = (products * DH ** (-0.5)).astype(out_ref.dtype)


def score_heads(order, key_t, heads, start, count, queries, earlier, after=()):
    rows = order.shape[0]
    step = math.gcd(count, 4)

    def block(query, first):
        return pl.BlockSpec((query.shape[0], step * DH), lambda j: (0, first // step + j))

    return pl.pallas_call(
        functools.partial(score_kernel, len(queries)),
        grid=(count // step,),
        in_specs=[
            pl.BlockSpec((rows, rows), lambda j: (0, 0)),
            pl.BlockSpec((DH, rows), lambda j: (0, 0)),
        ]
        + [block(query, first) for query, first in queries]
        + [pl.BlockSpec(memory_space=pl.ANY)] * (len(earlier) + len(after)),
        out_specs=[
            pl.BlockSpec((1, step, rows, rows), lambda j: (0, start // step + j, 0, 0)),
            pl.BlockSpec((8, DH), lambda j: (0, 0)),
        ],
        out_shape=[
            jax.ShapeDtypeStruct((1, heads, rows, rows), jnp.bfloat16),
            jax.ShapeDtypeStruct((8, DH), jnp.float32),
        ],
        input_output_aliases={2 + len(queries): 0} if earlier else {},
        compiler_params=pltpu.CompilerParams(vmem_limit_bytes=VMEM_BYTES),
        cost_estimate=LIGHT,
        name="score_heads",
    )(order, key_t, *[query for query, _ in queries], *earlier, *after)


def body(hidden, w_query, w_key, w_value, canary_rows, positions):
    shards = lax.axis_size("fsdp")
    findex = lax.axis_index("fsdp")
    tps = lax.axis_size("tp")
    tindex = lax.axis_index("tp")
    rindex = lax.axis_index("rep")
    local, depth = hidden.shape
    half = local // 2
    rows = local * tps
    head_cols = w_query.shape[1] // shards
    heads_here = head_cols // DH
    group = HQ // KV
    assert shards & (shards - 1) == 0 and lax.axis_size("rep") == 2

    def swap(x, bit):
        return lax.ppermute(x, "fsdp", [(i, i ^ bit) for i in range(shards)])

    def other_core(x):
        return lax.ppermute(x, "rep", [(0, 1), (1, 0)])

    def low(x):
        return x.astype(jnp.bfloat16)

    odd = list(range(3, shards, 2)) + [1]
    even = list(range(2, shards, 2))
    fast_pair = heads_here == group

    def spread(live):
        terms, first = [], None
        bit = 2
        while bit < shards:
            sent = [x for x in sorted(live) if x & bit]
            pack = jnp.stack([low(live[x]) for x in sent])
            first = pack if first is None else first
            landed = swap(pack, bit)
            for k, x in enumerate(sent):
                if x == bit:
                    terms.append(landed)
                else:
                    live[x ^ bit] = live[x ^ bit] + landed[k].astype(jnp.float32)
                del live[x]
            bit *= 2
        return terms, first

    blocks = [hidden] + [
        lax.ppermute(hidden, "tp", [(i, (i - b) % tps) for i in range(tps)]) for b in range(1, tps)
    ]

    block_ids = ((tindex + jnp.arange(tps, dtype=jnp.int32)) % tps * local)[:, None]
    own_ids = (block_ids + rindex * half + jnp.arange(half, dtype=jnp.int32)[None]).reshape(-1)
    other_ids = (block_ids + (1 - rindex) * half + jnp.arange(half, dtype=jnp.int32)[None]).reshape(-1)
    ids = jnp.concatenate([own_ids, other_ids])
    own_positions = jnp.sum(
        jnp.where(own_ids[:, None] == canary_rows[None, :], positions[None, :], 0), axis=1
    )
    cosine, sine = rope_tables(own_positions)

    tile = min(1024, head_cols)

    def project(slots, blocks, width, after=(), cost=LIGHT, by_slot=False):
        keep, gives = project_query(
            rindex, findex, slots, blocks, w_query, head_cols, tile, width, after, cost, by_slot
        )
        return keep, [other_core(give) for give in gives], gives[0]

    def rotate(b, p, split, terms, behind):
        cols = head_cols // split
        table = slice(b * half, (b + 1) * half)
        keep, slot, got = owns[b]
        added = [(keep, slot, 0, p * cols)] + terms
        gots = (0, 0, p, got) if len(got) == 1 else (0, 0, 0, got[p : p + 1])
        turned = sum_and_rotate(cosine[table], sine[table], added, gots, cols, behind)
        return turned, other_core(turned)

    def add_even(b, start, cols, pair, behind):
        if shards == 2:
            return [], behind
        keep, got = evens[b]
        each = len(got) * cols // head_cols
        got = got[start // cols * each :][:each]
        summed = add_rows(
            0, len(even), half, 0, keep, got, start, cols, pair, len(odd), (fars[b],), behind
        )
        terms, first = spread({x: summed[k] for k, x in enumerate(even)})
        return [(term, 0, 0, 0) for term in terms], (first,)

    last, split = tps - 1, head_cols // tile
    placed = in_hbm(blocks[:1]) + blocks[1:]
    evens, owns, fars, terms, pair, after = [], [], [], [], (), ()
    for b, block in enumerate(placed):
        if fast_pair and b == last:
            slots = odd + even + [0]
            pair_keep, give = project_pair(rindex, findex, slots, placed, w_key, w_value, after)
            pair = (pair_keep, other_core(give))
            after = (give,)
        sent = odd[:-1] if b == last else odd
        odd_keep, odd_got, given = project(sent, [block], tile, after)
        odd_sent = add_rows(0, len(sent), half, 0, odd_keep, odd_got, 0, head_cols, pair)
        fars.append(swap(odd_sent, 1))
        after = (odd_sent,)
        if b > 0:
            added, after = add_even(b - 1, 0, head_cols, (), after)
            terms.append([(fars[b - 1], len(odd) - 1, 0, 0)] + added)
            after = (odd_sent,) + after
        if b < last:
            keep, got, given = project(even + [0], [block], head_cols, after, LIGHT, True)
            evens.append((keep, got[:1] if len(even) == 1 else [jnp.concatenate(got[:-1])]))
            owns.append((keep, len(even), got[-1:]))
        else:
            keep, got, given = project(even, [block], tile, after, HEAVY)
            evens.append((keep, got))
        after = (given,)
    near_keep, near_got, given = project([1], placed[last:], tile, after)
    after = (given,)
    parts, behind = [], tuple(term[0] for row in terms for term in row[1:])
    for p in range(split):
        near_sent = add_rows(
            0, 1, half, 0, near_keep, near_got[p : p + 1], p * tile, tile,
            pair if p == 0 else (), len(odd) - 1, (), after,
        )
        parts.append([(swap(near_sent, 1), 0, 0, 0)])
        after = (near_sent,)
    after = after + behind
    for p in range(split):
        added, after = add_even(last, p * tile, tile, pair if p == 0 else (), after)
        parts[p] += added
    keep, got, _ = project([0], placed[last:], tile, after, HEAVY)
    owns.append((keep, 0, got))

    if fast_pair:
        width = 2 * DH * tps
        pieces = [(array, shards - 1, 0) for array in pair]
        pieces += [(term, 0, tile) for term, _, _, _ in parts[0]]
        key_rot, held = split_and_rotate(cosine, sine, pieces, width, after)
    else:
        x = jnp.concatenate(blocks, axis=0)
        key_sum, value_sum = lax.psum(
            (
                jnp.dot(x, w_key, preferred_element_type=jnp.float32),
                jnp.dot(x, w_value, preferred_element_type=jnp.float32),
            ),
            ("fsdp", "rep"),
        )

        def of_core(y, core):
            parts = y.reshape(tps, 2, half, -1)
            return lax.dynamic_index_in_dim(parts, core, 1, keepdims=False).reshape(tps * half, -1)

        mine = lax.dynamic_slice_in_dim(key_sum, findex * heads_here // group * DH, DH, 1)
        key_own = of_core(mine, rindex)
        key_rot = sum_and_rotate(cosine, sine, [(key_own[None], 0, 0, 0)], (0, 0, 0, []), DH, after)
        value_rows = low(jnp.concatenate([of_core(value_sum, rindex), of_core(value_sum, 1 - rindex)]))

    order, key_t = prepare(canary_rows, ids, key_rot, other_core(key_rot))
    if not fast_pair:
        values = low(jnp.dot(order, value_rows, preferred_element_type=jnp.float32))

    rotated = [rotate(b, 0, 1, terms[b], after) for b in range(last)]
    count = heads_here // split
    scores, mark = (), ()
    for p in range(split):
        turned = rotate(last, p, split, parts[p], mark or tuple(owns[last][2][1:]))
        queries = [(row[0], p * count) for row in rotated] + [(turned[0], 0)]
        queries += [(row[1], p * count) for row in rotated] + [(turned[1], 0)]
        behind = in_hbm([values]) if p == split - 1 and p > 0 else ()
        *scores, mark = score_heads(
            order, key_t, heads_here, p * count, count, queries, scores, behind
        )
        mark = (mark,)
        if fast_pair and p == 0:
            held = stack_slots([held] + [swap(held, x) for x in range(1, shards)], mark)
            values = order_values(findex, order, held, other_core(held))
    return (scores[0], values)


def solution(mesh):
    in_specs = (
        P(("groups", "tp"), ("fsdp", "rep")),
        P(("fsdp", "rep"), "tp"),
        P(("fsdp", "rep"), "tp"),
        P(("fsdp", "rep"), "tp"),
        P("groups"),
        P("groups"),
    )
    out_specs = (P("tp", "fsdp", "groups", None), P("groups", "tp"))
    return jax.shard_map(body, mesh=mesh, in_specs=in_specs, out_specs=out_specs, check_vma=False)
```

```python
import functools
import math

import jax
import jax.numpy as jnp
from jax import lax
from jax.experimental import pallas as pl
from jax.experimental.pallas import tpu as pltpu
from jax.sharding import PartitionSpec as P

HQ = 128
KV = 8
DH = 128
VMEM_BYTES = 28 * 1024 * 1024
LIGHT = pl.CostEstimate(flops=1000, bytes_accessed=1000, transcendentals=0)
HEAVY = pl.CostEstimate(flops=10**11, bytes_accessed=10**8, transcendentals=0)


def in_hbm(arrays):
    return [pltpu.with_memory_space_constraint(x, pltpu.HBM) for x in arrays]


def rope_tables(positions):
    half = DH // 2
    expo = jnp.arange(half, dtype=jnp.float32) * (2.0 / DH)
    freq = jnp.power(jnp.float32(500000.0), -expo)
    wavelen = 2.0 * math.pi / freq
    smooth = (8192.0 / wavelen - 1.0) / 3.0
    mixed = (1.0 - smooth) * freq / 8.0 + smooth * freq
    freq = jnp.where(wavelen > 8192.0, freq / 8.0, jnp.where(wavelen < 2048.0, freq, mixed))
    angle = positions.astype(jnp.float32)[:, None] * freq[None, :]
    cosine, sine = jnp.cos(angle), jnp.sin(angle)
    return jnp.concatenate([cosine, cosine], axis=1), jnp.concatenate([-sine, sine], axis=1)


def ordered_rows(place_ref, x_refs, rows_ref):
    core = place_ref[0]
    half = x_refs[0].shape[0] // 2
    for b, x_ref in enumerate(x_refs):
        kept, given = b * half, (len(x_refs) + b) * half
        rows_ref[kept : kept + half] = x_ref[pl.ds(pl.multiple_of(core * half, 16), half)]
        rows_ref[given : given + half] = x_ref[pl.ds(pl.multiple_of((1 - core) * half, 16), half)]


def query_kernel(count, pieces, by_slot, place_ref, *refs):
    x_refs, w_ref = refs[:count], refs[count]
    keep_ref, *give_refs, rows_ref = refs[-2 - pieces :]
    tile = pl.program_id(1)
    size = give_refs[0].shape[2]
    each = keep_ref.shape[2] // size

    @pl.when((pl.program_id(0) == 0) & (tile == 0))
    def _():
        ordered_rows(place_ref, x_refs, rows_ref)

    result = jnp.dot(rows_ref[...], w_ref[...], preferred_element_type=jnp.float32)
    half = result.shape[0] // 2
    keep_ref[0] = result[:half]
    for j, give_ref in enumerate(give_refs):

        @pl.when(pl.program_id(0) == j if by_slot else (tile == j // each) | (pieces == 1))
        def _():
            start = j % each * size
            give_ref[0] = result[half:, start : start + size].astype(give_ref.dtype)


def project_query(rindex, findex, slots, blocks, w, cols, tile, width, after, cost, by_slot):
    rows, depth = blocks[0].shape
    count = len(blocks)
    half = rows // 2 * count
    tiles, pieces = cols // tile, len(slots) if by_slot else cols // width
    place = jnp.stack([rindex] + [findex ^ slot for slot in slots]).astype(jnp.int32)
    keep_spec = pl.BlockSpec((1, half, tile), lambda s, j, place: (s, 0, j))
    give_spec = pl.BlockSpec((1, half, width), lambda s, j, place: (s, 0, 0))

    def slot_spec(k):
        def index(s, j, place):
            return (0, 0, jnp.where(s < k, 0, jnp.where(s > k, tiles - 1, j)))

        return pl.BlockSpec((1, half, tile), index)

    give_specs = [keep_spec] if pieces == 1 else [give_spec] * pieces
    given = (len(slots), half, width)
    if by_slot:
        give_specs, given = [slot_spec(k) for k in range(pieces)], (1, half, cols)
    x_spec = pl.BlockSpec((rows, depth), lambda s, j, place: (0, 0), pipeline_mode=pl.Buffered(1))
    outs = pl.pallas_call(
        functools.partial(query_kernel, count, pieces, by_slot),
        grid_spec=pltpu.PrefetchScalarGridSpec(
            num_scalar_prefetch=1,
            grid=(len(slots), tiles),
            in_specs=[x_spec] * count
            + [pl.BlockSpec((depth, tile), lambda s, j, place: (0, place[1 + s] * tiles + j))]
            + [pl.BlockSpec(memory_space=pl.ANY)] * len(after),
            out_specs=[keep_spec] + give_specs,
            scratch_shapes=[pltpu.VMEM((2 * half, depth), w.dtype)],
        ),
        out_shape=[pltpu.HBM((len(slots), half, cols), jnp.float32)]
        + [pltpu.HBM(given, jnp.bfloat16)] * pieces,
        compiler_params=pltpu.CompilerParams(vmem_limit_bytes=VMEM_BYTES),
        cost_estimate=cost,
        name="query_products",
    )(place, *blocks, *in_hbm([w]), *in_hbm(after[:1]), *after[1:])
    return outs[0], outs[1:]


def pair_kernel(count, place_ref, *refs):
    x_refs, (wk_ref, wv_ref) = refs[:count], refs[count : count + 2]
    keep_ref, give_ref, rows_ref = refs[-3:]

    @pl.when(pl.program_id(0) == 0)
    def _():
        ordered_rows(place_ref, x_refs, rows_ref)

    weights = jnp.concatenate([wk_ref[...], wv_ref[...]], axis=1)
    result = jnp.dot(rows_ref[...], weights, preferred_element_type=jnp.float32)
    half, width = x_refs[0].shape[0] // 2, weights.shape[1]
    for b in range(count):
        kept, given = b * half, (count + b) * half
        cols = slice(b * width, (b + 1) * width)
        keep_ref[0, :, cols] = result[kept : kept + half]
        give_ref[0, :, cols] = result[given : given + half].astype(give_ref.dtype)


def project_pair(rindex, findex, slots, blocks, w_key, w_value, after=()):
    rows, depth = blocks[0].shape
    count = len(blocks)
    place = jnp.stack([rindex] + [findex ^ slot for slot in slots]).astype(jnp.int32)
    weight = pl.BlockSpec((depth, DH), lambda s, place: (0, place[1 + s]))
    shape = (len(slots), rows // 2, 2 * DH * count)
    out = pl.BlockSpec((1,) + shape[1:], lambda s, place: (s, 0, 0))
    return pl.pallas_call(
        functools.partial(pair_kernel, count),
        grid_spec=pltpu.PrefetchScalarGridSpec(
            num_scalar_prefetch=1,
            grid=(len(slots),),
            in_specs=[pl.BlockSpec((rows, depth), lambda s, place: (0, 0))] * count
            + [weight, weight]
            + [pl.BlockSpec(memory_space=pl.ANY)] * len(after),
            out_specs=[out, out],
            scratch_shapes=[pltpu.VMEM((count * rows, depth), blocks[0].dtype)],
        ),
        out_shape=[
            pltpu.HBM(shape, jnp.float32),
            pltpu.HBM(shape, jnp.bfloat16),
        ],
        compiler_params=pltpu.CompilerParams(vmem_limit_bytes=VMEM_BYTES),
        cost_estimate=LIGHT,
        name="key_value_products",
    )(place, *blocks, *in_hbm([w_key, w_value, *after]))


def segments(arrays, start, stop):
    parts, first = [], 0
    for x in arrays:
        low, high = max(start, first) - first, min(stop - first, x.shape[2])
        if low < high:
            parts.append((x, high - low, low // (high - low)))
        first += x.shape[2]
    return parts


def add_kernel(gots, paired, extra, *refs):
    keep_ref, got_refs, out_ref = refs[0], refs[1 : 1 + gots], refs[-1]
    pair_refs = refs[1 + gots : 1 + gots + 2 * paired]
    landed_refs = refs[1 + gots + 2 * paired :][: extra * (1 + paired)]
    cols = sum(got_ref.shape[2] for got_ref in got_refs)

    def total(first, second, landed):
        value = first + second.astype(jnp.float32)
        for term in landed:
            value = value + term.astype(jnp.float32)
        return value.astype(out_ref.dtype)

    start = 0
    for got_ref in got_refs:
        part = slice(start, start + got_ref.shape[2])
        start = part.stop
        landed = [landed_refs[0][0, :, part]] if extra else []
        out_ref[0, :, part] = total(keep_ref[0, :, part], got_ref[0], landed)
    if paired:
        landed = [landed_refs[1][0]] if extra else []
        out_ref[0, :, cols:] = total(pair_refs[0][0], pair_refs[1][0], landed)


def add_rows(first, count, rows, b, keep, gots, start, cols, pair=(), slot=0, landed=(), after=()):
    whole = keep.shape[2]
    more = pair[0].shape[2] if pair else 0
    keep_spec = pl.BlockSpec((1, rows, cols), lambda s: (first + s, b, start // cols))
    gots = segments(gots, start, start + cols)

    def got_spec(width, column):
        return pl.BlockSpec((1, rows, width), lambda s: (first + s, b, column))

    pair_spec = pl.BlockSpec((1, rows, more), lambda s: (slot + s, 0, 0))
    landed_specs = [pl.BlockSpec((1, rows, cols), lambda s: (s, 0, start // cols))]
    if pair:
        landed_specs.append(pl.BlockSpec((1, rows, more), lambda s: (s, 0, whole // more)))
    landed_specs = landed_specs * len(landed)
    return pl.pallas_call(
        functools.partial(add_kernel, len(gots), len(pair) // 2, len(landed)),
        grid=(count,),
        in_specs=[keep_spec]
        + [got_spec(width, column) for _, width, column in gots]
        + [pair_spec] * len(pair)
        + landed_specs
        + [pl.BlockSpec(memory_space=pl.ANY)] * len(after),
        out_specs=pl.BlockSpec((1, rows, cols + more), lambda s: (s, 0, 0)),
        out_shape=pltpu.HBM((count, rows, cols + more), jnp.bfloat16),
        compiler_params=pltpu.CompilerParams(vmem_limit_bytes=VMEM_BYTES),
        cost_estimate=LIGHT,
        name="add_rows",
    )(
        *in_hbm([keep]),
        *[got for got, _, _ in gots],
        *in_hbm(pair[:1]),
        *pair[1:],
        *(list(landed) * (2 if pair else 1)),
        *in_hbm(after[:1]),
        *after[1:],
    )


def rotate_kernel(count, pieces, cos_ref, sin_ref, *refs):
    terms, gots, out_ref = refs[:count], refs[count : count + pieces], refs[-1]
    cosine, sine = cos_ref[...], sin_ref[...]
    start = 0
    for got in gots or terms[:1]:
        cols = slice(start, start + got.shape[2])
        start = cols.stop
        total = terms[0][0, :, cols].astype(jnp.float32)
        for term in terms[1:]:
            total = total + term[0, :, cols].astype(jnp.float32)
        if gots:
            total = total + got[0].astype(jnp.float32)
        for head in range(total.shape[1] // DH):
            part = total[:, head * DH : (head + 1) * DH]
            turned = pltpu.roll(part, DH // 2, axis=1)
            value = (part * cosine + turned * sine).astype(out_ref.dtype)
            out_ref[:, cols.start + head * DH : cols.start + (head + 1) * DH] = value


def sum_and_rotate(cosine, sine, terms, gots, cols, after=()):
    rows = cosine.shape[0]
    table = pl.BlockSpec((rows, DH), lambda j: (0, 0))

    def block(width, slot, column):
        return pl.BlockSpec((1, rows, width), lambda j: (slot, 0, column))

    return pl.pallas_call(
        functools.partial(rotate_kernel, len(terms), len(gots)),
        grid=(1,),
        in_specs=[table, table]
        + [block(cols, slot, start // cols) for _, slot, start in terms]
        + [block(width, 0, column) for _, width, column in gots]
        + [pl.BlockSpec(memory_space=pl.ANY)] * len(after),
        out_specs=pl.BlockSpec((rows, cols), lambda j: (0, 0)),
        out_shape=jax.ShapeDtypeStruct((rows, cols), jnp.bfloat16),
        compiler_params=pltpu.CompilerParams(vmem_limit_bytes=VMEM_BYTES),
        cost_estimate=LIGHT,
        name="sum_and_rotate",
    )(
        cosine,
        sine,
        *in_hbm([terms[0][0]]),
        *[term[0] for term in terms[1:]],
        *[got for got, _, _ in gots],
        *after,
    )


def split_kernel(count, cos_ref, sin_ref, *refs):
    terms, (key_ref, value_ref) = refs[:count], refs[-2:]
    total = terms[0][0].astype(jnp.float32)
    for term in terms[1:]:
        total = total + term[0].astype(jnp.float32)
    half = total.shape[0]
    for b in range(total.shape[1] // (2 * DH)):
        rows = slice(b * half, (b + 1) * half)
        key = total[:, 2 * b * DH : (2 * b + 1) * DH]
        turned = pltpu.roll(key, DH // 2, axis=1)
        key_ref[rows] = (key * cos_ref[rows] + turned * sin_ref[rows]).astype(key_ref.dtype)
        value_ref[0, rows] = total[:, (2 * b + 1) * DH : (2 * b + 2) * DH].astype(value_ref.dtype)


def split_and_rotate(cosine, sine, terms, width, after):
    rows = cosine.shape[0]
    half = terms[0][0].shape[1]
    table = pl.BlockSpec((rows, DH), lambda j: (0, 0))

    def block(slot, start):
        return pl.BlockSpec((1, half, width), lambda j: (slot, 0, start // width))

    return pl.pallas_call(
        functools.partial(split_kernel, len(terms)),
        grid=(1,),
        in_specs=[table, table]
        + [block(slot, start) for _, slot, start in terms]
        + [pl.BlockSpec(memory_space=pl.ANY)] * len(after),
        out_specs=[table, pl.BlockSpec((1, rows, DH), lambda j: (0, 0, 0))],
        out_shape=[
            jax.ShapeDtypeStruct((rows, DH), jnp.bfloat16),
            jax.ShapeDtypeStruct((1, rows, DH), jnp.bfloat16),
        ],
        compiler_params=pltpu.CompilerParams(vmem_limit_bytes=VMEM_BYTES),
        cost_estimate=LIGHT,
        name="split_and_rotate",
    )(cosine, sine, *in_hbm([terms[0][0]]), *[term for term, _, _ in terms[1:]], *after)


def prepare_kernel(canary_ref, ids_ref, own_ref, other_ref, order_ref, key_t_ref):
    order = jnp.where(canary_ref[...] == ids_ref[...], 1.0, 0.0).astype(jnp.bfloat16)
    order_ref[...] = order
    key = jnp.concatenate([own_ref[...], other_ref[...]], axis=0)
    key_t_ref[...] = jnp.dot(order, key, preferred_element_type=jnp.float32).T.astype(jnp.bfloat16)


def prepare(canary_rows, ids, own, other):
    rows = ids.shape[0]
    return pl.pallas_call(
        prepare_kernel,
        out_shape=[
            jax.ShapeDtypeStruct((rows, rows), jnp.bfloat16),
            jax.ShapeDtypeStruct((DH, rows), jnp.bfloat16),
        ],
        compiler_params=pltpu.CompilerParams(vmem_limit_bytes=VMEM_BYTES),
        name="order_and_keys",
    )(canary_rows.reshape(rows, 1), ids.reshape(1, rows), own, other)


def stack_kernel(count, *refs):
    out_ref, start = refs[-1], 0
    for ref in refs[:count]:
        out_ref[start : start + ref.shape[0]] = ref[...]
        start += ref.shape[0]


def stack_slots(arrays, after):
    slots = sum(x.shape[0] for x in arrays)
    shape = (slots,) + arrays[0].shape[1:]
    return pl.pallas_call(
        functools.partial(stack_kernel, len(arrays)),
        grid=(1,),
        in_specs=[pl.BlockSpec(x.shape, lambda j: (0, 0, 0)) for x in arrays]
        + [pl.BlockSpec(memory_space=pl.ANY)] * len(after),
        out_specs=pl.BlockSpec(shape, lambda j: (0, 0, 0)),
        out_shape=jax.ShapeDtypeStruct(shape, arrays[0].dtype),
        compiler_params=pltpu.CompilerParams(vmem_limit_bytes=VMEM_BYTES),
        cost_estimate=LIGHT,
        name="stack_slots",
    )(*arrays, *after)


def value_kernel(place_ref, order_ref, own_ref, other_ref, out_ref):
    rows = jnp.concatenate([own_ref[0], other_ref[0]], axis=0)
    out_ref[...] = jnp.dot(order_ref[...], rows, preferred_element_type=jnp.float32).astype(out_ref.dtype)


def order_values(findex, order, own, other):
    rows = order.shape[0]
    slots, part, width = own.shape
    place = jnp.stack([findex ^ s for s in range(slots)]).astype(jnp.int32)
    block = pl.BlockSpec((1, part, width), lambda s, place: (place[s], 0, 0))
    return pl.pallas_call(
        value_kernel,
        grid_spec=pltpu.PrefetchScalarGridSpec(
            num_scalar_prefetch=1,
            grid=(slots,),
            in_specs=[pl.BlockSpec((rows, rows), lambda s, place: (0, 0)), block, block],
            out_specs=pl.BlockSpec((rows, width), lambda s, place: (0, s)),
        ),
        out_shape=jax.ShapeDtypeStruct((rows, slots * width), jnp.bfloat16),
        compiler_params=pltpu.CompilerParams(vmem_limit_bytes=VMEM_BYTES),
        name="order_values",
    )(place, order, own, other)


def score_kernel(count, order_ref, key_t_ref, *refs):
    queries, (out_ref, mark_ref) = refs[:count], refs[-2:]
    mark_ref[...] = jnp.zeros_like(mark_ref)
    stacked = jnp.concatenate([query[...] for query in queries], axis=0)
    chosen = jnp.dot(order_ref[...], stacked, preferred_element_type=jnp.float32).astype(jnp.bfloat16)
    for head in range(stacked.shape[1] // DH):
        products = jnp.dot(
            chosen[:, head * DH : (head + 1) * DH], key_t_ref[...], preferred_element_type=jnp.float32
        )
        out_ref[0, head] = (products * DH ** (-0.5)).astype(out_ref.dtype)


def score_heads(order, key_t, heads, start, count, queries, earlier, after=()):
    rows = order.shape[0]
    step = math.gcd(count, 4)

    def block(query, first):
        return pl.BlockSpec((query.shape[0], step * DH), lambda j: (0, first // step + j))

    return pl.pallas_call(
        functools.partial(score_kernel, len(queries)),
        grid=(count // step,),
        in_specs=[
            pl.BlockSpec((rows, rows), lambda j: (0, 0)),
            pl.BlockSpec((DH, rows), lambda j: (0, 0)),
        ]
        + [block(query, first) for query, first in queries]
        + [pl.BlockSpec(memory_space=pl.ANY)] * (len(earlier) + len(after)),
        out_specs=[
            pl.BlockSpec((1, step, rows, rows), lambda j: (0, start // step + j, 0, 0)),
            pl.BlockSpec((8, DH), lambda j: (0, 0)),
        ],
        out_shape=[
            jax.ShapeDtypeStruct((1, heads, rows, rows), jnp.bfloat16),
            jax.ShapeDtypeStruct((8, DH), jnp.float32),
        ],
        input_output_aliases={2 + len(queries): 0} if earlier else {},
        compiler_params=pltpu.CompilerParams(vmem_limit_bytes=VMEM_BYTES),
        cost_estimate=LIGHT,
        name="score_heads",
    )(order, key_t, *[query for query, _ in queries], *earlier, *after)


def body(hidden, w_query, w_key, w_value, canary_rows, positions):
    shards = lax.axis_size("fsdp")
    findex = lax.axis_index("fsdp")
    tps = lax.axis_size("tp")
    tindex = lax.axis_index("tp")
    rindex = lax.axis_index("rep")
    local, depth = hidden.shape
    half = local // 2
    rows = local * tps
    head_cols = w_query.shape[1] // shards
    heads_here = head_cols // DH
    group = HQ // KV
    assert shards & (shards - 1) == 0 and lax.axis_size("rep") == 2

    def swap(x, bit):
        return lax.ppermute(x, "fsdp", [(i, i ^ bit) for i in range(shards)])

    def other_core(x):
        return lax.ppermute(x, "rep", [(0, 1), (1, 0)])

    def low(x):
        return x.astype(jnp.bfloat16)

    odd = list(range(3, shards, 2)) + [1]
    even = list(range(2, shards, 2))
    fast_pair = heads_here == group

    def spread(live):
        terms, first = [], None
        bit = 2
        while bit < shards:
            sent = [x for x in sorted(live) if x & bit]
            pack = jnp.stack([low(live[x]) for x in sent])
            first = pack if first is None else first
            landed = swap(pack, bit)
            for k, x in enumerate(sent):
                if x == bit:
                    terms.append(landed)
                else:
                    live[x ^ bit] = live[x ^ bit] + landed[k].astype(jnp.float32)
                del live[x]
            bit *= 2
        return terms, first

    blocks = [hidden] + [
        lax.ppermute(hidden, "tp", [(i, (i - b) % tps) for i in range(tps)]) for b in range(1, tps)
    ]

    block_ids = ((tindex + jnp.arange(tps, dtype=jnp.int32)) % tps * local)[:, None]
    own_ids = (block_ids + rindex * half + jnp.arange(half, dtype=jnp.int32)[None]).reshape(-1)
    other_ids = (block_ids + (1 - rindex) * half + jnp.arange(half, dtype=jnp.int32)[None]).reshape(-1)
    ids = jnp.concatenate([own_ids, other_ids])
    own_positions = jnp.sum(
        jnp.where(own_ids[:, None] == canary_rows[None, :], positions[None, :], 0), axis=1
    )
    cosine, sine = rope_tables(own_positions)

    tile = min(1024, head_cols)

    def project(slots, blocks, width, after=(), cost=LIGHT, by_slot=False):
        keep, gives = project_query(
            rindex, findex, slots, blocks, w_query, head_cols, tile, width, after, cost, by_slot
        )
        return keep, [other_core(give) for give in gives], gives[0]

    def rotate(b, start, stop, terms, behind):
        table = slice(b * half, (b + 1) * half)
        keep, slot, got = owns[b]
        added = [(keep, slot, start)] + terms
        gots = segments(got, start, stop)
        turned = sum_and_rotate(cosine[table], sine[table], added, gots, stop - start, behind)
        return turned, other_core(turned)

    def add_even(b, start, cols, pair, behind):
        if shards == 2:
            return [], behind
        keep, got = evens[b]
        summed = add_rows(
            0, len(even), half, 0, keep, got, start, cols, pair, len(odd), (fars[b],), behind
        )
        terms, first = spread({x: summed[k] for k, x in enumerate(even)})
        return [(term, 0, 0) for term in terms], (first,)

    last = tps - 1
    bounds = [0, head_cols] if tile == head_cols else [0, head_cols * 3 // 4, head_cols]
    ranges = list(zip(bounds, bounds[1:]))
    placed = in_hbm(blocks[:1]) + blocks[1:]
    evens, owns, fars, terms, pair, after = [], [], [], [], (), ()
    for b, block in enumerate(placed):
        if fast_pair and b == last:
            slots = odd + even + [0]
            pair_keep, give = project_pair(rindex, findex, slots, placed, w_key, w_value, after)
            pair = (pair_keep, other_core(give))
            after = (give,)
        sent = odd[:-1] if b == last else odd
        odd_keep, odd_got, given = project(sent, [block], tile, after)
        odd_sent = add_rows(0, len(sent), half, 0, odd_keep, odd_got, 0, head_cols, pair)
        fars.append(swap(odd_sent, 1))
        after = (odd_sent,)
        if b > 0:
            added, after = add_even(b - 1, 0, head_cols, (), after)
            terms.append([(fars[b - 1], len(odd) - 1, 0)] + added)
            after = (odd_sent,) + after
        if b < last:
            keep, got, given = project(even + [0], [block], head_cols, after, LIGHT, True)
            evens.append((keep, got[:1] if len(even) == 1 else [jnp.concatenate(got[:-1])]))
            owns.append((keep, len(even), got[-1:]))
        else:
            keep, got, given = project(even, [block], tile, after, HEAVY)
            evens.append((keep, got))
        after = (given,)
    near_keep, near_got, given = project([1], placed[last:], tile, after)
    after = (given,)
    parts, behind = [], tuple(term[0] for row in terms for term in row[1:])
    for start, stop in ranges:
        paired = () if start else pair
        near_sent = add_rows(
            0, 1, half, 0, near_keep, near_got, start, stop - start, paired, len(odd) - 1, (), after
        )
        parts.append([(swap(near_sent, 1), 0, 0)])
        after = (near_sent,)
    after = after + behind
    for part, (start, stop) in zip(parts, ranges):
        added, after = add_even(last, start, stop - start, () if start else pair, after)
        part += added
    keep, got, _ = project([0], placed[last:], tile, after, HEAVY)
    owns.append((keep, 0, got))

    if fast_pair:
        width = 2 * DH * tps
        pieces = [(array, shards - 1, 0) for array in pair]
        pieces += [(term, 0, bounds[1]) for term, _, _ in parts[0]]
        key_rot, held = split_and_rotate(cosine, sine, pieces, width, after)
    else:
        x = jnp.concatenate(blocks, axis=0)
        key_sum, value_sum = lax.psum(
            (
                jnp.dot(x, w_key, preferred_element_type=jnp.float32),
                jnp.dot(x, w_value, preferred_element_type=jnp.float32),
            ),
            ("fsdp", "rep"),
        )

        def of_core(y, core):
            parts = y.reshape(tps, 2, half, -1)
            return lax.dynamic_index_in_dim(parts, core, 1, keepdims=False).reshape(tps * half, -1)

        mine = lax.dynamic_slice_in_dim(key_sum, findex * heads_here // group * DH, DH, 1)
        key_own = of_core(mine, rindex)
        key_rot = sum_and_rotate(cosine, sine, [(key_own[None], 0, 0)], [], DH, after)
        value_rows = low(jnp.concatenate([of_core(value_sum, rindex), of_core(value_sum, 1 - rindex)]))

    order, key_t = prepare(canary_rows, ids, key_rot, other_core(key_rot))
    if not fast_pair:
        values = low(jnp.dot(order, value_rows, preferred_element_type=jnp.float32))

    rotated = [rotate(b, 0, head_cols, terms[b], after) for b in range(last)]
    scores, mark = (), ()
    for p, (start, stop) in enumerate(ranges):
        turned = rotate(last, start, stop, parts[p], mark or tuple(owns[last][2][1:]))
        first = start // DH
        queries = [(row[0], first) for row in rotated] + [(turned[0], 0)]
        queries += [(row[1], first) for row in rotated] + [(turned[1], 0)]
        behind = in_hbm([values]) if p > 0 else ()
        *scores, mark = score_heads(
            order, key_t, heads_here, first, (stop - start) // DH, queries, scores, behind
        )
        mark = (mark,)
        if fast_pair and p == 0:
            held = stack_slots([held] + [swap(held, x) for x in range(1, shards)], mark)
            values = order_values(findex, order, held, other_core(held))
    return (scores[0], values)


def solution(mesh):
    in_specs = (
        P(("groups", "tp"), ("fsdp", "rep")),
        P(("fsdp", "rep"), "tp"),
        P(("fsdp", "rep"), "tp"),
        P(("fsdp", "rep"), "tp"),
        P("groups"),
        P("groups"),
    )
    out_specs = (P("tp", "fsdp", "groups", None), P("groups", "tp"))
    return jax.shard_map(body, mesh=mesh, in_specs=in_specs, out_specs=out_specs, check_vma=False)
```

```python
import functools
import math

import jax
import jax.numpy as jnp
from jax import lax
from jax.experimental import pallas as pl
from jax.experimental.pallas import tpu as pltpu
from jax.sharding import PartitionSpec as P

HQ = 128
KV = 8
DH = 128
VMEM_BYTES = 28 * 1024 * 1024
LIGHT = pl.CostEstimate(flops=1000, bytes_accessed=1000, transcendentals=0)
HEAVY = pl.CostEstimate(flops=10**11, bytes_accessed=10**8, transcendentals=0)


def in_hbm(arrays):
    return [pltpu.with_memory_space_constraint(x, pltpu.HBM) for x in arrays]


def rope_tables(positions):
    half = DH // 2
    expo = jnp.arange(half, dtype=jnp.float32) * (2.0 / DH)
    freq = jnp.power(jnp.float32(500000.0), -expo)
    wavelen = 2.0 * math.pi / freq
    smooth = (8192.0 / wavelen - 1.0) / 3.0
    mixed = (1.0 - smooth) * freq / 8.0 + smooth * freq
    freq = jnp.where(wavelen > 8192.0, freq / 8.0, jnp.where(wavelen < 2048.0, freq, mixed))
    angle = positions.astype(jnp.float32)[:, None] * freq[None, :]
    cosine, sine = jnp.cos(angle), jnp.sin(angle)
    return jnp.concatenate([cosine, cosine], axis=1), jnp.concatenate([-sine, sine], axis=1)


def ordered_rows(place_ref, x_refs, rows_ref):
    core = place_ref[0]
    half = x_refs[0].shape[0] // 2
    for b, x_ref in enumerate(x_refs):
        kept, given = b * half, (len(x_refs) + b) * half
        rows_ref[kept : kept + half] = x_ref[pl.ds(pl.multiple_of(core * half, 16), half)]
        rows_ref[given : given + half] = x_ref[pl.ds(pl.multiple_of((1 - core) * half, 16), half)]


def query_kernel(count, pieces, by_slot, place_ref, *refs):
    x_refs, w_ref = refs[:count], refs[count]
    keep_ref, *give_refs, rows_ref = refs[-2 - pieces :]
    tile = pl.program_id(1)
    size = give_refs[0].shape[2]
    each = keep_ref.shape[2] // size

    @pl.when((pl.program_id(0) == 0) & (tile == 0))
    def _():
        ordered_rows(place_ref, x_refs, rows_ref)

    result = jnp.dot(rows_ref[...], w_ref[...], preferred_element_type=jnp.float32)
    half = result.shape[0] // 2
    keep_ref[0] = result[:half]
    for j, give_ref in enumerate(give_refs):

        @pl.when(pl.program_id(0) == j if by_slot else (tile == j // each) | (pieces == 1))
        def _():
            start = j % each * size
            give_ref[0] = result[half:, start : start + size].astype(give_ref.dtype)


def project_query(rindex, findex, slots, blocks, w, cols, tile, width, after, cost, by_slot):
    rows, depth = blocks[0].shape
    count = len(blocks)
    half = rows // 2 * count
    tiles, pieces = cols // tile, len(slots) if by_slot else cols // width
    place = jnp.stack([rindex] + [findex ^ slot for slot in slots]).astype(jnp.int32)
    keep_spec = pl.BlockSpec((1, half, tile), lambda s, j, place: (s, 0, j))
    give_spec = pl.BlockSpec((1, half, width), lambda s, j, place: (s, 0, 0))

    def slot_spec(k):
        def index(s, j, place):
            return (0, 0, jnp.where(s < k, 0, jnp.where(s > k, tiles - 1, j)))

        return pl.BlockSpec((1, half, tile), index)

    give_specs = [keep_spec] if pieces == 1 else [give_spec] * pieces
    given = (len(slots), half, width)
    if by_slot:
        give_specs, given = [slot_spec(k) for k in range(pieces)], (1, half, cols)
    x_spec = pl.BlockSpec((rows, depth), lambda s, j, place: (0, 0), pipeline_mode=pl.Buffered(1))
    outs = pl.pallas_call(
        functools.partial(query_kernel, count, pieces, by_slot),
        grid_spec=pltpu.PrefetchScalarGridSpec(
            num_scalar_prefetch=1,
            grid=(len(slots), tiles),
            in_specs=[x_spec] * count
            + [pl.BlockSpec((depth, tile), lambda s, j, place: (0, place[1 + s] * tiles + j))]
            + [pl.BlockSpec(memory_space=pl.ANY)] * len(after),
            out_specs=[keep_spec] + give_specs,
            scratch_shapes=[pltpu.VMEM((2 * half, depth), w.dtype)],
        ),
        out_shape=[pltpu.HBM((len(slots), half, cols), jnp.float32)]
        + [pltpu.HBM(given, jnp.bfloat16)] * pieces,
        compiler_params=pltpu.CompilerParams(vmem_limit_bytes=VMEM_BYTES),
        cost_estimate=cost,
        name="query_products",
    )(place, *blocks, *in_hbm([w]), *in_hbm(after[:1]), *after[1:])
    return outs[0], outs[1:]


def pair_kernel(count, place_ref, *refs):
    x_refs, (wk_ref, wv_ref) = refs[:count], refs[count : count + 2]
    keep_ref, give_ref, rows_ref = refs[-3:]

    @pl.when(pl.program_id(0) == 0)
    def _():
        ordered_rows(place_ref, x_refs, rows_ref)

    weights = jnp.concatenate([wk_ref[...], wv_ref[...]], axis=1)
    result = jnp.dot(rows_ref[...], weights, preferred_element_type=jnp.float32)
    half, width = x_refs[0].shape[0] // 2, weights.shape[1]
    for b in range(count):
        kept, given = b * half, (count + b) * half
        cols = slice(b * width, (b + 1) * width)
        keep_ref[0, :, cols] = result[kept : kept + half]
        give_ref[0, :, cols] = result[given : given + half].astype(give_ref.dtype)


def project_pair(rindex, findex, slots, blocks, w_key, w_value, after=()):
    rows, depth = blocks[0].shape
    count = len(blocks)
    place = jnp.stack([rindex] + [findex ^ slot for slot in slots]).astype(jnp.int32)
    weight = pl.BlockSpec((depth, DH), lambda s, place: (0, place[1 + s]))
    shape = (len(slots), rows // 2, 2 * DH * count)
    out = pl.BlockSpec((1,) + shape[1:], lambda s, place: (s, 0, 0))
    return pl.pallas_call(
        functools.partial(pair_kernel, count),
        grid_spec=pltpu.PrefetchScalarGridSpec(
            num_scalar_prefetch=1,
            grid=(len(slots),),
            in_specs=[pl.BlockSpec((rows, depth), lambda s, place: (0, 0))] * count
            + [weight, weight]
            + [pl.BlockSpec(memory_space=pl.ANY)] * len(after),
            out_specs=[out, out],
            scratch_shapes=[pltpu.VMEM((count * rows, depth), blocks[0].dtype)],
        ),
        out_shape=[
            pltpu.HBM(shape, jnp.float32),
            pltpu.HBM(shape, jnp.bfloat16),
        ],
        compiler_params=pltpu.CompilerParams(vmem_limit_bytes=VMEM_BYTES),
        cost_estimate=LIGHT,
        name="key_value_products",
    )(place, *blocks, *in_hbm([w_key, w_value, *after]))


def segments(arrays, start, stop):
    parts, first = [], 0
    for x in arrays:
        low, high = max(start, first) - first, min(stop - first, x.shape[2])
        if low < high:
            parts.append((x, high - low, low // (high - low)))
        first += x.shape[2]
    return parts


def add_kernel(gots, paired, extra, *refs):
    keep_ref, got_refs, out_ref = refs[0], refs[1 : 1 + gots], refs[-1]
    pair_refs = refs[1 + gots : 1 + gots + 2 * paired]
    landed_refs = refs[1 + gots + 2 * paired :][: extra * (1 + paired)]
    cols = sum(got_ref.shape[2] for got_ref in got_refs)

    def total(first, second, landed):
        value = first + second.astype(jnp.float32)
        for term in landed:
            value = value + term.astype(jnp.float32)
        return value.astype(out_ref.dtype)

    start = 0
    for got_ref in got_refs:
        part = slice(start, start + got_ref.shape[2])
        start = part.stop
        landed = [landed_refs[0][0, :, part]] if extra else []
        out_ref[0, :, part] = total(keep_ref[0, :, part], got_ref[0], landed)
    if paired:
        landed = [landed_refs[1][0]] if extra else []
        out_ref[0, :, cols:] = total(pair_refs[0][0], pair_refs[1][0], landed)


def add_rows(first, count, rows, b, keep, gots, start, cols, pair=(), slot=0, landed=(), after=(), shift=0):
    whole = keep.shape[2]
    more = pair[0].shape[2] if pair else 0
    keep_spec = pl.BlockSpec((1, rows, cols), lambda s: (first + s, b, start // cols))
    gots = segments(gots, start, start + cols)

    def got_spec(width, column):
        return pl.BlockSpec((1, rows, width), lambda s: (first + s, b, column))

    pair_spec = pl.BlockSpec((1, rows, more), lambda s: (slot + s, 0, 0))
    landed_specs = [pl.BlockSpec((1, rows, cols), lambda s: (s, 0, (start + shift) // cols))]
    if pair:
        landed_specs.append(pl.BlockSpec((1, rows, more), lambda s: (s, 0, whole // more)))
    landed_specs = landed_specs * len(landed)
    return pl.pallas_call(
        functools.partial(add_kernel, len(gots), len(pair) // 2, len(landed)),
        grid=(count,),
        in_specs=[keep_spec]
        + [got_spec(width, column) for _, width, column in gots]
        + [pair_spec] * len(pair)
        + landed_specs
        + [pl.BlockSpec(memory_space=pl.ANY)] * len(after),
        out_specs=pl.BlockSpec((1, rows, cols + more), lambda s: (s, 0, 0)),
        out_shape=pltpu.HBM((count, rows, cols + more), jnp.bfloat16),
        compiler_params=pltpu.CompilerParams(vmem_limit_bytes=VMEM_BYTES),
        cost_estimate=LIGHT,
        name="add_rows",
    )(
        *in_hbm([keep]),
        *[got for got, _, _ in gots],
        *in_hbm(pair[:1]),
        *pair[1:],
        *(list(landed) * (2 if pair else 1)),
        *in_hbm(after[:1]),
        *after[1:],
    )


def rotate_kernel(count, pieces, cos_ref, sin_ref, *refs):
    terms, gots, out_ref = refs[:count], refs[count : count + pieces], refs[-1]
    cosine, sine = cos_ref[...], sin_ref[...]
    start = 0
    for got in gots or terms[:1]:
        cols = slice(start, start + got.shape[2])
        start = cols.stop
        total = terms[0][0, :, cols].astype(jnp.float32)
        for term in terms[1:]:
            total = total + term[0, :, cols].astype(jnp.float32)
        if gots:
            total = total + got[0].astype(jnp.float32)
        for head in range(total.shape[1] // DH):
            part = total[:, head * DH : (head + 1) * DH]
            turned = pltpu.roll(part, DH // 2, axis=1)
            value = (part * cosine + turned * sine).astype(out_ref.dtype)
            out_ref[:, cols.start + head * DH : cols.start + (head + 1) * DH] = value


def sum_and_rotate(cosine, sine, terms, gots, cols, after=()):
    rows = cosine.shape[0]
    table = pl.BlockSpec((rows, DH), lambda j: (0, 0))

    def block(width, slot, column):
        return pl.BlockSpec((1, rows, width), lambda j: (slot, 0, column))

    return pl.pallas_call(
        functools.partial(rotate_kernel, len(terms), len(gots)),
        grid=(1,),
        in_specs=[table, table]
        + [block(cols, slot, start // cols) for _, slot, start in terms]
        + [block(width, 0, column) for _, width, column in gots]
        + [pl.BlockSpec(memory_space=pl.ANY)] * len(after),
        out_specs=pl.BlockSpec((rows, cols), lambda j: (0, 0)),
        out_shape=jax.ShapeDtypeStruct((rows, cols), jnp.bfloat16),
        compiler_params=pltpu.CompilerParams(vmem_limit_bytes=VMEM_BYTES),
        cost_estimate=LIGHT,
        name="sum_and_rotate",
    )(
        cosine,
        sine,
        *in_hbm([terms[0][0]]),
        *[term[0] for term in terms[1:]],
        *[got for got, _, _ in gots],
        *after,
    )


def split_kernel(count, cos_ref, sin_ref, *refs):
    terms, (key_ref, value_ref) = refs[:count], refs[-2:]
    total = terms[0][0].astype(jnp.float32)
    for term in terms[1:]:
        total = total + term[0].astype(jnp.float32)
    half = total.shape[0]
    for b in range(total.shape[1] // (2 * DH)):
        rows = slice(b * half, (b + 1) * half)
        key = total[:, 2 * b * DH : (2 * b + 1) * DH]
        turned = pltpu.roll(key, DH // 2, axis=1)
        key_ref[rows] = (key * cos_ref[rows] + turned * sin_ref[rows]).astype(key_ref.dtype)
        value_ref[0, rows] = total[:, (2 * b + 1) * DH : (2 * b + 2) * DH].astype(value_ref.dtype)


def split_and_rotate(cosine, sine, terms, width, after):
    rows = cosine.shape[0]
    half = terms[0][0].shape[1]
    table = pl.BlockSpec((rows, DH), lambda j: (0, 0))

    def block(slot, start):
        return pl.BlockSpec((1, half, width), lambda j: (slot, 0, start // width))

    return pl.pallas_call(
        functools.partial(split_kernel, len(terms)),
        grid=(1,),
        in_specs=[table, table]
        + [block(slot, start) for _, slot, start in terms]
        + [pl.BlockSpec(memory_space=pl.ANY)] * len(after),
        out_specs=[table, pl.BlockSpec((1, rows, DH), lambda j: (0, 0, 0))],
        out_shape=[
            jax.ShapeDtypeStruct((rows, DH), jnp.bfloat16),
            jax.ShapeDtypeStruct((1, rows, DH), jnp.bfloat16),
        ],
        compiler_params=pltpu.CompilerParams(vmem_limit_bytes=VMEM_BYTES),
        cost_estimate=LIGHT,
        name="split_and_rotate",
    )(cosine, sine, *in_hbm([terms[0][0]]), *[term for term, _, _ in terms[1:]], *after)


def prepare_kernel(canary_ref, ids_ref, own_ref, other_ref, order_ref, key_t_ref):
    order = jnp.where(canary_ref[...] == ids_ref[...], 1.0, 0.0).astype(jnp.bfloat16)
    order_ref[...] = order
    key = jnp.concatenate([own_ref[...], other_ref[...]], axis=0)
    key_t_ref[...] = jnp.dot(order, key, preferred_element_type=jnp.float32).T.astype(jnp.bfloat16)


def prepare(canary_rows, ids, own, other):
    rows = ids.shape[0]
    return pl.pallas_call(
        prepare_kernel,
        out_shape=[
            jax.ShapeDtypeStruct((rows, rows), jnp.bfloat16),
            jax.ShapeDtypeStruct((DH, rows), jnp.bfloat16),
        ],
        compiler_params=pltpu.CompilerParams(vmem_limit_bytes=VMEM_BYTES),
        name="order_and_keys",
    )(canary_rows.reshape(rows, 1), ids.reshape(1, rows), own, other)


def stack_kernel(count, *refs):
    out_ref, start = refs[-1], 0
    for ref in refs[:count]:
        out_ref[start : start + ref.shape[0]] = ref[...]
        start += ref.shape[0]


def stack_slots(arrays, after):
    slots = sum(x.shape[0] for x in arrays)
    shape = (slots,) + arrays[0].shape[1:]
    return pl.pallas_call(
        functools.partial(stack_kernel, len(arrays)),
        grid=(1,),
        in_specs=[pl.BlockSpec(x.shape, lambda j: (0, 0, 0)) for x in arrays]
        + [pl.BlockSpec(memory_space=pl.ANY)] * len(after),
        out_specs=pl.BlockSpec(shape, lambda j: (0, 0, 0)),
        out_shape=jax.ShapeDtypeStruct(shape, arrays[0].dtype),
        compiler_params=pltpu.CompilerParams(vmem_limit_bytes=VMEM_BYTES),
        cost_estimate=LIGHT,
        name="stack_slots",
    )(*arrays, *after)


def value_kernel(place_ref, order_ref, own_ref, other_ref, out_ref):
    rows = jnp.concatenate([own_ref[0], other_ref[0]], axis=0)
    out_ref[...] = jnp.dot(order_ref[...], rows, preferred_element_type=jnp.float32).astype(out_ref.dtype)


def order_values(findex, order, own, other):
    rows = order.shape[0]
    slots, part, width = own.shape
    place = jnp.stack([findex ^ s for s in range(slots)]).astype(jnp.int32)
    block = pl.BlockSpec((1, part, width), lambda s, place: (place[s], 0, 0))
    return pl.pallas_call(
        value_kernel,
        grid_spec=pltpu.PrefetchScalarGridSpec(
            num_scalar_prefetch=1,
            grid=(slots,),
            in_specs=[pl.BlockSpec((rows, rows), lambda s, place: (0, 0)), block, block],
            out_specs=pl.BlockSpec((rows, width), lambda s, place: (0, s)),
        ),
        out_shape=jax.ShapeDtypeStruct((rows, slots * width), jnp.bfloat16),
        compiler_params=pltpu.CompilerParams(vmem_limit_bytes=VMEM_BYTES),
        name="order_values",
    )(place, order, own, other)


def score_kernel(count, order_ref, key_t_ref, *refs):
    queries, (out_ref, mark_ref) = refs[:count], refs[-2:]
    mark_ref[...] = jnp.zeros_like(mark_ref)
    stacked = jnp.concatenate([query[...] for query in queries], axis=0)
    chosen = jnp.dot(order_ref[...], stacked, preferred_element_type=jnp.float32).astype(jnp.bfloat16)
    for head in range(stacked.shape[1] // DH):
        products = jnp.dot(
            chosen[:, head * DH : (head + 1) * DH], key_t_ref[...], preferred_element_type=jnp.float32
        )
        out_ref[0, head] = (products * DH ** (-0.5)).astype(out_ref.dtype)


def score_heads(order, key_t, heads, start, count, queries, earlier, after=()):
    rows = order.shape[0]
    step = math.gcd(count, 4)

    def block(query, first):
        return pl.BlockSpec((query.shape[0], step * DH), lambda j: (0, first // step + j))

    return pl.pallas_call(
        functools.partial(score_kernel, len(queries)),
        grid=(count // step,),
        in_specs=[
            pl.BlockSpec((rows, rows), lambda j: (0, 0)),
            pl.BlockSpec((DH, rows), lambda j: (0, 0)),
        ]
        + [block(query, first) for query, first in queries]
        + [pl.BlockSpec(memory_space=pl.ANY)] * (len(earlier) + len(after)),
        out_specs=[
            pl.BlockSpec((1, step, rows, rows), lambda j: (0, start // step + j, 0, 0)),
            pl.BlockSpec((8, DH), lambda j: (0, 0)),
        ],
        out_shape=[
            jax.ShapeDtypeStruct((1, heads, rows, rows), jnp.bfloat16),
            jax.ShapeDtypeStruct((8, DH), jnp.float32),
        ],
        input_output_aliases={2 + len(queries): 0} if earlier else {},
        compiler_params=pltpu.CompilerParams(vmem_limit_bytes=VMEM_BYTES),
        cost_estimate=LIGHT,
        name="score_heads",
    )(order, key_t, *[query for query, _ in queries], *earlier, *after)


def body(hidden, w_query, w_key, w_value, canary_rows, positions):
    shards = lax.axis_size("fsdp")
    findex = lax.axis_index("fsdp")
    tps = lax.axis_size("tp")
    tindex = lax.axis_index("tp")
    rindex = lax.axis_index("rep")
    local, depth = hidden.shape
    half = local // 2
    rows = local * tps
    head_cols = w_query.shape[1] // shards
    heads_here = head_cols // DH
    group = HQ // KV
    assert shards & (shards - 1) == 0 and lax.axis_size("rep") == 2

    def swap(x, bit):
        return lax.ppermute(x, "fsdp", [(i, i ^ bit) for i in range(shards)])

    def other_core(x):
        return lax.ppermute(x, "rep", [(0, 1), (1, 0)])

    def low(x):
        return x.astype(jnp.bfloat16)

    odd = list(range(3, shards, 2)) + [1]
    even = list(range(2, shards, 2))
    fast_pair = heads_here == group

    def spread(live):
        terms, first = [], None
        bit = 2
        while bit < shards:
            sent = [x for x in sorted(live) if x & bit]
            pack = jnp.stack([low(live[x]) for x in sent])
            first = pack if first is None else first
            landed = swap(pack, bit)
            for k, x in enumerate(sent):
                if x == bit:
                    terms.append(landed)
                else:
                    live[x ^ bit] = live[x ^ bit] + landed[k].astype(jnp.float32)
                del live[x]
            bit *= 2
        return terms, first

    blocks = [hidden] + [
        lax.ppermute(hidden, "tp", [(i, (i - b) % tps) for i in range(tps)]) for b in range(1, tps)
    ]

    block_ids = ((tindex + jnp.arange(tps, dtype=jnp.int32)) % tps * local)[:, None]
    own_ids = (block_ids + rindex * half + jnp.arange(half, dtype=jnp.int32)[None]).reshape(-1)
    other_ids = (block_ids + (1 - rindex) * half + jnp.arange(half, dtype=jnp.int32)[None]).reshape(-1)
    ids = jnp.concatenate([own_ids, other_ids])
    own_positions = jnp.sum(
        jnp.where(own_ids[:, None] == canary_rows[None, :], positions[None, :], 0), axis=1
    )
    cosine, sine = rope_tables(own_positions)

    tile = min(1024, head_cols)

    def project(slots, blocks, width, after=(), cost=LIGHT, by_slot=False):
        keep, gives = project_query(
            rindex, findex, slots, blocks, w_query, head_cols, tile, width, after, cost, by_slot
        )
        return keep, [other_core(give) for give in gives], gives[0]

    def rotate(b, start, stop, terms, behind):
        table = slice(b * half, (b + 1) * half)
        keep, slot, got = owns[b]
        added = [(keep, slot, start)] + terms
        gots = segments(got, start, stop)
        turned = sum_and_rotate(cosine[table], sine[table], added, gots, stop - start, behind)
        return turned, other_core(turned)

    def add_even(b, start, cols, pair, behind):
        if shards == 2:
            return [], behind
        keep, got = evens[b]
        summed = add_rows(
            0, len(even), half, 0, keep, got, start, cols, pair, len(odd), (fars[b],), behind
        )
        terms, first = spread({x: summed[k] for k, x in enumerate(even)})
        return [(term, 0, 0) for term in terms], (first,)

    last, width = tps - 1, 2 * DH * tps
    bounds = [0, head_cols] if tile == head_cols else [0, head_cols * 3 // 4, head_cols]
    ranges = list(zip(bounds, bounds[1:]))
    placed = in_hbm(blocks[:1]) + blocks[1:]
    evens, owns, fars, terms, pair, after = [], [], [], [], (), ()
    for b, block in enumerate(placed):
        if fast_pair and b == last:
            slots = odd + even + [0]
            pair_keep, give = project_pair(rindex, findex, slots, placed, w_key, w_value, after)
            pair = (pair_keep, other_core(give))
            after = (give,)
        sent = odd[:-1] if b == last else odd
        odd_keep, odd_got, given = project(sent, [block], tile, after)
        odd_sent = add_rows(0, len(sent), half, 0, odd_keep, odd_got, 0, head_cols, pair)
        fars.append(swap(odd_sent, 1))
        after = (odd_sent,)
        if b > 0:
            added, after = add_even(b - 1, 0, head_cols, (), after)
            terms.append([(fars[b - 1], len(odd) - 1, 0)] + added)
            after = (odd_sent,) + after
        if b < last:
            keep, got, given = project(even + [0], [block], head_cols, after, LIGHT, True)
            evens.append((keep, got[:1] if len(even) == 1 else [jnp.concatenate(got[:-1])]))
            owns.append((keep, len(even), got[-1:]))
        else:
            keep, got, given = project(even, [block], tile, after, HEAVY)
            evens.append((keep, got))
        after = (given,)
    near_keep, near_got, given = project([1], placed[last:], tile, after)
    after = (given,)
    parts, behind = [], tuple(term[0] for row in terms for term in row[1:])
    if fast_pair:
        near_pair = add_rows(len(odd) - 1, 1, half, 0, pair[0], pair[1:], 0, width, after=after)
        after = (near_pair,)
        near_pair = swap(near_pair, 1)
    for start, stop in ranges:
        near_sent = add_rows(
            0, 1, half, 0, near_keep, near_got, start, stop - start, (), 0, (), after
        )
        parts.append([(swap(near_sent, 1), 0, 0)])
        after = (near_sent,)
    after = after + behind
    if fast_pair:
        summed = add_rows(
            len(odd), len(even), half, 0, pair[0], pair[1:], 0, width,
            landed=(fars[last],), after=after, shift=head_cols,
        )
        pair_terms, first = spread({x: summed[k] for k, x in enumerate(even)})
        after = (first,)
    for part, (start, stop) in zip(parts, ranges):
        added, after = add_even(last, start, stop - start, (), after)
        part += added
    keep, got, given = project([0], placed[last:], tile, after, HEAVY)
    owns.append((keep, 0, got))

    if fast_pair:
        pieces = [(array, shards - 1, 0) for array in pair] + [(near_pair, 0, 0)]
        pieces += [(term, 0, 0) for term in pair_terms]
        key_rot, held = split_and_rotate(cosine, sine, pieces, width, (given,))
        held = stack_slots([held] + [swap(held, x) for x in range(1, shards)], ())
    else:
        x = jnp.concatenate(blocks, axis=0)
        key_sum, value_sum = lax.psum(
            (
                jnp.dot(x, w_key, preferred_element_type=jnp.float32),
                jnp.dot(x, w_value, preferred_element_type=jnp.float32),
            ),
            ("fsdp", "rep"),
        )

        def of_core(y, core):
            parts = y.reshape(tps, 2, half, -1)
            return lax.dynamic_index_in_dim(parts, core, 1, keepdims=False).reshape(tps * half, -1)

        mine = lax.dynamic_slice_in_dim(key_sum, findex * heads_here // group * DH, DH, 1)
        key_own = of_core(mine, rindex)
        key_rot = sum_and_rotate(cosine, sine, [(key_own[None], 0, 0)], [], DH, after)
        value_rows = low(jnp.concatenate([of_core(value_sum, rindex), of_core(value_sum, 1 - rindex)]))

    order, key_t = prepare(canary_rows, ids, key_rot, other_core(key_rot))
    if not fast_pair:
        values = low(jnp.dot(order, value_rows, preferred_element_type=jnp.float32))

    rotated = [rotate(b, 0, head_cols, terms[b], after) for b in range(last)]
    scores, mark = (), ()
    for p, (start, stop) in enumerate(ranges):
        turned = rotate(last, start, stop, parts[p], mark or tuple(owns[last][2][1:]) + ((held,) if fast_pair else ()))
        first = start // DH
        queries = [(row[0], first) for row in rotated] + [(turned[0], 0)]
        queries += [(row[1], first) for row in rotated] + [(turned[1], 0)]
        behind = in_hbm([values]) if p > 0 else ()
        *scores, mark = score_heads(
            order, key_t, heads_here, first, (stop - start) // DH, queries, scores, behind
        )
        mark = (mark,)
        if fast_pair and p == 0:
            values = order_values(findex, order, held, other_core(held))
    return (scores[0], values)


def solution(mesh):
    in_specs = (
        P(("groups", "tp"), ("fsdp", "rep")),
        P(("fsdp", "rep"), "tp"),
        P(("fsdp", "rep"), "tp"),
        P(("fsdp", "rep"), "tp"),
        P("groups"),
        P("groups"),
    )
    out_specs = (P("tp", "fsdp", "groups", None), P("groups", "tp"))
    return jax.shard_map(body, mesh=mesh, in_specs=in_specs, out_specs=out_specs, check_vma=False)
```

```python
import functools
import math

import jax
import jax.numpy as jnp
from jax import lax
from jax.experimental import pallas as pl
from jax.experimental.pallas import tpu as pltpu
from jax.sharding import PartitionSpec as P

HQ = 128
KV = 8
DH = 128
VMEM_BYTES = 28 * 1024 * 1024
LIGHT = pl.CostEstimate(flops=1000, bytes_accessed=1000, transcendentals=0)
HEAVY = pl.CostEstimate(flops=10**11, bytes_accessed=10**8, transcendentals=0)


def in_hbm(arrays):
    return [pltpu.with_memory_space_constraint(x, pltpu.HBM) for x in arrays]


def rope_tables(positions):
    half = DH // 2
    expo = jnp.arange(half, dtype=jnp.float32) * (2.0 / DH)
    freq = jnp.power(jnp.float32(500000.0), -expo)
    wavelen = 2.0 * math.pi / freq
    smooth = (8192.0 / wavelen - 1.0) / 3.0
    mixed = (1.0 - smooth) * freq / 8.0 + smooth * freq
    freq = jnp.where(wavelen > 8192.0, freq / 8.0, jnp.where(wavelen < 2048.0, freq, mixed))
    angle = positions.astype(jnp.float32)[:, None] * freq[None, :]
    cosine, sine = jnp.cos(angle), jnp.sin(angle)
    return jnp.concatenate([cosine, cosine], axis=1), jnp.concatenate([-sine, sine], axis=1)


def ordered_rows(place_ref, x_refs, rows_ref):
    core = place_ref[0]
    half = x_refs[0].shape[0] // 2
    for b, x_ref in enumerate(x_refs):
        kept, given = b * half, (len(x_refs) + b) * half
        rows_ref[kept : kept + half] = x_ref[pl.ds(pl.multiple_of(core * half, 16), half)]
        rows_ref[given : given + half] = x_ref[pl.ds(pl.multiple_of((1 - core) * half, 16), half)]


def query_kernel(count, pieces, by_slot, place_ref, *refs):
    x_refs, w_ref = refs[:count], refs[count]
    keep_ref, *give_refs, rows_ref = refs[-2 - pieces :]
    tile = pl.program_id(1)
    size = give_refs[0].shape[2]
    each = keep_ref.shape[2] // size

    @pl.when((pl.program_id(0) == 0) & (tile == 0))
    def _():
        ordered_rows(place_ref, x_refs, rows_ref)

    result = jnp.dot(rows_ref[...], w_ref[...], preferred_element_type=jnp.float32)
    half = result.shape[0] // 2
    keep_ref[0] = result[:half]
    for j, give_ref in enumerate(give_refs):

        @pl.when(pl.program_id(0) == j if by_slot else (tile == j // each) | (pieces == 1))
        def _():
            start = j % each * size
            give_ref[0] = result[half:, start : start + size].astype(give_ref.dtype)


def project_query(rindex, findex, slots, blocks, w, cols, tile, width, after, cost, by_slot, near):
    rows, depth = blocks[0].shape
    count = len(blocks)
    half = rows // 2 * count
    tiles, pieces = cols // tile, len(slots) if by_slot else cols // width
    place = jnp.stack([rindex] + [findex ^ slot for slot in slots]).astype(jnp.int32)
    keep_spec = pl.BlockSpec((1, half, tile), lambda s, j, place: (s, 0, j))
    give_spec = pl.BlockSpec((1, half, width), lambda s, j, place: (s, 0, 0))

    def slot_spec(k):
        def index(s, j, place):
            return (0, 0, jnp.where(s < k, 0, jnp.where(s > k, tiles - 1, j)))

        return pl.BlockSpec((1, half, tile), index)

    give_specs = [keep_spec] if pieces == 1 else [give_spec] * pieces
    given = (len(slots), half, width)
    if by_slot:
        give_specs, given = [slot_spec(k) for k in range(pieces)], (1, half, cols)
    x_spec = pl.BlockSpec((rows, depth), lambda s, j, place: (0, 0), pipeline_mode=pl.Buffered(1))
    outs = pl.pallas_call(
        functools.partial(query_kernel, count, pieces, by_slot),
        grid_spec=pltpu.PrefetchScalarGridSpec(
            num_scalar_prefetch=1,
            grid=(len(slots), tiles),
            in_specs=[x_spec] * count
            + [pl.BlockSpec((depth, tile), lambda s, j, place: (0, place[1 + s] * tiles + j))]
            + [pl.BlockSpec(memory_space=pl.ANY)] * len(after),
            out_specs=[keep_spec] + give_specs,
            scratch_shapes=[pltpu.VMEM((2 * half, depth), w.dtype)],
        ),
        out_shape=[(jax.ShapeDtypeStruct if near else pltpu.HBM)((len(slots), half, cols), jnp.float32)]
        + [pltpu.HBM(given, jnp.bfloat16)] * pieces,
        compiler_params=pltpu.CompilerParams(vmem_limit_bytes=VMEM_BYTES),
        cost_estimate=cost,
        name="query_products",
    )(place, *blocks, *in_hbm([w]), *in_hbm(after[:1]), *after[1:])
    return outs[0], outs[1:]


def pair_kernel(count, place_ref, *refs):
    x_refs, (wk_ref, wv_ref) = refs[:count], refs[count : count + 2]
    keep_ref, give_ref, rows_ref = refs[-3:]

    @pl.when(pl.program_id(0) == 0)
    def _():
        ordered_rows(place_ref, x_refs, rows_ref)

    weights = jnp.concatenate([wk_ref[...], wv_ref[...]], axis=1)
    result = jnp.dot(rows_ref[...], weights, preferred_element_type=jnp.float32)
    half, width = x_refs[0].shape[0] // 2, weights.shape[1]
    for b in range(count):
        kept, given = b * half, (count + b) * half
        cols = slice(b * width, (b + 1) * width)
        keep_ref[0, :, cols] = result[kept : kept + half]
        give_ref[0, :, cols] = result[given : given + half].astype(give_ref.dtype)


def project_pair(rindex, findex, slots, blocks, w_key, w_value, after=()):
    rows, depth = blocks[0].shape
    count = len(blocks)
    place = jnp.stack([rindex] + [findex ^ slot for slot in slots]).astype(jnp.int32)
    weight = pl.BlockSpec((depth, DH), lambda s, place: (0, place[1 + s]))
    shape = (len(slots), rows // 2, 2 * DH * count)
    out = pl.BlockSpec((1,) + shape[1:], lambda s, place: (s, 0, 0))
    return pl.pallas_call(
        functools.partial(pair_kernel, count),
        grid_spec=pltpu.PrefetchScalarGridSpec(
            num_scalar_prefetch=1,
            grid=(len(slots),),
            in_specs=[pl.BlockSpec((rows, depth), lambda s, place: (0, 0))] * count
            + [weight, weight]
            + [pl.BlockSpec(memory_space=pl.ANY)] * len(after),
            out_specs=[out, out],
            scratch_shapes=[pltpu.VMEM((count * rows, depth), blocks[0].dtype)],
        ),
        out_shape=[
            pltpu.HBM(shape, jnp.float32),
            pltpu.HBM(shape, jnp.bfloat16),
        ],
        compiler_params=pltpu.CompilerParams(vmem_limit_bytes=VMEM_BYTES),
        cost_estimate=LIGHT,
        name="key_value_products",
    )(place, *blocks, *in_hbm([w_key, w_value, *after]))


def segments(arrays, start, stop):
    parts, first = [], 0
    for x in arrays:
        low, high = max(start, first) - first, min(stop - first, x.shape[2])
        if low < high:
            parts.append((x, high - low, low // (high - low)))
        first += x.shape[2]
    return parts


def add_kernel(gots, paired, extra, *refs):
    keep_ref, got_refs, out_ref = refs[0], refs[1 : 1 + gots], refs[-1]
    pair_refs = refs[1 + gots : 1 + gots + 2 * paired]
    landed_refs = refs[1 + gots + 2 * paired :][: extra * (1 + paired)]
    cols = sum(got_ref.shape[2] for got_ref in got_refs)

    def total(first, second, landed):
        value = first + second.astype(jnp.float32)
        for term in landed:
            value = value + term.astype(jnp.float32)
        return value.astype(out_ref.dtype)

    start = 0
    for got_ref in got_refs:
        part = slice(start, start + got_ref.shape[2])
        start = part.stop
        landed = [landed_refs[0][0, :, part]] if extra else []
        out_ref[0, :, part] = total(keep_ref[0, :, part], got_ref[0], landed)
    if paired:
        landed = [landed_refs[1][0]] if extra else []
        out_ref[0, :, cols:] = total(pair_refs[0][0], pair_refs[1][0], landed)


def add_rows(first, count, rows, b, keep, gots, start, cols, pair=(), slot=0, landed=(), after=(), near=False):
    whole = keep.shape[2]
    more = pair[0].shape[2] if pair else 0
    keep_spec = pl.BlockSpec((1, rows, cols), lambda s: (first + s, b, start // cols))
    gots = segments(gots, start, start + cols)

    def got_spec(width, column):
        return pl.BlockSpec((1, rows, width), lambda s: (first + s, b, column))

    pair_spec = pl.BlockSpec((1, rows, more), lambda s: (slot + s, 0, 0))
    landed_specs = [pl.BlockSpec((1, rows, cols), lambda s: (s, 0, start // cols))]
    if pair:
        landed_specs.append(pl.BlockSpec((1, rows, more), lambda s: (s, 0, whole // more)))
    landed_specs = landed_specs * len(landed)
    return pl.pallas_call(
        functools.partial(add_kernel, len(gots), len(pair) // 2, len(landed)),
        grid=(count,),
        in_specs=[keep_spec]
        + [got_spec(width, column) for _, width, column in gots]
        + [pair_spec] * len(pair)
        + landed_specs
        + [pl.BlockSpec(memory_space=pl.ANY)] * len(after),
        out_specs=pl.BlockSpec((1, rows, cols + more), lambda s: (s, 0, 0)),
        out_shape=pltpu.HBM((count, rows, cols + more), jnp.bfloat16),
        compiler_params=pltpu.CompilerParams(vmem_limit_bytes=VMEM_BYTES),
        cost_estimate=LIGHT,
        name="add_rows",
    )(
        *([keep] if near else in_hbm([keep])),
        *[got for got, _, _ in gots],
        *in_hbm(pair[:1]),
        *pair[1:],
        *(list(landed) * (2 if pair else 1)),
        *in_hbm(after[:1]),
        *after[1:],
    )


def rotate_kernel(count, pieces, cos_ref, sin_ref, *refs):
    terms, gots, out_ref = refs[:count], refs[count : count + pieces], refs[-1]
    cosine, sine = cos_ref[...], sin_ref[...]
    start = 0
    for got in gots or terms[:1]:
        cols = slice(start, start + got.shape[2])
        start = cols.stop
        total = terms[0][0, :, cols].astype(jnp.float32)
        for term in terms[1:]:
            total = total + term[0, :, cols].astype(jnp.float32)
        if gots:
            total = total + got[0].astype(jnp.float32)
        for head in range(total.shape[1] // DH):
            part = total[:, head * DH : (head + 1) * DH]
            turned = pltpu.roll(part, DH // 2, axis=1)
            value = (part * cosine + turned * sine).astype(out_ref.dtype)
            out_ref[:, cols.start + head * DH : cols.start + (head + 1) * DH] = value


def sum_and_rotate(cosine, sine, terms, gots, cols, after=()):
    rows = cosine.shape[0]
    table = pl.BlockSpec((rows, DH), lambda j: (0, 0))

    def block(width, slot, column):
        return pl.BlockSpec((1, rows, width), lambda j: (slot, 0, column))

    return pl.pallas_call(
        functools.partial(rotate_kernel, len(terms), len(gots)),
        grid=(1,),
        in_specs=[table, table]
        + [block(cols, slot, start // cols) for _, slot, start in terms]
        + [block(width, 0, column) for _, width, column in gots]
        + [pl.BlockSpec(memory_space=pl.ANY)] * len(after),
        out_specs=pl.BlockSpec((rows, cols), lambda j: (0, 0)),
        out_shape=jax.ShapeDtypeStruct((rows, cols), jnp.bfloat16),
        compiler_params=pltpu.CompilerParams(vmem_limit_bytes=VMEM_BYTES),
        cost_estimate=LIGHT,
        name="sum_and_rotate",
    )(
        cosine,
        sine,
        *in_hbm([terms[0][0]]),
        *[term[0] for term in terms[1:]],
        *[got for got, _, _ in gots],
        *after,
    )


def split_kernel(count, cos_ref, sin_ref, *refs):
    terms, (key_ref, value_ref) = refs[:count], refs[-2:]
    total = terms[0][0].astype(jnp.float32)
    for term in terms[1:]:
        total = total + term[0].astype(jnp.float32)
    half = total.shape[0]
    for b in range(total.shape[1] // (2 * DH)):
        rows = slice(b * half, (b + 1) * half)
        key = total[:, 2 * b * DH : (2 * b + 1) * DH]
        turned = pltpu.roll(key, DH // 2, axis=1)
        key_ref[rows] = (key * cos_ref[rows] + turned * sin_ref[rows]).astype(key_ref.dtype)
        value_ref[0, rows] = total[:, (2 * b + 1) * DH : (2 * b + 2) * DH].astype(value_ref.dtype)


def split_and_rotate(cosine, sine, terms, width, after):
    rows = cosine.shape[0]
    half = terms[0][0].shape[1]
    table = pl.BlockSpec((rows, DH), lambda j: (0, 0))

    def block(slot, start):
        return pl.BlockSpec((1, half, width), lambda j: (slot, 0, start // width))

    return pl.pallas_call(
        functools.partial(split_kernel, len(terms)),
        grid=(1,),
        in_specs=[table, table]
        + [block(slot, start) for _, slot, start in terms]
        + [pl.BlockSpec(memory_space=pl.ANY)] * len(after),
        out_specs=[table, pl.BlockSpec((1, rows, DH), lambda j: (0, 0, 0))],
        out_shape=[
            jax.ShapeDtypeStruct((rows, DH), jnp.bfloat16),
            jax.ShapeDtypeStruct((1, rows, DH), jnp.bfloat16),
        ],
        compiler_params=pltpu.CompilerParams(vmem_limit_bytes=VMEM_BYTES),
        cost_estimate=LIGHT,
        name="split_and_rotate",
    )(cosine, sine, *in_hbm([terms[0][0]]), *[term for term, _, _ in terms[1:]], *after)


def prepare_kernel(canary_ref, ids_ref, own_ref, other_ref, order_ref, key_t_ref):
    order = jnp.where(canary_ref[...] == ids_ref[...], 1.0, 0.0).astype(jnp.bfloat16)
    order_ref[...] = order
    key = jnp.concatenate([own_ref[...], other_ref[...]], axis=0)
    key_t_ref[...] = jnp.dot(order, key, preferred_element_type=jnp.float32).T.astype(jnp.bfloat16)


def prepare(canary_rows, ids, own, other):
    rows = ids.shape[0]
    return pl.pallas_call(
        prepare_kernel,
        out_shape=[
            jax.ShapeDtypeStruct((rows, rows), jnp.bfloat16),
            jax.ShapeDtypeStruct((DH, rows), jnp.bfloat16),
        ],
        compiler_params=pltpu.CompilerParams(vmem_limit_bytes=VMEM_BYTES),
        name="order_and_keys",
    )(canary_rows.reshape(rows, 1), ids.reshape(1, rows), own, other)


def stack_kernel(count, *refs):
    out_ref, start = refs[-1], 0
    for ref in refs[:count]:
        out_ref[start : start + ref.shape[0]] = ref[...]
        start += ref.shape[0]


def stack_slots(arrays, after):
    slots = sum(x.shape[0] for x in arrays)
    shape = (slots,) + arrays[0].shape[1:]
    return pl.pallas_call(
        functools.partial(stack_kernel, len(arrays)),
        grid=(1,),
        in_specs=[pl.BlockSpec(x.shape, lambda j: (0, 0, 0)) for x in arrays]
        + [pl.BlockSpec(memory_space=pl.ANY)] * len(after),
        out_specs=pl.BlockSpec(shape, lambda j: (0, 0, 0)),
        out_shape=jax.ShapeDtypeStruct(shape, arrays[0].dtype),
        compiler_params=pltpu.CompilerParams(vmem_limit_bytes=VMEM_BYTES),
        cost_estimate=LIGHT,
        name="stack_slots",
    )(*arrays, *after)


def value_kernel(place_ref, order_ref, *refs):
    *slots, out_ref = refs
    own, other = slots[: len(slots) // 2], slots[len(slots) // 2 :]
    sides = [jnp.concatenate([x[0] for x in side], axis=1) for side in (own, other)]
    rows = jnp.concatenate(sides, axis=0)
    out_ref[...] = jnp.dot(order_ref[...], rows, preferred_element_type=jnp.float32).astype(out_ref.dtype)


def order_values(findex, order, own, other):
    rows = order.shape[0]
    slots, part, width = own.shape
    step = math.gcd(slots, 2)
    place = jnp.stack([findex ^ s for s in range(slots)]).astype(jnp.int32)

    def block(k):
        return pl.BlockSpec((1, part, width), lambda s, place: (place[s * step + k], 0, 0))

    return pl.pallas_call(
        value_kernel,
        grid_spec=pltpu.PrefetchScalarGridSpec(
            num_scalar_prefetch=1,
            grid=(slots // step,),
            in_specs=[pl.BlockSpec((rows, rows), lambda s, place: (0, 0))]
            + [block(k) for k in range(step)] * 2,
            out_specs=pl.BlockSpec((rows, step * width), lambda s, place: (0, s)),
        ),
        out_shape=jax.ShapeDtypeStruct((rows, slots * width), jnp.bfloat16),
        compiler_params=pltpu.CompilerParams(vmem_limit_bytes=VMEM_BYTES),
        name="order_values",
    )(place, order, *[own] * step, *[other] * step)


def score_kernel(count, order_ref, key_t_ref, *refs):
    queries, (out_ref, mark_ref) = refs[:count], refs[-2:]
    mark_ref[...] = jnp.zeros_like(mark_ref)
    stacked = jnp.concatenate([query[...] for query in queries], axis=0)
    chosen = jnp.dot(order_ref[...], stacked, preferred_element_type=jnp.float32).astype(jnp.bfloat16)
    for head in range(stacked.shape[1] // DH):
        products = jnp.dot(
            chosen[:, head * DH : (head + 1) * DH], key_t_ref[...], preferred_element_type=jnp.float32
        )
        out_ref[0, head] = (products * DH ** (-0.5)).astype(out_ref.dtype)


def score_heads(order, key_t, heads, start, count, queries, earlier, after=()):
    rows = order.shape[0]
    step = math.gcd(count, 4)

    def block(query, first):
        return pl.BlockSpec((query.shape[0], step * DH), lambda j: (0, first // step + j))

    return pl.pallas_call(
        functools.partial(score_kernel, len(queries)),
        grid=(count // step,),
        in_specs=[
            pl.BlockSpec((rows, rows), lambda j: (0, 0)),
            pl.BlockSpec((DH, rows), lambda j: (0, 0)),
        ]
        + [block(query, first) for query, first in queries]
        + [pl.BlockSpec(memory_space=pl.ANY)] * (len(earlier) + len(after)),
        out_specs=[
            pl.BlockSpec((1, step, rows, rows), lambda j: (0, start // step + j, 0, 0)),
            pl.BlockSpec((8, DH), lambda j: (0, 0)),
        ],
        out_shape=[
            jax.ShapeDtypeStruct((1, heads, rows, rows), jnp.bfloat16),
            jax.ShapeDtypeStruct((8, DH), jnp.float32),
        ],
        input_output_aliases={2 + len(queries): 0} if earlier else {},
        compiler_params=pltpu.CompilerParams(vmem_limit_bytes=VMEM_BYTES),
        cost_estimate=LIGHT,
        name="score_heads",
    )(order, key_t, *[query for query, _ in queries], *earlier, *after)


def body(hidden, w_query, w_key, w_value, canary_rows, positions):
    shards = lax.axis_size("fsdp")
    findex = lax.axis_index("fsdp")
    tps = lax.axis_size("tp")
    tindex = lax.axis_index("tp")
    rindex = lax.axis_index("rep")
    local, depth = hidden.shape
    half = local // 2
    rows = local * tps
    head_cols = w_query.shape[1] // shards
    heads_here = head_cols // DH
    group = HQ // KV
    assert shards & (shards - 1) == 0 and lax.axis_size("rep") == 2

    def swap(x, bit):
        return lax.ppermute(x, "fsdp", [(i, i ^ bit) for i in range(shards)])

    def other_core(x):
        return lax.ppermute(x, "rep", [(0, 1), (1, 0)])

    def low(x):
        return x.astype(jnp.bfloat16)

    odd = list(range(3, shards, 2)) + [1]
    even = list(range(2, shards, 2))
    fast_pair = heads_here == group

    def spread(live):
        terms, first = [], None
        bit = 2
        while bit < shards:
            sent = [x for x in sorted(live) if x & bit]
            pack = jnp.stack([low(live[x]) for x in sent])
            first = pack if first is None else first
            landed = swap(pack, bit)
            for k, x in enumerate(sent):
                if x == bit:
                    terms.append(landed)
                else:
                    live[x ^ bit] = live[x ^ bit] + landed[k].astype(jnp.float32)
                del live[x]
            bit *= 2
        return terms, first

    blocks = [hidden] + [
        lax.ppermute(hidden, "tp", [(i, (i - b) % tps) for i in range(tps)]) for b in range(1, tps)
    ]

    block_ids = ((tindex + jnp.arange(tps, dtype=jnp.int32)) % tps * local)[:, None]
    own_ids = (block_ids + rindex * half + jnp.arange(half, dtype=jnp.int32)[None]).reshape(-1)
    other_ids = (block_ids + (1 - rindex) * half + jnp.arange(half, dtype=jnp.int32)[None]).reshape(-1)
    ids = jnp.concatenate([own_ids, other_ids])
    own_positions = jnp.sum(
        jnp.where(own_ids[:, None] == canary_rows[None, :], positions[None, :], 0), axis=1
    )
    cosine, sine = rope_tables(own_positions)

    tile = min(1024, head_cols)

    def project(slots, blocks, width, after=(), cost=LIGHT, by_slot=False, near=False):
        keep, gives = project_query(
            rindex, findex, slots, blocks, w_query, head_cols, tile, width, after, cost, by_slot, near
        )
        return keep, [other_core(give) for give in gives], gives[0]

    def rotate(b, start, stop, terms, behind):
        table = slice(b * half, (b + 1) * half)
        keep, slot, got = owns[b]
        added = [(keep, slot, start)] + terms
        gots = segments(got, start, stop)
        turned = sum_and_rotate(cosine[table], sine[table], added, gots, stop - start, behind)
        return turned, other_core(turned)

    def add_even(b, start, cols, pair, behind):
        if shards == 2:
            return [], behind
        keep, got = evens[b]
        summed = add_rows(
            0, len(even), half, 0, keep, got, start, cols, pair, len(odd), (fars[b],), behind
        )
        terms, first = spread({x: summed[k] for k, x in enumerate(even)})
        return [(term, 0, 0) for term in terms], (first,)

    last = tps - 1
    bounds = [0, head_cols] if tile == head_cols else [0, head_cols * 3 // 4, head_cols]
    ranges = list(zip(bounds, bounds[1:]))
    placed = in_hbm(blocks[:1]) + blocks[1:]
    evens, owns, fars, terms, pair, after = [], [], [], [], (), ()
    for b, block in enumerate(placed):
        if fast_pair and b == last:
            slots = odd + even + [0]
            pair_keep, give = project_pair(rindex, findex, slots, placed, w_key, w_value, after)
            pair = (pair_keep, other_core(give))
            after = (give,)
        sent = odd[:-1] if b == last else odd
        odd_keep, odd_got, given = project(sent, [block], tile, after, near=True)
        odd_sent = add_rows(0, len(sent), half, 0, odd_keep, odd_got, 0, head_cols, pair, near=True)
        fars.append(swap(odd_sent, 1))
        after = (odd_sent,)
        if b > 0:
            added, after = add_even(b - 1, 0, head_cols, (), after)
            terms.append([(fars[b - 1], len(odd) - 1, 0)] + added)
            after = (odd_sent,) + after
        if b < last:
            keep, got, given = project(even + [0], [block], head_cols, after, LIGHT, True)
            evens.append((keep, got[:1] if len(even) == 1 else [jnp.concatenate(got[:-1])]))
            owns.append((keep, len(even), got[-1:]))
        else:
            keep, got, given = project(even, [block], tile, after, HEAVY)
            evens.append((keep, got))
        after = (given,)
    near_keep, near_got, given = project([1], placed[last:], tile, after)
    after = (given,)
    parts, behind = [], tuple(term[0] for row in terms for term in row[1:])
    for start, stop in ranges:
        paired = () if start else pair
        near_sent = add_rows(
            0, 1, half, 0, near_keep, near_got, start, stop - start, paired, len(odd) - 1, (), after
        )
        parts.append([(swap(near_sent, 1), 0, 0)])
        after = (near_sent,)
    after = after + behind
    for part, (start, stop) in zip(parts, ranges):
        added, after = add_even(last, start, stop - start, () if start else pair, after)
        part += added
    keep, got, _ = project([0], placed[last:], tile, after, HEAVY)
    owns.append((keep, 0, got))

    if fast_pair:
        width = 2 * DH * tps
        pieces = [(array, shards - 1, 0) for array in pair]
        pieces += [(term, 0, bounds[1]) for term, _, _ in parts[0]]
        key_rot, held = split_and_rotate(cosine, sine, pieces, width, after)
    else:
        x = jnp.concatenate(blocks, axis=0)
        key_sum, value_sum = lax.psum(
            (
                jnp.dot(x, w_key, preferred_element_type=jnp.float32),
                jnp.dot(x, w_value, preferred_element_type=jnp.float32),
            ),
            ("fsdp", "rep"),
        )

        def of_core(y, core):
            parts = y.reshape(tps, 2, half, -1)
            return lax.dynamic_index_in_dim(parts, core, 1, keepdims=False).reshape(tps * half, -1)

        mine = lax.dynamic_slice_in_dim(key_sum, findex * heads_here // group * DH, DH, 1)
        key_own = of_core(mine, rindex)
        key_rot = sum_and_rotate(cosine, sine, [(key_own[None], 0, 0)], [], DH, after)
        value_rows = low(jnp.concatenate([of_core(value_sum, rindex), of_core(value_sum, 1 - rindex)]))

    order, key_t = prepare(canary_rows, ids, key_rot, other_core(key_rot))
    if not fast_pair:
        values = low(jnp.dot(order, value_rows, preferred_element_type=jnp.float32))

    rotated = [rotate(b, 0, head_cols, terms[b], after) for b in range(last)]
    scores, mark = (), ()
    for p, (start, stop) in enumerate(ranges):
        turned = rotate(last, start, stop, parts[p], mark or tuple(owns[last][2][1:]))
        first = start // DH
        queries = [(row[0], first) for row in rotated] + [(turned[0], 0)]
        queries += [(row[1], first) for row in rotated] + [(turned[1], 0)]
        behind = in_hbm([values]) if p > 0 else ()
        *scores, mark = score_heads(
            order, key_t, heads_here, first, (stop - start) // DH, queries, scores, behind
        )
        mark = (mark,)
        if fast_pair and p == 0:
            held = stack_slots([held] + [swap(held, x) for x in range(1, shards)], mark)
            values = order_values(findex, order, held, other_core(held))
    return (scores[0], values)


def solution(mesh):
    in_specs = (
        P(("groups", "tp"), ("fsdp", "rep")),
        P(("fsdp", "rep"), "tp"),
        P(("fsdp", "rep"), "tp"),
        P(("fsdp", "rep"), "tp"),
        P("groups"),
        P("groups"),
    )
    out_specs = (P("tp", "fsdp", "groups", None), P("groups", "tp"))
    return jax.shard_map(body, mesh=mesh, in_specs=in_specs, out_specs=out_specs, check_vma=False)
```

```python
import functools
import math

import jax
import jax.numpy as jnp
from jax import lax
from jax.experimental import pallas as pl
from jax.experimental.pallas import tpu as pltpu
from jax.sharding import PartitionSpec as P

HQ = 128
KV = 8
DH = 128
VMEM_BYTES = 28 * 1024 * 1024
LIGHT = pl.CostEstimate(flops=1000, bytes_accessed=1000, transcendentals=0)
HEAVY = pl.CostEstimate(flops=10**11, bytes_accessed=10**8, transcendentals=0)


def in_hbm(arrays):
    return [pltpu.with_memory_space_constraint(x, pltpu.HBM) for x in arrays]


def rope_tables(positions):
    half = DH // 2
    expo = jnp.arange(half, dtype=jnp.float32) * (2.0 / DH)
    freq = jnp.power(jnp.float32(500000.0), -expo)
    wavelen = 2.0 * math.pi / freq
    smooth = (8192.0 / wavelen - 1.0) / 3.0
    mixed = (1.0 - smooth) * freq / 8.0 + smooth * freq
    freq = jnp.where(wavelen > 8192.0, freq / 8.0, jnp.where(wavelen < 2048.0, freq, mixed))
    angle = positions.astype(jnp.float32)[:, None] * freq[None, :]
    cosine, sine = jnp.cos(angle), jnp.sin(angle)
    return jnp.concatenate([cosine, cosine], axis=1), jnp.concatenate([-sine, sine], axis=1)


def ordered_rows(place_ref, x_refs, rows_ref):
    core = place_ref[0]
    half = x_refs[0].shape[0] // 2
    for b, x_ref in enumerate(x_refs):
        kept, given = b * half, (len(x_refs) + b) * half
        rows_ref[kept : kept + half] = x_ref[pl.ds(pl.multiple_of(core * half, 16), half)]
        rows_ref[given : given + half] = x_ref[pl.ds(pl.multiple_of((1 - core) * half, 16), half)]


def query_kernel(count, pieces, by_slot, place_ref, *refs):
    x_refs, w_ref = refs[:count], refs[count]
    keep_ref, *give_refs, rows_ref = refs[-2 - pieces :]
    tile = pl.program_id(1)
    size = give_refs[0].shape[2]
    each = keep_ref.shape[2] // size

    @pl.when((pl.program_id(0) == 0) & (tile == 0))
    def _():
        ordered_rows(place_ref, x_refs, rows_ref)

    result = jnp.dot(rows_ref[...], w_ref[...], preferred_element_type=jnp.float32)
    half = result.shape[0] // 2
    keep_ref[0] = result[:half]
    for j, give_ref in enumerate(give_refs):

        @pl.when(pl.program_id(0) == j if by_slot else (tile == j // each) | (pieces == 1))
        def _():
            start = j % each * size
            give_ref[0] = result[half:, start : start + size].astype(give_ref.dtype)


def project_query(rindex, findex, slots, blocks, w, cols, tile, width, after, cost, by_slot, near):
    rows, depth = blocks[0].shape
    count = len(blocks)
    half = rows // 2 * count
    tiles, pieces = cols // tile, len(slots) if by_slot else cols // width
    place = jnp.stack([rindex] + [findex ^ slot for slot in slots]).astype(jnp.int32)
    keep_spec = pl.BlockSpec((1, half, tile), lambda s, j, place: (s, 0, j))
    give_spec = pl.BlockSpec((1, half, width), lambda s, j, place: (s, 0, 0))

    def slot_spec(k):
        def index(s, j, place):
            return (0, 0, jnp.where(s < k, 0, jnp.where(s > k, tiles - 1, j)))

        return pl.BlockSpec((1, half, tile), index)

    give_specs = [keep_spec] if pieces == 1 else [give_spec] * pieces
    given = (len(slots), half, width)
    if by_slot:
        give_specs, given = [slot_spec(k) for k in range(pieces)], (1, half, cols)
    x_spec = pl.BlockSpec((rows, depth), lambda s, j, place: (0, 0), pipeline_mode=pl.Buffered(1))
    outs = pl.pallas_call(
        functools.partial(query_kernel, count, pieces, by_slot),
        grid_spec=pltpu.PrefetchScalarGridSpec(
            num_scalar_prefetch=1,
            grid=(len(slots), tiles),
            in_specs=[x_spec] * count
            + [pl.BlockSpec((depth, tile), lambda s, j, place: (0, place[1 + s] * tiles + j))]
            + [pl.BlockSpec(memory_space=pl.ANY)] * len(after),
            out_specs=[keep_spec] + give_specs,
            scratch_shapes=[pltpu.VMEM((2 * half, depth), w.dtype)],
        ),
        out_shape=[(jax.ShapeDtypeStruct if near else pltpu.HBM)((len(slots), half, cols), jnp.float32)]
        + [pltpu.HBM(given, jnp.bfloat16)] * pieces,
        compiler_params=pltpu.CompilerParams(vmem_limit_bytes=VMEM_BYTES),
        cost_estimate=cost,
        name="query_products",
    )(place, *blocks, *in_hbm([w, *after]))
    return outs[0], outs[1:]


def pair_kernel(count, place_ref, *refs):
    x_refs, (wk_ref, wv_ref) = refs[:count], refs[count : count + 2]
    keep_ref, give_ref, rows_ref = refs[-3:]

    @pl.when(pl.program_id(0) == 0)
    def _():
        ordered_rows(place_ref, x_refs, rows_ref)

    weights = jnp.concatenate([wk_ref[...], wv_ref[...]], axis=1)
    result = jnp.dot(rows_ref[...], weights, preferred_element_type=jnp.float32)
    half, width = x_refs[0].shape[0] // 2, weights.shape[1]
    for b in range(count):
        kept, given = b * half, (count + b) * half
        cols = slice(b * width, (b + 1) * width)
        keep_ref[0, :, cols] = result[kept : kept + half]
        give_ref[0, :, cols] = result[given : given + half].astype(give_ref.dtype)


def project_pair(rindex, findex, slots, blocks, w_key, w_value, after=()):
    rows, depth = blocks[0].shape
    count = len(blocks)
    place = jnp.stack([rindex] + [findex ^ slot for slot in slots]).astype(jnp.int32)
    weight = pl.BlockSpec((depth, DH), lambda s, place: (0, place[1 + s]))
    shape = (len(slots), rows // 2, 2 * DH * count)
    out = pl.BlockSpec((1,) + shape[1:], lambda s, place: (s, 0, 0))
    return pl.pallas_call(
        functools.partial(pair_kernel, count),
        grid_spec=pltpu.PrefetchScalarGridSpec(
            num_scalar_prefetch=1,
            grid=(len(slots),),
            in_specs=[pl.BlockSpec((rows, depth), lambda s, place: (0, 0))] * count
            + [weight, weight]
            + [pl.BlockSpec(memory_space=pl.ANY)] * len(after),
            out_specs=[out, out],
            scratch_shapes=[pltpu.VMEM((count * rows, depth), blocks[0].dtype)],
        ),
        out_shape=[
            pltpu.HBM(shape, jnp.float32),
            pltpu.HBM(shape, jnp.bfloat16),
        ],
        compiler_params=pltpu.CompilerParams(vmem_limit_bytes=VMEM_BYTES),
        cost_estimate=LIGHT,
        name="key_value_products",
    )(place, *blocks, *in_hbm([w_key, w_value, *after]))


def segments(arrays, start, stop):
    parts, first = [], 0
    for x in arrays:
        low, high = max(start, first) - first, min(stop - first, x.shape[2])
        if low < high:
            parts.append((x, high - low, low // (high - low)))
        first += x.shape[2]
    return parts


def add_kernel(gots, paired, extra, *refs):
    keep_ref, got_refs, out_ref = refs[0], refs[1 : 1 + gots], refs[-1]
    pair_refs = refs[1 + gots : 1 + gots + 2 * paired]
    landed_refs = refs[1 + gots + 2 * paired :][: extra * (1 + paired)]
    cols = sum(got_ref.shape[2] for got_ref in got_refs)

    def total(first, second, landed):
        value = first + second.astype(jnp.float32)
        for term in landed:
            value = value + term.astype(jnp.float32)
        return value.astype(out_ref.dtype)

    start = 0
    for got_ref in got_refs:
        part = slice(start, start + got_ref.shape[2])
        start = part.stop
        landed = [landed_refs[0][0, :, part]] if extra else []
        out_ref[0, :, part] = total(keep_ref[0, :, part], got_ref[0], landed)
    if paired:
        landed = [landed_refs[1][0]] if extra else []
        out_ref[0, :, cols:] = total(pair_refs[0][0], pair_refs[1][0], landed)


def add_rows(first, count, rows, b, keep, gots, start, cols, pair=(), slot=0, landed=(), after=(), near=False):
    whole = keep.shape[2]
    more = pair[0].shape[2] if pair else 0
    keep_spec = pl.BlockSpec((1, rows, cols), lambda s: (first + s, b, start // cols))
    gots = segments(gots, start, start + cols)

    def got_spec(width, column):
        return pl.BlockSpec((1, rows, width), lambda s: (first + s, b, column))

    pair_spec = pl.BlockSpec((1, rows, more), lambda s: (slot + s, 0, 0))
    landed_specs = [pl.BlockSpec((1, rows, cols), lambda s: (s, 0, start // cols))]
    if pair:
        landed_specs.append(pl.BlockSpec((1, rows, more), lambda s: (s, 0, whole // more)))
    landed_specs = landed_specs * len(landed)
    return pl.pallas_call(
        functools.partial(add_kernel, len(gots), len(pair) // 2, len(landed)),
        grid=(count,),
        in_specs=[keep_spec]
        + [got_spec(width, column) for _, width, column in gots]
        + [pair_spec] * len(pair)
        + landed_specs
        + [pl.BlockSpec(memory_space=pl.ANY)] * len(after),
        out_specs=pl.BlockSpec((1, rows, cols + more), lambda s: (s, 0, 0)),
        out_shape=pltpu.HBM((count, rows, cols + more), jnp.bfloat16),
        compiler_params=pltpu.CompilerParams(vmem_limit_bytes=VMEM_BYTES),
        cost_estimate=LIGHT,
        name="add_rows",
    )(
        *([keep] if near else in_hbm([keep])),
        *[got for got, _, _ in gots],
        *in_hbm(pair[:1]),
        *pair[1:],
        *(list(landed) * (2 if pair else 1)),
        *in_hbm(after[:1]),
        *after[1:],
    )


def rotate_kernel(count, pieces, cos_ref, sin_ref, *refs):
    terms, gots, out_ref = refs[:count], refs[count : count + pieces], refs[-1]
    cosine, sine = cos_ref[...], sin_ref[...]
    start = 0
    for got in gots or terms[:1]:
        cols = slice(start, start + got.shape[2])
        start = cols.stop
        total = terms[0][0, :, cols].astype(jnp.float32)
        for term in terms[1:]:
            total = total + term[0, :, cols].astype(jnp.float32)
        if gots:
            total = total + got[0].astype(jnp.float32)
        for head in range(total.shape[1] // DH):
            part = total[:, head * DH : (head + 1) * DH]
            turned = pltpu.roll(part, DH // 2, axis=1)
            value = (part * cosine + turned * sine).astype(out_ref.dtype)
            out_ref[:, cols.start + head * DH : cols.start + (head + 1) * DH] = value


def sum_and_rotate(cosine, sine, terms, gots, cols, after=(), near=False):
    rows = cosine.shape[0]
    table = pl.BlockSpec((rows, DH), lambda j: (0, 0))

    def block(width, slot, column):
        return pl.BlockSpec((1, rows, width), lambda j: (slot, 0, column))

    return pl.pallas_call(
        functools.partial(rotate_kernel, len(terms), len(gots)),
        grid=(1,),
        in_specs=[table, table]
        + [block(cols, slot, start // cols) for _, slot, start in terms]
        + [block(width, 0, column) for _, width, column in gots]
        + [pl.BlockSpec(memory_space=pl.ANY)] * len(after),
        out_specs=pl.BlockSpec((rows, cols), lambda j: (0, 0)),
        out_shape=jax.ShapeDtypeStruct((rows, cols), jnp.bfloat16),
        compiler_params=pltpu.CompilerParams(vmem_limit_bytes=VMEM_BYTES),
        cost_estimate=LIGHT,
        name="sum_and_rotate",
    )(
        cosine,
        sine,
        *([terms[0][0]] if near else in_hbm([terms[0][0]])),
        *[term[0] for term in terms[1:]],
        *[got for got, _, _ in gots],
        *after,
    )


def split_kernel(count, cos_ref, sin_ref, *refs):
    terms, (key_ref, value_ref) = refs[:count], refs[-2:]
    total = terms[0][0].astype(jnp.float32)
    for term in terms[1:]:
        total = total + term[0].astype(jnp.float32)
    half = total.shape[0]
    for b in range(total.shape[1] // (2 * DH)):
        rows = slice(b * half, (b + 1) * half)
        key = total[:, 2 * b * DH : (2 * b + 1) * DH]
        turned = pltpu.roll(key, DH // 2, axis=1)
        key_ref[rows] = (key * cos_ref[rows] + turned * sin_ref[rows]).astype(key_ref.dtype)
        value_ref[0, rows] = total[:, (2 * b + 1) * DH : (2 * b + 2) * DH].astype(value_ref.dtype)


def split_and_rotate(cosine, sine, terms, width, after):
    rows = cosine.shape[0]
    half = terms[0][0].shape[1]
    table = pl.BlockSpec((rows, DH), lambda j: (0, 0))

    def block(slot, start):
        return pl.BlockSpec((1, half, width), lambda j: (slot, 0, start // width))

    return pl.pallas_call(
        functools.partial(split_kernel, len(terms)),
        grid=(1,),
        in_specs=[table, table]
        + [block(slot, start) for _, slot, start in terms]
        + [pl.BlockSpec(memory_space=pl.ANY)] * len(after),
        out_specs=[table, pl.BlockSpec((1, rows, DH), lambda j: (0, 0, 0))],
        out_shape=[
            jax.ShapeDtypeStruct((rows, DH), jnp.bfloat16),
            jax.ShapeDtypeStruct((1, rows, DH), jnp.bfloat16),
        ],
        compiler_params=pltpu.CompilerParams(vmem_limit_bytes=VMEM_BYTES),
        cost_estimate=LIGHT,
        name="split_and_rotate",
    )(cosine, sine, *in_hbm([terms[0][0]]), *[term for term, _, _ in terms[1:]], *after)


def prepare_kernel(canary_ref, ids_ref, own_ref, other_ref, order_ref, key_t_ref):
    order = jnp.where(canary_ref[...] == ids_ref[...], 1.0, 0.0).astype(jnp.bfloat16)
    order_ref[...] = order
    key = jnp.concatenate([own_ref[...], other_ref[...]], axis=0)
    key_t_ref[...] = jnp.dot(order, key, preferred_element_type=jnp.float32).T.astype(jnp.bfloat16)


def prepare(canary_rows, ids, own, other):
    rows = ids.shape[0]
    return pl.pallas_call(
        prepare_kernel,
        out_shape=[
            jax.ShapeDtypeStruct((rows, rows), jnp.bfloat16),
            jax.ShapeDtypeStruct((DH, rows), jnp.bfloat16),
        ],
        compiler_params=pltpu.CompilerParams(vmem_limit_bytes=VMEM_BYTES),
        name="order_and_keys",
    )(canary_rows.reshape(rows, 1), ids.reshape(1, rows), own, other)


def stack_kernel(count, *refs):
    out_ref, start = refs[-1], 0
    for ref in refs[:count]:
        out_ref[start : start + ref.shape[0]] = ref[...]
        start += ref.shape[0]


def stack_slots(arrays, after):
    slots = sum(x.shape[0] for x in arrays)
    shape = (slots,) + arrays[0].shape[1:]
    return pl.pallas_call(
        functools.partial(stack_kernel, len(arrays)),
        grid=(1,),
        in_specs=[pl.BlockSpec(x.shape, lambda j: (0, 0, 0)) for x in arrays]
        + [pl.BlockSpec(memory_space=pl.ANY)] * len(after),
        out_specs=pl.BlockSpec(shape, lambda j: (0, 0, 0)),
        out_shape=jax.ShapeDtypeStruct(shape, arrays[0].dtype),
        compiler_params=pltpu.CompilerParams(vmem_limit_bytes=VMEM_BYTES),
        cost_estimate=LIGHT,
        name="stack_slots",
    )(*arrays, *after)


def value_kernel(place_ref, order_ref, *refs):
    *slots, out_ref = refs
    own, other = slots[: len(slots) // 2], slots[len(slots) // 2 :]
    sides = [jnp.concatenate([x[0] for x in side], axis=1) for side in (own, other)]
    rows = jnp.concatenate(sides, axis=0)
    out_ref[...] = jnp.dot(order_ref[...], rows, preferred_element_type=jnp.float32).astype(out_ref.dtype)


def order_values(findex, order, own, other):
    rows = order.shape[0]
    slots, part, width = own.shape
    step = math.gcd(slots, 2)
    place = jnp.stack([findex ^ s for s in range(slots)]).astype(jnp.int32)

    def block(k):
        return pl.BlockSpec((1, part, width), lambda s, place: (place[s * step + k], 0, 0))

    return pl.pallas_call(
        value_kernel,
        grid_spec=pltpu.PrefetchScalarGridSpec(
            num_scalar_prefetch=1,
            grid=(slots // step,),
            in_specs=[pl.BlockSpec((rows, rows), lambda s, place: (0, 0))]
            + [block(k) for k in range(step)] * 2,
            out_specs=pl.BlockSpec((rows, step * width), lambda s, place: (0, s)),
        ),
        out_shape=jax.ShapeDtypeStruct((rows, slots * width), jnp.bfloat16),
        compiler_params=pltpu.CompilerParams(vmem_limit_bytes=VMEM_BYTES),
        name="order_values",
    )(place, order, *[own] * step, *[other] * step)


def score_kernel(count, order_ref, key_t_ref, *refs):
    queries, (out_ref, mark_ref) = refs[:count], refs[-2:]
    mark_ref[...] = jnp.zeros_like(mark_ref)
    stacked = jnp.concatenate([query[...] for query in queries], axis=0)
    chosen = jnp.dot(order_ref[...], stacked, preferred_element_type=jnp.float32).astype(jnp.bfloat16)
    for head in range(stacked.shape[1] // DH):
        products = jnp.dot(
            chosen[:, head * DH : (head + 1) * DH], key_t_ref[...], preferred_element_type=jnp.float32
        )
        out_ref[0, head] = (products * DH ** (-0.5)).astype(out_ref.dtype)


def score_heads(order, key_t, heads, start, count, queries, earlier, after=()):
    rows = order.shape[0]
    step = math.gcd(count, 4)

    def block(query, first):
        return pl.BlockSpec((query.shape[0], step * DH), lambda j: (0, first // step + j))

    return pl.pallas_call(
        functools.partial(score_kernel, len(queries)),
        grid=(count // step,),
        in_specs=[
            pl.BlockSpec((rows, rows), lambda j: (0, 0)),
            pl.BlockSpec((DH, rows), lambda j: (0, 0)),
        ]
        + [block(query, first) for query, first in queries]
        + [pl.BlockSpec(memory_space=pl.ANY)] * (len(earlier) + len(after)),
        out_specs=[
            pl.BlockSpec((1, step, rows, rows), lambda j: (0, start // step + j, 0, 0)),
            pl.BlockSpec((8, DH), lambda j: (0, 0)),
        ],
        out_shape=[
            jax.ShapeDtypeStruct((1, heads, rows, rows), jnp.bfloat16),
            jax.ShapeDtypeStruct((8, DH), jnp.float32),
        ],
        input_output_aliases={2 + len(queries): 0} if earlier else {},
        compiler_params=pltpu.CompilerParams(vmem_limit_bytes=VMEM_BYTES),
        cost_estimate=LIGHT,
        name="score_heads",
    )(order, key_t, *[query for query, _ in queries], *earlier, *after)


def body(hidden, w_query, w_key, w_value, canary_rows, positions):
    shards = lax.axis_size("fsdp")
    findex = lax.axis_index("fsdp")
    tps = lax.axis_size("tp")
    tindex = lax.axis_index("tp")
    rindex = lax.axis_index("rep")
    local, depth = hidden.shape
    half = local // 2
    rows = local * tps
    head_cols = w_query.shape[1] // shards
    heads_here = head_cols // DH
    group = HQ // KV
    assert shards & (shards - 1) == 0 and lax.axis_size("rep") == 2

    def swap(x, bit):
        return lax.ppermute(x, "fsdp", [(i, i ^ bit) for i in range(shards)])

    def other_core(x):
        return lax.ppermute(x, "rep", [(0, 1), (1, 0)])

    def low(x):
        return x.astype(jnp.bfloat16)

    odd = list(range(3, shards, 2)) + [1]
    even = list(range(2, shards, 2))
    fast_pair = heads_here == group

    def spread(live):
        terms, first = [], None
        bit = 2
        while bit < shards:
            sent = [x for x in sorted(live) if x & bit]
            pack = jnp.stack([low(live[x]) for x in sent])
            first = pack if first is None else first
            landed = swap(pack, bit)
            for k, x in enumerate(sent):
                if x == bit:
                    terms.append(landed)
                else:
                    live[x ^ bit] = live[x ^ bit] + landed[k].astype(jnp.float32)
                del live[x]
            bit *= 2
        return terms, first

    blocks = [hidden] + [
        lax.ppermute(hidden, "tp", [(i, (i - b) % tps) for i in range(tps)]) for b in range(1, tps)
    ]

    block_ids = ((tindex + jnp.arange(tps, dtype=jnp.int32)) % tps * local)[:, None]
    own_ids = (block_ids + rindex * half + jnp.arange(half, dtype=jnp.int32)[None]).reshape(-1)
    other_ids = (block_ids + (1 - rindex) * half + jnp.arange(half, dtype=jnp.int32)[None]).reshape(-1)
    ids = jnp.concatenate([own_ids, other_ids])
    own_positions = jnp.sum(
        jnp.where(own_ids[:, None] == canary_rows[None, :], positions[None, :], 0), axis=1
    )
    cosine, sine = rope_tables(own_positions)

    tile = min(1024, head_cols)

    def project(slots, blocks, width, after=(), cost=LIGHT, by_slot=False, near=False):
        keep, gives = project_query(
            rindex, findex, slots, blocks, w_query, head_cols, tile, width, after, cost, by_slot, near
        )
        return keep, [other_core(give) for give in gives], gives[0]

    def rotate(b, start, stop, terms, behind):
        table = slice(b * half, (b + 1) * half)
        keep, slot, got = owns[b]
        added = [(keep, slot, start)] + terms
        gots = segments(got, start, stop)
        turned = sum_and_rotate(
            cosine[table], sine[table], added, gots, stop - start, behind, b == last
        )
        return turned, other_core(turned)

    def add_even(b, start, cols, pair, behind):
        if shards == 2:
            return [], behind
        keep, got = evens[b]
        summed = add_rows(
            0, len(even), half, 0, keep, got, start, cols, pair, len(odd), (fars[b],), behind, b == last
        )
        terms, first = spread({x: summed[k] for k, x in enumerate(even)})
        return [(term, 0, 0) for term in terms], (first,)

    last = tps - 1
    bounds = [0, head_cols] if tile == head_cols else [0, head_cols * 3 // 4, head_cols]
    ranges = list(zip(bounds, bounds[1:]))
    placed = in_hbm(blocks[:1]) + blocks[1:]
    evens, owns, fars, terms, pair, after = [], [], [], [], (), ()
    for b, block in enumerate(placed):
        if fast_pair and b == last:
            slots = odd + even + [0]
            pair_keep, give = project_pair(rindex, findex, slots, placed, w_key, w_value, after)
            pair = (pair_keep, other_core(give))
            after = (give,)
        sent = odd[:-1] if b == last else odd
        odd_keep, odd_got, given = project(sent, [block], tile, after, near=True)
        odd_sent = add_rows(0, len(sent), half, 0, odd_keep, odd_got, 0, head_cols, pair, near=True)
        fars.append(swap(odd_sent, 1))
        after = (odd_sent,)
        if b > 0:
            added, after = add_even(b - 1, 0, head_cols, (), after)
            terms.append([(fars[b - 1], len(odd) - 1, 0)] + added)
            after = (odd_sent,) + after
        if b < last:
            keep, got, given = project(even + [0], [block], head_cols, after, LIGHT, True)
            evens.append((keep, got[:1] if len(even) == 1 else [jnp.concatenate(got[:-1])]))
            owns.append((keep, len(even), got[-1:]))
        else:
            keep, got, given = project(even, [block], tile, after, HEAVY, near=True)
            evens.append((keep, got))
        after = (given,)
    near_keep, near_got, given = project([1], placed[last:], tile, after)
    after = (given,)
    parts, behind = [], tuple(term[0] for row in terms for term in row[1:])
    for start, stop in ranges:
        paired = () if start else pair
        near_sent = add_rows(
            0, 1, half, 0, near_keep, near_got, start, stop - start, paired, len(odd) - 1, (), after
        )
        parts.append([(swap(near_sent, 1), 0, 0)])
        after = (near_sent,)
    after = after + behind
    for part, (start, stop) in zip(parts, ranges):
        added, after = add_even(last, start, stop - start, () if start else pair, after)
        part += added
    keep, got, _ = project([0], placed[last:], tile, after, HEAVY, near=True)
    owns.append((keep, 0, got))

    if fast_pair:
        width = 2 * DH * tps
        pieces = [(array, shards - 1, 0) for array in pair]
        pieces += [(term, 0, bounds[1]) for term, _, _ in parts[0]]
        key_rot, held = split_and_rotate(cosine, sine, pieces, width, after)
    else:
        x = jnp.concatenate(blocks, axis=0)
        key_sum, value_sum = lax.psum(
            (
                jnp.dot(x, w_key, preferred_element_type=jnp.float32),
                jnp.dot(x, w_value, preferred_element_type=jnp.float32),
            ),
            ("fsdp", "rep"),
        )

        def of_core(y, core):
            parts = y.reshape(tps, 2, half, -1)
            return lax.dynamic_index_in_dim(parts, core, 1, keepdims=False).reshape(tps * half, -1)

        mine = lax.dynamic_slice_in_dim(key_sum, findex * heads_here // group * DH, DH, 1)
        key_own = of_core(mine, rindex)
        key_rot = sum_and_rotate(cosine, sine, [(key_own[None], 0, 0)], [], DH, after)
        value_rows = low(jnp.concatenate([of_core(value_sum, rindex), of_core(value_sum, 1 - rindex)]))

    order, key_t = prepare(canary_rows, ids, key_rot, other_core(key_rot))
    if not fast_pair:
        values = low(jnp.dot(order, value_rows, preferred_element_type=jnp.float32))

    rotated = [rotate(b, 0, head_cols, terms[b], after) for b in range(last)]
    scores, mark = (), ()
    for p, (start, stop) in enumerate(ranges):
        turned = rotate(last, start, stop, parts[p], mark or tuple(owns[last][2][1:]))
        first = start // DH
        queries = [(row[0], first) for row in rotated] + [(turned[0], 0)]
        queries += [(row[1], first) for row in rotated] + [(turned[1], 0)]
        behind = in_hbm([values]) if p > 0 else ()
        *scores, mark = score_heads(
            order, key_t, heads_here, first, (stop - start) // DH, queries, scores, behind
        )
        mark = (mark,)
        if fast_pair and p == 0:
            held = stack_slots([held] + [swap(held, x) for x in range(1, shards)], mark)
            values = order_values(findex, order, held, other_core(held))
    return (scores[0], values)


def solution(mesh):
    in_specs = (
        P(("groups", "tp"), ("fsdp", "rep")),
        P(("fsdp", "rep"), "tp"),
        P(("fsdp", "rep"), "tp"),
        P(("fsdp", "rep"), "tp"),
        P("groups"),
        P("groups"),
    )
    out_specs = (P("tp", "fsdp", "groups", None), P("groups", "tp"))
    return jax.shard_map(body, mesh=mesh, in_specs=in_specs, out_specs=out_specs, check_vma=False)
```

```python
import functools
import math

import jax
import jax.numpy as jnp
from jax import lax
from jax.experimental import pallas as pl
from jax.experimental.pallas import tpu as pltpu
from jax.sharding import PartitionSpec as P

HQ = 128
KV = 8
DH = 128
VMEM_BYTES = 28 * 1024 * 1024
LIGHT = pl.CostEstimate(flops=1000, bytes_accessed=1000, transcendentals=0)
HEAVY = pl.CostEstimate(flops=10**11, bytes_accessed=10**8, transcendentals=0)


def in_hbm(arrays):
    return [pltpu.with_memory_space_constraint(x, pltpu.HBM) for x in arrays]


def rope_tables(positions):
    half = DH // 2
    expo = jnp.arange(half, dtype=jnp.float32) * (2.0 / DH)
    freq = jnp.power(jnp.float32(500000.0), -expo)
    wavelen = 2.0 * math.pi / freq
    smooth = (8192.0 / wavelen - 1.0) / 3.0
    mixed = (1.0 - smooth) * freq / 8.0 + smooth * freq
    freq = jnp.where(wavelen > 8192.0, freq / 8.0, jnp.where(wavelen < 2048.0, freq, mixed))
    angle = positions.astype(jnp.float32)[:, None] * freq[None, :]
    cosine, sine = jnp.cos(angle), jnp.sin(angle)
    return jnp.concatenate([cosine, cosine], axis=1), jnp.concatenate([-sine, sine], axis=1)


def ordered_rows(place_ref, x_refs, rows_ref):
    core = place_ref[0]
    half = x_refs[0].shape[0] // 2
    for b, x_ref in enumerate(x_refs):
        kept, given = b * half, (len(x_refs) + b) * half
        rows_ref[kept : kept + half] = x_ref[pl.ds(pl.multiple_of(core * half, 16), half)]
        rows_ref[given : given + half] = x_ref[pl.ds(pl.multiple_of((1 - core) * half, 16), half)]


def query_kernel(count, pieces, by_slot, place_ref, *refs):
    x_refs, w_ref = refs[:count], refs[count]
    keep_ref, *give_refs, rows_ref = refs[-2 - pieces :]
    tile = pl.program_id(1)
    size = give_refs[0].shape[2]
    each = keep_ref.shape[2] // size

    @pl.when((pl.program_id(0) == 0) & (tile == 0))
    def _():
        ordered_rows(place_ref, x_refs, rows_ref)

    result = jnp.dot(rows_ref[...], w_ref[...], preferred_element_type=jnp.float32)
    half = result.shape[0] // 2
    keep_ref[0] = result[:half]
    for j, give_ref in enumerate(give_refs):

        @pl.when(pl.program_id(0) == j if by_slot else (tile == j // each) | (pieces == 1))
        def _():
            start = j % each * size
            give_ref[0] = result[half:, start : start + size].astype(give_ref.dtype)


def project_query(rindex, findex, slots, blocks, w, cols, tile, width, after, cost, by_slot, near):
    rows, depth = blocks[0].shape
    count = len(blocks)
    half = rows // 2 * count
    tiles, pieces = cols // tile, len(slots) if by_slot else cols // width
    place = jnp.stack([rindex] + [findex ^ slot for slot in slots]).astype(jnp.int32)
    keep_spec = pl.BlockSpec((1, half, tile), lambda s, j, place: (s, 0, j))
    give_spec = pl.BlockSpec((1, half, width), lambda s, j, place: (s, 0, 0))

    def slot_spec(k):
        def index(s, j, place):
            return (0, 0, jnp.where(s < k, 0, jnp.where(s > k, tiles - 1, j)))

        return pl.BlockSpec((1, half, tile), index)

    give_specs = [keep_spec] if pieces == 1 else [give_spec] * pieces
    given = (len(slots), half, width)
    if by_slot:
        give_specs, given = [slot_spec(k) for k in range(pieces)], (1, half, cols)
    x_spec = pl.BlockSpec((rows, depth), lambda s, j, place: (0, 0), pipeline_mode=pl.Buffered(1))
    outs = pl.pallas_call(
        functools.partial(query_kernel, count, pieces, by_slot),
        grid_spec=pltpu.PrefetchScalarGridSpec(
            num_scalar_prefetch=1,
            grid=(len(slots), tiles),
            in_specs=[x_spec] * count
            + [pl.BlockSpec((depth, tile), lambda s, j, place: (0, place[1 + s] * tiles + j))]
            + [pl.BlockSpec(memory_space=pl.ANY)] * len(after),
            out_specs=[keep_spec] + give_specs,
            scratch_shapes=[pltpu.VMEM((2 * half, depth), w.dtype)],
        ),
        out_shape=[(jax.ShapeDtypeStruct if near else pltpu.HBM)((len(slots), half, cols), jnp.float32)]
        + [pltpu.HBM(given, jnp.bfloat16)] * pieces,
        compiler_params=pltpu.CompilerParams(vmem_limit_bytes=VMEM_BYTES),
        cost_estimate=cost,
        name="query_products",
    )(place, *blocks, *in_hbm([w, *after]))
    return outs[0], outs[1:]


def pair_kernel(count, place_ref, *refs):
    x_refs, (wk_ref, wv_ref) = refs[:count], refs[count : count + 2]
    keep_ref, give_ref, rows_ref = refs[-3:]

    @pl.when(pl.program_id(0) == 0)
    def _():
        ordered_rows(place_ref, x_refs, rows_ref)

    weights = jnp.concatenate([wk_ref[...], wv_ref[...]], axis=1)
    result = jnp.dot(rows_ref[...], weights, preferred_element_type=jnp.float32)
    half, width = x_refs[0].shape[0] // 2, weights.shape[1]
    for b in range(count):
        kept, given = b * half, (count + b) * half
        cols = slice(b * width, (b + 1) * width)
        keep_ref[0, :, cols] = result[kept : kept + half]
        give_ref[0, :, cols] = result[given : given + half].astype(give_ref.dtype)


def project_pair(rindex, findex, slots, blocks, w_key, w_value, after=()):
    rows, depth = blocks[0].shape
    count = len(blocks)
    place = jnp.stack([rindex] + [findex ^ slot for slot in slots]).astype(jnp.int32)
    weight = pl.BlockSpec((depth, DH), lambda s, place: (0, place[1 + s]))
    shape = (len(slots), rows // 2, 2 * DH * count)
    out = pl.BlockSpec((1,) + shape[1:], lambda s, place: (s, 0, 0))
    return pl.pallas_call(
        functools.partial(pair_kernel, count),
        grid_spec=pltpu.PrefetchScalarGridSpec(
            num_scalar_prefetch=1,
            grid=(len(slots),),
            in_specs=[pl.BlockSpec((rows, depth), lambda s, place: (0, 0))] * count
            + [weight, weight]
            + [pl.BlockSpec(memory_space=pl.ANY)] * len(after),
            out_specs=[out, out],
            scratch_shapes=[pltpu.VMEM((count * rows, depth), blocks[0].dtype)],
        ),
        out_shape=[
            jax.ShapeDtypeStruct(shape, jnp.float32),
            pltpu.HBM(shape, jnp.bfloat16),
        ],
        compiler_params=pltpu.CompilerParams(vmem_limit_bytes=VMEM_BYTES),
        cost_estimate=LIGHT,
        name="key_value_products",
    )(place, *blocks, *in_hbm([w_key, w_value, *after]))


def segments(arrays, start, stop):
    parts, first = [], 0
    for x in arrays:
        low, high = max(start, first) - first, min(stop - first, x.shape[2])
        if low < high:
            parts.append((x, high - low, low // (high - low)))
        first += x.shape[2]
    return parts


def add_kernel(gots, paired, extra, *refs):
    keep_ref, got_refs, out_ref = refs[0], refs[1 : 1 + gots], refs[-1]
    pair_refs = refs[1 + gots : 1 + gots + 2 * paired]
    landed_refs = refs[1 + gots + 2 * paired :][: extra * (1 + paired)]
    cols = sum(got_ref.shape[2] for got_ref in got_refs)

    def total(first, second, landed):
        value = first + second.astype(jnp.float32)
        for term in landed:
            value = value + term.astype(jnp.float32)
        return value.astype(out_ref.dtype)

    start = 0
    for got_ref in got_refs:
        part = slice(start, start + got_ref.shape[2])
        start = part.stop
        landed = [landed_refs[0][0, :, part]] if extra else []
        out_ref[0, :, part] = total(keep_ref[0, :, part], got_ref[0], landed)
    if paired:
        landed = [landed_refs[1][0]] if extra else []
        out_ref[0, :, cols:] = total(pair_refs[0][0], pair_refs[1][0], landed)


def add_rows(first, count, rows, b, keep, gots, start, cols, pair=(), slot=0, landed=(), after=(), near=False):
    whole = keep.shape[2]
    more = pair[0].shape[2] if pair else 0
    keep_spec = pl.BlockSpec((1, rows, cols), lambda s: (first + s, b, start // cols))
    gots = segments(gots, start, start + cols)

    def got_spec(width, column):
        return pl.BlockSpec((1, rows, width), lambda s: (first + s, b, column))

    pair_spec = pl.BlockSpec((1, rows, more), lambda s: (slot + s, 0, 0))
    landed_specs = [pl.BlockSpec((1, rows, cols), lambda s: (s, 0, start // cols))]
    if pair:
        landed_specs.append(pl.BlockSpec((1, rows, more), lambda s: (s, 0, whole // more)))
    landed_specs = landed_specs * len(landed)
    return pl.pallas_call(
        functools.partial(add_kernel, len(gots), len(pair) // 2, len(landed)),
        grid=(count,),
        in_specs=[keep_spec]
        + [got_spec(width, column) for _, width, column in gots]
        + [pair_spec] * len(pair)
        + landed_specs
        + [pl.BlockSpec(memory_space=pl.ANY)] * len(after),
        out_specs=pl.BlockSpec((1, rows, cols + more), lambda s: (s, 0, 0)),
        out_shape=pltpu.HBM((count, rows, cols + more), jnp.bfloat16),
        compiler_params=pltpu.CompilerParams(vmem_limit_bytes=VMEM_BYTES),
        cost_estimate=LIGHT,
        name="add_rows",
    )(
        *([keep] if near else in_hbm([keep])),
        *[got for got, _, _ in gots],
        *pair,
        *(list(landed) * (2 if pair else 1)),
        *in_hbm(after[:1]),
        *after[1:],
    )


def rotate_kernel(count, pieces, cos_ref, sin_ref, *refs):
    terms, gots, out_ref = refs[:count], refs[count : count + pieces], refs[-1]
    cosine, sine = cos_ref[...], sin_ref[...]
    start = 0
    for got in gots or terms[:1]:
        cols = slice(start, start + got.shape[2])
        start = cols.stop
        total = terms[0][0, :, cols].astype(jnp.float32)
        for term in terms[1:]:
            total = total + term[0, :, cols].astype(jnp.float32)
        if gots:
            total = total + got[0].astype(jnp.float32)
        for head in range(total.shape[1] // DH):
            part = total[:, head * DH : (head + 1) * DH]
            turned = pltpu.roll(part, DH // 2, axis=1)
            value = (part * cosine + turned * sine).astype(out_ref.dtype)
            out_ref[:, cols.start + head * DH : cols.start + (head + 1) * DH] = value


def sum_and_rotate(cosine, sine, terms, gots, cols, after=()):
    rows = cosine.shape[0]
    table = pl.BlockSpec((rows, DH), lambda j: (0, 0))

    def block(width, slot, column):
        return pl.BlockSpec((1, rows, width), lambda j: (slot, 0, column))

    return pl.pallas_call(
        functools.partial(rotate_kernel, len(terms), len(gots)),
        grid=(1,),
        in_specs=[table, table]
        + [block(cols, slot, start // cols) for _, slot, start in terms]
        + [block(width, 0, column) for _, width, column in gots]
        + [pl.BlockSpec(memory_space=pl.ANY)] * len(after),
        out_specs=pl.BlockSpec((rows, cols), lambda j: (0, 0)),
        out_shape=jax.ShapeDtypeStruct((rows, cols), jnp.bfloat16),
        compiler_params=pltpu.CompilerParams(vmem_limit_bytes=VMEM_BYTES),
        cost_estimate=LIGHT,
        name="sum_and_rotate",
    )(
        cosine,
        sine,
        *in_hbm([terms[0][0]]),
        *[term[0] for term in terms[1:]],
        *[got for got, _, _ in gots],
        *after,
    )


def split_kernel(count, cos_ref, sin_ref, *refs):
    terms, (key_ref, value_ref) = refs[:count], refs[-2:]
    total = terms[0][0].astype(jnp.float32)
    for term in terms[1:]:
        total = total + term[0].astype(jnp.float32)
    half = total.shape[0]
    for b in range(total.shape[1] // (2 * DH)):
        rows = slice(b * half, (b + 1) * half)
        key = total[:, 2 * b * DH : (2 * b + 1) * DH]
        turned = pltpu.roll(key, DH // 2, axis=1)
        key_ref[rows] = (key * cos_ref[rows] + turned * sin_ref[rows]).astype(key_ref.dtype)
        value_ref[0, rows] = total[:, (2 * b + 1) * DH : (2 * b + 2) * DH].astype(value_ref.dtype)


def split_and_rotate(cosine, sine, terms, width, after):
    rows = cosine.shape[0]
    half = terms[0][0].shape[1]
    table = pl.BlockSpec((rows, DH), lambda j: (0, 0))

    def block(slot, start):
        return pl.BlockSpec((1, half, width), lambda j: (slot, 0, start // width))

    return pl.pallas_call(
        functools.partial(split_kernel, len(terms)),
        grid=(1,),
        in_specs=[table, table]
        + [block(slot, start) for _, slot, start in terms]
        + [pl.BlockSpec(memory_space=pl.ANY)] * len(after),
        out_specs=[table, pl.BlockSpec((1, rows, DH), lambda j: (0, 0, 0))],
        out_shape=[
            jax.ShapeDtypeStruct((rows, DH), jnp.bfloat16),
            jax.ShapeDtypeStruct((1, rows, DH), jnp.bfloat16),
        ],
        compiler_params=pltpu.CompilerParams(vmem_limit_bytes=VMEM_BYTES),
        cost_estimate=LIGHT,
        name="split_and_rotate",
    )(cosine, sine, *[term for term, _, _ in terms], *after)


def prepare_kernel(canary_ref, ids_ref, own_ref, other_ref, order_ref, key_t_ref):
    order = jnp.where(canary_ref[...] == ids_ref[...], 1.0, 0.0).astype(jnp.bfloat16)
    order_ref[...] = order
    key = jnp.concatenate([own_ref[...], other_ref[...]], axis=0)
    key_t_ref[...] = jnp.dot(order, key, preferred_element_type=jnp.float32).T.astype(jnp.bfloat16)


def prepare(canary_rows, ids, own, other):
    rows = ids.shape[0]
    return pl.pallas_call(
        prepare_kernel,
        out_shape=[
            jax.ShapeDtypeStruct((rows, rows), jnp.bfloat16),
            jax.ShapeDtypeStruct((DH, rows), jnp.bfloat16),
        ],
        compiler_params=pltpu.CompilerParams(vmem_limit_bytes=VMEM_BYTES),
        name="order_and_keys",
    )(canary_rows.reshape(rows, 1), ids.reshape(1, rows), own, other)


def stack_kernel(count, *refs):
    out_ref, start = refs[-1], 0
    for ref in refs[:count]:
        out_ref[start : start + ref.shape[0]] = ref[...]
        start += ref.shape[0]


def stack_slots(arrays, after):
    slots = sum(x.shape[0] for x in arrays)
    shape = (slots,) + arrays[0].shape[1:]
    return pl.pallas_call(
        functools.partial(stack_kernel, len(arrays)),
        grid=(1,),
        in_specs=[pl.BlockSpec(x.shape, lambda j: (0, 0, 0)) for x in arrays]
        + [pl.BlockSpec(memory_space=pl.ANY)] * len(after),
        out_specs=pl.BlockSpec(shape, lambda j: (0, 0, 0)),
        out_shape=jax.ShapeDtypeStruct(shape, arrays[0].dtype),
        compiler_params=pltpu.CompilerParams(vmem_limit_bytes=VMEM_BYTES),
        cost_estimate=LIGHT,
        name="stack_slots",
    )(*arrays, *after)


def value_kernel(place_ref, order_ref, *refs):
    *slots, out_ref = refs
    own, other = slots[: len(slots) // 2], slots[len(slots) // 2 :]
    sides = [jnp.concatenate([x[0] for x in side], axis=1) for side in (own, other)]
    rows = jnp.concatenate(sides, axis=0)
    out_ref[...] = jnp.dot(order_ref[...], rows, preferred_element_type=jnp.float32).astype(out_ref.dtype)


def order_values(findex, order, own, other):
    rows = order.shape[0]
    slots, part, width = own.shape
    step = math.gcd(slots, 2)
    place = jnp.stack([findex ^ s for s in range(slots)]).astype(jnp.int32)

    def block(k):
        return pl.BlockSpec((1, part, width), lambda s, place: (place[s * step + k], 0, 0))

    return pl.pallas_call(
        value_kernel,
        grid_spec=pltpu.PrefetchScalarGridSpec(
            num_scalar_prefetch=1,
            grid=(slots // step,),
            in_specs=[pl.BlockSpec((rows, rows), lambda s, place: (0, 0))]
            + [block(k) for k in range(step)] * 2,
            out_specs=pl.BlockSpec((rows, step * width), lambda s, place: (0, s)),
        ),
        out_shape=jax.ShapeDtypeStruct((rows, slots * width), jnp.bfloat16),
        compiler_params=pltpu.CompilerParams(vmem_limit_bytes=VMEM_BYTES),
        name="order_values",
    )(place, order, *[own] * step, *[other] * step)


def score_kernel(count, order_ref, key_t_ref, *refs):
    queries, (out_ref, mark_ref) = refs[:count], refs[-2:]
    mark_ref[...] = jnp.zeros_like(mark_ref)
    stacked = jnp.concatenate([query[...] for query in queries], axis=0)
    chosen = jnp.dot(order_ref[...], stacked, preferred_element_type=jnp.float32).astype(jnp.bfloat16)
    for head in range(stacked.shape[1] // DH):
        products = jnp.dot(
            chosen[:, head * DH : (head + 1) * DH], key_t_ref[...], preferred_element_type=jnp.float32
        )
        out_ref[0, head] = (products * DH ** (-0.5)).astype(out_ref.dtype)


def score_heads(order, key_t, heads, start, count, queries, earlier, after=()):
    rows = order.shape[0]
    step = math.gcd(count, 4)

    def block(query, first):
        return pl.BlockSpec((query.shape[0], step * DH), lambda j: (0, first // step + j))

    return pl.pallas_call(
        functools.partial(score_kernel, len(queries)),
        grid=(count // step,),
        in_specs=[
            pl.BlockSpec((rows, rows), lambda j: (0, 0)),
            pl.BlockSpec((DH, rows), lambda j: (0, 0)),
        ]
        + [block(query, first) for query, first in queries]
        + [pl.BlockSpec(memory_space=pl.ANY)] * (len(earlier) + len(after)),
        out_specs=[
            pl.BlockSpec((1, step, rows, rows), lambda j: (0, start // step + j, 0, 0)),
            pl.BlockSpec((8, DH), lambda j: (0, 0)),
        ],
        out_shape=[
            jax.ShapeDtypeStruct((1, heads, rows, rows), jnp.bfloat16),
            jax.ShapeDtypeStruct((8, DH), jnp.float32),
        ],
        input_output_aliases={2 + len(queries): 0} if earlier else {},
        compiler_params=pltpu.CompilerParams(vmem_limit_bytes=VMEM_BYTES),
        cost_estimate=LIGHT,
        name="score_heads",
    )(order, key_t, *[query for query, _ in queries], *earlier, *after)


def body(hidden, w_query, w_key, w_value, canary_rows, positions):
    shards = lax.axis_size("fsdp")
    findex = lax.axis_index("fsdp")
    tps = lax.axis_size("tp")
    tindex = lax.axis_index("tp")
    rindex = lax.axis_index("rep")
    local, depth = hidden.shape
    half = local // 2
    rows = local * tps
    head_cols = w_query.shape[1] // shards
    heads_here = head_cols // DH
    group = HQ // KV
    assert shards & (shards - 1) == 0 and lax.axis_size("rep") == 2

    def swap(x, bit):
        return lax.ppermute(x, "fsdp", [(i, i ^ bit) for i in range(shards)])

    def other_core(x):
        return lax.ppermute(x, "rep", [(0, 1), (1, 0)])

    def low(x):
        return x.astype(jnp.bfloat16)

    odd = list(range(3, shards, 2)) + [1]
    even = list(range(2, shards, 2))
    fast_pair = heads_here == group

    def spread(live):
        terms, first = [], None
        bit = 2
        while bit < shards:
            sent = [x for x in sorted(live) if x & bit]
            pack = jnp.stack([low(live[x]) for x in sent])
            first = pack if first is None else first
            landed = swap(pack, bit)
            for k, x in enumerate(sent):
                if x == bit:
                    terms.append(landed)
                else:
                    live[x ^ bit] = live[x ^ bit] + landed[k].astype(jnp.float32)
                del live[x]
            bit *= 2
        return terms, first

    blocks = [hidden] + [
        lax.ppermute(hidden, "tp", [(i, (i - b) % tps) for i in range(tps)]) for b in range(1, tps)
    ]

    block_ids = ((tindex + jnp.arange(tps, dtype=jnp.int32)) % tps * local)[:, None]
    own_ids = (block_ids + rindex * half + jnp.arange(half, dtype=jnp.int32)[None]).reshape(-1)
    other_ids = (block_ids + (1 - rindex) * half + jnp.arange(half, dtype=jnp.int32)[None]).reshape(-1)
    ids = jnp.concatenate([own_ids, other_ids])
    own_positions = jnp.sum(
        jnp.where(own_ids[:, None] == canary_rows[None, :], positions[None, :], 0), axis=1
    )
    cosine, sine = rope_tables(own_positions)

    tile = min(1024, head_cols)

    def project(slots, blocks, width, after=(), cost=LIGHT, by_slot=False, near=False):
        keep, gives = project_query(
            rindex, findex, slots, blocks, w_query, head_cols, tile, width, after, cost, by_slot, near
        )
        return keep, [other_core(give) for give in gives], gives[0]

    def rotate(b, start, stop, terms, behind):
        table = slice(b * half, (b + 1) * half)
        keep, slot, got = owns[b]
        added = [(keep, slot, start)] + terms
        gots = segments(got, start, stop)
        turned = sum_and_rotate(cosine[table], sine[table], added, gots, stop - start, behind)
        return turned, other_core(turned)

    def add_even(b, start, cols, pair, behind):
        if shards == 2:
            return [], behind
        keep, got = evens[b]
        summed = add_rows(
            0, len(even), half, 0, keep, got, start, cols, pair, len(odd), (fars[b],), behind
        )
        terms, first = spread({x: summed[k] for k, x in enumerate(even)})
        return [(term, 0, 0) for term in terms], (first,)

    last = tps - 1
    bounds = [0, head_cols] if tile == head_cols else [0, head_cols * 3 // 4, head_cols]
    ranges = list(zip(bounds, bounds[1:]))
    placed = in_hbm(blocks[:1]) + blocks[1:]
    evens, owns, fars, terms, pair, after = [], [], [], [], (), ()
    for b, block in enumerate(placed):
        if fast_pair and b == last:
            slots = odd + even + [0]
            pair_keep, give = project_pair(rindex, findex, slots, placed, w_key, w_value, after)
            pair = (pair_keep, other_core(give))
            after = (give,)
        sent = odd[:-1] if b == last else odd
        odd_keep, odd_got, given = project(sent, [block], tile, after, near=True)
        odd_sent = add_rows(0, len(sent), half, 0, odd_keep, odd_got, 0, head_cols, pair, near=True)
        fars.append(swap(odd_sent, 1))
        after = (odd_sent,)
        if b > 0:
            added, after = add_even(b - 1, 0, head_cols, (), after)
            terms.append([(fars[b - 1], len(odd) - 1, 0)] + added)
            after = (odd_sent,) + after
        if b < last:
            keep, got, given = project(even + [0], [block], head_cols, after, LIGHT, True)
            evens.append((keep, got[:1] if len(even) == 1 else [jnp.concatenate(got[:-1])]))
            owns.append((keep, len(even), got[-1:]))
        else:
            keep, got, given = project(even, [block], tile, after, HEAVY)
            evens.append((keep, got))
        after = (given,)
    near_keep, near_got, given = project([1], placed[last:], tile, after)
    after = (given,)
    parts, behind = [], tuple(term[0] for row in terms for term in row[1:])
    for start, stop in ranges:
        paired = () if start else pair
        near_sent = add_rows(
            0, 1, half, 0, near_keep, near_got, start, stop - start, paired, len(odd) - 1, (), after
        )
        parts.append([(swap(near_sent, 1), 0, 0)])
        after = (near_sent,)
    after = after + behind
    for part, (start, stop) in zip(parts, ranges):
        added, after = add_even(last, start, stop - start, () if start else pair, after)
        part += added
    keep, got, _ = project([0], placed[last:], tile, after, HEAVY)
    owns.append((keep, 0, got))

    if fast_pair:
        width = 2 * DH * tps
        pieces = [(array, shards - 1, 0) for array in pair]
        pieces += [(term, 0, bounds[1]) for term, _, _ in parts[0]]
        key_rot, held = split_and_rotate(cosine, sine, pieces, width, after)
    else:
        x = jnp.concatenate(blocks, axis=0)
        key_sum, value_sum = lax.psum(
            (
                jnp.dot(x, w_key, preferred_element_type=jnp.float32),
                jnp.dot(x, w_value, preferred_element_type=jnp.float32),
            ),
            ("fsdp", "rep"),
        )

        def of_core(y, core):
            parts = y.reshape(tps, 2, half, -1)
            return lax.dynamic_index_in_dim(parts, core, 1, keepdims=False).reshape(tps * half, -1)

        mine = lax.dynamic_slice_in_dim(key_sum, findex * heads_here // group * DH, DH, 1)
        key_own = of_core(mine, rindex)
        key_rot = sum_and_rotate(cosine, sine, [(key_own[None], 0, 0)], [], DH, after)
        value_rows = low(jnp.concatenate([of_core(value_sum, rindex), of_core(value_sum, 1 - rindex)]))

    order, key_t = prepare(canary_rows, ids, key_rot, other_core(key_rot))
    if not fast_pair:
        values = low(jnp.dot(order, value_rows, preferred_element_type=jnp.float32))

    rotated = [rotate(b, 0, head_cols, terms[b], after) for b in range(last)]
    scores, mark = (), ()
    for p, (start, stop) in enumerate(ranges):
        turned = rotate(last, start, stop, parts[p], mark or tuple(owns[last][2][1:]))
        first = start // DH
        queries = [(row[0], first) for row in rotated] + [(turned[0], 0)]
        queries += [(row[1], first) for row in rotated] + [(turned[1], 0)]
        behind = in_hbm([values]) if p > 0 else ()
        *scores, mark = score_heads(
            order, key_t, heads_here, first, (stop - start) // DH, queries, scores, behind
        )
        mark = (mark,)
        if fast_pair and p == 0:
            held = stack_slots([held] + [swap(held, x) for x in range(1, shards)], mark)
            values = order_values(findex, order, held, other_core(held))
    return (scores[0], values)


def solution(mesh):
    in_specs = (
        P(("groups", "tp"), ("fsdp", "rep")),
        P(("fsdp", "rep"), "tp"),
        P(("fsdp", "rep"), "tp"),
        P(("fsdp", "rep"), "tp"),
        P("groups"),
        P("groups"),
    )
    out_specs = (P("tp", "fsdp", "groups", None), P("groups", "tp"))
    return jax.shard_map(body, mesh=mesh, in_specs=in_specs, out_specs=out_specs, check_vma=False)
```

```python
import functools
import math

import jax
import jax.numpy as jnp
from jax import lax
from jax.experimental import pallas as pl
from jax.experimental.pallas import tpu as pltpu
from jax.sharding import PartitionSpec as P

HQ = 128
KV = 8
DH = 128
VMEM_BYTES = 28 * 1024 * 1024
LIGHT = pl.CostEstimate(flops=1000, bytes_accessed=1000, transcendentals=0)
HEAVY = pl.CostEstimate(flops=10**11, bytes_accessed=10**8, transcendentals=0)


def in_hbm(arrays):
    return [pltpu.with_memory_space_constraint(x, pltpu.HBM) for x in arrays]


def rope_tables(positions):
    half = DH // 2
    expo = jnp.arange(half, dtype=jnp.float32) * (2.0 / DH)
    freq = jnp.power(jnp.float32(500000.0), -expo)
    wavelen = 2.0 * math.pi / freq
    smooth = (8192.0 / wavelen - 1.0) / 3.0
    mixed = (1.0 - smooth) * freq / 8.0 + smooth * freq
    freq = jnp.where(wavelen > 8192.0, freq / 8.0, jnp.where(wavelen < 2048.0, freq, mixed))
    angle = positions.astype(jnp.float32)[:, None] * freq[None, :]
    cosine, sine = jnp.cos(angle), jnp.sin(angle)
    return jnp.concatenate([cosine, cosine], axis=1), jnp.concatenate([-sine, sine], axis=1)


def ordered_rows(place_ref, x_refs, rows_ref):
    core = place_ref[0]
    half = x_refs[0].shape[0] // 2
    for b, x_ref in enumerate(x_refs):
        kept, given = b * half, (len(x_refs) + b) * half
        rows_ref[kept : kept + half] = x_ref[pl.ds(pl.multiple_of(core * half, 16), half)]
        rows_ref[given : given + half] = x_ref[pl.ds(pl.multiple_of((1 - core) * half, 16), half)]


def query_kernel(count, pieces, by_slot, place_ref, *refs):
    x_refs, w_ref = refs[:count], refs[count]
    keep_ref, *give_refs, rows_ref = refs[-2 - pieces :]
    tile = pl.program_id(1)
    size = give_refs[0].shape[2]
    each = keep_ref.shape[2] // size

    @pl.when((pl.program_id(0) == 0) & (tile == 0))
    def _():
        ordered_rows(place_ref, x_refs, rows_ref)

    result = jnp.dot(rows_ref[...], w_ref[...], preferred_element_type=jnp.float32)
    half = result.shape[0] // 2
    keep_ref[0] = result[:half]
    for j, give_ref in enumerate(give_refs):

        @pl.when(pl.program_id(0) == j if by_slot else (tile == j // each) | (pieces == 1))
        def _():
            start = j % each * size
            give_ref[0] = result[half:, start : start + size].astype(give_ref.dtype)


def project_query(rindex, findex, slots, blocks, w, cols, tile, width, after, cost, by_slot, near):
    rows, depth = blocks[0].shape
    count = len(blocks)
    half = rows // 2 * count
    tiles, pieces = cols // tile, len(slots) if by_slot else cols // width
    place = jnp.stack([rindex] + [findex ^ slot for slot in slots]).astype(jnp.int32)
    keep_spec = pl.BlockSpec((1, half, tile), lambda s, j, place: (s, 0, j))
    give_spec = pl.BlockSpec((1, half, width), lambda s, j, place: (s, 0, 0))

    def slot_spec(k):
        def index(s, j, place):
            return (0, 0, jnp.where(s < k, 0, jnp.where(s > k, tiles - 1, j)))

        return pl.BlockSpec((1, half, tile), index)

    give_specs = [keep_spec] if pieces == 1 else [give_spec] * pieces
    given = (len(slots), half, width)
    if by_slot:
        give_specs, given = [slot_spec(k) for k in range(pieces)], (1, half, cols)
    x_spec = pl.BlockSpec((rows, depth), lambda s, j, place: (0, 0), pipeline_mode=pl.Buffered(1))
    outs = pl.pallas_call(
        functools.partial(query_kernel, count, pieces, by_slot),
        grid_spec=pltpu.PrefetchScalarGridSpec(
            num_scalar_prefetch=1,
            grid=(len(slots), tiles),
            in_specs=[x_spec] * count
            + [pl.BlockSpec((depth, tile), lambda s, j, place: (0, place[1 + s] * tiles + j))]
            + [pl.BlockSpec(memory_space=pl.ANY)] * len(after),
            out_specs=[keep_spec] + give_specs,
            scratch_shapes=[pltpu.VMEM((2 * half, depth), w.dtype)],
        ),
        out_shape=[(jax.ShapeDtypeStruct if near else pltpu.HBM)((len(slots), half, cols), jnp.float32)]
        + [pltpu.HBM(given, jnp.bfloat16)] * pieces,
        compiler_params=pltpu.CompilerParams(vmem_limit_bytes=VMEM_BYTES),
        cost_estimate=cost,
        name="query_products",
    )(place, *blocks, *in_hbm([w, *after]))
    return outs[0], outs[1:]


def pair_kernel(count, place_ref, *refs):
    x_refs, (wk_ref, wv_ref) = refs[:count], refs[count : count + 2]
    keep_ref, give_ref, rows_ref = refs[-3:]

    @pl.when(pl.program_id(0) == 0)
    def _():
        ordered_rows(place_ref, x_refs, rows_ref)

    weights = jnp.concatenate([wk_ref[...], wv_ref[...]], axis=1)
    result = jnp.dot(rows_ref[...], weights, preferred_element_type=jnp.float32)
    half, width = x_refs[0].shape[0] // 2, weights.shape[1]
    for b in range(count):
        kept, given = b * half, (count + b) * half
        cols = slice(b * width, (b + 1) * width)
        keep_ref[0, :, cols] = result[kept : kept + half]
        give_ref[0, :, cols] = result[given : given + half].astype(give_ref.dtype)


def project_pair(rindex, findex, slots, blocks, w_key, w_value, after=()):
    rows, depth = blocks[0].shape
    count = len(blocks)
    place = jnp.stack([rindex] + [findex ^ slot for slot in slots]).astype(jnp.int32)
    weight = pl.BlockSpec((depth, DH), lambda s, place: (0, place[1 + s]))
    shape = (len(slots), rows // 2, 2 * DH * count)
    out = pl.BlockSpec((1,) + shape[1:], lambda s, place: (s, 0, 0))
    return pl.pallas_call(
        functools.partial(pair_kernel, count),
        grid_spec=pltpu.PrefetchScalarGridSpec(
            num_scalar_prefetch=1,
            grid=(len(slots),),
            in_specs=[pl.BlockSpec((rows, depth), lambda s, place: (0, 0))] * count
            + [weight, weight]
            + [pl.BlockSpec(memory_space=pl.ANY)] * len(after),
            out_specs=[out, out],
            scratch_shapes=[pltpu.VMEM((count * rows, depth), blocks[0].dtype)],
        ),
        out_shape=[
            pltpu.HBM(shape, jnp.float32),
            pltpu.HBM(shape, jnp.bfloat16),
        ],
        compiler_params=pltpu.CompilerParams(vmem_limit_bytes=VMEM_BYTES),
        cost_estimate=LIGHT,
        name="key_value_products",
    )(place, *blocks, *in_hbm([w_key, w_value, *after]))


def segments(arrays, start, stop):
    parts, first = [], 0
    for x in arrays:
        low, high = max(start, first) - first, min(stop - first, x.shape[2])
        if low < high:
            parts.append((x, high - low, low // (high - low)))
        first += x.shape[2]
    return parts


def add_kernel(gots, paired, extra, *refs):
    keep_ref, got_refs, out_ref = refs[0], refs[1 : 1 + gots], refs[-1]
    pair_refs = refs[1 + gots : 1 + gots + 2 * paired]
    landed_refs = refs[1 + gots + 2 * paired :][: extra * (1 + paired)]
    cols = sum(got_ref.shape[2] for got_ref in got_refs)

    def total(first, second, landed):
        value = first + second.astype(jnp.float32)
        for term in landed:
            value = value + term.astype(jnp.float32)
        return value.astype(out_ref.dtype)

    start = 0
    for got_ref in got_refs:
        part = slice(start, start + got_ref.shape[2])
        start = part.stop
        landed = [landed_refs[0][0, :, part]] if extra else []
        out_ref[0, :, part] = total(keep_ref[0, :, part], got_ref[0], landed)
    if paired:
        landed = [landed_refs[1][0]] if extra else []
        out_ref[0, :, cols:] = total(pair_refs[0][0], pair_refs[1][0], landed)


def add_rows(first, count, rows, b, keep, gots, start, cols, pair=(), slot=0, landed=(), after=(), near=False):
    whole = keep.shape[2]
    more = pair[0].shape[2] if pair else 0
    keep_spec = pl.BlockSpec((1, rows, cols), lambda s: (first + s, b, start // cols))
    gots = segments(gots, start, start + cols)

    def got_spec(width, column):
        return pl.BlockSpec((1, rows, width), lambda s: (first + s, b, column))

    pair_spec = pl.BlockSpec((1, rows, more), lambda s: (slot + s, 0, 0))
    landed_specs = [pl.BlockSpec((1, rows, cols), lambda s: (s, 0, start // cols))]
    if pair:
        landed_specs.append(pl.BlockSpec((1, rows, more), lambda s: (s, 0, whole // more)))
    landed_specs = landed_specs * len(landed)
    return pl.pallas_call(
        functools.partial(add_kernel, len(gots), len(pair) // 2, len(landed)),
        grid=(count,),
        in_specs=[keep_spec]
        + [got_spec(width, column) for _, width, column in gots]
        + [pair_spec] * len(pair)
        + landed_specs
        + [pl.BlockSpec(memory_space=pl.ANY)] * len(after),
        out_specs=pl.BlockSpec((1, rows, cols + more), lambda s: (s, 0, 0)),
        out_shape=pltpu.HBM((count, rows, cols + more), jnp.bfloat16),
        compiler_params=pltpu.CompilerParams(vmem_limit_bytes=VMEM_BYTES),
        cost_estimate=LIGHT,
        name="add_rows",
    )(
        *([keep] if near else in_hbm([keep])),
        *[got for got, _, _ in gots],
        *in_hbm(pair[:1]),
        *pair[1:],
        *(list(landed) * (2 if pair else 1)),
        *in_hbm(after[:1]),
        *after[1:],
    )


def rotate_kernel(count, pieces, cos_ref, sin_ref, *refs):
    terms, gots, out_ref = refs[:count], refs[count : count + pieces], refs[-1]
    cosine, sine = cos_ref[...], sin_ref[...]
    start = 0
    for got in gots or terms[:1]:
        cols = slice(start, start + got.shape[2])
        start = cols.stop
        total = terms[0][0, :, cols].astype(jnp.float32)
        for term in terms[1:]:
            total = total + term[0, :, cols].astype(jnp.float32)
        if gots:
            total = total + got[0].astype(jnp.float32)
        for head in range(total.shape[1] // DH):
            part = total[:, head * DH : (head + 1) * DH]
            turned = pltpu.roll(part, DH // 2, axis=1)
            value = (part * cosine + turned * sine).astype(out_ref.dtype)
            out_ref[:, cols.start + head * DH : cols.start + (head + 1) * DH] = value


def sum_and_rotate(cosine, sine, terms, gots, cols, after=()):
    rows = cosine.shape[0]
    table = pl.BlockSpec((rows, DH), lambda j: (0, 0))

    def block(width, slot, column):
        return pl.BlockSpec((1, rows, width), lambda j: (slot, 0, column))

    return pl.pallas_call(
        functools.partial(rotate_kernel, len(terms), len(gots)),
        grid=(1,),
        in_specs=[table, table]
        + [block(cols, slot, start // cols) for _, slot, start in terms]
        + [block(width, 0, column) for _, width, column in gots]
        + [pl.BlockSpec(memory_space=pl.ANY)] * len(after),
        out_specs=pl.BlockSpec((rows, cols), lambda j: (0, 0)),
        out_shape=jax.ShapeDtypeStruct((rows, cols), jnp.bfloat16),
        compiler_params=pltpu.CompilerParams(vmem_limit_bytes=VMEM_BYTES),
        cost_estimate=LIGHT,
        name="sum_and_rotate",
    )(
        cosine,
        sine,
        *in_hbm([terms[0][0]]),
        *[term[0] for term in terms[1:]],
        *[got for got, _, _ in gots],
        *after,
    )


def split_kernel(count, cos_ref, sin_ref, *refs):
    terms, (key_ref, value_ref) = refs[:count], refs[-2:]
    total = terms[0][0].astype(jnp.float32)
    for term in terms[1:]:
        total = total + term[0].astype(jnp.float32)
    half = total.shape[0]
    for b in range(total.shape[1] // (2 * DH)):
        rows = slice(b * half, (b + 1) * half)
        key = total[:, 2 * b * DH : (2 * b + 1) * DH]
        turned = pltpu.roll(key, DH // 2, axis=1)
        key_ref[rows] = (key * cos_ref[rows] + turned * sin_ref[rows]).astype(key_ref.dtype)
        value_ref[0, rows] = total[:, (2 * b + 1) * DH : (2 * b + 2) * DH].astype(value_ref.dtype)


def split_and_rotate(cosine, sine, terms, width, after):
    rows = cosine.shape[0]
    half = terms[0][0].shape[1]
    table = pl.BlockSpec((rows, DH), lambda j: (0, 0))

    def block(slot, start):
        return pl.BlockSpec((1, half, width), lambda j: (slot, 0, start // width))

    return pl.pallas_call(
        functools.partial(split_kernel, len(terms)),
        grid=(1,),
        in_specs=[table, table]
        + [block(slot, start) for _, slot, start in terms]
        + [pl.BlockSpec(memory_space=pl.ANY)] * len(after),
        out_specs=[table, pl.BlockSpec((1, rows, DH), lambda j: (0, 0, 0))],
        out_shape=[
            jax.ShapeDtypeStruct((rows, DH), jnp.bfloat16),
            jax.ShapeDtypeStruct((1, rows, DH), jnp.bfloat16),
        ],
        compiler_params=pltpu.CompilerParams(vmem_limit_bytes=VMEM_BYTES),
        cost_estimate=LIGHT,
        name="split_and_rotate",
    )(cosine, sine, *in_hbm([terms[0][0]]), *[term for term, _, _ in terms[1:]], *after)


def prepare_kernel(canary_ref, ids_ref, own_ref, other_ref, order_ref, key_t_ref):
    order = jnp.where(canary_ref[...] == ids_ref[...], 1.0, 0.0).astype(jnp.bfloat16)
    order_ref[...] = order
    key = jnp.concatenate([own_ref[...], other_ref[...]], axis=0)
    key_t_ref[...] = jnp.dot(order, key, preferred_element_type=jnp.float32).T.astype(jnp.bfloat16)


def prepare(canary_rows, ids, own, other):
    rows = ids.shape[0]
    return pl.pallas_call(
        prepare_kernel,
        out_shape=[
            jax.ShapeDtypeStruct((rows, rows), jnp.bfloat16),
            jax.ShapeDtypeStruct((DH, rows), jnp.bfloat16),
        ],
        compiler_params=pltpu.CompilerParams(vmem_limit_bytes=VMEM_BYTES),
        name="order_and_keys",
    )(canary_rows.reshape(rows, 1), ids.reshape(1, rows), own, other)


def stack_kernel(count, *refs):
    out_ref, start = refs[-1], 0
    for ref in refs[:count]:
        out_ref[start : start + ref.shape[0]] = ref[...]
        start += ref.shape[0]


def stack_slots(arrays, after):
    slots = sum(x.shape[0] for x in arrays)
    shape = (slots,) + arrays[0].shape[1:]
    return pl.pallas_call(
        functools.partial(stack_kernel, len(arrays)),
        grid=(1,),
        in_specs=[pl.BlockSpec(x.shape, lambda j: (0, 0, 0)) for x in arrays]
        + [pl.BlockSpec(memory_space=pl.ANY)] * len(after),
        out_specs=pl.BlockSpec(shape, lambda j: (0, 0, 0)),
        out_shape=jax.ShapeDtypeStruct(shape, arrays[0].dtype),
        compiler_params=pltpu.CompilerParams(vmem_limit_bytes=VMEM_BYTES),
        cost_estimate=LIGHT,
        name="stack_slots",
    )(*arrays, *after)


def value_kernel(place_ref, order_ref, *refs):
    *slots, out_ref = refs
    own, other = slots[: len(slots) // 2], slots[len(slots) // 2 :]
    sides = [jnp.concatenate([x[0] for x in side], axis=1) for side in (own, other)]
    rows = jnp.concatenate(sides, axis=0)
    out_ref[...] = jnp.dot(order_ref[...], rows, preferred_element_type=jnp.float32).astype(out_ref.dtype)


def order_values(findex, order, own, other):
    rows = order.shape[0]
    slots, part, width = own.shape
    step = math.gcd(slots, 2)
    place = jnp.stack([findex ^ s for s in range(slots)]).astype(jnp.int32)

    def block(k):
        return pl.BlockSpec((1, part, width), lambda s, place: (place[s * step + k], 0, 0))

    return pl.pallas_call(
        value_kernel,
        grid_spec=pltpu.PrefetchScalarGridSpec(
            num_scalar_prefetch=1,
            grid=(slots // step,),
            in_specs=[pl.BlockSpec((rows, rows), lambda s, place: (0, 0))]
            + [block(k) for k in range(step)] * 2,
            out_specs=pl.BlockSpec((rows, step * width), lambda s, place: (0, s)),
        ),
        out_shape=jax.ShapeDtypeStruct((rows, slots * width), jnp.bfloat16),
        compiler_params=pltpu.CompilerParams(vmem_limit_bytes=VMEM_BYTES),
        name="order_values",
    )(place, order, *[own] * step, *[other] * step)


def score_kernel(count, order_ref, key_t_ref, *refs):
    queries, (out_ref, mark_ref) = refs[:count], refs[-2:]
    mark_ref[...] = jnp.zeros_like(mark_ref)
    stacked = jnp.concatenate([query[...] for query in queries], axis=0)
    chosen = jnp.dot(order_ref[...], stacked, preferred_element_type=jnp.float32).astype(jnp.bfloat16)
    for head in range(stacked.shape[1] // DH):
        products = jnp.dot(
            chosen[:, head * DH : (head + 1) * DH], key_t_ref[...], preferred_element_type=jnp.float32
        )
        out_ref[0, head] = (products * DH ** (-0.5)).astype(out_ref.dtype)


def score_heads(order, key_t, heads, start, count, queries, earlier, after=()):
    rows = order.shape[0]
    step = math.gcd(count, 4)

    def block(query, first):
        return pl.BlockSpec((query.shape[0], step * DH), lambda j: (0, first // step + j))

    return pl.pallas_call(
        functools.partial(score_kernel, len(queries)),
        grid=(count // step,),
        in_specs=[
            pl.BlockSpec((rows, rows), lambda j: (0, 0)),
            pl.BlockSpec((DH, rows), lambda j: (0, 0)),
        ]
        + [block(query, first) for query, first in queries]
        + [pl.BlockSpec(memory_space=pl.ANY)] * (len(earlier) + len(after)),
        out_specs=[
            pl.BlockSpec((1, step, rows, rows), lambda j: (0, start // step + j, 0, 0)),
            pl.BlockSpec((8, DH), lambda j: (0, 0)),
        ],
        out_shape=[
            jax.ShapeDtypeStruct((1, heads, rows, rows), jnp.bfloat16),
            jax.ShapeDtypeStruct((8, DH), jnp.float32),
        ],
        input_output_aliases={2 + len(queries): 0} if earlier else {},
        compiler_params=pltpu.CompilerParams(vmem_limit_bytes=VMEM_BYTES),
        cost_estimate=LIGHT,
        name="score_heads",
    )(order, key_t, *[query for query, _ in queries], *earlier, *after)


def body(hidden, w_query, w_key, w_value, canary_rows, positions):
    shards = lax.axis_size("fsdp")
    findex = lax.axis_index("fsdp")
    tps = lax.axis_size("tp")
    tindex = lax.axis_index("tp")
    rindex = lax.axis_index("rep")
    local, depth = hidden.shape
    half = local // 2
    rows = local * tps
    head_cols = w_query.shape[1] // shards
    heads_here = head_cols // DH
    group = HQ // KV
    assert shards & (shards - 1) == 0 and lax.axis_size("rep") == 2

    def swap(x, bit):
        return lax.ppermute(x, "fsdp", [(i, i ^ bit) for i in range(shards)])

    def other_core(x):
        return lax.ppermute(x, "rep", [(0, 1), (1, 0)])

    def low(x):
        return x.astype(jnp.bfloat16)

    odd = list(range(3, shards, 2)) + [1]
    even = list(range(2, shards, 2))
    fast_pair = heads_here == group

    def spread(live):
        terms, first = [], None
        bit = 2
        while bit < shards:
            sent = [x for x in sorted(live) if x & bit]
            pack = jnp.stack([low(live[x]) for x in sent])
            first = pack if first is None else first
            landed = swap(pack, bit)
            for k, x in enumerate(sent):
                if x == bit:
                    terms.append(landed)
                else:
                    live[x ^ bit] = live[x ^ bit] + landed[k].astype(jnp.float32)
                del live[x]
            bit *= 2
        return terms, first

    blocks = [hidden] + [
        lax.ppermute(hidden, "tp", [(i, (i - b) % tps) for i in range(tps)]) for b in range(1, tps)
    ]

    block_ids = ((tindex + jnp.arange(tps, dtype=jnp.int32)) % tps * local)[:, None]
    own_ids = (block_ids + rindex * half + jnp.arange(half, dtype=jnp.int32)[None]).reshape(-1)
    other_ids = (block_ids + (1 - rindex) * half + jnp.arange(half, dtype=jnp.int32)[None]).reshape(-1)
    ids = jnp.concatenate([own_ids, other_ids])
    own_positions = jnp.sum(
        jnp.where(own_ids[:, None] == canary_rows[None, :], positions[None, :], 0), axis=1
    )
    cosine, sine = rope_tables(own_positions)

    tile = min(1024, head_cols)

    def project(slots, blocks, width, after=(), cost=LIGHT, by_slot=False, near=False):
        keep, gives = project_query(
            rindex, findex, slots, blocks, w_query, head_cols, tile, width, after, cost, by_slot, near
        )
        return keep, [other_core(give) for give in gives], gives[0]

    def rotate(b, start, stop, terms, behind):
        table = slice(b * half, (b + 1) * half)
        keep, slot, got = owns[b]
        added = [(keep, slot, start)] + terms
        gots = segments(got, start, stop)
        turned = sum_and_rotate(cosine[table], sine[table], added, gots, stop - start, behind)
        return turned, other_core(turned)

    def add_even(b, start, cols, pair, behind):
        if shards == 2:
            return [], behind
        keep, got = evens[b]
        summed = add_rows(
            0, len(even), half, 0, keep, got, start, cols, pair, len(odd), (fars[b],), behind, b == last
        )
        terms, first = spread({x: summed[k] for k, x in enumerate(even)})
        return [(term, 0, 0) for term in terms], (first,)

    last = tps - 1
    bounds = [0, head_cols] if tile == head_cols else [0, head_cols * 3 // 4, head_cols]
    ranges = list(zip(bounds, bounds[1:]))
    placed = in_hbm(blocks[:1]) + blocks[1:]
    evens, owns, fars, terms, pair, after = [], [], [], [], (), ()
    for b, block in enumerate(placed):
        if fast_pair and b == last:
            slots = odd + even + [0]
            pair_keep, give = project_pair(rindex, findex, slots, placed, w_key, w_value, after)
            pair = (pair_keep, other_core(give))
            after = (give,)
        sent = odd[:-1] if b == last else odd
        odd_keep, odd_got, given = project(sent, [block], tile, after, near=True)
        odd_sent = add_rows(0, len(sent), half, 0, odd_keep, odd_got, 0, head_cols, pair, near=True)
        fars.append(swap(odd_sent, 1))
        after = (odd_sent,)
        if b > 0:
            added, after = add_even(b - 1, 0, head_cols, (), after)
            terms.append([(fars[b - 1], len(odd) - 1, 0)] + added)
            after = (odd_sent,) + after
        if b < last:
            keep, got, given = project(even + [0], [block], head_cols, after, LIGHT, True)
            evens.append((keep, got[:1] if len(even) == 1 else [jnp.concatenate(got[:-1])]))
            owns.append((keep, len(even), got[-1:]))
        else:
            keep, got, given = project(even, [block], tile, after, HEAVY, near=True)
            evens.append((keep, got))
        after = (given,)
    near_keep, near_got, given = project([1], placed[last:], tile, after)
    after = (given,)
    parts, behind = [], tuple(term[0] for row in terms for term in row[1:])
    for start, stop in ranges:
        paired = () if start else pair
        near_sent = add_rows(
            0, 1, half, 0, near_keep, near_got, start, stop - start, paired, len(odd) - 1, (), after
        )
        parts.append([(swap(near_sent, 1), 0, 0)])
        after = (near_sent,)
    after = after + behind
    for part, (start, stop) in zip(parts, ranges):
        added, after = add_even(last, start, stop - start, () if start else pair, after)
        part += added
    keep, got, _ = project([0], placed[last:], tile, after, HEAVY)
    owns.append((keep, 0, got))

    if fast_pair:
        width = 2 * DH * tps
        pieces = [(array, shards - 1, 0) for array in pair]
        pieces += [(term, 0, bounds[1]) for term, _, _ in parts[0]]
        key_rot, held = split_and_rotate(cosine, sine, pieces, width, after)
    else:
        x = jnp.concatenate(blocks, axis=0)
        key_sum, value_sum = lax.psum(
            (
                jnp.dot(x, w_key, preferred_element_type=jnp.float32),
                jnp.dot(x, w_value, preferred_element_type=jnp.float32),
            ),
            ("fsdp", "rep"),
        )

        def of_core(y, core):
            parts = y.reshape(tps, 2, half, -1)
            return lax.dynamic_index_in_dim(parts, core, 1, keepdims=False).reshape(tps * half, -1)

        mine = lax.dynamic_slice_in_dim(key_sum, findex * heads_here // group * DH, DH, 1)
        key_own = of_core(mine, rindex)
        key_rot = sum_and_rotate(cosine, sine, [(key_own[None], 0, 0)], [], DH, after)
        value_rows = low(jnp.concatenate([of_core(value_sum, rindex), of_core(value_sum, 1 - rindex)]))

    order, key_t = prepare(canary_rows, ids, key_rot, other_core(key_rot))
    if not fast_pair:
        values = low(jnp.dot(order, value_rows, preferred_element_type=jnp.float32))

    rotated = [rotate(b, 0, head_cols, terms[b], after) for b in range(last)]
    scores, mark = (), ()
    for p, (start, stop) in enumerate(ranges):
        turned = rotate(last, start, stop, parts[p], mark or tuple(owns[last][2][1:]))
        first = start // DH
        queries = [(row[0], first) for row in rotated] + [(turned[0], 0)]
        queries += [(row[1], first) for row in rotated] + [(turned[1], 0)]
        behind = in_hbm([values]) if p > 0 else ()
        *scores, mark = score_heads(
            order, key_t, heads_here, first, (stop - start) // DH, queries, scores, behind
        )
        mark = (mark,)
        if fast_pair and p == 0:
            held = stack_slots([held] + [swap(held, x) for x in range(1, shards)], mark)
            values = order_values(findex, order, held, other_core(held))
    return (scores[0], values)


def solution(mesh):
    in_specs = (
        P(("groups", "tp"), ("fsdp", "rep")),
        P(("fsdp", "rep"), "tp"),
        P(("fsdp", "rep"), "tp"),
        P(("fsdp", "rep"), "tp"),
        P("groups"),
        P("groups"),
    )
    out_specs = (P("tp", "fsdp", "groups", None), P("groups", "tp"))
    return jax.shard_map(body, mesh=mesh, in_specs=in_specs, out_specs=out_specs, check_vma=False)
```
